32 devices in a mesh: grp: 2 (over y), seq: 4 (over x, core), mlp: 4 (over z).
Axes of the slice: x: 2, y: 2, z: 4, core: 2. Of those that a mesh axis runs over, the one named last changes fastest.
Arguments:
- inputs: bfloat16 [16, 1024, 768], P(('grp', 'mlp'), 'seq'), parts along dimension 0, may hold values from -6 to 6
- condition: bfloat16 [16, 128], P(('grp', 'mlp')), parts along dimension 0, may hold values from -6 to 6
- attn_gain: float32 [768], replicated, may hold values from 0.1 to 1.9
- ada_weight: bfloat16 [128, 4608], replicated, may hold values from -0.25 to 0.25
- ada_bias: float32 [4608], replicated, may hold values from -3 to 3
- qkv_weight: bfloat16 [768, 2304], replicated, may hold values from -0.21875 to 0.21875
- out_weight: bfloat16 [768, 768], replicated, may hold values from -0.625 to 0.625
- ffn_gain: float32 [768], replicated, may hold values from 0.1 to 1.9
- up_weight: bfloat16 [768, 3072], P(None, 'mlp'), may hold values from -0.21875 to 0.21875
- up_bias: float32 [3072], P('mlp'), may hold values from -3 to 3
- down_weight: bfloat16 [3072, 768], P('mlp'), may hold values from -0.21875 to 0.21875
- down_bias: float32 [768], replicated, may hold values from -4 to 4
- cotangent: bfloat16 [16, 1024, 768], P(('grp', 'mlp'), 'seq'), parts along dimension 0, may hold values from -6 to 6
Outputs:
- output: float32 [16, 1024, 768], P(('grp', 'mlp'), 'seq'), parts along dimension 0
- grad_inputs: float32 [16, 1024, 768], P(('grp', 'mlp'), 'seq'), parts along dimension 0
- grad_condition: float32 [16, 128], P(('grp', 'mlp')), parts along dimension 0
- grad_attn_gain: float32 [1536], P('grp'), parts along dimension 0
- grad_ada_weight: float32 [256, 4608], P('grp'), parts along dimension 0
- grad_ada_bias: float32 [9216], P('grp'), parts along dimension 0
- grad_qkv_weight: float32 [1536, 2304], P('grp'), parts along dimension 0
- grad_out_weight: float32 [1536, 768], P('grp'), parts along dimension 0
- grad_ffn_gain: float32 [1536], P('grp'), parts along dimension 0
- grad_up_weight: float32 [1536, 3072], P('grp', 'mlp'), parts along dimension 0
- grad_up_bias: float32 [6144], P(('grp', 'mlp')), parts along dimension 0
- grad_down_weight: float32 [6144, 768], P(('grp', 'mlp')), parts along dimension 0
- grad_down_bias: float32 [1536], P('grp'), parts along dimension 0
The draws below stay inside these ranges and needn't reach their ends.
There are 2 independent parts, one for each index of `grp`. The reference program is written for one: setup_inputs(seed, part) draws one part's arguments, and reference() takes and returns one part's arrays. A program takes and returns all parts, laid end to end along the dimension named above; an argument that names none is the same for every part. Nothing has to cross between parts.
All inputs are finite; a program needn't handle non-finite values.
Results may differ from the reference program's by a relative error of at most 0.019.
The reference program's roundings to bfloat16 on the way count: a program that leaves them out, or rounds other values in their place, can miss the bound.
Values may be sent and summed in bfloat16 or wider, within the bound.
A program may use at most 256 MiB of HBM per device.

```python
import math
import jax
import jax.numpy as jnp
from jax import lax

D = 768
HEADS = 12
HEAD_DIM = 64
FF = 3072
COND = 128
LEN = 1024
SEQS = 8


def steps_of(rng, extent, shards, smallest, largest):
    def one(position, blocks):
        heights = jax.random.uniform(jax.random.fold_in(jax.random.fold_in(rng, 6), position), (blocks,), jnp.float32, smallest / len(shards), largest / len(shards))
        return jnp.repeat(jnp.exp(heights), extent[position] // blocks).reshape((-1,) + (1,) * (len(extent) - position - 1))

    level = one(*shards[0])
    for cut in shards[1:]:
        level = level * one(*cut)
    return level


def centred(own_key, shape, spread, reach, shards=(), kind=jnp.bfloat16):
    result = jax.random.normal(own_key, shape, jnp.float32) * spread
    if len(shards) > 0:
        result = steps_of(own_key, shape, shards, -0.22, 0.18) * result
    return jnp.clip(result, min=-reach, max=reach).astype(kind)


def setup_inputs(seed: int = 0, part: int = 0) -> dict:
    key_list = jax.random.split(jax.random.key(seed), 14)
    part_keys = jax.random.split(jax.random.fold_in(key_list[13], part), 14)
    inputs = centred(part_keys[0], (SEQS, LEN, D), 1.0, 6.0, ((0, 4), (1, 4)))
    condition = centred(part_keys[1], (SEQS, COND), 1.0, 6.0, ((0, 4),))
    attn_gain = jnp.clip(1.0 + 0.18 * jax.random.normal(key_list[2], (D,), jnp.float32), 0.1, 1.9)
    ada_weight = centred(key_list[3], (COND, 6 * D), (4 * COND) ** -0.5, 0.25)
    ada_bias = centred(key_list[4], (6 * D,), 0.3, 3.0, (), jnp.float32)
    qkv_weight = centred(key_list[5], (D, 3 * D), D ** -0.5, 0.21875)
    out_weight = centred(key_list[6], (D, D), (max(D // 8, 1)) ** -0.5, 0.625)
    ffn_gain = jnp.clip(1.0 + 0.18 * jax.random.normal(key_list[7], (D,), jnp.float32), 0.1, 1.9)
    up_weight = centred(key_list[8], (D, FF), D ** -0.5, 0.21875, ((1, 4),))
    up_bias = centred(key_list[9], (FF,), 0.5, 3.0, ((0, 4),), jnp.float32)
    down_weight = centred(key_list[10], (FF, D), (FF // 4) ** -0.5, 0.21875, ((0, 4),))
    down_bias = centred(key_list[11], (D,), 1.0, 4.0, (), jnp.float32)
    cotangent = centred(part_keys[12], (SEQS, LEN, D), 1.0, 6.0, ((0, 4), (1, 4)))
    return dict(inputs=inputs, condition=condition, attn_gain=attn_gain, ada_weight=ada_weight, ada_bias=ada_bias, qkv_weight=qkv_weight, out_weight=out_weight, ffn_gain=ffn_gain, up_weight=up_weight, up_bias=up_bias, down_weight=down_weight, down_bias=down_bias, cotangent=cotangent)


@jax.custom_vjp
def low(v):
    return lax.optimization_barrier(v.astype(jnp.bfloat16)).astype(jnp.float32)

@jax.custom_vjp
def low_back(v):
    return v

def low_keep(v):
    return (low(v), None)

def low_pass(kept, grad):
    return (grad,)

def back_keep(v):
    return (v, None)

def back_low(kept, grad):
    return (low(grad),)
low.defvjp(low_keep, low_pass)
low_back.defvjp(back_keep, back_low)
highest = lax.Precision.HIGHEST
gelu_coef = 0.7978845608028654

def layer_norm(values):
    center = values - lax.optimization_barrier(jnp.mean(values, axis=-1, keepdims=True))
    return center * lax.rsqrt(lax.optimization_barrier(jnp.mean(center * center, axis=-1, keepdims=True)) + 1e-05)

def gelu_tanh(values):
    return 0.5 * values * (1.0 + jnp.tanh(gelu_coef * (values + 0.044715 * values * values * values)))

def rotary_tables(positions, head_size):
    half_dim = head_size // 2
    frequencies = jnp.power(10000.0, -2.0 * jnp.arange(half_dim, dtype=jnp.float32) / head_size)
    angles = positions[:, None] * frequencies[None, :]
    return (jnp.cos(angles), jnp.sin(angles))

def rotate(tensor, cos_tab, sine_tab):
    half_dim = tensor.shape[-1] // 2
    first_half = tensor[..., :half_dim]
    second_half = tensor[..., half_dim:]
    return jnp.concatenate([first_half * cos_tab - second_half * sine_tab, second_half * cos_tab + first_half * sine_tab], axis=-1)

def one_sequence(weights, packed):
    attn_gain, ada_weight, ada_bias, qkv_weight, out_weight, ffn_gain, up_weight, up_bias, down_weight, down_bias = weights
    x_seq, cond_seq = packed
    modulate = jnp.dot(cond_seq, ada_weight, precision=highest) + ada_bias
    shift_one, scale_one, gate_one, shift_two, scale_two, gate_two = [modulate[member * D:(member + 1) * D] for member in range(6)]
    attn_in = low(layer_norm(x_seq) * attn_gain * (1.0 + scale_one) + shift_one)
    projected = low_back(jnp.dot(attn_in, qkv_weight, precision=highest))
    cos_tab, sine_tab = rotary_tables(jnp.arange(LEN, dtype=jnp.float32), HEAD_DIM)
    cos_tab = cos_tab[:, None, :]
    sine_tab = sine_tab[:, None, :]
    queries = low(rotate(projected[:, :D].reshape(LEN, HEADS, HEAD_DIM), cos_tab, sine_tab))
    key_rot = low(rotate(projected[:, D:2 * D].reshape(LEN, HEADS, HEAD_DIM), cos_tab, sine_tab))
    value_low = low(projected[:, 2 * D:].reshape(LEN, HEADS, HEAD_DIM))
    query_len = math.gcd(LEN, 512)

    def attend(query_rows):
        scores = low_back(jnp.einsum('qhd,khd->hqk', query_rows, key_rot, precision=highest) * HEAD_DIM ** (-0.5))
        prob_rows = low(jax.nn.softmax(scores, axis=-1))
        return low(low_back(jnp.einsum('hqk,khd->qhd', prob_rows, value_low, precision=highest)))
    attn = lax.map(jax.checkpoint(attend), queries.reshape(LEN // query_len, query_len, HEADS, HEAD_DIM)).reshape(LEN, D)
    middle = x_seq + gate_one * low_back(jnp.dot(attn, out_weight, precision=highest))
    ffn_in = low(layer_norm(middle) * ffn_gain * (1.0 + scale_two) + shift_two)
    pre_act = low_back(jnp.dot(ffn_in, up_weight, precision=highest) + up_bias)
    act = low(gelu_tanh(pre_act))
    ffn_out = low_back(jnp.dot(act, down_weight, precision=highest) + down_bias)
    return middle + gate_two * ffn_out

def forward(x_all, cond_all, weights):

    def run_one(packed):
        return one_sequence(weights, packed)
    return lax.map(jax.checkpoint(run_one), (x_all, cond_all))

def reference(inputs, condition, attn_gain, ada_weight, ada_bias, qkv_weight, out_weight, ffn_gain, up_weight, up_bias, down_weight, down_bias, cotangent):
    weights = tuple((member.astype(jnp.float32) for member in (attn_gain, ada_weight, ada_bias, qkv_weight, out_weight, ffn_gain, up_weight, up_bias, down_weight, down_bias)))
    output, pullback = jax.vjp(forward, inputs.astype(jnp.float32), condition.astype(jnp.float32), weights)
    grad_x, grad_cond, grad_list = pullback(cotangent.astype(jnp.float32))
    return (output, grad_x, grad_cond, grad_list[0], grad_list[1], grad_list[2], grad_list[3], grad_list[4], grad_list[5], grad_list[6], grad_list[7], grad_list[8], grad_list[9])
```

```python
import functools
import math

import jax
import jax.numpy as jnp
import numpy as np
from jax import lax
from jax.experimental import pallas as pl
from jax.experimental.pallas import tpu as pltpu
from jax.sharding import PartitionSpec as P

HEADS = 12
VMEM_LIMIT = 62 * 2**20


gelu_coef = 0.7978845608028654


def layer_norm(values):
    center = values - jnp.mean(values, axis=-1, keepdims=True)
    inv_std = lax.rsqrt(jnp.mean(center * center, axis=-1, keepdims=True) + 1e-05)
    return (center * inv_std, inv_std)


def norm_back(grad_norm, normed, inv_std):
    return inv_std * (
        grad_norm
        - jnp.mean(grad_norm, axis=-1, keepdims=True)
        - normed * jnp.mean(grad_norm * normed, axis=-1, keepdims=True)
    )


def gelu_tanh(values):
    return (
        0.5 * values * (1.0 + jnp.tanh(gelu_coef * (values + 0.044715 * values * values * values)))
    )


def gelu_slope(values):
    tanh_val = jnp.tanh(gelu_coef * (values + 0.044715 * values * values * values))
    return 0.5 * (1.0 + tanh_val) + 0.5 * values * (1.0 - tanh_val * tanh_val) * gelu_coef * (
        1.0 + 3.0 * 0.044715 * values * values
    )


def rotary_tables(positions, head_size):
    half_dim = head_size // 2
    frequencies = jnp.power(10000.0, -2.0 * jnp.arange(half_dim, dtype=jnp.float32) / head_size)
    angles = positions[:, None] * frequencies[None, :]
    return (jnp.cos(angles), jnp.sin(angles))


def rotate(tensor, cos_tab, sine_tab):
    half_dim = tensor.shape[-1] // 2
    first_half = tensor[..., :half_dim]
    second_half = tensor[..., half_dim:]
    return jnp.concatenate(
        [
            first_half * cos_tab - second_half * sine_tab,
            second_half * cos_tab + first_half * sine_tab,
        ],
        axis=-1,
    )


def unrotate(tensor, cos_tab, sine_tab):
    half_dim = tensor.shape[-1] // 2
    first_half = tensor[..., :half_dim]
    second_half = tensor[..., half_dim:]
    return jnp.concatenate(
        [
            first_half * cos_tab + second_half * sine_tab,
            second_half * cos_tab - first_half * sine_tab,
        ],
        axis=-1,
    )


def score_of(query_rows, key_rows, scale_factor):
    return (
        jnp.einsum("sghd,skhd->shgk", query_rows, key_rows, preferred_element_type=jnp.float32)
        * scale_factor
    )


def score_grads(query_rows, dout_rows, lse_rows, delta_rows, key_rows, value_rows, scale_factor):
    prob_rows = jnp.exp(score_of(query_rows, key_rows, scale_factor) - lse_rows[..., None])
    grad_probs = jnp.einsum(
        "sghd,skhd->shgk", dout_rows, value_rows, preferred_element_type=jnp.float32
    )
    grad_scores = (prob_rows * (grad_probs - delta_rows[..., None])).astype(jnp.bfloat16)
    return (prob_rows.astype(jnp.bfloat16), grad_scores)


def shards(
    inputs,
    condition,
    attn_gain,
    ada_weight,
    ada_bias,
    qkv_weight,
    out_weight,
    ffn_gain,
    up_weight,
    up_bias,
    down_weight,
    down_bias,
    cotangent,
):
    seq_count, seg_len, model_width = inputs.shape
    head_count = HEADS
    head_size = model_width // head_count
    full_len = seg_len * lax.axis_size("seq")
    block_len = math.gcd(full_len, 512)
    block_count = full_len // block_len
    scale_factor = float(head_size) ** (-0.5)
    positions = (lax.axis_index("seq") * seg_len + jnp.arange(seg_len, dtype=jnp.int32)).astype(
        jnp.float32
    )
    cos_tab, sine_tab = rotary_tables(positions, head_size)
    cos_tab = cos_tab[None, :, None, :]
    sine_tab = sine_tab[None, :, None, :]

    def heads_view(matrix):
        return matrix.reshape(seq_count, seg_len, head_count, head_size)

    x_float = inputs.astype(jnp.float32)
    modulate = jnp.dot(condition, ada_weight, preferred_element_type=jnp.float32) + ada_bias
    shift_one, scale_one, gate_one, shift_two, scale_two, gate_two = [
        modulate[:, None, member * model_width : (member + 1) * model_width] for member in range(6)
    ]
    norm_one, inv_one = layer_norm(x_float)
    attn_in = (norm_one * attn_gain * (1.0 + scale_one) + shift_one).astype(jnp.bfloat16)
    projected = jnp.dot(attn_in, qkv_weight, preferred_element_type=jnp.float32)
    queries = rotate(heads_view(projected[..., :model_width]), cos_tab, sine_tab).astype(
        jnp.bfloat16
    )
    key_rot = rotate(
        heads_view(projected[..., model_width : 2 * model_width]), cos_tab, sine_tab
    ).astype(jnp.bfloat16)
    value_low = projected[..., 2 * model_width :].astype(jnp.bfloat16)
    kv_local = jnp.concatenate(
        [key_rot.reshape(seq_count, seg_len, model_width), value_low], axis=-1
    )
    kv_whole = lax.all_gather(kv_local, "seq", axis=1, tiled=True)
    kv_view = kv_whole.reshape(seq_count, full_len, 2, head_count, head_size)

    def key_block(block_num):
        sliced = lax.dynamic_slice_in_dim(kv_view, block_num * block_len, block_len, 1)
        return (sliced[:, :, 0], sliced[:, :, 1])

    def max_pass(block_num, running):
        run_max, run_sum = running
        key_rows, value_rows = key_block(block_num)
        scores = score_of(queries, key_rows, scale_factor)
        new_max = jnp.maximum(run_max, jnp.max(scores, axis=-1))
        run_sum = run_sum * jnp.exp(run_max - new_max) + jnp.sum(
            jnp.exp(scores - new_max[..., None]), axis=-1
        )
        return (new_max, run_sum)

    stat_shape = (seq_count, head_count, seg_len)
    run_max, run_sum = lax.fori_loop(
        0,
        block_count,
        max_pass,
        (jnp.full(stat_shape, -1e30, jnp.float32), jnp.zeros(stat_shape, jnp.float32)),
    )
    log_sum = run_max + jnp.log(run_sum)

    def out_pass(block_num, accums):
        accum_out, accum_exact = accums
        key_rows, value_rows = key_block(block_num)
        prob_rows = jnp.exp(score_of(queries, key_rows, scale_factor) - log_sum[..., None])
        accum_out = accum_out + jnp.einsum(
            "shgk,skhd->sghd",
            prob_rows.astype(jnp.bfloat16),
            value_rows,
            preferred_element_type=jnp.float32,
        )
        accum_exact = accum_exact + jnp.einsum(
            "shgk,skhd->sghd",
            prob_rows,
            value_rows.astype(jnp.float32),
            preferred_element_type=jnp.float32,
        )
        return (accum_out, accum_exact)

    head_shape = (seq_count, seg_len, head_count, head_size)
    attn_float, attn_exact = lax.fori_loop(
        0,
        block_count,
        out_pass,
        (jnp.zeros(head_shape, jnp.float32), jnp.zeros(head_shape, jnp.float32)),
    )
    attn_low = attn_float.reshape(seq_count, seg_len, model_width).astype(jnp.bfloat16)
    attn_proj = jnp.dot(attn_low, out_weight, preferred_element_type=jnp.float32)
    middle = x_float + gate_one * attn_proj
    norm_two, inv_two = layer_norm(middle)
    ffn_in = (norm_two * ffn_gain * (1.0 + scale_two) + shift_two).astype(jnp.bfloat16)
    ffn_rows = lax.all_gather(ffn_in, "mlp", axis=0, tiled=True)
    pre_act = jnp.dot(ffn_rows, up_weight, preferred_element_type=jnp.float32) + up_bias
    act_low = gelu_tanh(pre_act).astype(jnp.bfloat16)
    ffn_out = (
        lax.psum_scatter(
            jnp.dot(act_low, down_weight, preferred_element_type=jnp.float32).astype(jnp.bfloat16),
            "mlp",
            scatter_dimension=0,
            tiled=True,
        ).astype(jnp.float32)
        + down_bias
    )
    output = middle + gate_two * ffn_out
    cot_float = cotangent.astype(jnp.float32)
    grad_ffn = (gate_two * cot_float).astype(jnp.bfloat16)
    down_bias_part = jnp.sum(grad_ffn.astype(jnp.float32), axis=(0, 1))
    dgate_two = jnp.sum(cot_float * ffn_out, axis=1)
    grad_ffn_rows = lax.all_gather(grad_ffn, "mlp", axis=0, tiled=True)
    down_part = jnp.einsum(
        "sgf,sgd->fd", act_low, grad_ffn_rows, preferred_element_type=jnp.float32
    )
    grad_act = jnp.einsum(
        "sgd,fd->sgf", grad_ffn_rows, down_weight, preferred_element_type=jnp.float32
    )
    grad_pre = (grad_act * gelu_slope(pre_act)).astype(jnp.bfloat16)
    up_bias_part = jnp.sum(grad_pre.astype(jnp.float32), axis=(0, 1))
    up_part = jnp.einsum("sgd,sgf->df", ffn_rows, grad_pre, preferred_element_type=jnp.float32)
    grad_ffn_in = lax.psum_scatter(
        jnp.einsum("sgf,df->sgd", grad_pre, up_weight, preferred_element_type=jnp.float32).astype(
            jnp.bfloat16
        ),
        "mlp",
        scatter_dimension=0,
        tiled=True,
    ).astype(jnp.float32)
    dshift_two = jnp.sum(grad_ffn_in, axis=1)
    dscale_two = jnp.sum(grad_ffn_in * norm_two * ffn_gain, axis=1)
    gain_two_part = jnp.sum(grad_ffn_in * (1.0 + scale_two) * norm_two, axis=(0, 1))
    grad_middle = cot_float + norm_back(
        grad_ffn_in * (1.0 + scale_two) * ffn_gain, norm_two, inv_two
    )
    grad_proj = (gate_one * grad_middle).astype(jnp.bfloat16)
    dgate_one = jnp.sum(grad_middle * attn_proj, axis=1)
    out_part = jnp.einsum("sgd,sge->de", attn_low, grad_proj, preferred_element_type=jnp.float32)
    grad_attn = jnp.einsum(
        "sge,de->sgd", grad_proj, out_weight, preferred_element_type=jnp.float32
    ).astype(jnp.bfloat16)
    grad_attn_heads = heads_view(grad_attn)
    delta_rows = jnp.sum(grad_attn_heads.astype(jnp.float32) * attn_exact, axis=-1)
    delta_heads = jnp.transpose(delta_rows, (0, 2, 1))

    def back_pass(block_num, state_in):
        grad_query, key_grads = state_in
        key_rows, value_rows = key_block(block_num)
        prob_low, grad_scores = score_grads(
            queries, grad_attn_heads, log_sum, delta_heads, key_rows, value_rows, scale_factor
        )
        grad_query = (
            grad_query
            + jnp.einsum(
                "shgk,skhd->sghd", grad_scores, key_rows, preferred_element_type=jnp.float32
            )
            * scale_factor
        )
        grad_key = (
            jnp.einsum("shgk,sghd->skhd", grad_scores, queries, preferred_element_type=jnp.float32)
            * scale_factor
        )
        grad_value = jnp.einsum(
            "shgk,sghd->skhd", prob_low, grad_attn_heads, preferred_element_type=jnp.float32
        )
        stacked = jnp.concatenate(
            [
                grad_key.reshape(seq_count, block_len, model_width),
                grad_value.reshape(seq_count, block_len, model_width),
            ],
            axis=-1,
        )
        key_grads = lax.dynamic_update_slice_in_dim(key_grads, stacked, block_num * block_len, 1)
        return (grad_query, key_grads)

    grad_query, key_grads = lax.fori_loop(
        0,
        block_count,
        back_pass,
        (
            jnp.zeros(head_shape, jnp.float32),
            jnp.zeros((seq_count, full_len, 2 * model_width), jnp.float32),
        ),
    )
    kv_grads = lax.psum_scatter(
        key_grads.astype(jnp.bfloat16), "seq", scatter_dimension=1, tiled=True
    ).astype(jnp.float32)
    grad_key_rot = heads_view(kv_grads[..., :model_width])
    grad_values = kv_grads[..., model_width:]
    grad_qkv = jnp.concatenate(
        [
            unrotate(grad_query, cos_tab, sine_tab).reshape(seq_count, seg_len, model_width),
            unrotate(grad_key_rot, cos_tab, sine_tab).reshape(seq_count, seg_len, model_width),
            grad_values,
        ],
        axis=-1,
    ).astype(jnp.bfloat16)
    qkv_part = jnp.einsum("sgd,sge->de", attn_in, grad_qkv, preferred_element_type=jnp.float32)
    grad_attn_in = jnp.einsum(
        "sge,de->sgd", grad_qkv, qkv_weight, preferred_element_type=jnp.float32
    )
    dshift_one = jnp.sum(grad_attn_in, axis=1)
    dscale_one = jnp.sum(grad_attn_in * norm_one * attn_gain, axis=1)
    gain_one_part = jnp.sum(grad_attn_in * (1.0 + scale_one) * norm_one, axis=(0, 1))
    grad_inputs = grad_middle + norm_back(
        grad_attn_in * (1.0 + scale_one) * attn_gain, norm_one, inv_one
    )
    grad_modulate = jnp.concatenate(
        [dshift_one, dscale_one, dgate_one, dshift_two, dscale_two, dgate_two], axis=-1
    )
    ada_weight_part = jnp.dot(
        condition.astype(jnp.float32).T, grad_modulate, precision=lax.Precision.HIGHEST
    )
    ada_bias_part = jnp.sum(grad_modulate, axis=0)
    cond_part = jnp.dot(
        grad_modulate, ada_weight.astype(jnp.float32).T, precision=lax.Precision.HIGHEST
    )
    summed_all = lax.psum(
        (
            qkv_part,
            out_part,
            ada_weight_part,
            ada_bias_part,
            gain_one_part,
            gain_two_part,
            down_bias_part,
        ),
        ("seq", "mlp"),
    )
    summed_seq = (
        lax.psum(up_part.astype(jnp.bfloat16), "seq").astype(jnp.float32),
        lax.psum(up_bias_part.astype(jnp.bfloat16), "seq").astype(jnp.float32),
        lax.psum(down_part.astype(jnp.bfloat16), "seq").astype(jnp.float32),
        lax.psum(cond_part.astype(jnp.bfloat16), "seq").astype(jnp.float32),
    )
    return (
        output,
        grad_inputs,
        summed_seq[3],
        summed_all[4],
        summed_all[2],
        summed_all[3],
        summed_all[0],
        summed_all[1],
        summed_all[5],
        summed_seq[0],
        summed_seq[1],
        summed_seq[2],
        summed_all[6],
    )


BF = jnp.bfloat16
F32 = jnp.float32
MESH = pl.DeviceIdType.MESH


def dot(a, b):
    return jnp.dot(a, b, preferred_element_type=F32)


def dot_t(a, b):
    return lax.dot_general(a, b, (((1,), (1,)), ((), ())), preferred_element_type=F32)


def rows_of(start, size):
    return pl.ds(pl.multiple_of(start, size), size)


def pick(table, index):
    value = jnp.int32(table[0])
    for place in range(1, len(table)):
        value = jnp.where(index == place, jnp.int32(table[place]), value)
    return value


def swap_halves(tile):
    lane = lax.broadcasted_iota(jnp.int32, tile.shape, 1)
    return jnp.where(
        lane % 64 < 32, pltpu.roll(tile, 96, 1), pltpu.roll(tile, 32, 1)
    )


def fast_kernel(
    chain,
    inputs, cond, again, adaw_h, adab, qkv_h, outw_h, fgain, up_h, upb, down_h, downb, cot_h,
    cos_h, sin_h, cost_h, sint_h,
    out_o, gin_o, g_o, b_o, vec_o, ubg_o,
    adaw, wq, wo, wu, wd, ub, cos_v, sin_v, cost, sint,
    xb, ctb, mod2, n1, i1, ai, ait, q_s, k_s, v_s, kt_s, vt_s, ot_s, lse, att, att_s,
    ap, n2, i2, fi, fit, gf, gft, oacc, gacc, a_s, gp_s, g_s, osend, orecv, gsend, grecv,
    gm, do_s, dlt, qm, dom, dqt, gq, b_s, xs, xr, fst, vec, ubg,
    lsem, ssem, rsem, wss, wrs, yss, yrs,
):
    Z = chain
    grp = lax.axis_index("grp")
    seq = lax.axis_index("seq")
    z = lax.axis_index("mlp")
    x, c = seq // 2, seq % 2
    D = 768
    own = c * 512
    other = (1 - c) * 512
    TO_CORE = {"seq": x * 2 + (1 - c)}
    TO_X = {"seq": (1 - x) * 2 + c}
    TO_Y = {"grp": 1 - grp}
    RIGHT = {"mlp": jnp.minimum(z + 1, Z - 1)}
    LEFT = {"mlp": jnp.maximum(z - 1, 0)}

    def remote(src, dst, index, device):
        return pltpu.make_async_remote_copy(
            src_ref=src, dst_ref=dst, send_sem=ssem.at[index], recv_sem=rsem.at[index],
            device_id=device, device_id_type=MESH,
        )

    def local(src, dst, index):
        return pltpu.make_async_copy(src, dst, lsem.at[index])

    half = pl.ds(pl.multiple_of(c * 384, 128), 384)
    loads = [local(inputs.at[x], xb.at[rows_of(x * 256, 256)], 0), local(adaw_h, adaw, 1)]
    loads += [local(cos_h, cos_v, 2), local(sin_h, sin_v, 3), local(cost_h, cost, 4), local(sint_h, sint, 5)]
    for p in range(3):
        for part in range(3):
            loads.append(
                local(
                    qkv_h.at[:, pl.ds(pl.multiple_of(part * D + c * 384 + p * 128, 128), 128)],
                    wq.at[p, :, pl.ds(part * 128, 128)],
                    6 + p * 3 + part,
                )
            )
    loads.append(local(outw_h, wo, 15))
    loads.append(local(up_h.at[:, half], wu.at[z], 16))
    loads.append(local(down_h.at[rows_of(c * 384, 384)], wd.at[z], 17))
    loads.append(local(cot_h.at[x], ctb.at[rows_of(x * 256, 256)], 18))
    loads.append(local(upb, ub.at[z], 19))
    for item in loads:
        item.start()

    barrier = pltpu.get_barrier_semaphore()
    for device in (TO_CORE, TO_X, TO_Y):
        pl.semaphore_signal(barrier, 1, device_id=device, device_id_type=MESH)

    @pl.when(z > 0)
    def _():
        pl.semaphore_signal(barrier, 1, device_id=LEFT, device_id_type=MESH)

    @pl.when(z < Z - 1)
    def _():
        pl.semaphore_signal(barrier, 1, device_id=RIGHT, device_id_type=MESH)

    ends = jnp.where(z > 0, 1, 0) + jnp.where(z < Z - 1, 1, 0)
    pl.semaphore_wait(barrier, 3 + ends)

    swap_x = remote(inputs.at[1 - x], xb.at[rows_of(x * 256, 256)], 0, TO_X)
    swap_x.start()
    swap_c = remote(cot_h.at[1 - x], ctb.at[rows_of(x * 256, 256)], 1, TO_X)
    swap_c.start()

    def up_half(ref, which):
        return ref.at[rows_of(which * 384, 384)]

    def down_half(ref, which):
        return ref.at[rows_of(which * 192, 192)]

    def z_copies(j, way, device, first):
        if first:
            src = (
                up_h.at[rows_of(grp * 384, 384), half],
                down_h.at[rows_of(c * 384 + grp * 192, 192)],
                upb,
            )
        else:
            src = (up_half(wu.at[j], grp), down_half(wd.at[j], grp), ub.at[j])
        dst = (up_half(wu.at[j], grp), down_half(wd.at[j], grp), ub.at[j])
        return [
            pltpu.make_async_remote_copy(
                src_ref=src[i], dst_ref=dst[i], send_sem=wss.at[way, j, i], recv_sem=wrs.at[way, j, i],
                device_id=device, device_id_type=MESH,
            )
            for i in range(3)
        ]

    def y_copies(j, which):
        return [
            pltpu.make_async_remote_copy(
                src_ref=ref, dst_ref=ref, send_sem=yss.at[j, i], recv_sem=yrs.at[j, i],
                device_id=TO_Y, device_id_type=MESH,
            )
            for i, ref in enumerate((up_half(wu.at[j], which), down_half(wd.at[j], which)))
        ]

    def start_all(items):
        for item in items:
            item.start()

    @pl.when(z < Z - 1)
    def _():
        start_all(z_copies(z, 0, RIGHT, True))

    @pl.when(z > 0)
    def _():
        start_all(z_copies(z, 1, LEFT, True))

    def weight_step(k):
        @pl.when(z - k >= 0)
        def _():
            j = z - k
            for item in z_copies(j, 0, RIGHT, False):
                item.wait_recv()

            @pl.when(z < Z - 1)
            def _():
                start_all(z_copies(j, 0, RIGHT, False))

            start_all(y_copies(j, grp))

        @pl.when(z + k <= Z - 1)
        def _():
            j = z + k
            for item in z_copies(j, 1, LEFT, False):
                item.wait_recv()

            @pl.when(z > 0)
            def _():
                start_all(z_copies(j, 1, LEFT, False))

            start_all(y_copies(j, grp))

    local(adaw_h, adaw, 1).wait()
    for part in range(6):
        span = pl.ds(part * D, D)
        mod2[:, span] = dot(cond[...], adaw[:, span]) + adab[:, span]
    modrow = mod2[pl.ds(x, 1), :]
    shift_one, scale_one, gate_one, shift_two, scale_two, gate_two = [
        modrow[:, part * D : (part + 1) * D] for part in range(6)
    ]

    def layer_norm(values):
        center = values - jnp.mean(values, axis=-1, keepdims=True)
        inv = lax.rsqrt(jnp.mean(center * center, axis=-1, keepdims=True) + 1e-05)
        return center * inv, inv

    TILE = 64
    mul_one = again[...] * (1.0 + scale_one)
    mul_two = fgain[...] * (1.0 + scale_two)

    def norm_one_block(block):
        @pl.loop(0, 256 // TILE)
        def _(i):
            at = block * 256 + i * TILE
            rows = rows_of(at, TILE)
            normed, inv = layer_norm(xb[rows].astype(F32))
            n1[rows] = normed
            i1[rows] = inv
            ai[rows_of(own + at, TILE)] = (normed * mul_one + shift_one).astype(BF)

    def core_rows(ref, start, size, index):
        part = ref.at[rows_of(start, size)]
        return remote(part, part, index, TO_CORE)

    for item in loads[2:15]:
        item.wait()

    def project_block(block):
        @pl.loop(0, 2)
        def _(half_core):
            start = half_core * 512 + block * 256
            rows = rows_of(start, 256)
            tile = ai[rows]
            ait[:, rows] = tile.T
            cos_t, sin_t = cos_v[rows], sin_v[rows]

            @pl.loop(0, 3)
            def _(p):
                projected = dot(tile, wq[p])
                query = projected[:, :128]
                key = projected[:, 128:256]
                value = projected[:, 256:].astype(BF)
                query = (query * cos_t + swap_halves(query) * sin_t).astype(BF)
                key = (key * cos_t + swap_halves(key) * sin_t).astype(BF)
                q_s[p, rows] = query * jnp.asarray(0.125, BF)
                k_s[p, rows] = key
                v_s[p, rows] = value
                kt_s[p, :, rows] = key.T
                vt_s[p, :, rows] = value.T

    loads[0].wait()
    norm_one_block(x)
    core_rows(ai, own + x * 256, 256, 2).start()
    core_rows(ai, other + x * 256, 256, 2).wait_recv()
    project_block(x)
    swap_x.wait_recv()
    norm_one_block(1 - x)
    core_rows(ai, own + (1 - x) * 256, 256, 3).start()
    core_rows(ai, other + (1 - x) * 256, 256, 3).wait_recv()
    project_block(1 - x)
    loads[16].wait()
    loads[17].wait()
    loads[19].wait()
    weight_step(1)

    low_lane = lax.broadcasted_iota(jnp.int32, (1, 128), 1) < 64
    keep = [low_lane.astype(F32).astype(BF), (~low_lane).astype(F32).astype(BF)]

    def att_copy(p, start):
        return remote(
            att_s.at[:, pl.ds(p * 128, 128)],
            att.at[:, pl.ds(pl.multiple_of(c * 384 + p * 128, 128), 128)],
            4 + p,
            TO_CORE,
        )

    def attend(p):
        @pl.loop(0, 4)
        def _(t):
            cols = rows_of(t * 256, 256)
            query = q_s[p, cols]
            keys = k_s[p]
            outs = []
            for h in range(2):
                masked = query * keep[h]
                scores = dot_t(keys, masked)
                top = jnp.max(scores, axis=0, keepdims=True)
                expd = jnp.exp(scores - top)
                total = jnp.sum(expd, axis=0, keepdims=True)
                lse[p, pl.ds(h, 1), cols] = top + jnp.log(total)
                out = dot(vt_s[p, pl.ds(h * 64, 64), :], expd.astype(BF)) / total
                ot_s[p, pl.ds(h * 64, 64), cols] = out
                outs.append(out)
            natural = jnp.concatenate(outs, axis=0).T.astype(BF)
            lanes = pl.ds(pl.multiple_of(c * 384 + p * 128, 128), 128)

            @pl.when(t // 2 == c)
            def _():
                att[rows_of((t % 2) * 256, 256), lanes] = natural

            @pl.when(t // 2 != c)
            def _():
                att_s[rows_of((t % 2) * 256, 256), pl.ds(p * 128, 128)] = natural

        att_copy(p, True).start()

    attend(0)
    attend(1)
    weight_step(2)

    loads[18].wait()
    swap_c.wait_recv()

    @pl.loop(0, 512 // TILE)
    def _(i):
        at = i * TILE
        gf[rows_of(own + at, TILE)] = (gate_two * ctb[rows_of(at, TILE)].astype(F32)).astype(BF)

    core_rows(gf, own, 512, 7).start()
    attend(2)
    vec[...] = jnp.zeros_like(vec)

    @pl.loop(0, 512 // TILE)
    def _(i):
        vec[8:9] += jnp.sum(gf[rows_of(own + i * TILE, TILE)].astype(F32), axis=0, keepdims=True)

    for p in range(3):
        remote(
            att_s.at[:, pl.ds(p * 128, 128)],
            att.at[:, pl.ds(pl.multiple_of((1 - c) * 384 + p * 128, 128), 128)],
            4 + p,
            TO_CORE,
        ).wait_recv()
    loads[15].wait()

    @pl.loop(0, 2)
    def _(b):
        rows = rows_of(b * 256, 256)
        ap[rows] = dot(att[rows], wo[...])

        @pl.loop(0, 256 // TILE)
        def _(i):
            at = b * 256 + i * TILE
            tile = rows_of(at, TILE)
            middle = xb[tile].astype(F32) + gate_one * ap[tile]
            normed, inv = layer_norm(middle)
            n2[tile] = normed
            i2[tile] = inv
            fi[rows_of(own + at, TILE)] = (normed * mul_two + shift_two).astype(BF)

    core_rows(fi, own, 512, 8).start()
    core_rows(gf, other, 512, 7).wait_recv()

    @pl.loop(0, 4)
    def _(t):
        rows = rows_of(t * 256, 256)
        gft[:, rows] = gf[rows].T

    core_rows(fi, other, 512, 8).wait_recv()

    @pl.loop(0, 4)
    def _(t):
        rows = rows_of(t * 256, 256)
        fit[:, rows] = fi[rows].T

    orders = [sorted(range(Z), key=lambda j, a=a: (abs(j - a), j)) for a in range(Z)]
    coef = 0.7978845608028654

    @pl.loop(0, Z)
    def _(k):
        j = pick([pick([orders[a][n] for a in range(Z)], z) for n in range(Z)], k)

        @pl.when(k >= 3)
        def _():
            weight_step(k)

        @pl.when(k > 0)
        def _():
            for item in y_copies(j, 1 - grp):
                item.wait_recv()

        bias = ub[j][:, pl.ds(0, 384)]
        bias = jnp.where(c == 0, bias, ub[j][:, pl.ds(384, 384)])
        up_j, down_j = wu[j], wd[j]

        @pl.loop(0, 4)
        def _(t):
            rows = rows_of(t * 256, 256)
            pre = dot(fi[rows], wu[j]) + bias
            sq = pre * pre
            th = jnp.tanh(coef * (pre + 0.044715 * pre * sq))
            act = (0.5 * pre * (1.0 + th)).astype(BF)
            slope = 0.5 * (1.0 + th) + 0.5 * pre * (1.0 - th * th) * coef * (1.0 + 3.0 * 0.044715 * sq)
            a_s[rows] = act
            grad_pre = (dot_t(gf[rows], wd[j]) * slope).astype(BF)
            gp_s[rows] = grad_pre
            bsum = jnp.sum(grad_pre.astype(F32), axis=0, keepdims=True)
            out = dot(act, wd[j])
            gin = dot_t(grad_pre, wu[j])

            @pl.when(k == 0)
            def _():
                oacc[rows] = out
                gacc[rows] = gin

            @pl.when(k > 0)
            def _():
                oacc[rows] += out
                gacc[rows] += gin

            @pl.when(t == 0)
            def _():
                ubg[j] = bsum

            @pl.when(t > 0)
            def _():
                ubg[j] += bsum

        @pl.loop(0, 3)
        def _(r):
            rows = rows_of(r * 256, 256)
            g_s[0, j, rows] = dot(fit[rows], gp_s[...]).astype(BF)
            g_s[1, j, rows] = dot(gft[rows], a_s[...]).astype(BF)

    g_out = local(g_s, g_o, 0)
    g_out.start()

    @pl.loop(0, 512 // TILE)
    def _(i):
        tile = rows_of(i * TILE, TILE)
        far = rows_of(other + i * TILE, TILE)
        gsend[tile] = gacc[far].astype(BF)
        osend[tile] = oacc[far].astype(BF)

    remote(gsend, grecv, 9, TO_CORE).start()
    remote(osend, orecv, 10, TO_CORE).start()
    remote(gsend, grecv, 9, TO_CORE).wait_recv()
    core_rows(gf, own, 512, 7).wait_send()

    def norm_back(grad, normed, inv):
        return inv * (
            grad
            - jnp.mean(grad, axis=-1, keepdims=True)
            - normed * jnp.mean(grad * normed, axis=-1, keepdims=True)
        )

    @pl.loop(0, 512 // TILE)
    def _(i):
        tile = rows_of(i * TILE, TILE)
        near = rows_of(own + i * TILE, TILE)
        grad = gacc[near] + grecv[tile].astype(F32)
        normed = n2[tile]
        vec[3:4] += jnp.sum(grad, axis=0, keepdims=True)
        vec[4:5] += jnp.sum(grad * normed, axis=0, keepdims=True)
        middle = ctb[tile].astype(F32) + norm_back(grad * mul_two, normed, i2[tile])
        gm[tile] = middle
        gf[near] = (gate_one * middle).astype(BF)
        vec[2:3] += jnp.sum(middle * ap[tile], axis=0, keepdims=True)

    gproj = gf
    core_rows(gproj, own, 512, 11).start()

    remote(osend, orecv, 10, TO_CORE).wait_recv()

    @pl.loop(0, 512 // TILE)
    def _(i):
        tile = rows_of(i * TILE, TILE)
        ffn = oacc[rows_of(own + i * TILE, TILE)] + orecv[tile].astype(F32) + downb[...]
        vec[5:6] += jnp.sum(ctb[tile].astype(F32) * ffn, axis=0, keepdims=True)
        oacc[rows_of(own + i * TILE, TILE)] = (
            xb[tile].astype(F32) + gate_one * ap[tile] + gate_two * ffn
        )

    def hand_over(src, out_ref, number):
        @pl.loop(0, 256 // TILE)
        def _(i):
            xs[number, rows_of(i * TILE, TILE)] = src[
                rows_of(own + (1 - x) * 256 + i * TILE, TILE)
            ].astype(BF)
            fst[2 * number, rows_of(i * TILE, TILE)] = src[rows_of(own + x * 256 + i * TILE, TILE)]

        remote(xs.at[number], xr.at[number], 12 + number, TO_X).start()
        local(fst.at[2 * number], out_ref.at[x], 1 + 2 * number).start()

    def take_over(out_ref, number):
        remote(xs.at[number], xr.at[number], 12 + number, TO_X).wait_recv()
        fst[2 * number + 1] = xr[number].astype(F32)
        local(fst.at[2 * number + 1], out_ref.at[1 - x], 2 + 2 * number).start()

    hand_over(oacc, out_o, 0)

    core_rows(gproj, other, 512, 11).wait_recv()

    @pl.loop(0, 4)
    def _(t):
        rows = rows_of(t * 256, 256)
        grad = dot_t(gproj[rows], wo[rows_of(c * 384, 384)])
        for p in range(3):
            part = grad[:, p * 128 : (p + 1) * 128].astype(BF)
            do_s[p, rows] = part
            product = part.astype(F32).T * ot_s[p, :, rows]
            for h in range(2):
                dlt[p, pl.ds(h, 1), rows] = jnp.sum(
                    product[h * 64 : (h + 1) * 64], axis=0, keepdims=True
                )

    for p in range(3):
        @pl.loop(0, 2)
        def _(n):
            lanes = pl.ds(pl.multiple_of(n * 384, 128), 384)
            b_s[0, rows_of(n * 384 + p * 128, 128)] = dot(
                ot_s[p].astype(BF), gproj[:, lanes]
            ).astype(BF)

    def attend_back(p):
        for h in range(2):
            qm[h] = q_s[p] * keep[h]
            dom[h] = do_s[p] * keep[h]
        dqt[...] = jnp.zeros_like(dqt)

        @pl.loop(0, 4)
        def _(t):
            rows = rows_of(t * 256, 256)
            keys, values = k_s[p, rows], v_s[p, rows]
            dv, dk = None, None
            for h in range(2):
                probs = jnp.exp(dot_t(keys, qm[h]) - lse[p, pl.ds(h, 1), :])
                grads = dot_t(values, dom[h])
                ds = (probs * (grads - dlt[p, pl.ds(h, 1), :])).astype(BF)
                dv_h = dot(probs.astype(BF), dom[h])
                dk_h = dot(ds, qm[h])
                dv = dv_h if dv is None else dv + dv_h
                dk = dk_h if dk is None else dk + dk_h
                dqt[pl.ds(h * 64, 64)] += dot(kt_s[p, pl.ds(h * 64, 64), rows], ds)
            cos_t, sin_t = cos_v[rows], sin_v[rows]
            gq[rows, pl.ds(128, 128)] = (dk * cos_t - swap_halves(dk) * sin_t).astype(BF)
            gq[rows, pl.ds(256, 128)] = dv.astype(BF)

        @pl.loop(0, 4)
        def _(t):
            rows = rows_of(t * 256, 256)
            block = dqt[:, rows] * 0.125
            cos_t, sin_t = cost[:, rows], sint[:, rows]
            parts = []
            for h in range(2):
                u, w = block[h * 64 : h * 64 + 32], block[h * 64 + 32 : h * 64 + 64]
                parts += [u * cos_t + w * sin_t, w * cos_t - u * sin_t]
            gq[rows, pl.ds(0, 128)] = jnp.concatenate(parts, axis=0).T.astype(BF)

        @pl.loop(0, 3)
        def _(r):
            rows = rows_of(r * 256, 256)
            b_s[1 + p, rows] = dot(ait[rows], gq[...]).astype(BF)

        @pl.loop(0, 4)
        def _(t):
            rows = rows_of(t * 256, 256)
            part = dot_t(gq[rows], wq[p])
            if p == 0:
                gacc[rows] = part
            else:
                gacc[rows] += part

    for p in range(3):
        attend_back(p)
        if p == 0:
            take_over(out_o, 0)
    remote(gsend, grecv, 9, TO_CORE).wait_send()

    b_out = local(b_s, b_o, 6)
    b_out.start()

    @pl.loop(0, 512 // TILE)
    def _(i):
        gsend[rows_of(i * TILE, TILE)] = gacc[rows_of(other + i * TILE, TILE)].astype(BF)

    remote(gsend, grecv, 14, TO_CORE).start()
    remote(gsend, grecv, 14, TO_CORE).wait_recv()

    @pl.loop(0, 512 // TILE)
    def _(i):
        tile = rows_of(i * TILE, TILE)
        near = rows_of(own + i * TILE, TILE)
        grad = gacc[near] + grecv[tile].astype(F32)
        normed = n1[tile]
        vec[0:1] += jnp.sum(grad, axis=0, keepdims=True)
        vec[1:2] += jnp.sum(grad * normed, axis=0, keepdims=True)
        gacc[near] = gm[tile] + norm_back(grad * mul_one, normed, i1[tile])

    hand_over(gacc, gin_o, 1)
    sums = vec[...]
    vec[6:7] = sums[1:2] * (1.0 + scale_one)
    vec[7:8] = sums[4:5] * (1.0 + scale_two)
    vec[1:2] = sums[1:2] * again[...]
    vec[4:5] = sums[4:5] * fgain[...]
    take_over(gin_o, 1)
    v_out = local(vec, vec_o, 7)
    v_out.start()
    u_out = local(ubg, ubg_o, 8)
    u_out.start()

    v_out.wait()
    u_out.wait()
    g_out.wait()
    b_out.wait()
    for number, ref in ((0, out_o), (1, gin_o)):
        local(fst.at[2 * number], ref.at[x], 1 + 2 * number).wait()
        local(fst.at[2 * number + 1], ref.at[1 - x], 2 + 2 * number).wait()
        remote(xs.at[number], xr.at[number], 12 + number, TO_X).wait_send()
    swap_x.wait_send()
    swap_c.wait_send()
    core_rows(ai, own + x * 256, 256, 2).wait_send()
    core_rows(ai, own + (1 - x) * 256, 256, 3).wait_send()
    for p in range(3):
        att_copy(p, False).wait_send()
    core_rows(fi, own, 512, 8).wait_send()
    remote(osend, orecv, 10, TO_CORE).wait_send()
    core_rows(gproj, own, 512, 11).wait_send()
    remote(gsend, grecv, 14, TO_CORE).wait_send()

    @pl.when(z < Z - 1)
    def _():
        for item in z_copies(z, 0, RIGHT, False):
            item.wait_send()

    @pl.when(z > 0)
    def _():
        for item in z_copies(z, 1, LEFT, False):
            item.wait_send()

    @pl.loop(1, Z)
    def _(k):
        @pl.when(z - k >= 0)
        def _():
            @pl.when(z < Z - 1)
            def _():
                for item in z_copies(z - k, 0, RIGHT, False):
                    item.wait_send()

            for item in y_copies(z - k, grp):
                item.wait_send()

        @pl.when(z + k <= Z - 1)
        def _():
            @pl.when(z > 0)
            def _():
                for item in z_copies(z + k, 1, LEFT, False):
                    item.wait_send()

            for item in y_copies(z + k, grp):
                item.wait_send()


def tables(seg_len, seq_size):
    half = np.arange(32)
    frequency = 10000.0 ** (-2.0 * half / 64)
    core, chip, token = np.meshgrid(
        np.arange(2), np.arange(seq_size // 2), np.arange(seg_len), indexing="ij"
    )
    place = ((chip * 2 + core) * seg_len + token).reshape(-1)
    angle = place[:, None] * frequency[None, :]
    cos, sin = np.cos(angle).astype(np.float32), np.sin(angle).astype(np.float32)
    return (
        np.tile(cos, (1, 4)),
        np.concatenate([-sin, sin, -sin, sin], axis=1),
        np.ascontiguousarray(cos.T),
        np.ascontiguousarray(sin.T),
    )


def fast_shards(
    inputs, condition, attn_gain, ada_weight, ada_bias, qkv_weight, out_weight, ffn_gain,
    up_weight, up_bias, down_weight, down_bias, cotangent,
):
    Z = lax.axis_size("mlp")
    tabs = [jnp.asarray(t) for t in tables(inputs.shape[1], lax.axis_size("seq"))]
    hbm, vm = pl.BlockSpec(memory_space=pl.ANY), pl.BlockSpec(memory_space=pltpu.VMEM)
    shape = jax.ShapeDtypeStruct
    row = lambda v: v.reshape(1, -1)
    V = pltpu.VMEM
    dma = pltpu.SemaphoreType.DMA
    scratch = [
        V((128, 4608), BF), V((3, 768, 384), BF), V((768, 768), BF), V((Z, 768, 384), BF),
        V((Z, 384, 768), BF), V((Z, 1, 768), F32), V((1024, 128), F32), V((1024, 128), F32),
        V((32, 1024), F32), V((32, 1024), F32),
        V((512, 768), BF), V((512, 768), BF), V((2, 4608), F32), V((512, 768), F32), V((512, 1), F32),
        V((1024, 768), BF), V((768, 1024), BF),
        V((3, 1024, 128), BF), V((3, 1024, 128), BF), V((3, 1024, 128), BF),
        V((3, 128, 1024), BF), V((3, 128, 1024), BF), V((3, 128, 1024), F32), V((3, 2, 1024), F32),
        V((512, 768), BF), V((512, 384), BF),
        V((512, 768), F32), V((512, 768), F32), V((512, 1), F32),
        V((1024, 768), BF), V((768, 1024), BF), V((1024, 768), BF), V((768, 1024), BF),
        V((1024, 768), F32), V((1024, 768), F32), V((1024, 384), BF), V((1024, 384), BF),
        V((2, Z, 768, 384), BF), V((512, 768), BF), V((512, 768), BF), V((512, 768), BF), V((512, 768), BF),
        V((512, 768), F32), V((3, 1024, 128), BF), V((3, 2, 1024), F32),
        V((2, 1024, 128), BF), V((2, 1024, 128), BF), V((128, 1024), F32), V((1024, 384), BF),
        V((4, 768, 384), BF), V((2, 256, 768), BF), V((2, 256, 768), BF), V((4, 256, 768), F32),
        V((16, 768), F32), V((Z, 1, 384), F32),
        dma((20,)), dma((16,)), dma((16,)), dma((2, Z, 3)), dma((2, Z, 3)), dma((Z, 2)), dma((Z, 2)),
    ]
    token = shape(inputs.shape, F32)
    out, gin, g, b, vec, ubg = pl.pallas_call(
        functools.partial(fast_kernel, Z),
        out_shape=[
            token, token, shape((2, Z, 768, 384), BF), shape((4, 768, 384), BF),
            shape((16, 768), F32), shape((Z, 1, 384), F32),
        ],
        in_specs=[hbm, vm, vm, hbm, vm, hbm, hbm, vm, hbm, vm, hbm, vm, hbm, hbm, hbm, hbm, hbm],
        out_specs=[hbm] * 6,
        scratch_shapes=scratch,
        compiler_params=pltpu.CompilerParams(
            collective_id=0, has_side_effects=True, vmem_limit_bytes=VMEM_LIMIT
        ),
        name="block",
    )(
        inputs, condition, row(attn_gain), ada_weight, row(ada_bias), qkv_weight, out_weight,
        row(ffn_gain), up_weight, row(up_bias), down_weight, row(down_bias), cotangent, *tabs,
    )
    g = lax.psum_scatter(g, "mlp", scatter_dimension=1, tiled=True)
    g = lax.all_gather(g, "seq").astype(F32)[:, :, 0]
    g = g[:2] + g[2:]
    grad_up = jnp.concatenate([g[0, 0], g[1, 0]], axis=-1)
    grad_down = jnp.concatenate([g[0, 1], g[1, 1]], axis=-1).T
    b = lax.all_gather(lax.psum(b, "mlp"), "seq").astype(F32)
    b = b[:2] + b[2:]
    grad_out = b[:, 0].reshape(2, 2, 384, 384).transpose(0, 2, 1, 3).reshape(768, 768)
    grad_qkv = b[:, 1:].reshape(2, 3, 768, 3, 128).transpose(2, 3, 0, 1, 4).reshape(768, 2304)
    vec = lax.all_gather(lax.all_gather(vec, "seq"), "mlp")
    vec = vec.reshape(Z, 2, 2, 16, 768).sum(axis=2)
    dmod = vec[:, :, :6].reshape(2 * Z, 4608)
    cond = lax.all_gather(condition, "mlp", tiled=True).astype(F32)
    high = lax.Precision.HIGHEST
    grad_ada = jnp.dot(cond.T, dmod, precision=high)
    mine = lax.dynamic_slice_in_dim(dmod, lax.axis_index("mlp") * 2, 2, 0)
    grad_cond = jnp.dot(mine, ada_weight.astype(F32).T, precision=high)
    tail = vec[:, :, 6:9].sum(axis=(0, 1))
    ubg = lax.all_gather(lax.all_gather(ubg[:, 0], "seq"), "mlp").reshape(Z, 2, 2, Z, 384).sum(axis=(0, 1))
    grad_ub = lax.dynamic_index_in_dim(ubg, lax.axis_index("mlp"), 1, False).reshape(-1)
    return (
        out, gin, grad_cond, tail[0], grad_ada, dmod.sum(axis=0), grad_qkv, grad_out, tail[1],
        grad_up, grad_ub, grad_down, tail[2],
    )


def solution(mesh):
    placed = (
        P(("grp", "mlp"), "seq", None),
        P(("grp", "mlp"), None),
        P(),
        P(),
        P(),
        P(),
        P(),
        P(),
        P(None, "mlp"),
        P("mlp"),
        P("mlp", None),
        P(),
        P(("grp", "mlp"), "seq", None),
    )
    sizes = dict(mesh.shape)
    small = sizes["seq"] == 4 and sizes["grp"] == 2 and sizes["mlp"] == 4
    return jax.shard_map(
        fast_shards if small else shards,
        mesh=mesh,
        in_specs=placed,
        out_specs=(
            P(("grp", "mlp"), "seq", None),
            P(("grp", "mlp"), "seq", None),
            P(("grp", "mlp"), None),
            P("grp"),
            P("grp", None),
            P("grp"),
            P("grp", None),
            P("grp", None),
            P("grp"),
            P("grp", "mlp"),
            P(("grp", "mlp")),
            P(("grp", "mlp"), None),
            P("grp"),
        ),
        check_vma=False,
    )
```

```python
import functools
import math

import jax
import jax.numpy as jnp
import numpy as np
from jax import lax
from jax.experimental import pallas as pl
from jax.experimental.pallas import tpu as pltpu
from jax.sharding import PartitionSpec as P

HEADS = 12
VMEM_LIMIT = 62 * 2**20


gelu_coef = 0.7978845608028654


def layer_norm(values):
    center = values - jnp.mean(values, axis=-1, keepdims=True)
    inv_std = lax.rsqrt(jnp.mean(center * center, axis=-1, keepdims=True) + 1e-05)
    return (center * inv_std, inv_std)


def norm_back(grad_norm, normed, inv_std):
    return inv_std * (
        grad_norm
        - jnp.mean(grad_norm, axis=-1, keepdims=True)
        - normed * jnp.mean(grad_norm * normed, axis=-1, keepdims=True)
    )


def gelu_tanh(values):
    return (
        0.5 * values * (1.0 + jnp.tanh(gelu_coef * (values + 0.044715 * values * values * values)))
    )


def gelu_slope(values):
    tanh_val = jnp.tanh(gelu_coef * (values + 0.044715 * values * values * values))
    return 0.5 * (1.0 + tanh_val) + 0.5 * values * (1.0 - tanh_val * tanh_val) * gelu_coef * (
        1.0 + 3.0 * 0.044715 * values * values
    )


def rotary_tables(positions, head_size):
    half_dim = head_size // 2
    frequencies = jnp.power(10000.0, -2.0 * jnp.arange(half_dim, dtype=jnp.float32) / head_size)
    angles = positions[:, None] * frequencies[None, :]
    return (jnp.cos(angles), jnp.sin(angles))


def rotate(tensor, cos_tab, sine_tab):
    half_dim = tensor.shape[-1] // 2
    first_half = tensor[..., :half_dim]
    second_half = tensor[..., half_dim:]
    return jnp.concatenate(
        [
            first_half * cos_tab - second_half * sine_tab,
            second_half * cos_tab + first_half * sine_tab,
        ],
        axis=-1,
    )


def unrotate(tensor, cos_tab, sine_tab):
    half_dim = tensor.shape[-1] // 2
    first_half = tensor[..., :half_dim]
    second_half = tensor[..., half_dim:]
    return jnp.concatenate(
        [
            first_half * cos_tab + second_half * sine_tab,
            second_half * cos_tab - first_half * sine_tab,
        ],
        axis=-1,
    )


def score_of(query_rows, key_rows, scale_factor):
    return (
        jnp.einsum("sghd,skhd->shgk", query_rows, key_rows, preferred_element_type=jnp.float32)
        * scale_factor
    )


def score_grads(query_rows, dout_rows, lse_rows, delta_rows, key_rows, value_rows, scale_factor):
    prob_rows = jnp.exp(score_of(query_rows, key_rows, scale_factor) - lse_rows[..., None])
    grad_probs = jnp.einsum(
        "sghd,skhd->shgk", dout_rows, value_rows, preferred_element_type=jnp.float32
    )
    grad_scores = (prob_rows * (grad_probs - delta_rows[..., None])).astype(jnp.bfloat16)
    return (prob_rows.astype(jnp.bfloat16), grad_scores)


def shards(
    inputs,
    condition,
    attn_gain,
    ada_weight,
    ada_bias,
    qkv_weight,
    out_weight,
    ffn_gain,
    up_weight,
    up_bias,
    down_weight,
    down_bias,
    cotangent,
):
    seq_count, seg_len, model_width = inputs.shape
    head_count = HEADS
    head_size = model_width // head_count
    full_len = seg_len * lax.axis_size("seq")
    block_len = math.gcd(full_len, 512)
    block_count = full_len // block_len
    scale_factor = float(head_size) ** (-0.5)
    positions = (lax.axis_index("seq") * seg_len + jnp.arange(seg_len, dtype=jnp.int32)).astype(
        jnp.float32
    )
    cos_tab, sine_tab = rotary_tables(positions, head_size)
    cos_tab = cos_tab[None, :, None, :]
    sine_tab = sine_tab[None, :, None, :]

    def heads_view(matrix):
        return matrix.reshape(seq_count, seg_len, head_count, head_size)

    x_float = inputs.astype(jnp.float32)
    modulate = jnp.dot(condition, ada_weight, preferred_element_type=jnp.float32) + ada_bias
    shift_one, scale_one, gate_one, shift_two, scale_two, gate_two = [
        modulate[:, None, member * model_width : (member + 1) * model_width] for member in range(6)
    ]
    norm_one, inv_one = layer_norm(x_float)
    attn_in = (norm_one * attn_gain * (1.0 + scale_one) + shift_one).astype(jnp.bfloat16)
    projected = jnp.dot(attn_in, qkv_weight, preferred_element_type=jnp.float32)
    queries = rotate(heads_view(projected[..., :model_width]), cos_tab, sine_tab).astype(
        jnp.bfloat16
    )
    key_rot = rotate(
        heads_view(projected[..., model_width : 2 * model_width]), cos_tab, sine_tab
    ).astype(jnp.bfloat16)
    value_low = projected[..., 2 * model_width :].astype(jnp.bfloat16)
    kv_local = jnp.concatenate(
        [key_rot.reshape(seq_count, seg_len, model_width), value_low], axis=-1
    )
    kv_whole = lax.all_gather(kv_local, "seq", axis=1, tiled=True)
    kv_view = kv_whole.reshape(seq_count, full_len, 2, head_count, head_size)

    def key_block(block_num):
        sliced = lax.dynamic_slice_in_dim(kv_view, block_num * block_len, block_len, 1)
        return (sliced[:, :, 0], sliced[:, :, 1])

    def max_pass(block_num, running):
        run_max, run_sum = running
        key_rows, value_rows = key_block(block_num)
        scores = score_of(queries, key_rows, scale_factor)
        new_max = jnp.maximum(run_max, jnp.max(scores, axis=-1))
        run_sum = run_sum * jnp.exp(run_max - new_max) + jnp.sum(
            jnp.exp(scores - new_max[..., None]), axis=-1
        )
        return (new_max, run_sum)

    stat_shape = (seq_count, head_count, seg_len)
    run_max, run_sum = lax.fori_loop(
        0,
        block_count,
        max_pass,
        (jnp.full(stat_shape, -1e30, jnp.float32), jnp.zeros(stat_shape, jnp.float32)),
    )
    log_sum = run_max + jnp.log(run_sum)

    def out_pass(block_num, accums):
        accum_out, accum_exact = accums
        key_rows, value_rows = key_block(block_num)
        prob_rows = jnp.exp(score_of(queries, key_rows, scale_factor) - log_sum[..., None])
        accum_out = accum_out + jnp.einsum(
            "shgk,skhd->sghd",
            prob_rows.astype(jnp.bfloat16),
            value_rows,
            preferred_element_type=jnp.float32,
        )
        accum_exact = accum_exact + jnp.einsum(
            "shgk,skhd->sghd",
            prob_rows,
            value_rows.astype(jnp.float32),
            preferred_element_type=jnp.float32,
        )
        return (accum_out, accum_exact)

    head_shape = (seq_count, seg_len, head_count, head_size)
    attn_float, attn_exact = lax.fori_loop(
        0,
        block_count,
        out_pass,
        (jnp.zeros(head_shape, jnp.float32), jnp.zeros(head_shape, jnp.float32)),
    )
    attn_low = attn_float.reshape(seq_count, seg_len, model_width).astype(jnp.bfloat16)
    attn_proj = jnp.dot(attn_low, out_weight, preferred_element_type=jnp.float32)
    middle = x_float + gate_one * attn_proj
    norm_two, inv_two = layer_norm(middle)
    ffn_in = (norm_two * ffn_gain * (1.0 + scale_two) + shift_two).astype(jnp.bfloat16)
    ffn_rows = lax.all_gather(ffn_in, "mlp", axis=0, tiled=True)
    pre_act = jnp.dot(ffn_rows, up_weight, preferred_element_type=jnp.float32) + up_bias
    act_low = gelu_tanh(pre_act).astype(jnp.bfloat16)
    ffn_out = (
        lax.psum_scatter(
            jnp.dot(act_low, down_weight, preferred_element_type=jnp.float32).astype(jnp.bfloat16),
            "mlp",
            scatter_dimension=0,
            tiled=True,
        ).astype(jnp.float32)
        + down_bias
    )
    output = middle + gate_two * ffn_out
    cot_float = cotangent.astype(jnp.float32)
    grad_ffn = (gate_two * cot_float).astype(jnp.bfloat16)
    down_bias_part = jnp.sum(grad_ffn.astype(jnp.float32), axis=(0, 1))
    dgate_two = jnp.sum(cot_float * ffn_out, axis=1)
    grad_ffn_rows = lax.all_gather(grad_ffn, "mlp", axis=0, tiled=True)
    down_part = jnp.einsum(
        "sgf,sgd->fd", act_low, grad_ffn_rows, preferred_element_type=jnp.float32
    )
    grad_act = jnp.einsum(
        "sgd,fd->sgf", grad_ffn_rows, down_weight, preferred_element_type=jnp.float32
    )
    grad_pre = (grad_act * gelu_slope(pre_act)).astype(jnp.bfloat16)
    up_bias_part = jnp.sum(grad_pre.astype(jnp.float32), axis=(0, 1))
    up_part = jnp.einsum("sgd,sgf->df", ffn_rows, grad_pre, preferred_element_type=jnp.float32)
    grad_ffn_in = lax.psum_scatter(
        jnp.einsum("sgf,df->sgd", grad_pre, up_weight, preferred_element_type=jnp.float32).astype(
            jnp.bfloat16
        ),
        "mlp",
        scatter_dimension=0,
        tiled=True,
    ).astype(jnp.float32)
    dshift_two = jnp.sum(grad_ffn_in, axis=1)
    dscale_two = jnp.sum(grad_ffn_in * norm_two * ffn_gain, axis=1)
    gain_two_part = jnp.sum(grad_ffn_in * (1.0 + scale_two) * norm_two, axis=(0, 1))
    grad_middle = cot_float + norm_back(
        grad_ffn_in * (1.0 + scale_two) * ffn_gain, norm_two, inv_two
    )
    grad_proj = (gate_one * grad_middle).astype(jnp.bfloat16)
    dgate_one = jnp.sum(grad_middle * attn_proj, axis=1)
    out_part = jnp.einsum("sgd,sge->de", attn_low, grad_proj, preferred_element_type=jnp.float32)
    grad_attn = jnp.einsum(
        "sge,de->sgd", grad_proj, out_weight, preferred_element_type=jnp.float32
    ).astype(jnp.bfloat16)
    grad_attn_heads = heads_view(grad_attn)
    delta_rows = jnp.sum(grad_attn_heads.astype(jnp.float32) * attn_exact, axis=-1)
    delta_heads = jnp.transpose(delta_rows, (0, 2, 1))

    def back_pass(block_num, state_in):
        grad_query, key_grads = state_in
        key_rows, value_rows = key_block(block_num)
        prob_low, grad_scores = score_grads(
            queries, grad_attn_heads, log_sum, delta_heads, key_rows, value_rows, scale_factor
        )
        grad_query = (
            grad_query
            + jnp.einsum(
                "shgk,skhd->sghd", grad_scores, key_rows, preferred_element_type=jnp.float32
            )
            * scale_factor
        )
        grad_key = (
            jnp.einsum("shgk,sghd->skhd", grad_scores, queries, preferred_element_type=jnp.float32)
            * scale_factor
        )
        grad_value = jnp.einsum(
            "shgk,sghd->skhd", prob_low, grad_attn_heads, preferred_element_type=jnp.float32
        )
        stacked = jnp.concatenate(
            [
                grad_key.reshape(seq_count, block_len, model_width),
                grad_value.reshape(seq_count, block_len, model_width),
            ],
            axis=-1,
        )
        key_grads = lax.dynamic_update_slice_in_dim(key_grads, stacked, block_num * block_len, 1)
        return (grad_query, key_grads)

    grad_query, key_grads = lax.fori_loop(
        0,
        block_count,
        back_pass,
        (
            jnp.zeros(head_shape, jnp.float32),
            jnp.zeros((seq_count, full_len, 2 * model_width), jnp.float32),
        ),
    )
    kv_grads = lax.psum_scatter(
        key_grads.astype(jnp.bfloat16), "seq", scatter_dimension=1, tiled=True
    ).astype(jnp.float32)
    grad_key_rot = heads_view(kv_grads[..., :model_width])
    grad_values = kv_grads[..., model_width:]
    grad_qkv = jnp.concatenate(
        [
            unrotate(grad_query, cos_tab, sine_tab).reshape(seq_count, seg_len, model_width),
            unrotate(grad_key_rot, cos_tab, sine_tab).reshape(seq_count, seg_len, model_width),
            grad_values,
        ],
        axis=-1,
    ).astype(jnp.bfloat16)
    qkv_part = jnp.einsum("sgd,sge->de", attn_in, grad_qkv, preferred_element_type=jnp.float32)
    grad_attn_in = jnp.einsum(
        "sge,de->sgd", grad_qkv, qkv_weight, preferred_element_type=jnp.float32
    )
    dshift_one = jnp.sum(grad_attn_in, axis=1)
    dscale_one = jnp.sum(grad_attn_in * norm_one * attn_gain, axis=1)
    gain_one_part = jnp.sum(grad_attn_in * (1.0 + scale_one) * norm_one, axis=(0, 1))
    grad_inputs = grad_middle + norm_back(
        grad_attn_in * (1.0 + scale_one) * attn_gain, norm_one, inv_one
    )
    grad_modulate = jnp.concatenate(
        [dshift_one, dscale_one, dgate_one, dshift_two, dscale_two, dgate_two], axis=-1
    )
    ada_weight_part = jnp.dot(
        condition.astype(jnp.float32).T, grad_modulate, precision=lax.Precision.HIGHEST
    )
    ada_bias_part = jnp.sum(grad_modulate, axis=0)
    cond_part = jnp.dot(
        grad_modulate, ada_weight.astype(jnp.float32).T, precision=lax.Precision.HIGHEST
    )
    summed_all = lax.psum(
        (
            qkv_part,
            out_part,
            ada_weight_part,
            ada_bias_part,
            gain_one_part,
            gain_two_part,
            down_bias_part,
        ),
        ("seq", "mlp"),
    )
    summed_seq = (
        lax.psum(up_part.astype(jnp.bfloat16), "seq").astype(jnp.float32),
        lax.psum(up_bias_part.astype(jnp.bfloat16), "seq").astype(jnp.float32),
        lax.psum(down_part.astype(jnp.bfloat16), "seq").astype(jnp.float32),
        lax.psum(cond_part.astype(jnp.bfloat16), "seq").astype(jnp.float32),
    )
    return (
        output,
        grad_inputs,
        summed_seq[3],
        summed_all[4],
        summed_all[2],
        summed_all[3],
        summed_all[0],
        summed_all[1],
        summed_all[5],
        summed_seq[0],
        summed_seq[1],
        summed_seq[2],
        summed_all[6],
    )


BF = jnp.bfloat16
F32 = jnp.float32
MESH = pl.DeviceIdType.MESH


def dot(a, b):
    return jnp.dot(a, b, preferred_element_type=F32)


def dot_t(a, b):
    return lax.dot_general(a, b, (((1,), (1,)), ((), ())), preferred_element_type=F32)


def rows_of(start, size):
    return pl.ds(pl.multiple_of(start, size), size)


def pick(table, index):
    value = jnp.int32(table[0])
    for place in range(1, len(table)):
        value = jnp.where(index == place, jnp.int32(table[place]), value)
    return value


def swap_halves(tile):
    lane = lax.broadcasted_iota(jnp.int32, tile.shape, 1)
    return jnp.where(
        lane % 64 < 32, pltpu.roll(tile, 96, 1), pltpu.roll(tile, 32, 1)
    )


def fast_kernel(
    inputs, cond, again, adaw_h, adab, qkv_h, outw_h, fgain, up_h, upb, down_h, downb, cot_h,
    cos_h, sin_h, cost_h, sint_h,
    out_o, gin_o, cond_o, adaw_o, small_o, qkv_o, outw_o, ffn_o,
    adaw, wq, wo, wu, wd, ub, cos_v, sin_v, cost, sint,
    xb, ctb, mod2, n1, i1, ai, ait, q_s, k_s, v_s, kt_s, vt_s, ot_s, lse, att, att_s,
    ap, n2, i2, fit, gf, gft, oacc, gacc, a_s, gp_s, g_s, grecv,
    gm, do_s, dlt, dqt, gq, b_s, xs, vec, vecr, vall, ubg, cstage, sstage,
    rx, rz, fxr, rxb, fb,
    lsem, ssem, rsem, wss, wrs, yss, yrs, fss, frs, bss, brs, hss, hrs, vss, vrs, credit,
):
    Z = 4
    grp = lax.axis_index("grp")
    seq = lax.axis_index("seq")
    z = lax.axis_index("mlp")
    x, c = seq // 2, seq % 2
    D = 768
    own = c * 512
    other = (1 - c) * 512
    TO_CORE = {"seq": x * 2 + (1 - c)}
    TO_X = {"seq": (1 - x) * 2 + c}
    TO_Y = {"grp": 1 - grp}
    RIGHT = {"mlp": jnp.minimum(z + 1, Z - 1)}
    LEFT = {"mlp": jnp.maximum(z - 1, 0)}

    def remote(src, dst, index, device):
        return pltpu.make_async_remote_copy(
            src_ref=src, dst_ref=dst, send_sem=ssem.at[index], recv_sem=rsem.at[index],
            device_id=device, device_id_type=MESH,
        )

    def local(src, dst, index):
        return pltpu.make_async_copy(src, dst, lsem.at[index])

    half = pl.ds(pl.multiple_of(c * 384, 128), 384)
    loads = [local(inputs.at[x], xb.at[rows_of(x * 256, 256)], 0), local(adaw_h, adaw, 1)]
    loads += [local(cos_h, cos_v, 2), local(sin_h, sin_v, 3), local(cost_h, cost, 4), local(sint_h, sint, 5)]
    for p in range(3):
        for part in range(3):
            loads.append(
                local(
                    qkv_h.at[:, pl.ds(pl.multiple_of(part * D + c * 384 + p * 128, 128), 128)],
                    wq.at[p, :, pl.ds(part * 128, 128)],
                    6 + p * 3 + part,
                )
            )
    loads.append(local(outw_h, wo, 15))
    loads.append(local(up_h.at[:, half], wu.at[z], 16))
    for n in range(2):
        loads.append(
            local(
                down_h.at[rows_of(c * 384, 384), pl.ds(n * 384, 384)],
                wd.at[z, pl.ds(n * 384, 384)],
                17 + 3 * n,
            )
        )
    loads.append(local(cot_h.at[x], ctb.at[rows_of(x * 256, 256)], 18))
    loads.append(local(upb, ub.at[z], 19))
    for item in loads:
        item.start()

    barrier = pltpu.get_barrier_semaphore()
    peers = [{"seq": (x ^ dx) * 2 + c, "mlp": z ^ dz} for dx in range(2) for dz in range(Z) if dx or dz]
    for device in [TO_CORE, TO_Y] + peers:
        pl.semaphore_signal(barrier, 1, device_id=device, device_id_type=MESH)
    pl.semaphore_wait(barrier, 2 + len(peers))

    swap_x = remote(inputs.at[1 - x], xb.at[rows_of(x * 256, 256)], 0, TO_X)
    swap_x.start()
    swap_c = remote(cot_h.at[1 - x], ctb.at[rows_of(x * 256, 256)], 1, TO_X)
    swap_c.start()

    def up_half(ref, which):
        return ref.at[rows_of(which * 384, 384)]

    down_half = up_half

    def z_copies(j, way, device, first):
        if first:
            src = (
                up_h.at[rows_of(grp * 384, 384), half],
                down_h.at[
                    rows_of(c * 384, 384), pl.ds(pl.multiple_of(grp * 384, 128), 384)
                ],
                upb,
            )
        else:
            src = (up_half(wu.at[j], grp), down_half(wd.at[j], grp), ub.at[j])
        dst = (up_half(wu.at[j], grp), down_half(wd.at[j], grp), ub.at[j])
        return [
            pltpu.make_async_remote_copy(
                src_ref=src[i], dst_ref=dst[i], send_sem=wss.at[way, j, i], recv_sem=wrs.at[way, j, i],
                device_id=device, device_id_type=MESH,
            )
            for i in range(3)
        ]

    def y_copies(j, which):
        return [
            pltpu.make_async_remote_copy(
                src_ref=ref, dst_ref=ref, send_sem=yss.at[j, i], recv_sem=yrs.at[j, i],
                device_id=TO_Y, device_id_type=MESH,
            )
            for i, ref in enumerate((up_half(wu.at[j], which), down_half(wd.at[j], which)))
        ]

    def start_all(items):
        for item in items:
            item.start()

    @pl.when(z < Z - 1)
    def _():
        start_all(z_copies(z, 0, RIGHT, True))

    @pl.when(z > 0)
    def _():
        start_all(z_copies(z, 1, LEFT, True))

    def weight_step(k):
        @pl.when(z - k >= 0)
        def _():
            j = z - k
            for item in z_copies(j, 0, RIGHT, False):
                item.wait_recv()

            @pl.when(z < Z - 1)
            def _():
                start_all(z_copies(j, 0, RIGHT, False))

            start_all(y_copies(j, grp))

        @pl.when(z + k <= Z - 1)
        def _():
            j = z + k
            for item in z_copies(j, 1, LEFT, False):
                item.wait_recv()

            @pl.when(z > 0)
            def _():
                start_all(z_copies(j, 1, LEFT, False))

            start_all(y_copies(j, grp))

    orders = ((1, 2, 3, 0), (0, 2, 3, 1), (3, 1, 0, 2), (2, 1, 0, 3))

    def order(n):
        return pick([orders[a][n] for a in range(Z)], z)

    pending = []

    def act(places, body, sends=()):
        for place in places:
            @pl.when(z == place)
            def _(place=place):
                body(place)
                for make in sends:
                    make(place).start()

            pending.extend((place, make) for make in sends)

    EVERY = (0, 1, 2, 3)

    def ffn_copy(j):
        return pltpu.make_async_remote_copy(
            src_ref=g_s.at[1 - x, j], dst_ref=rx.at[j], send_sem=hss.at[j], recv_sem=hrs.at[j],
            device_id=TO_X, device_id_type=MESH,
        )

    def add_rows(ref, others):
        @pl.loop(0, 6)
        def _(i):
            rows = rows_of(i * 128, 128)
            total = ref[rows].astype(F32)
            for other_ref in others:
                total = total + other_ref[rows].astype(F32)
            ref[rows] = total.astype(BF)

    def z_send(n, place):
        j = orders[place][n]
        end = place in (0, 3)
        adjacent_end = 0 if place == 1 else 3
        if end:
            target, slot = (1 if place == 0 else 2), j
        elif j == adjacent_end:
            target, slot = j, place
        elif j in (0, 3):
            target, slot = j, place
        else:
            target, slot = j, (0 if j == 1 else 3)
        return pltpu.make_async_remote_copy(
            src_ref=g_s.at[x, j], dst_ref=rz.at[slot], send_sem=fss.at[n], recv_sem=frs.at[slot],
            device_id={"mlp": target}, device_id_type=MESH,
        )

    def z_wait(slot):
        pltpu.make_async_remote_copy(
            src_ref=rz.at[slot], dst_ref=rz.at[slot], send_sem=fss.at[0], recv_sem=frs.at[slot],
            device_id=LEFT, device_id_type=MESH,
        ).wait_recv()

    def ffn_x(n):
        j = order(n)
        ffn_copy(j).wait_recv()
        add_rows(g_s.at[x, j], [rx.at[j]])
        if n < 3:
            places = EVERY if n == 0 else (0, 3)
            act(places, lambda place: None, [lambda place: z_send(n, place)])

    def ffn_z(n):
        def body(place):
            j = orders[place][n]
            z_wait(j)
            add_rows(g_s.at[x, j], [rz.at[j]])

        act((1, 2), body, [lambda place: z_send(n, place)])

    def final_copies(src, kind, first):
        lanes = pl.ds(pl.multiple_of(c * 384, 128), 384)
        return [
            local(src, ffn_o.at[kind, :, lanes], 21 + first),
            remote(src, ffn_o.at[kind, :, lanes], 16 + first, TO_CORE),
        ]

    def ffn_own():
        def body(place):
            slots = {0: (1, 2), 3: (1, 2), 1: (1, 0), 2: (2, 3)}[place]
            for slot in slots:
                z_wait(slot)
            add_rows(g_s.at[x, place], [rz.at[slot] for slot in slots])

        act(EVERY, body)
        remote(g_s.at[x, z], fxr, 15, TO_X).start()
        for item in final_copies(g_s.at[x, z], x, 0):
            item.start()

    def ffn_last():
        remote(g_s.at[x, z], fxr, 15, TO_X).wait_recv()
        for item in final_copies(fxr, 1 - x, 1):
            item.start()

    def quarter(ref, p, q):
        return ref.at[p, pl.ds(q * 192, 192)]

    def hop(kind, p, q, place):
        step = 1 if kind in (0, 2) else -1
        src = quarter(b_s if kind < 2 else fb, p, q)
        dst = quarter((wu, wd, fb, fb)[kind], p, q)
        return pltpu.make_async_remote_copy(
            src_ref=src, dst_ref=dst, send_sem=bss.at[kind, p, q], recv_sem=brs.at[kind, p, q],
            device_id={"mlp": place + step}, device_id_type=MESH,
        )

    def hop_wait(kind, p, q):
        dst = quarter((wu, wd, fb, fb)[kind], p, q)
        pltpu.make_async_remote_copy(
            src_ref=dst, dst_ref=dst, send_sem=bss.at[kind, p, q], recv_sem=brs.at[kind, p, q],
            device_id=LEFT, device_id_type=MESH,
        ).wait_recv()

    def hops(kind, p, *qs):
        return [lambda place, q=q: hop(kind, p, q, place) for q in qs]

    def add_quarter(p, q, refs):
        total = quarter(b_s, p, q)[...].astype(F32)
        for ref in refs:
            total = total + quarter(ref, p, q)[...].astype(F32)
        quarter(b_s, p, q)[...] = total.astype(BF)

    def sum_0(p):
        act((0,), lambda place: None, hops(0, p, 3, 2, 1))
        act((3,), lambda place: None, hops(1, p, 0, 1, 2))

    def relay(kind, p, q):
        hop_wait(kind, p, q)
        add_quarter(p, q, [wu if kind == 0 else wd])

    def sum_1(p):
        act((1,), lambda place: relay(0, p, 3), hops(0, p, 3))
        act((2,), lambda place: relay(1, p, 0), hops(1, p, 0))
        act((1,), lambda place: relay(0, p, 2), hops(0, p, 2))
        act((2,), lambda place: relay(1, p, 1), hops(1, p, 1))

    def sum_2(p):
        act((2,), lambda place: relay(0, p, 3), hops(0, p, 3))
        act((1,), lambda place: relay(1, p, 0), hops(1, p, 0))

    def cross(p, place):
        return pltpu.make_async_remote_copy(
            src_ref=quarter(b_s, p, place), dst_ref=rxb.at[p], send_sem=hss.at[4 + p],
            recv_sem=hrs.at[4 + p], device_id=TO_X, device_id_type=MESH,
        )

    def sum_3(p):
        def body(place):
            refs = []
            if place > 0:
                hop_wait(0, p, place)
                refs.append(wu)
            if place < 3:
                hop_wait(1, p, place)
                refs.append(wd)
            add_quarter(p, place, refs)

        act(EVERY, body, [lambda place: cross(p, place)])

    def sum_4(p):
        def body(place):
            cross(p, place).wait_recv()
            total = quarter(b_s, p, place)[...].astype(F32) + rxb[p].astype(F32)
            quarter(fb, p, place)[...] = total.astype(BF)

        for place in EVERY:
            sends = hops(2, p, place) if place < 3 else []
            sends += hops(3, p, place) if place > 0 else []
            act((place,), body, sends)

    def sum_5(p):
        act((1,), lambda place: hop_wait(2, p, 0), hops(2, p, 0))
        act((2,), lambda place: hop_wait(3, p, 3), hops(3, p, 3))
        act((1,), lambda place: hop_wait(3, p, 2), hops(3, p, 2))
        act((2,), lambda place: hop_wait(2, p, 1), hops(2, p, 1))

    def sum_6(p):
        act((1,), lambda place: hop_wait(3, p, 3), hops(3, p, 3))
        act((2,), lambda place: hop_wait(2, p, 0), hops(2, p, 0))

    def piece_copies(p):
        if p == 0:
            pairs = [
                (fb.at[0, pl.ds(n * 384, 384)], outw_o.at[rows_of(c * 384, 384), pl.ds(n * 384, 384)])
                for n in range(2)
            ]
        else:
            pairs = [
                (
                    fb.at[p, :, pl.ds(part * 128, 128)],
                    qkv_o.at[
                        :, pl.ds(pl.multiple_of(part * D + c * 384 + (p - 1) * 128, 128), 128)
                    ],
                )
                for part in range(3)
            ]
        copies = []
        for n, (src, dst) in enumerate(pairs):
            copies.append(local(src, dst, 23 + p * 3 + n))
            copies.append(remote(src, dst, 18 + p * 3 + n, TO_CORE))
        return copies

    def sum_7(p):
        def body(place):
            for q in range(4):
                if place == 0 and q > 0:
                    hop_wait(3, p, q)
                if place == 3 and q < 3:
                    hop_wait(2, p, q)

        act((0, 3), body)
        for item in piece_copies(p):
            item.start()

    plan = {
        0: [],
        1: [lambda: ffn_x(1)],
        2: [lambda: sum_1(0)],
        3: [lambda: ffn_z(1)],
        4: [lambda: ffn_x(2), lambda: sum_2(0)],
        5: [lambda: sum_3(0), lambda: sum_1(1)],
        6: [lambda: ffn_z(2)],
        7: [lambda: ffn_x(3), lambda: sum_4(0), lambda: sum_2(1), lambda: out_copies(out_o, 0)[1].start()],
        8: [lambda: sum_5(0), lambda: sum_3(1), lambda: sum_1(2)],
        9: [],
        10: [lambda: sum_6(0), lambda: sum_4(1), lambda: sum_2(2)],
        11: [lambda: sum_7(0), lambda: sum_5(1), lambda: sum_3(2), lambda: sum_1(3), lambda: ffn_own()],
        12: [lambda: sum_6(1), lambda: sum_4(2), lambda: sum_2(3)],
        13: [lambda: sum_7(1), lambda: sum_5(2), lambda: sum_3(3)],
        14: [
            lambda: sum_6(2), lambda: sum_4(3), lambda: ffn_last(), lambda: sum_7(2),
            lambda: sum_5(3), lambda: sum_6(3), lambda: sum_7(3),
        ],
    }

    def slot(number):
        for task in plan[number]:
            task()

    local(adaw_h, adaw, 1).wait()
    for part in range(6):
        span = pl.ds(part * D, D)
        mod2[:, span] = dot(cond[...], adaw[:, span]) + adab[:, span]
    modrow = mod2[pl.ds(x, 1), :]
    shift_one, scale_one, gate_one, shift_two, scale_two, gate_two = [
        modrow[:, part * D : (part + 1) * D] for part in range(6)
    ]

    def layer_norm(values):
        center = values - jnp.mean(values, axis=-1, keepdims=True)
        inv = lax.rsqrt(jnp.mean(center * center, axis=-1, keepdims=True) + 1e-05)
        return center * inv, inv

    TILE = 64
    mul_one = again[...] * (1.0 + scale_one)
    mul_two = fgain[...] * (1.0 + scale_two)

    def norm_one_block(block):
        @pl.loop(0, 256 // TILE)
        def _(i):
            at = block * 256 + i * TILE
            rows = rows_of(at, TILE)
            normed, inv = layer_norm(xb[rows].astype(F32))
            n1[rows] = normed
            i1[rows] = inv
            ai[rows_of(own + at, TILE)] = (normed * mul_one + shift_one).astype(BF)

    def core_rows(ref, start, size, index):
        part = ref.at[rows_of(start, size)]
        return remote(part, part, index, TO_CORE)

    for item in loads[2:15]:
        item.wait()

    def project_block(block):
        @pl.loop(0, 2)
        def _(half_core):
            start = half_core * 512 + block * 256
            rows = rows_of(start, 256)
            tile = ai[rows]
            ait[:, rows] = tile.T
            cos_t, sin_t = cos_v[rows], sin_v[rows]

            @pl.loop(0, 3)
            def _(p):
                projected = dot(tile, wq[p])
                query = projected[:, :128]
                key = projected[:, 128:256]
                value = projected[:, 256:].astype(BF)
                query = (query * cos_t + swap_halves(query) * sin_t).astype(BF)
                key = (key * cos_t + swap_halves(key) * sin_t).astype(BF)
                q_s[p, rows] = query * jnp.asarray(0.125, BF)
                k_s[p, rows] = key
                v_s[p, rows] = value
                kt_s[p, :, rows] = key.T
                vt_s[p, :, rows] = value.T

    loads[0].wait()
    norm_one_block(x)
    core_rows(ai, own + x * 256, 256, 2).start()
    core_rows(ai, other + x * 256, 256, 2).wait_recv()
    project_block(x)
    swap_x.wait_recv()
    norm_one_block(1 - x)
    core_rows(ai, own + (1 - x) * 256, 256, 3).start()
    core_rows(ai, other + (1 - x) * 256, 256, 3).wait_recv()
    project_block(1 - x)
    for item in loads[16:19] + loads[20:]:
        item.wait()
    weight_step(1)

    low_lane = lax.broadcasted_iota(jnp.int32, (1, 128), 1) < 64
    keep = [low_lane.astype(F32).astype(BF), (~low_lane).astype(F32).astype(BF)]

    def att_copy(p, start):
        return remote(
            att_s.at[:, pl.ds(p * 128, 128)],
            att.at[:, pl.ds(pl.multiple_of(c * 384 + p * 128, 128), 128)],
            4 + p,
            TO_CORE,
        )

    def attend(p):
        @pl.loop(0, 4)
        def _(t):
            cols = rows_of(t * 256, 256)
            query = q_s[p, cols]
            keys = k_s[p]
            outs = []
            for h in range(2):
                masked = query * keep[h]
                scores = dot_t(keys, masked)
                top = jnp.max(scores, axis=0, keepdims=True)
                expd = jnp.exp(scores - top)
                total = jnp.sum(expd, axis=0, keepdims=True)
                lse[p, pl.ds(h, 1), cols] = top + jnp.log(total)
                out = dot(vt_s[p, pl.ds(h * 64, 64), :], expd.astype(BF)) / total
                ot_s[p, pl.ds(h * 64, 64), cols] = out
                outs.append(out)
            natural = jnp.concatenate(outs, axis=0).T.astype(BF)
            lanes = pl.ds(pl.multiple_of(c * 384 + p * 128, 128), 128)

            @pl.when(t // 2 == c)
            def _():
                att[rows_of((t % 2) * 256, 256), lanes] = natural

            @pl.when(t // 2 != c)
            def _():
                att_s[rows_of((t % 2) * 256, 256), pl.ds(p * 128, 128)] = natural

        att_copy(p, True).start()

    attend(0)
    attend(1)
    weight_step(2)

    loads[19].wait()
    swap_c.wait_recv()

    @pl.loop(0, 512 // TILE)
    def _(i):
        at = i * TILE
        gf[rows_of(own + at, TILE)] = (gate_two * ctb[rows_of(at, TILE)].astype(F32)).astype(BF)

    core_rows(gf, own, 512, 7).start()
    attend(2)
    vec[...] = jnp.zeros_like(vec)

    @pl.loop(0, 512 // TILE)
    def _(i):
        vec[8:9] += jnp.sum(gf[rows_of(own + i * TILE, TILE)].astype(F32), axis=0, keepdims=True)

    for p in range(3):
        remote(
            att_s.at[:, pl.ds(p * 128, 128)],
            att.at[:, pl.ds(pl.multiple_of((1 - c) * 384 + p * 128, 128), 128)],
            4 + p,
            TO_CORE,
        ).wait_recv()
    loads[15].wait()

    core_rows(ai, own + x * 256, 256, 2).wait_send()
    core_rows(ai, own + (1 - x) * 256, 256, 3).wait_send()
    fi = ai

    @pl.loop(0, 2)
    def _(b):
        rows = rows_of(b * 256, 256)
        ap[rows] = dot(att[rows], wo[...])

        @pl.loop(0, 256 // TILE)
        def _(i):
            at = b * 256 + i * TILE
            tile = rows_of(at, TILE)
            middle = xb[tile].astype(F32) + gate_one * ap[tile]
            normed, inv = layer_norm(middle)
            n2[tile] = normed
            i2[tile] = inv
            fi[rows_of(own + at, TILE)] = (normed * mul_two + shift_two).astype(BF)

    core_rows(fi, own, 512, 8).start()
    core_rows(gf, other, 512, 7).wait_recv()

    @pl.loop(0, 4)
    def _(t):
        rows = rows_of(t * 256, 256)
        gft[:, rows] = gf[rows].T

    core_rows(fi, other, 512, 8).wait_recv()

    @pl.loop(0, 4)
    def _(t):
        rows = rows_of(t * 256, 256)
        fit[:, rows] = fi[rows].T

    coef = 0.7978845608028654

    @pl.loop(0, Z)
    def _(k):
        j = pick([order(n) for n in range(Z)], k)

        @pl.when(k == 2)
        def _():
            weight_step(3)

        @pl.when(k == 3)
        def _():
            ffn_x(0)

        @pl.when(k < 3)
        def _():
            for item in y_copies(j, 1 - grp):
                item.wait_recv()

        bias = ub[j][:, pl.ds(0, 384)]
        bias = jnp.where(c == 0, bias, ub[j][:, pl.ds(384, 384)])

        @pl.loop(0, 4)
        def _(t):
            rows = rows_of(t * 256, 256)
            pre = dot(fi[rows], wu[j]) + bias
            sq = pre * pre
            th = jnp.tanh(coef * (pre + 0.044715 * pre * sq))
            act = (0.5 * pre * (1.0 + th)).astype(BF)
            slope = 0.5 * (1.0 + th) + 0.5 * pre * (1.0 - th * th) * coef * (1.0 + 3.0 * 0.044715 * sq)
            a_s[rows] = act
            grad_act = dot_t(gf[rows, :384], wd[j, :384]) + dot_t(gf[rows, 384:], wd[j, 384:])
            grad_pre = (grad_act * slope).astype(BF)
            gp_s[rows] = grad_pre
            bsum = jnp.sum(grad_pre.astype(F32), axis=0, keepdims=True)
            out_a = dot(act, wd[j, :384])
            out_b = dot(act, wd[j, 384:])
            gin = dot_t(grad_pre, wu[j])

            @pl.when(k == 0)
            def _():
                oacc[rows, :384] = out_a
                oacc[rows, 384:] = out_b
                gacc[rows] = gin

            @pl.when(k > 0)
            def _():
                oacc[rows, :384] += out_a
                oacc[rows, 384:] += out_b
                gacc[rows] += gin

            @pl.when(t == 0)
            def _():
                ubg[j] = bsum

            @pl.when(t > 0)
            def _():
                ubg[j] += bsum

        @pl.loop(0, 3)
        def _(r):
            rows = rows_of(r * 256, 256)
            g_s[0, j, rows] = dot(fit[rows], gp_s[...]).astype(BF)
            g_s[1, j, rows] = dot(gft[rows], a_s[...]).astype(BF)

        ffn_copy(j).start()

    def give_credit():
        @pl.when(z > 0)
        def _():
            pl.semaphore_signal(credit.at[0], 1, device_id=LEFT, device_id_type=MESH)

        @pl.when(z < Z - 1)
        def _():
            pl.semaphore_signal(credit.at[1], 1, device_id=RIGHT, device_id_type=MESH)

    def take_credit():
        @pl.when(z < Z - 1)
        def _():
            pl.semaphore_wait(credit.at[0], 1)

        @pl.when(z > 0)
        def _():
            pl.semaphore_wait(credit.at[1], 1)


    def weight_waits(k):
        @pl.when(z - k >= 0)
        def _():
            @pl.when(z < Z - 1)
            def _():
                for item in z_copies(z - k, 0, RIGHT, False):
                    item.wait_send()

            for item in y_copies(z - k, grp):
                item.wait_send()

        @pl.when(z + k <= Z - 1)
        def _():
            @pl.when(z > 0)
            def _():
                for item in z_copies(z + k, 1, LEFT, False):
                    item.wait_send()

            for item in y_copies(z + k, grp):
                item.wait_send()

    @pl.when(z < Z - 1)
    def _():
        for item in z_copies(z, 0, RIGHT, False):
            item.wait_send()

    @pl.when(z > 0)
    def _():
        for item in z_copies(z, 1, LEFT, False):
            item.wait_send()

    pl.loop(1, Z)(weight_waits)
    give_credit()

    osend, gsend = xs.at[0], xs.at[1]

    @pl.loop(0, 512 // TILE)
    def _(i):
        tile = rows_of(i * TILE, TILE)
        far = rows_of(other + i * TILE, TILE)
        gsend[tile] = gacc[far].astype(BF)

    remote(gsend, grecv, 9, TO_CORE).start()

    @pl.loop(0, 512 // TILE)
    def _(i):
        osend[rows_of(i * TILE, TILE)] = oacc[rows_of(other + i * TILE, TILE)].astype(BF)

    orecv = att
    remote(osend, orecv, 10, TO_CORE).start()
    remote(gsend, grecv, 9, TO_CORE).wait_recv()
    core_rows(gf, own, 512, 7).wait_send()

    def norm_back(grad, normed, inv):
        return inv * (
            grad
            - jnp.mean(grad, axis=-1, keepdims=True)
            - normed * jnp.mean(grad * normed, axis=-1, keepdims=True)
        )

    @pl.loop(0, 512 // TILE)
    def _(i):
        tile = rows_of(i * TILE, TILE)
        near = rows_of(own + i * TILE, TILE)
        grad = gacc[near] + grecv[tile].astype(F32)
        normed = n2[tile]
        vec[3:4] += jnp.sum(grad, axis=0, keepdims=True)
        vec[4:5] += jnp.sum(grad * normed, axis=0, keepdims=True)
        middle = ctb[tile].astype(F32) + norm_back(grad * mul_two, normed, i2[tile])
        gm[tile] = middle
        gf[near] = (gate_one * middle).astype(BF)
        vec[2:3] += jnp.sum(middle * ap[tile], axis=0, keepdims=True)

    gproj = gf
    core_rows(gproj, own, 512, 11).start()
    slot(0)

    remote(osend, orecv, 10, TO_CORE).wait()

    def rows_out(number, i, values):
        xs[number, rows_of(i * TILE, TILE)] = values.astype(BF)

    def out_copies(out_ref, number):
        here, there = rows_of(x * 256, 256), rows_of((1 - x) * 256, 256)
        return [
            local(xs.at[number, here], out_ref.at[x], 35 + number),
            remote(xs.at[number, there], out_ref.at[x], 12 + number, TO_X),
        ]

    @pl.loop(0, 512 // TILE)
    def _(i):
        tile = rows_of(i * TILE, TILE)
        ffn = oacc[rows_of(own + i * TILE, TILE)] + orecv[tile].astype(F32) + downb[...]
        vec[5:6] += jnp.sum(ctb[tile].astype(F32) * ffn, axis=0, keepdims=True)
        rows_out(0, i, xb[tile].astype(F32) + gate_one * ap[tile] + gate_two * ffn)

    out_copies(out_o, 0)[0].start()

    core_rows(gproj, other, 512, 11).wait_recv()

    @pl.loop(0, 4)
    def _(t):
        rows = rows_of(t * 256, 256)
        grad = dot_t(gproj[rows], wo[rows_of(c * 384, 384)])
        for p in range(3):
            part = grad[:, p * 128 : (p + 1) * 128].astype(BF)
            do_s[p, rows] = part
            product = part.astype(F32).T * ot_s[p, :, rows]
            for h in range(2):
                dlt[p, pl.ds(h, 1), rows] = jnp.sum(
                    product[h * 64 : (h + 1) * 64], axis=0, keepdims=True
                )

    for p in range(3):
        @pl.loop(0, 2)
        def _(n):
            lanes = pl.ds(pl.multiple_of(n * 384, 128), 384)
            b_s[0, rows_of(n * 384 + p * 128, 128)] = dot(
                ot_s[p].astype(BF), gproj[:, lanes]
            ).astype(BF)

    take_credit()
    sum_0(0)
    slot(1)

    def attend_back(p):
        for h in range(2):
            a_s[:, h * 128 : (h + 1) * 128] = q_s[p] * keep[h]
            gp_s[:, h * 128 : (h + 1) * 128] = do_s[p] * keep[h]
        dqt[...] = jnp.zeros_like(dqt)

        @pl.loop(0, 4)
        def _(t):
            rows = rows_of(t * 256, 256)
            keys, values = k_s[p, rows], v_s[p, rows]
            dv, dk = None, None
            for h in range(2):
                qm, dom = a_s[:, h * 128 : (h + 1) * 128], gp_s[:, h * 128 : (h + 1) * 128]
                probs = jnp.exp(dot_t(keys, qm) - lse[p, pl.ds(h, 1), :])
                grads = dot_t(values, dom)
                ds = (probs * (grads - dlt[p, pl.ds(h, 1), :])).astype(BF)
                dv_h = dot(probs.astype(BF), dom)
                dk_h = dot(ds, qm)
                dv = dv_h if dv is None else dv + dv_h
                dk = dk_h if dk is None else dk + dk_h
                dqt[pl.ds(h * 64, 64)] += dot(kt_s[p, pl.ds(h * 64, 64), rows], ds)
            cos_t, sin_t = cos_v[rows], sin_v[rows]
            gq[rows, pl.ds(128, 128)] = (dk * cos_t - swap_halves(dk) * sin_t).astype(BF)
            gq[rows, pl.ds(256, 128)] = dv.astype(BF)

            @pl.when(t == 1)
            def _():
                slot(2 + 3 * p)

        slot(3 + 3 * p)

        @pl.loop(0, 4)
        def _(t):
            rows = rows_of(t * 256, 256)
            block = dqt[:, rows] * 0.125
            cos_t, sin_t = cost[:, rows], sint[:, rows]
            parts = []
            for h in range(2):
                u, w = block[h * 64 : h * 64 + 32], block[h * 64 + 32 : h * 64 + 64]
                parts += [u * cos_t + w * sin_t, w * cos_t - u * sin_t]
            gq[rows, pl.ds(0, 128)] = jnp.concatenate(parts, axis=0).T.astype(BF)

        @pl.loop(0, 3)
        def _(r):
            rows = rows_of(r * 256, 256)
            b_s[1 + p, rows] = dot(ait[rows], gq[...]).astype(BF)

        sum_0(1 + p)

        @pl.loop(0, 4)
        def _(t):
            rows = rows_of(t * 256, 256)
            part = dot_t(gq[rows], wq[p])
            if p == 0:
                gacc[rows] = part
            else:
                gacc[rows] += part

        slot(4 + 3 * p)

    remote(gsend, grecv, 9, TO_CORE).wait_send()
    for p in range(3):
        attend_back(p)

    @pl.loop(0, 512 // TILE)
    def _(i):
        gsend[rows_of(i * TILE, TILE)] = gacc[rows_of(other + i * TILE, TILE)].astype(BF)

    remote(gsend, grecv, 14, TO_CORE).start()
    slot(11)
    remote(gsend, grecv, 14, TO_CORE).wait()

    @pl.loop(0, 512 // TILE)
    def _(i):
        tile = rows_of(i * TILE, TILE)
        near = rows_of(own + i * TILE, TILE)
        grad = gacc[near] + grecv[tile].astype(F32)
        normed = n1[tile]
        vec[0:1] += jnp.sum(grad, axis=0, keepdims=True)
        vec[1:2] += jnp.sum(grad * normed, axis=0, keepdims=True)
        rows_out(1, i, gm[tile] + norm_back(grad * mul_one, normed, i1[tile]))

    for item in out_copies(gin_o, 1):
        item.start()
    sums = vec[...]
    vec[6:7] = sums[1:2] * (1.0 + scale_one)
    vec[7:8] = sums[4:5] * (1.0 + scale_two)
    vec[1:2] = sums[1:2] * again[...]
    vec[4:5] = sums[4:5] * fgain[...]
    for core in range(2):
        @pl.when(c == core)
        def _():
            for j in range(4):
                vec[9 + 2 * core + j // 2, pl.ds((j % 2) * 384, 384)] = ubg[j, 0]

    both = cond[...].astype(F32)
    vec[13:14, :128] = 0.5 * jnp.where(x == 0, both[0:1], both[1:2])
    remote(vec, vecr, 30, TO_CORE).start()
    slot(12)
    remote(vec, vecr, 30, TO_CORE).wait_recv()
    chip = 2 * z + x
    vall[chip] = vec[...] + vecr[...]

    def vec_copy(n, slot):
        return pltpu.make_async_remote_copy(
            src_ref=vall.at[slot], dst_ref=vall.at[slot], send_sem=vss.at[n], recv_sem=vrs.at[n],
            device_id=peers[n], device_id_type=MESH,
        )

    for n in range(len(peers)):
        vec_copy(n, chip).start()
    slot(13)
    for n in range(len(peers)):
        vec_copy(n, 2 * peers[n]["mlp"] + peers[n]["seq"] // 2).wait_recv()

    high = lax.Precision.HIGHEST
    everyone = vall[:, 13, :128]
    total = vall[0]
    for n in range(1, 8):
        total = total + vall[n]
    acc = None
    ada_out = []
    sstage[...] = jnp.zeros_like(sstage)
    for part in range(6):
        span = pl.ds(part * D, D)
        grads = vall[:, part, :]
        sstage[part : part + 1] = total[part : part + 1]
        oacc[pl.ds(part * 128, 128)] = lax.dot_general(
            everyone, grads, (((0,), (0,)), ((), ())), precision=high, preferred_element_type=F32
        )
        ada_out.append(local(oacc.at[pl.ds(part * 128, 128)], adaw_o.at[:, span], 37 + part))
        ada_out[-1].start()
        piece = lax.dot_general(
            grads, adaw[:, span].astype(F32), (((1,), (1,)), ((), ())), precision=high,
            preferred_element_type=F32,
        )
        acc = piece if acc is None else acc + piece
    cstage[...] = acc
    for n in range(3):
        sstage[6 + n : 7 + n] = total[6 + n : 7 + n]
    for core in range(2):
        halves = [total[9 + 2 * core + j // 2, (j % 2) * 384 : (j % 2 + 1) * 384] for j in range(4)]
        mine = halves[0]
        for j in range(1, 4):
            mine = jnp.where(z == j, halves[j], mine)
        sstage[9, pl.ds(core * 384, 384)] = mine
    cond_o[...] = cstage[pl.ds(2 * z, 2), :]
    small_o[...] = sstage[...]
    slot(14)
    for item in ada_out:
        item.wait()

    for number, ref in ((0, out_o), (1, gin_o)):
        out_copies(ref, number)[0].wait()
        out_copies(ref, number)[1].wait()
    for p in range(4):
        for item in piece_copies(p):
            item.wait()
    for first, (src, kind) in enumerate(((g_s.at[x, z], x), (fxr, 1 - x))):
        for item in final_copies(src, kind, first):
            item.wait()
    for n in range(len(peers)):
        vec_copy(n, chip).wait_send()
    swap_x.wait_send()
    swap_c.wait_send()
    for p in range(3):
        att_copy(p, False).wait_send()
    core_rows(fi, own, 512, 8).wait_send()
    core_rows(gproj, own, 512, 11).wait_send()
    remote(vec, vecr, 30, TO_CORE).wait_send()
    remote(g_s.at[x, z], fxr, 15, TO_X).wait_send()
    for j in range(4):
        ffn_copy(j).wait_send()
    for place in EVERY:
        @pl.when(z == place)
        def _(place=place):
            for where, make in pending:
                if where == place:
                    make(place).wait_send()


def tables(seg_len, seq_size):
    half = np.arange(32)
    frequency = 10000.0 ** (-2.0 * half / 64)
    core, chip, token = np.meshgrid(
        np.arange(2), np.arange(seq_size // 2), np.arange(seg_len), indexing="ij"
    )
    place = ((chip * 2 + core) * seg_len + token).reshape(-1)
    angle = place[:, None] * frequency[None, :]
    cos, sin = np.cos(angle).astype(np.float32), np.sin(angle).astype(np.float32)
    return (
        np.tile(cos, (1, 4)),
        np.concatenate([-sin, sin, -sin, sin], axis=1),
        np.ascontiguousarray(cos.T),
        np.ascontiguousarray(sin.T),
    )


def fast_shards(
    inputs, condition, attn_gain, ada_weight, ada_bias, qkv_weight, out_weight, ffn_gain,
    up_weight, up_bias, down_weight, down_bias, cotangent,
):
    Z = lax.axis_size("mlp")
    tabs = [jnp.asarray(t) for t in tables(inputs.shape[1], lax.axis_size("seq"))]
    hbm, vm = pl.BlockSpec(memory_space=pl.ANY), pl.BlockSpec(memory_space=pltpu.VMEM)
    shape = jax.ShapeDtypeStruct
    row = lambda v: v.reshape(1, -1)
    V = pltpu.VMEM
    dma = pltpu.SemaphoreType.DMA
    scratch = [
        V((128, 4608), BF), V((3, 768, 384), BF), V((768, 768), BF), V((Z, 768, 384), BF),
        V((Z, 768, 384), BF), V((Z, 1, 768), F32), V((1024, 128), F32), V((1024, 128), F32),
        V((32, 1024), F32), V((32, 1024), F32),
        V((512, 768), BF), V((512, 768), BF), V((2, 4608), F32), V((512, 768), F32), V((512, 1), F32),
        V((1024, 768), BF), V((768, 1024), BF),
        V((3, 1024, 128), BF), V((3, 1024, 128), BF), V((3, 1024, 128), BF),
        V((3, 128, 1024), BF), V((3, 128, 1024), BF), V((3, 128, 1024), F32), V((3, 2, 1024), F32),
        V((512, 768), BF), V((512, 384), BF),
        V((512, 768), F32), V((512, 768), F32), V((512, 1), F32),
        V((768, 1024), BF), V((1024, 768), BF), V((768, 1024), BF),
        V((1024, 768), F32), V((1024, 768), F32), V((1024, 384), BF), V((1024, 384), BF),
        V((2, Z, 768, 384), BF), V((512, 768), BF),
        V((512, 768), F32), V((3, 1024, 128), BF), V((3, 2, 1024), F32), V((128, 1024), F32),
        V((1024, 384), BF), V((4, 768, 384), BF), V((2, 512, 768), BF),
        V((16, 768), F32), V((16, 768), F32), V((2 * Z, 16, 768), F32), V((Z, 1, 384), F32),
        V((2 * Z, 128), F32), V((16, 768), F32),
        V((Z, 768, 384), BF), V((Z, 768, 384), BF), V((768, 384), BF), V((4, 192, 384), BF),
        V((4, 768, 384), BF),
        dma((43,)), dma((31,)), dma((31,)), dma((2, Z, 3)), dma((2, Z, 3)), dma((Z, 2)), dma((Z, 2)),
        dma((3,)), dma((4,)), dma((4, 4, 4)), dma((4, 4, 4)), dma((8,)), dma((8,)), dma((7,)), dma((7,)),
        pltpu.SemaphoreType.REGULAR((2,)),
    ]
    token = shape(inputs.shape, BF)
    out, gin, grad_cond, grad_ada, small, grad_qkv, grad_out, ffn = pl.pallas_call(
        fast_kernel,
        out_shape=[
            token, token, shape(condition.shape, F32), shape(ada_weight.shape, F32), shape((16, 768), F32),
            shape(qkv_weight.shape, BF), shape(out_weight.shape, BF), shape((2, 768, 768), BF),
        ],
        in_specs=[hbm, vm, vm, hbm, vm, hbm, hbm, vm, hbm, vm, hbm, vm, hbm, hbm, hbm, hbm, hbm],
        out_specs=[hbm, hbm, vm, hbm, vm, hbm, hbm, hbm],
        scratch_shapes=scratch,
        compiler_params=pltpu.CompilerParams(
            collective_id=0, has_side_effects=True, vmem_limit_bytes=VMEM_LIMIT
        ),
        name="block",
    )(
        inputs, condition, row(attn_gain), ada_weight, row(ada_bias), qkv_weight, out_weight,
        row(ffn_gain), up_weight, row(up_bias), down_weight, row(down_bias), cotangent, *tabs,
    )
    wide = lambda v: v.astype(F32)
    return (
        wide(out), wide(gin), grad_cond, small[6], grad_ada, small[:6].reshape(-1), wide(grad_qkv),
        wide(grad_out), small[7], wide(ffn[0]), small[9], wide(ffn[1]).T, small[8],
    )


def solution(mesh):
    placed = (
        P(("grp", "mlp"), "seq", None),
        P(("grp", "mlp"), None),
        P(),
        P(),
        P(),
        P(),
        P(),
        P(),
        P(None, "mlp"),
        P("mlp"),
        P("mlp", None),
        P(),
        P(("grp", "mlp"), "seq", None),
    )
    sizes = dict(mesh.shape)
    small = sizes["seq"] == 4 and sizes["grp"] == 2 and sizes["mlp"] == 4
    return jax.shard_map(
        fast_shards if small else shards,
        mesh=mesh,
        in_specs=placed,
        out_specs=(
            P(("grp", "mlp"), "seq", None),
            P(("grp", "mlp"), "seq", None),
            P(("grp", "mlp"), None),
            P("grp"),
            P("grp", None),
            P("grp"),
            P("grp", None),
            P("grp", None),
            P("grp"),
            P("grp", "mlp"),
            P(("grp", "mlp")),
            P(("grp", "mlp"), None),
            P("grp"),
        ),
        check_vma=False,
    )
```

```python
import math

import jax
import jax.numpy as jnp
import numpy as np
from jax import lax
from jax.experimental import pallas as pl
from jax.experimental.pallas import tpu as pltpu
from jax.sharding import PartitionSpec as P

HEADS = 12
VMEM_LIMIT = 62 * 2**20


gelu_coef = 0.7978845608028654


def layer_norm(values):
    center = values - jnp.mean(values, axis=-1, keepdims=True)
    inv_std = lax.rsqrt(jnp.mean(center * center, axis=-1, keepdims=True) + 1e-05)
    return (center * inv_std, inv_std)


def norm_back(grad_norm, normed, inv_std):
    return inv_std * (
        grad_norm
        - jnp.mean(grad_norm, axis=-1, keepdims=True)
        - normed * jnp.mean(grad_norm * normed, axis=-1, keepdims=True)
    )


def gelu_tanh(values):
    return (
        0.5 * values * (1.0 + jnp.tanh(gelu_coef * (values + 0.044715 * values * values * values)))
    )


def gelu_slope(values):
    tanh_val = jnp.tanh(gelu_coef * (values + 0.044715 * values * values * values))
    return 0.5 * (1.0 + tanh_val) + 0.5 * values * (1.0 - tanh_val * tanh_val) * gelu_coef * (
        1.0 + 3.0 * 0.044715 * values * values
    )


def rotary_tables(positions, head_size):
    half_dim = head_size // 2
    frequencies = jnp.power(10000.0, -2.0 * jnp.arange(half_dim, dtype=jnp.float32) / head_size)
    angles = positions[:, None] * frequencies[None, :]
    return (jnp.cos(angles), jnp.sin(angles))


def rotate(tensor, cos_tab, sine_tab):
    half_dim = tensor.shape[-1] // 2
    first_half = tensor[..., :half_dim]
    second_half = tensor[..., half_dim:]
    return jnp.concatenate(
        [
            first_half * cos_tab - second_half * sine_tab,
            second_half * cos_tab + first_half * sine_tab,
        ],
        axis=-1,
    )


def unrotate(tensor, cos_tab, sine_tab):
    half_dim = tensor.shape[-1] // 2
    first_half = tensor[..., :half_dim]
    second_half = tensor[..., half_dim:]
    return jnp.concatenate(
        [
            first_half * cos_tab + second_half * sine_tab,
            second_half * cos_tab - first_half * sine_tab,
        ],
        axis=-1,
    )


def score_of(query_rows, key_rows, scale_factor):
    return (
        jnp.einsum("sghd,skhd->shgk", query_rows, key_rows, preferred_element_type=jnp.float32)
        * scale_factor
    )


def score_grads(query_rows, dout_rows, lse_rows, delta_rows, key_rows, value_rows, scale_factor):
    prob_rows = jnp.exp(score_of(query_rows, key_rows, scale_factor) - lse_rows[..., None])
    grad_probs = jnp.einsum(
        "sghd,skhd->shgk", dout_rows, value_rows, preferred_element_type=jnp.float32
    )
    grad_scores = (prob_rows * (grad_probs - delta_rows[..., None])).astype(jnp.bfloat16)
    return (prob_rows.astype(jnp.bfloat16), grad_scores)


def shards(
    inputs,
    condition,
    attn_gain,
    ada_weight,
    ada_bias,
    qkv_weight,
    out_weight,
    ffn_gain,
    up_weight,
    up_bias,
    down_weight,
    down_bias,
    cotangent,
):
    seq_count, seg_len, model_width = inputs.shape
    head_count = HEADS
    head_size = model_width // head_count
    full_len = seg_len * lax.axis_size("seq")
    block_len = math.gcd(full_len, 512)
    block_count = full_len // block_len
    scale_factor = float(head_size) ** (-0.5)
    positions = (lax.axis_index("seq") * seg_len + jnp.arange(seg_len, dtype=jnp.int32)).astype(
        jnp.float32
    )
    cos_tab, sine_tab = rotary_tables(positions, head_size)
    cos_tab = cos_tab[None, :, None, :]
    sine_tab = sine_tab[None, :, None, :]

    def heads_view(matrix):
        return matrix.reshape(seq_count, seg_len, head_count, head_size)

    x_float = inputs.astype(jnp.float32)
    modulate = jnp.dot(condition, ada_weight, preferred_element_type=jnp.float32) + ada_bias
    shift_one, scale_one, gate_one, shift_two, scale_two, gate_two = [
        modulate[:, None, member * model_width : (member + 1) * model_width] for member in range(6)
    ]
    norm_one, inv_one = layer_norm(x_float)
    attn_in = (norm_one * attn_gain * (1.0 + scale_one) + shift_one).astype(jnp.bfloat16)
    projected = jnp.dot(attn_in, qkv_weight, preferred_element_type=jnp.float32)
    queries = rotate(heads_view(projected[..., :model_width]), cos_tab, sine_tab).astype(
        jnp.bfloat16
    )
    key_rot = rotate(
        heads_view(projected[..., model_width : 2 * model_width]), cos_tab, sine_tab
    ).astype(jnp.bfloat16)
    value_low = projected[..., 2 * model_width :].astype(jnp.bfloat16)
    kv_local = jnp.concatenate(
        [key_rot.reshape(seq_count, seg_len, model_width), value_low], axis=-1
    )
    kv_whole = lax.all_gather(kv_local, "seq", axis=1, tiled=True)
    kv_view = kv_whole.reshape(seq_count, full_len, 2, head_count, head_size)

    def key_block(block_num):
        sliced = lax.dynamic_slice_in_dim(kv_view, block_num * block_len, block_len, 1)
        return (sliced[:, :, 0], sliced[:, :, 1])

    def max_pass(block_num, running):
        run_max, run_sum = running
        key_rows, value_rows = key_block(block_num)
        scores = score_of(queries, key_rows, scale_factor)
        new_max = jnp.maximum(run_max, jnp.max(scores, axis=-1))
        run_sum = run_sum * jnp.exp(run_max - new_max) + jnp.sum(
            jnp.exp(scores - new_max[..., None]), axis=-1
        )
        return (new_max, run_sum)

    stat_shape = (seq_count, head_count, seg_len)
    run_max, run_sum = lax.fori_loop(
        0,
        block_count,
        max_pass,
        (jnp.full(stat_shape, -1e30, jnp.float32), jnp.zeros(stat_shape, jnp.float32)),
    )
    log_sum = run_max + jnp.log(run_sum)

    def out_pass(block_num, accums):
        accum_out, accum_exact = accums
        key_rows, value_rows = key_block(block_num)
        prob_rows = jnp.exp(score_of(queries, key_rows, scale_factor) - log_sum[..., None])
        accum_out = accum_out + jnp.einsum(
            "shgk,skhd->sghd",
            prob_rows.astype(jnp.bfloat16),
            value_rows,
            preferred_element_type=jnp.float32,
        )
        accum_exact = accum_exact + jnp.einsum(
            "shgk,skhd->sghd",
            prob_rows,
            value_rows.astype(jnp.float32),
            preferred_element_type=jnp.float32,
        )
        return (accum_out, accum_exact)

    head_shape = (seq_count, seg_len, head_count, head_size)
    attn_float, attn_exact = lax.fori_loop(
        0,
        block_count,
        out_pass,
        (jnp.zeros(head_shape, jnp.float32), jnp.zeros(head_shape, jnp.float32)),
    )
    attn_low = attn_float.reshape(seq_count, seg_len, model_width).astype(jnp.bfloat16)
    attn_proj = jnp.dot(attn_low, out_weight, preferred_element_type=jnp.float32)
    middle = x_float + gate_one * attn_proj
    norm_two, inv_two = layer_norm(middle)
    ffn_in = (norm_two * ffn_gain * (1.0 + scale_two) + shift_two).astype(jnp.bfloat16)
    ffn_rows = lax.all_gather(ffn_in, "mlp", axis=0, tiled=True)
    pre_act = jnp.dot(ffn_rows, up_weight, preferred_element_type=jnp.float32) + up_bias
    act_low = gelu_tanh(pre_act).astype(jnp.bfloat16)
    ffn_out = (
        lax.psum_scatter(
            jnp.dot(act_low, down_weight, preferred_element_type=jnp.float32).astype(jnp.bfloat16),
            "mlp",
            scatter_dimension=0,
            tiled=True,
        ).astype(jnp.float32)
        + down_bias
    )
    output = middle + gate_two * ffn_out
    cot_float = cotangent.astype(jnp.float32)
    grad_ffn = (gate_two * cot_float).astype(jnp.bfloat16)
    down_bias_part = jnp.sum(grad_ffn.astype(jnp.float32), axis=(0, 1))
    dgate_two = jnp.sum(cot_float * ffn_out, axis=1)
    grad_ffn_rows = lax.all_gather(grad_ffn, "mlp", axis=0, tiled=True)
    down_part = jnp.einsum(
        "sgf,sgd->fd", act_low, grad_ffn_rows, preferred_element_type=jnp.float32
    )
    grad_act = jnp.einsum(
        "sgd,fd->sgf", grad_ffn_rows, down_weight, preferred_element_type=jnp.float32
    )
    grad_pre = (grad_act * gelu_slope(pre_act)).astype(jnp.bfloat16)
    up_bias_part = jnp.sum(grad_pre.astype(jnp.float32), axis=(0, 1))
    up_part = jnp.einsum("sgd,sgf->df", ffn_rows, grad_pre, preferred_element_type=jnp.float32)
    grad_ffn_in = lax.psum_scatter(
        jnp.einsum("sgf,df->sgd", grad_pre, up_weight, preferred_element_type=jnp.float32).astype(
            jnp.bfloat16
        ),
        "mlp",
        scatter_dimension=0,
        tiled=True,
    ).astype(jnp.float32)
    dshift_two = jnp.sum(grad_ffn_in, axis=1)
    dscale_two = jnp.sum(grad_ffn_in * norm_two * ffn_gain, axis=1)
    gain_two_part = jnp.sum(grad_ffn_in * (1.0 + scale_two) * norm_two, axis=(0, 1))
    grad_middle = cot_float + norm_back(
        grad_ffn_in * (1.0 + scale_two) * ffn_gain, norm_two, inv_two
    )
    grad_proj = (gate_one * grad_middle).astype(jnp.bfloat16)
    dgate_one = jnp.sum(grad_middle * attn_proj, axis=1)
    out_part = jnp.einsum("sgd,sge->de", attn_low, grad_proj, preferred_element_type=jnp.float32)
    grad_attn = jnp.einsum(
        "sge,de->sgd", grad_proj, out_weight, preferred_element_type=jnp.float32
    ).astype(jnp.bfloat16)
    grad_attn_heads = heads_view(grad_attn)
    delta_rows = jnp.sum(grad_attn_heads.astype(jnp.float32) * attn_exact, axis=-1)
    delta_heads = jnp.transpose(delta_rows, (0, 2, 1))

    def back_pass(block_num, state_in):
        grad_query, key_grads = state_in
        key_rows, value_rows = key_block(block_num)
        prob_low, grad_scores = score_grads(
            queries, grad_attn_heads, log_sum, delta_heads, key_rows, value_rows, scale_factor
        )
        grad_query = (
            grad_query
            + jnp.einsum(
                "shgk,skhd->sghd", grad_scores, key_rows, preferred_element_type=jnp.float32
            )
            * scale_factor
        )
        grad_key = (
            jnp.einsum("shgk,sghd->skhd", grad_scores, queries, preferred_element_type=jnp.float32)
            * scale_factor
        )
        grad_value = jnp.einsum(
            "shgk,sghd->skhd", prob_low, grad_attn_heads, preferred_element_type=jnp.float32
        )
        stacked = jnp.concatenate(
            [
                grad_key.reshape(seq_count, block_len, model_width),
                grad_value.reshape(seq_count, block_len, model_width),
            ],
            axis=-1,
        )
        key_grads = lax.dynamic_update_slice_in_dim(key_grads, stacked, block_num * block_len, 1)
        return (grad_query, key_grads)

    grad_query, key_grads = lax.fori_loop(
        0,
        block_count,
        back_pass,
        (
            jnp.zeros(head_shape, jnp.float32),
            jnp.zeros((seq_count, full_len, 2 * model_width), jnp.float32),
        ),
    )
    kv_grads = lax.psum_scatter(
        key_grads.astype(jnp.bfloat16), "seq", scatter_dimension=1, tiled=True
    ).astype(jnp.float32)
    grad_key_rot = heads_view(kv_grads[..., :model_width])
    grad_values = kv_grads[..., model_width:]
    grad_qkv = jnp.concatenate(
        [
            unrotate(grad_query, cos_tab, sine_tab).reshape(seq_count, seg_len, model_width),
            unrotate(grad_key_rot, cos_tab, sine_tab).reshape(seq_count, seg_len, model_width),
            grad_values,
        ],
        axis=-1,
    ).astype(jnp.bfloat16)
    qkv_part = jnp.einsum("sgd,sge->de", attn_in, grad_qkv, preferred_element_type=jnp.float32)
    grad_attn_in = jnp.einsum(
        "sge,de->sgd", grad_qkv, qkv_weight, preferred_element_type=jnp.float32
    )
    dshift_one = jnp.sum(grad_attn_in, axis=1)
    dscale_one = jnp.sum(grad_attn_in * norm_one * attn_gain, axis=1)
    gain_one_part = jnp.sum(grad_attn_in * (1.0 + scale_one) * norm_one, axis=(0, 1))
    grad_inputs = grad_middle + norm_back(
        grad_attn_in * (1.0 + scale_one) * attn_gain, norm_one, inv_one
    )
    grad_modulate = jnp.concatenate(
        [dshift_one, dscale_one, dgate_one, dshift_two, dscale_two, dgate_two], axis=-1
    )
    ada_weight_part = jnp.dot(
        condition.astype(jnp.float32).T, grad_modulate, precision=lax.Precision.HIGHEST
    )
    ada_bias_part = jnp.sum(grad_modulate, axis=0)
    cond_part = jnp.dot(
        grad_modulate, ada_weight.astype(jnp.float32).T, precision=lax.Precision.HIGHEST
    )
    summed_all = lax.psum(
        (
            qkv_part,
            out_part,
            ada_weight_part,
            ada_bias_part,
            gain_one_part,
            gain_two_part,
            down_bias_part,
        ),
        ("seq", "mlp"),
    )
    summed_seq = (
        lax.psum(up_part.astype(jnp.bfloat16), "seq").astype(jnp.float32),
        lax.psum(up_bias_part.astype(jnp.bfloat16), "seq").astype(jnp.float32),
        lax.psum(down_part.astype(jnp.bfloat16), "seq").astype(jnp.float32),
        lax.psum(cond_part.astype(jnp.bfloat16), "seq").astype(jnp.float32),
    )
    return (
        output,
        grad_inputs,
        summed_seq[3],
        summed_all[4],
        summed_all[2],
        summed_all[3],
        summed_all[0],
        summed_all[1],
        summed_all[5],
        summed_seq[0],
        summed_seq[1],
        summed_seq[2],
        summed_all[6],
    )


FFN_X, FFN_Z, FFN_OWN, FFN_LAST, SUM_0, REL, SUM_3, SUM_4, FW, SUM_7, WL, WR, XS_, ZS, XO, OX, GX = range(17)
AT_W, AT_F, AT_A, AT_T, AT_N, AT_B, AT_E, AT_D, AT_G = range(9)
ORDERS = ((1, 2, 0, 3), (0, 2, 1, 3), (3, 1, 2, 0), (2, 1, 3, 0))
OWN_STEP = 2
PLAN = {(AT_A, 0, 0): {0: [(WR, 1)], 1: [(WL, 1), (WR, 1)], 2: [(WL, 1), (WR, 1)], 3: [(WL, 1)]},
 (AT_B, 0, 0): {0: [(OX, 1)], 1: [(OX, 1), (FFN_X, 3, 0)], 2: [(FFN_Z, 0, 0), (ZS, 0, 0), (OX, 1)], 3: [(OX, 1)]},
 (AT_B, 0, 1): {1: [(FFN_Z, 2, 2), (ZS, 2, 2)], 2: [(REL, 1, 0, 0)]},
 (AT_B, 0, 2): {0: [(XS_, 3, 2)], 1: [(XS_, 3, 1)], 2: [(XS_, 0, 1)], 3: [(XS_, 0, 2)]},
 (AT_B, 0, 3): {0: [(ZS, 3, 1)], 1: [(FFN_Z, 3, 0), (ZS, 3, 0)], 2: [(REL, 1, 1, 0)], 3: [(ZS, 0, 1)]},
 (AT_B, 0, 5): {0: [(SUM_0, 1), (XS_, 0, 0)],
                1: [(REL, 0, 3, 0), (XS_, 3, 2)],
                2: [(REL, 0, 3, 0), (XS_, 0, 2)],
                3: [(SUM_0, 1), (XS_, 3, 0)]},
 (AT_B, 0, 6): {0: [(FFN_X, 3, 2)], 1: [(FFN_X, 3, 1)], 2: [(SUM_3, 0), (FFN_X, 0, 1)], 3: [(FFN_X, 0, 2)]},
 (AT_B, 1, 0): {0: [(XS_, 0, 1)], 1: [(REL, 0, 2, 0), (XS_, 1, 0)], 2: [(FFN_Z, 0, 1), (ZS, 0, 1)], 3: [(XS_, 3, 1)]},
 (AT_B, 1, 1): {0: [(FFN_X, 0, 0), (FFN_OWN, 0)],
                1: [(FFN_X, 3, 2)],
                2: [(REL, 1, 0, 1), (XS_, 2, 0), (FFN_X, 0, 2)],
                3: [(FFN_X, 3, 0), (FFN_OWN, 0)]},
 (AT_B, 1, 2): {0: [(XO, 0)], 1: [(REL, 1, 0, 0), (XS_, 1, 1)], 2: [(REL, 1, 1, 1), (SUM_4, 0)], 3: [(SUM_3, 0)]},
 (AT_B, 1, 3): {0: [(SUM_3, 0), (ZS, 3, 2), (FFN_X, 0, 1)],
                1: [(FFN_Z, 3, 1), (SUM_3, 0), (ZS, 3, 1), (FFN_X, 1, 0), (FFN_OWN, 0)],
                2: [(XS_, 2, 1)],
                3: [(ZS, 0, 2), (FFN_X, 3, 1)]},
 (AT_B, 1, 5): {0: [(SUM_0, 2)],
                1: [(REL, 0, 3, 1)],
                2: [(REL, 0, 3, 1), (FFN_X, 2, 0), (FFN_OWN, 0)],
                3: [(SUM_4, 0), (SUM_0, 2), (XO, 0), (FFN_OWN, 1)]},
 (AT_B, 1, 6): {0: [(FFN_LAST, 0), (XS_, 0, 2), (FFN_OWN, 1)],
                1: [(REL, 0, 2, 1), (XO, 0), (FFN_X, 1, 1), (FFN_OWN, 1)],
                2: [(FFN_Z, 0, 2), (ZS, 0, 2), (XO, 0), (SUM_3, 1)]},
 (AT_B, 2, 0): {0: [(SUM_4, 0)],
                1: [(SUM_4, 0)],
                2: [(FFN_X, 2, 1), (FW, 2, 1, 0), (FW, 3, 3, 0), (FFN_OWN, 1)],
                3: [(XO, 1)]},
 (AT_B, 2, 1): {0: [(XO, 1)], 1: [(REL, 1, 0, 1), (XO, 1)], 3: [(FFN_LAST, 0)]},
 (AT_B, 2, 2): {0: [(FFN_X, 0, 2)],
                1: [(FFN_Z, 3, 2), (ZS, 3, 2), (FFN_LAST, 0)],
                2: [(REL, 1, 0, 2), (XO, 1), (FFN_LAST, 0)],
                3: [(XS_, 3, 2)]},
 (AT_B, 2, 3): {0: [(SUM_3, 1)], 1: [(SUM_3, 1)], 2: [(REL, 1, 1, 2), (SUM_4, 1)], 3: [(SUM_3, 1), (FFN_LAST, 1)]},
 (AT_B, 2, 5): {0: [(SUM_0, 3), (FFN_LAST, 1), (FFN_OWN, 2), (XO, 2)],
                1: [(FW, 3, 2, 0), (REL, 0, 3, 2), (FFN_LAST, 1), (XS_, 1, 2)],
                2: [(REL, 0, 3, 2), (XS_, 2, 2)],
                3: [(SUM_0, 3)]},
 (AT_B, 2, 6): {0: [(SUM_4, 1)],
                1: [(SUM_4, 1), (REL, 0, 2, 2)],
                2: [(FW, 2, 1, 1), (FFN_LAST, 1)],
                3: [(FFN_X, 3, 2), (FFN_OWN, 2), (XO, 2)]},
 (AT_D, 0): {0: [(SUM_7, 0), (SUM_3, 2), (GX, 1), (SUM_3, 3), (SUM_4, 2), (SUM_7, 1), (SUM_4, 3), (SUM_7, 2),
                 (SUM_7, 3)],
             1: [(REL, 1, 0, 2), (REL, 0, 3, 3), (SUM_3, 2), (REL, 0, 2, 3), (FW, 3, 2, 1), (REL, 1, 0, 3), (XO, 2),
                 (FW, 2, 0, 1), (SUM_4, 2), (SUM_3, 3), (FW, 3, 3, 1), (SUM_7, 1), (FFN_LAST, 2), (GX, 1),
                 (FW, 3, 2, 2), (FW, 2, 0, 2), (SUM_4, 3), (FW, 3, 2, 3), (FW, 2, 0, 3), (FW, 3, 3, 2), (SUM_7, 2),
                 (FW, 3, 3, 3), (SUM_7, 3)],
             2: [(REL, 0, 3, 3), (FW, 3, 3, 1), (SUM_4, 2), (SUM_3, 3), (FW, 2, 0, 1), (SUM_7, 1), (XO, 2),
                 (SUM_4, 3), (FW, 2, 1, 2), (FW, 3, 3, 2), (GX, 0), (FFN_LAST, 2), (FW, 2, 0, 2), (SUM_7, 2), (GX, 1),
                 (FW, 3, 3, 3), (FW, 2, 1, 3), (FW, 2, 0, 3), (SUM_7, 3)],
             3: [(FFN_LAST, 2), (SUM_3, 2), (SUM_7, 0), (GX, 1), (SUM_3, 3), (SUM_4, 2), (SUM_7, 1), (SUM_4, 3),
                 (SUM_7, 2), (SUM_7, 3)]},
 (AT_E, 0): {2: [(REL, 1, 0, 3)]},
 (AT_E, 1): {0: [(GX, 0), (FFN_LAST, 2)],
             1: [(FW, 3, 3, 0), (FW, 2, 0, 0), (SUM_7, 0), (GX, 0), (FFN_X, 1, 2), (FFN_OWN, 2)],
             2: [(FW, 2, 0, 0), (REL, 1, 1, 3), (SUM_7, 0), (SUM_3, 2), (FFN_X, 2, 2), (FFN_OWN, 2)],
             3: [(SUM_4, 1), (GX, 0)]},
 (AT_G, 0): {0: [(XS_, 1, 0)], 1: [(XS_, 0, 0)], 2: [(XS_, 3, 0)], 3: [(XS_, 2, 0)]},
 (AT_G, 1): {1: [(XS_, 0, 2)], 2: [(FFN_X, 3, 0), (ZS, 3, 0)]},
 (AT_G, 2): {0: [(XS_, 2, 1)], 1: [(FFN_X, 0, 2), (ZS, 0, 2)], 3: [(XS_, 1, 1)]},
 (AT_G, 3): {0: [(XS_, 3, 0), (FFN_X, 2, 1), (ZS, 2, 1)],
             2: [(XS_, 1, 2)],
             3: [(XS_, 0, 0), (FFN_X, 1, 1), (ZS, 1, 1)]},
 (AT_N, 1): {0: [(XS_, 3, 1), (FFN_X, 2, 2), (ZS, 2, 2)],
             1: [(FFN_Z, 2, 0), (ZS, 2, 0), (FFN_X, 2, 1), (FFN_X, 2, 2), (XS_, 3, 0)],
             2: [(FFN_X, 1, 1), (FFN_Z, 1, 1), (ZS, 1, 1), (XS_, 0, 0)],
             3: [(XS_, 0, 1), (FFN_X, 1, 2), (ZS, 1, 2)]},
 (AT_N, 2): {0: [(FFN_X, 3, 0), (ZS, 3, 0)], 2: [(FFN_X, 1, 2)], 3: [(FFN_X, 0, 0), (ZS, 0, 0)]},
 (AT_N, 3): {0: [(OX, 0)], 1: [(OX, 0)], 2: [(FFN_Z, 1, 2), (ZS, 1, 2), (OX, 0)], 3: [(OX, 0)]},
 (AT_N, 4): {0: [(SUM_0, 0), (FFN_X, 3, 1)],
             1: [(FFN_Z, 2, 1), (ZS, 2, 1)],
             2: [(FFN_X, 0, 0)],
             3: [(SUM_0, 0), (FFN_X, 0, 1)]},
 (AT_T, 1, 0): {0: [(WR, 3), (XS_, 1, 1), (FFN_X, 1, 0), (ZS, 1, 0)],
                3: [(WL, 3), (XS_, 2, 1), (FFN_X, 2, 0), (ZS, 2, 0)]},
 (AT_T, 1, 1): {1: [(XS_, 0, 1)]},
 (AT_T, 1, 2): {2: [(XS_, 3, 1)]},
 (AT_T, 1, 3): {0: [(XS_, 1, 2)], 1: [(FFN_X, 0, 0), (ZS, 0, 0)], 3: [(XS_, 2, 2)]},
 (AT_T, 2, 0): {0: [(FFN_X, 1, 1), (ZS, 1, 1)], 2: [(XS_, 3, 2)], 3: [(FFN_X, 2, 1), (ZS, 2, 1)]},
 (AT_T, 2, 1): {0: [(XS_, 2, 0)], 1: [(FFN_X, 0, 1), (ZS, 0, 1)], 3: [(XS_, 1, 0)]},
 (AT_T, 2, 2): {1: [(XS_, 2, 0)], 2: [(FFN_X, 3, 1), (ZS, 3, 1)]},
 (AT_T, 2, 3): {0: [(FFN_X, 1, 2), (ZS, 1, 2)], 2: [(XS_, 1, 0)], 3: [(FFN_X, 2, 2), (ZS, 2, 2)]},
 (AT_T, 3, 0): {0: [(FFN_X, 2, 0), (ZS, 2, 0)],
                1: [(XS_, 2, 1)],
                2: [(FFN_X, 3, 2), (ZS, 3, 2)],
                3: [(FFN_X, 1, 0), (ZS, 1, 0)]},
 (AT_T, 3, 1): {0: [(XS_, 2, 2)], 2: [(XS_, 1, 1)], 3: [(XS_, 1, 2)]},
 (AT_T, 3, 2): {1: [(FFN_X, 2, 0)]},
 (AT_T, 3, 3): {1: [(XS_, 2, 2)], 2: [(FFN_X, 1, 0), (FFN_Z, 1, 0), (ZS, 1, 0)]},
 (AT_W, 1): {0: [(WR, 2)], 1: [(WR, 2)], 2: [(WL, 2)], 3: [(WL, 2)]}}
HALF = (0, 0, 0, 0)


BF = jnp.bfloat16
F32 = jnp.float32
MESH = pl.DeviceIdType.MESH


def dot(a, b):
    return jnp.dot(a, b, preferred_element_type=F32)


def dot_t(a, b):
    return lax.dot_general(a, b, (((1,), (1,)), ((), ())), preferred_element_type=F32)


def rows_of(start, size):
    return pl.ds(pl.multiple_of(start, size), size)


def pick(table, index):
    value = table[0]
    for place in range(1, len(table)):
        value = jnp.where(index == place, table[place], value)
    return value


def swap_halves(tile):
    lane = lax.broadcasted_iota(jnp.int32, tile.shape, 1)
    return jnp.where(
        lane % 64 < 32, pltpu.roll(tile, 96, 1), pltpu.roll(tile, 32, 1)
    )


def fast_kernel(
    inputs, cond, again, adaw_h, adab, qkv_h, outw_h, fgain, up_h, upb, down_h, downb, cot_h,
    cos_h, sin_h, cost_h, sint_h,
    out_o, gin_o, qkv_o, outw_o, ffn_o, vall_o,
    adaw, wq, wo, wu, wd, ub, cos_v, sin_v, cost, sint,
    xb, ctb, mod2, n1, i1, ai, ait, q_s, k_s, v_s, kt_s, vt_s, ot_s, lse, att, att_s,
    ap, n2, i2, fit, gf, gft, oacc, gacc, a_s, gp_s, g_s, grecv,
    gm, do_s, dlt, dqt, gq, b_s, xs, vec, vecr, vall, ubg,
    rx, rz, fxr, rxb, fb,
    lsem, ssem, rsem, wss, wrs, yss, yrs, fss, frs, bss, brs, hss, hrs, vss, vrs, credit,
):
    Z = 4
    grp = lax.axis_index("grp")
    seq = lax.axis_index("seq")
    z = lax.axis_index("mlp")
    x, c = seq // 2, seq % 2
    D = 768
    flat = lambda ref: ref[...].reshape(1, -1)
    again, adab, fgain, downb = flat(again), flat(adab), flat(fgain), flat(downb)
    own = c * 512
    other = (1 - c) * 512
    TO_CORE = {"seq": x * 2 + (1 - c)}
    TO_X = {"seq": (1 - x) * 2 + c}
    TO_Y = {"grp": 1 - grp}
    RIGHT = {"mlp": jnp.minimum(z + 1, Z - 1)}
    LEFT = {"mlp": jnp.maximum(z - 1, 0)}

    def remote(src, dst, index, device):
        return pltpu.make_async_remote_copy(
            src_ref=src, dst_ref=dst, send_sem=ssem.at[index], recv_sem=rsem.at[index],
            device_id=device, device_id_type=MESH,
        )

    def local(src, dst, index):
        return pltpu.make_async_copy(src, dst, lsem.at[index])

    half = pl.ds(pl.multiple_of(c * 384, 128), 384)
    loads = [local(inputs.at[x], xb.at[rows_of(x * 256, 256)], 0), local(adaw_h, adaw, 1)]
    loads += [local(cos_h, cos_v, 2), local(sin_h, sin_v, 3), local(cost_h, cost, 4), local(sint_h, sint, 5)]
    for p in range(3):
        for part in range(3):
            loads.append(
                local(
                    qkv_h.at[:, pl.ds(pl.multiple_of(part * D + c * 384 + p * 128, 128), 128)],
                    wq.at[p, :, pl.ds(part * 128, 128)],
                    6 + p * 3 + part,
                )
            )
    loads.append(local(outw_h, wo, 15))
    loads.append(local(up_h.at[:, half], wu.at[z], 16))
    loads.append(local(down_h.at[rows_of(c * 384, 384)], wd.at[z], 17))
    loads.append(local(cot_h.at[x], ctb.at[rows_of(x * 256, 256)], 18))
    for item in loads:
        item.start()

    ub[z] = flat(upb)

    barrier = pltpu.get_barrier_semaphore()
    peers = [{"seq": (x ^ dx) * 2 + c, "mlp": z ^ dz} for dx in range(2) for dz in range(Z) if dx or dz]
    for device in [TO_CORE, TO_Y] + peers:
        pl.semaphore_signal(barrier, 1, device_id=device, device_id_type=MESH)
    pl.semaphore_wait(barrier, 2 + len(peers))

    swap_x = remote(inputs.at[1 - x], xb.at[rows_of(x * 256, 256)], 0, TO_X)
    swap_x.start()
    swap_c = remote(cot_h.at[1 - x], ctb.at[rows_of(x * 256, 256)], 1, TO_X)
    swap_c.start()

    def up_half(ref, which):
        return ref.at[rows_of(which * 384, 384)]

    def down_half(ref, which):
        return ref.at[rows_of(which * 192, 192)]

    def z_copies(j, way, device, first):
        if first:
            src = (
                up_h.at[rows_of(grp * 384, 384), half],
                down_h.at[rows_of(c * 384 + grp * 192, 192)],
                ub.at[z],
            )
        else:
            src = (up_half(wu.at[j], grp), down_half(wd.at[j], grp), ub.at[j])
        dst = (up_half(wu.at[j], grp), down_half(wd.at[j], grp), ub.at[j])
        return [
            pltpu.make_async_remote_copy(
                src_ref=src[i], dst_ref=dst[i], send_sem=wss.at[way, j, i], recv_sem=wrs.at[way, j, i],
                device_id=device, device_id_type=MESH,
            )
            for i in range(3)
        ]

    def y_copies(j, which):
        return [
            pltpu.make_async_remote_copy(
                src_ref=ref, dst_ref=ref, send_sem=yss.at[j, i], recv_sem=yrs.at[j, i],
                device_id=TO_Y, device_id_type=MESH,
            )
            for i, ref in enumerate((up_half(wu.at[j], which), down_half(wd.at[j], which)))
        ]

    def start_all(items):
        for item in items:
            item.start()

    @pl.when(z < Z - 1)
    def _():
        start_all(z_copies(z, 0, RIGHT, True))

    @pl.when(z > 0)
    def _():
        start_all(z_copies(z, 1, LEFT, True))

    def order(n):
        return pick([ORDERS[a][n] for a in range(Z)], z)

    pending = {place: [] for place in range(Z)}
    CH = 3

    def send(place, *makes):
        for make in makes:
            make().start()
            pending[place].append(make)

    def span(h):
        return pl.ds(h * (768 // CH), 768 // CH)

    def ffn_copy(j, h):
        return pltpu.make_async_remote_copy(
            src_ref=g_s.at[1 - x, j, span(h)], dst_ref=rx.at[j, span(h)], send_sem=hss.at[j, h],
            recv_sem=hrs.at[j, h], device_id=TO_X, device_id_type=MESH,
        )

    def add_rows(ref, others):
        @pl.loop(0, 768 // CH // 64)
        def _(i):
            rows = rows_of(i * 64, 64)
            total = ref[rows].astype(F32)
            for other_ref in others:
                total = total + other_ref[rows].astype(F32)
            ref[rows] = total.astype(BF)

    def z_send(j, h, place):
        if place in (0, 3):
            target, slot = (1 if place == 0 else 2), j
        elif j in (0, 3):
            target, slot = j, place
        else:
            target, slot = j, (0 if j == 1 else 3)
        return lambda: pltpu.make_async_remote_copy(
            src_ref=g_s.at[x, j, span(h)], dst_ref=rz.at[slot, span(h)], send_sem=fss.at[j, h],
            recv_sem=frs.at[slot, h], device_id={"mlp": target}, device_id_type=MESH,
        )

    def z_wait(slot, h):
        ref = rz.at[slot, span(h)]
        pltpu.make_async_remote_copy(
            src_ref=ref, dst_ref=ref, send_sem=fss.at[0, h], recv_sem=frs.at[slot, h],
            device_id=LEFT, device_id_type=MESH,
        ).wait_recv()

    def ffn_x(place, j, h):
        ffn_copy(j, h).wait_recv()
        add_rows(g_s.at[x, j, span(h)], [rx.at[j, span(h)]])

    def ffn_z(place, j, h):
        z_wait(j, h)
        add_rows(g_s.at[x, j, span(h)], [rz.at[j, span(h)]])

    def zs(place, j, h):
        send(place, z_send(j, h, place))

    def xs_(place, j, h):
        send(place, lambda: ffn_copy(j, h))

    def final_copies(src, kind, h, first):
        dst = ffn_o.at[kind, span(h), half]
        return [local(src, dst, 21 + first * CH + h), remote(src, dst, 31 + first * CH + h, TO_CORE)]

    def own_copy(h):
        return pltpu.make_async_remote_copy(
            src_ref=g_s.at[x, z, span(h)], dst_ref=fxr.at[span(h)], send_sem=hss.at[5, h],
            recv_sem=hrs.at[5, h], device_id=TO_X, device_id_type=MESH,
        )

    def ffn_own(place, h):
        slots = {0: (1, 2), 3: (1, 2), 1: (1, 0), 2: (2, 3)}[place]
        for slot in slots:
            z_wait(slot, h)
        add_rows(g_s.at[x, place, span(h)], [rz.at[slot, span(h)] for slot in slots])
        for item in final_copies(g_s.at[x, z, span(h)], x, h, 0):
            item.start()

    def xo(place, h):
        own_copy(h).start()

    def ffn_last(place, h):
        own_copy(h).wait_recv()
        for item in final_copies(fxr.at[span(h)], 1 - x, h, 1):
            item.start()

    def quarter(ref, p, q):
        if ref is wd:
            return ref.at[p, pl.ds(q // 2 * 192, 192), pl.ds(q % 2 * 384, 384)]
        return ref.at[p, pl.ds(q * 192, 192)]

    def hop(kind, p, q, place):
        step = 1 if kind in (0, 2) else -1
        return lambda: pltpu.make_async_remote_copy(
            src_ref=quarter(b_s if kind < 2 else fb, p, q),
            dst_ref=quarter((wu, wd, fb, fb)[kind], p, q),
            send_sem=bss.at[kind, p, q],
            recv_sem=brs.at[kind, p, q],
            device_id={"mlp": place + step},
            device_id_type=MESH,
        )

    def hop_wait(kind, p, q):
        dst = quarter((wu, wd, fb, fb)[kind], p, q)
        pltpu.make_async_remote_copy(
            src_ref=dst, dst_ref=dst, send_sem=bss.at[kind, p, q], recv_sem=brs.at[kind, p, q],
            device_id=LEFT, device_id_type=MESH,
        ).wait_recv()

    def add_quarter(p, q, refs):
        total = quarter(b_s, p, q)[...].astype(F32)
        for ref in refs:
            total = total + quarter(ref, p, q)[...].astype(F32)
        quarter(b_s, p, q)[...] = total.astype(BF)

    def sum_0(place, p):
        kind, blocks = (0, (3, 2, 1)) if place == 0 else (1, (0, 1, 2))
        send(place, *[hop(kind, p, q, place) for q in blocks])

    def rel(place, kind, q, p):
        hop_wait(kind, p, q)
        add_quarter(p, q, [wd if kind else wu])
        send(place, hop(kind, p, q, place))

    def cross(p, place):
        return lambda: pltpu.make_async_remote_copy(
            src_ref=quarter(b_s, p, place), dst_ref=rxb.at[p], send_sem=hss.at[4, p],
            recv_sem=hrs.at[4, p], device_id=TO_X, device_id_type=MESH,
        )

    def sum_3(place, p):
        refs = []
        if place > 0:
            hop_wait(0, p, place)
            refs.append(wu)
        if place < 3:
            hop_wait(1, p, place)
            refs.append(wd)
        add_quarter(p, place, refs)
        send(place, cross(p, place))

    def sum_4(place, p):
        cross(p, place)().wait_recv()
        total = quarter(b_s, p, place)[...].astype(F32) + rxb[p].astype(F32)
        quarter(fb, p, place)[...] = total.astype(BF)
        if place < 3:
            send(place, hop(2, p, place, place))
        if place > 0:
            send(place, hop(3, p, place, place))

    def fw(place, kind, q, p):
        hop_wait(kind, p, q)
        send(place, hop(kind, p, q, place))

    def piece_copies(p):
        if p == 0:
            pairs = [
                (fb.at[0, pl.ds(n * 384, 384)], outw_o.at[rows_of(c * 384, 384), pl.ds(n * 384, 384)])
                for n in range(2)
            ]
        else:
            pairs = [
                (
                    fb.at[p, :, pl.ds(part * 128, 128)],
                    qkv_o.at[
                        :, pl.ds(pl.multiple_of(part * D + c * 384 + (p - 1) * 128, 128), 128)
                    ],
                )
                for part in range(3)
            ]
        copies = []
        for n, (src, dst) in enumerate(pairs):
            copies.append(local(src, dst, 43 + p * 3 + n))
            copies.append(remote(src, dst, 18 + p * 3 + n, TO_CORE))
        return copies

    def sum_7(place, p):
        for q in range(4):
            if place == 0 and q > 0:
                hop_wait(3, p, q)
            if place == 3 and q < 3:
                hop_wait(2, p, q)
        for item in piece_copies(p):
            item.start()

    def wl(place, k):
        for item in z_copies(place - k, 0, RIGHT, False):
            item.wait_recv()
        if place < 3:
            start_all(z_copies(place - k, 0, RIGHT, False))
        start_all(y_copies(place - k, grp))

    def wr(place, k):
        for item in z_copies(place + k, 1, LEFT, False):
            item.wait_recv()
        if place > 0:
            start_all(z_copies(place + k, 1, LEFT, False))
        start_all(y_copies(place + k, grp))

    def cross_rows(out_ref, number, part):
        rows = rows_of((1 - x) * 256 + part * 128, 128)
        return remote(
            xs.at[number, rows], out_ref.at[x, pl.ds(part * 128, 128)], 12 + number * 2 + part, TO_X
        )

    def ox(place, part):
        cross_rows(out_o, 0, part).start()

    def gx(place, part):
        cross_rows(gin_o, 1, part).start()

    jobs = (ffn_x, ffn_z, ffn_own, ffn_last, sum_0, rel, sum_3, sum_4, fw, sum_7, wl, wr, xs_, zs, xo, ox, gx)

    def slot(name, here=None):
        for place, names in PLAN.get(name, {}).items():
            @pl.when(z == place if here is None else (z == place) & here)
            def _(place=place, names=names):
                for job, *rest in names:
                    jobs[job](place, *rest)

    local(adaw_h, adaw, 1).wait()
    for part in range(6):
        lanes = pl.ds(part * D, D)
        mod2[:, lanes] = dot(cond[...], adaw[:, lanes]) + adab[:, part * D : (part + 1) * D]
    modrow = mod2[pl.ds(x, 1), :]
    shift_one, scale_one, gate_one, shift_two, scale_two, gate_two = [
        modrow[:, part * D : (part + 1) * D] for part in range(6)
    ]

    def layer_norm(values):
        center = values - jnp.mean(values, axis=-1, keepdims=True)
        inv = lax.rsqrt(jnp.mean(center * center, axis=-1, keepdims=True) + 1e-05)
        return center * inv, inv

    TILE = 64
    mul_one = again * (1.0 + scale_one)
    mul_two = fgain * (1.0 + scale_two)

    def norm_one_block(block):
        @pl.loop(0, 256 // TILE)
        def _(i):
            at = block * 256 + i * TILE
            rows = rows_of(at, TILE)
            normed, inv = layer_norm(xb[rows].astype(F32))
            n1[rows] = normed
            i1[rows] = inv
            ai[rows_of(own + at, TILE)] = (normed * mul_one + shift_one).astype(BF)

    def core_rows(ref, start, size, index):
        part = ref.at[rows_of(start, size)]
        return remote(part, part, index, TO_CORE)

    for item in loads[2:15]:
        item.wait()

    def project_rows(start):
        rows = rows_of(start, 256)
        tile = ai[rows]
        cos_t, sin_t = cos_v[rows], sin_v[rows]

        @pl.loop(0, 3)
        def _(p):
            projected = dot(tile, wq[p])
            query = projected[:, :128]
            key = projected[:, 128:256]
            value = projected[:, 256:].astype(BF)
            query = (query * cos_t + swap_halves(query) * sin_t).astype(BF)
            key = (key * cos_t + swap_halves(key) * sin_t).astype(BF)
            q_s[p, rows] = query * jnp.asarray(0.125, BF)
            k_s[p, rows] = key
            v_s[p, rows] = value
            kt_s[p, :, rows] = key.T
            vt_s[p, :, rows] = value.T

        ait[:, rows] = tile.T

    loads[0].wait()
    norm_one_block(x)
    core_rows(ai, own + x * 256, 256, 2).start()
    project_rows(own + x * 256)
    core_rows(ai, other + x * 256, 256, 2).wait_recv()
    project_rows(other + x * 256)
    swap_x.wait_recv()
    norm_one_block(1 - x)
    core_rows(ai, own + (1 - x) * 256, 256, 3).start()
    project_rows(own + (1 - x) * 256)
    core_rows(ai, other + (1 - x) * 256, 256, 3).wait_recv()
    project_rows(other + (1 - x) * 256)
    for item in loads[16:18]:
        item.wait()
    slot((AT_W, 0))

    low_lane = lax.broadcasted_iota(jnp.int32, (1, 128), 1) < 64
    keep = [low_lane.astype(F32).astype(BF), (~low_lane).astype(F32).astype(BF)]

    def att_copy(p, start):
        return remote(
            att_s.at[:, pl.ds(p * 128, 128)],
            att.at[:, pl.ds(pl.multiple_of(c * 384 + p * 128, 128), 128)],
            4 + p,
            TO_CORE,
        )

    def attend(p):
        @pl.loop(0, 2)
        def _(t):
            cols = rows_of(t * 512, 512)
            query = q_s[p, cols]
            outs = []
            for h in range(2):
                masked = query * keep[h]
                held = (oacc, gacc)[h]
                top = None
                for i in range(4):
                    keys = pl.ds(i * 256, 256)
                    scores = dot_t(k_s[p, keys], masked)
                    held[keys, :512] = scores
                    top = scores if top is None else jnp.maximum(top, scores)
                top = jnp.max(top, axis=0, keepdims=True)
                out, total = None, None
                for i in range(4):
                    keys = pl.ds(i * 256, 256)
                    expd = jnp.exp(held[keys, :512] - top)
                    part = dot(vt_s[p, pl.ds(h * 64, 64), keys], expd.astype(BF))
                    out = part if out is None else out + part
                    total = expd if total is None else total + expd
                total = jnp.sum(total, axis=0, keepdims=True)
                lse[p, pl.ds(h, 1), cols] = top + jnp.log(total)
                out = out / total
                ot_s[p, pl.ds(h * 64, 64), cols] = out
                outs.append(out)
            natural = jnp.concatenate(outs, axis=0).T.astype(BF)
            lanes = pl.ds(pl.multiple_of(c * 384 + p * 128, 128), 128)

            @pl.when(t == c)
            def _():
                att[:, lanes] = natural

            @pl.when(t != c)
            def _():
                att_s[:, pl.ds(p * 128, 128)] = natural

            for n in range(2):
                slot((AT_A, p, n), t == n)

        att_copy(p, True).start()

    attend(0)
    attend(1)

    loads[18].wait()
    swap_c.wait_recv()

    @pl.loop(0, 512 // TILE)
    def _(i):
        at = i * TILE
        gf[rows_of(own + at, TILE)] = (gate_two * ctb[rows_of(at, TILE)].astype(F32)).astype(BF)

    core_rows(gf, own, 512, 7).start()
    attend(2)
    vec[...] = jnp.zeros_like(vec)

    @pl.loop(0, 512 // TILE)
    def _(i):
        vec[8:9] += jnp.sum(gf[rows_of(own + i * TILE, TILE)].astype(F32), axis=0, keepdims=True)

    for p in range(3):
        remote(
            att_s.at[:, pl.ds(p * 128, 128)],
            att.at[:, pl.ds(pl.multiple_of((1 - c) * 384 + p * 128, 128), 128)],
            4 + p,
            TO_CORE,
        ).wait_recv()
    loads[15].wait()

    core_rows(ai, own + x * 256, 256, 2).wait_send()
    core_rows(ai, own + (1 - x) * 256, 256, 3).wait_send()
    fi = ai

    @pl.loop(0, 2)
    def _(b):
        rows = rows_of(b * 256, 256)
        ap[rows] = dot(att[rows], wo[...])

        @pl.loop(0, 256 // TILE)
        def _(i):
            at = b * 256 + i * TILE
            tile = rows_of(at, TILE)
            middle = xb[tile].astype(F32) + gate_one * ap[tile]
            normed, inv = layer_norm(middle)
            n2[tile] = normed
            i2[tile] = inv
            fi[rows_of(own + at, TILE)] = (normed * mul_two + shift_two).astype(BF)

    core_rows(fi, own, 512, 8).start()
    slot((AT_W, 1))

    def turn(src, dst, start):
        @pl.loop(0, 2)
        def _(t):
            rows = rows_of(start + t * 256, 256)
            dst[:, rows] = src[rows].T

    turn(gf, gft, own)
    core_rows(gf, other, 512, 7).wait_recv()
    turn(gf, gft, other)
    turn(fi, fit, own)
    core_rows(fi, other, 512, 8).wait_recv()
    turn(fi, fit, other)
    slot((AT_W, 2))

    coef = 0.7978845608028654

    @pl.loop(0, Z)
    def _(k):
        j = pick([order(n) for n in range(Z)], k)

        for n in range(Z):
            slot((AT_F, n), k == n)

        @pl.when(k != OWN_STEP)
        def _():
            for item in y_copies(j, 1 - grp):
                item.wait_recv()

        bias = ub[j][:, pl.ds(0, 384)]
        bias = jnp.where(c == 0, bias, ub[j][:, pl.ds(384, 384)])

        @pl.loop(0, 4)
        def _(t):
            rows = rows_of(t * 256, 256)
            pre = dot(fi[rows], wu[j]) + bias
            sq = pre * pre
            th = jnp.tanh(coef * (pre + 0.044715 * pre * sq))
            act = (0.5 * pre * (1.0 + th)).astype(BF)
            slope = 0.5 * (1.0 + th) + 0.5 * pre * (1.0 - th * th) * coef * (1.0 + 3.0 * 0.044715 * sq)
            a_s[rows] = act
            grad_pre = (dot_t(gf[rows], wd[j]) * slope).astype(BF)
            gp_s[rows] = grad_pre
            bsum = jnp.sum(grad_pre.astype(F32), axis=0, keepdims=True)
            out = dot(act, wd[j])
            gin = dot_t(grad_pre, wu[j])

            @pl.when(k == 0)
            def _():
                oacc[rows] = out
                gacc[rows] = gin

            @pl.when(k > 0)
            def _():
                oacc[rows] += out
                gacc[rows] += gin

            for m in range(Z):
                for n in range(4):
                    slot((AT_T, m, n), (k == m) & (t == n))

            @pl.when(t == 0)
            def _():
                ubg[j] = bsum

            @pl.when(t > 0)
            def _():
                ubg[j] += bsum

        @pl.loop(0, 3)
        def _(r):
            rows = rows_of(r * 256, 256)
            g_s[0, j, rows] = dot(fit[rows], gp_s[...]).astype(BF)
            g_s[1, j, rows] = dot(gft[rows], a_s[...]).astype(BF)

        for n in range(Z):
            slot((AT_G, n), k == n)

    def give_credit():
        @pl.when(z > 0)
        def _():
            pl.semaphore_signal(credit.at[0], 1, device_id=LEFT, device_id_type=MESH)

        @pl.when(z < Z - 1)
        def _():
            pl.semaphore_signal(credit.at[1], 1, device_id=RIGHT, device_id_type=MESH)

    def take_credit():
        @pl.when(z < Z - 1)
        def _():
            pl.semaphore_wait(credit.at[0], 1)

        @pl.when(z > 0)
        def _():
            pl.semaphore_wait(credit.at[1], 1)


    def weight_waits(k):
        @pl.when(z - k >= 0)
        def _():
            @pl.when(z < Z - 1)
            def _():
                for item in z_copies(z - k, 0, RIGHT, False):
                    item.wait_send()

            for item in y_copies(z - k, grp):
                item.wait_send()

        @pl.when(z + k <= Z - 1)
        def _():
            @pl.when(z > 0)
            def _():
                for item in z_copies(z + k, 1, LEFT, False):
                    item.wait_send()

            for item in y_copies(z + k, grp):
                item.wait_send()

    @pl.when(z < Z - 1)
    def _():
        for item in z_copies(z, 0, RIGHT, False):
            item.wait_send()

    @pl.when(z > 0)
    def _():
        for item in z_copies(z, 1, LEFT, False):
            item.wait_send()

    pl.loop(1, Z)(weight_waits)
    give_credit()

    osend, gsend = xs.at[0], xs.at[1]

    @pl.loop(0, 512 // TILE)
    def _(i):
        tile = rows_of(i * TILE, TILE)
        far = rows_of(other + i * TILE, TILE)
        gsend[tile] = gacc[far].astype(BF)

    remote(gsend, grecv, 9, TO_CORE).start()

    @pl.loop(0, 512 // TILE)
    def _(i):
        osend[rows_of(i * TILE, TILE)] = oacc[rows_of(other + i * TILE, TILE)].astype(BF)

    orecv = att
    remote(osend, orecv, 10, TO_CORE).start()
    remote(gsend, grecv, 9, TO_CORE).wait_recv()
    core_rows(gf, own, 512, 7).wait_send()

    def norm_back(grad, normed, inv):
        return inv * (
            grad
            - jnp.mean(grad, axis=-1, keepdims=True)
            - normed * jnp.mean(grad * normed, axis=-1, keepdims=True)
        )

    @pl.loop(0, 512 // TILE)
    def _(i):
        tile = rows_of(i * TILE, TILE)
        near = rows_of(own + i * TILE, TILE)
        grad = gacc[near] + grecv[tile].astype(F32)
        normed = n2[tile]
        vec[3:4] += jnp.sum(grad, axis=0, keepdims=True)
        vec[4:5] += jnp.sum(grad * normed, axis=0, keepdims=True)
        middle = ctb[tile].astype(F32) + norm_back(grad * mul_two, normed, i2[tile])
        gm[tile] = middle
        gf[near] = (gate_one * middle).astype(BF)
        vec[2:3] += jnp.sum(middle * ap[tile], axis=0, keepdims=True)

    gproj = gf
    core_rows(gproj, own, 512, 11).start()
    slot((AT_N, 1))

    remote(osend, orecv, 10, TO_CORE).wait()

    def rows_out(number, i, values):
        xs[number, rows_of(i * TILE, TILE)] = values.astype(BF)

    def out_copy(out_ref, number):
        return local(xs.at[number, rows_of(x * 256, 256)], out_ref.at[x], 55 + number)

    @pl.loop(0, 512 // TILE)
    def _(i):
        tile = rows_of(i * TILE, TILE)
        ffn = oacc[rows_of(own + i * TILE, TILE)] + orecv[tile].astype(F32) + downb
        vec[5:6] += jnp.sum(ctb[tile].astype(F32) * ffn, axis=0, keepdims=True)
        rows_out(0, i, xb[tile].astype(F32) + gate_one * ap[tile] + gate_two * ffn)

    out_copy(out_o, 0).start()

    core_rows(gproj, other, 512, 11).wait_recv()
    slot((AT_N, 2))

    @pl.loop(0, 4)
    def _(t):
        rows = rows_of(t * 256, 256)
        grad = dot_t(gproj[rows], wo[rows_of(c * 384, 384)])
        for p in range(3):
            part = grad[:, p * 128 : (p + 1) * 128].astype(BF)
            do_s[p, rows] = part
            product = part.astype(F32).T * ot_s[p, :, rows]
            for h in range(2):
                dlt[p, pl.ds(h, 1), rows] = jnp.sum(
                    product[h * 64 : (h + 1) * 64], axis=0, keepdims=True
                )

    slot((AT_N, 3))

    for p in range(3):
        @pl.loop(0, 2)
        def _(n):
            lanes = pl.ds(pl.multiple_of(n * 384, 128), 384)
            b_s[0, rows_of(n * 384 + p * 128, 128)] = dot(
                ot_s[p].astype(BF), gproj[:, lanes]
            ).astype(BF)

    take_credit()
    slot((AT_N, 4))

    def attend_back(p):
        for h in range(2):
            a_s[:, h * 128 : (h + 1) * 128] = q_s[p] * keep[h]
            gp_s[:, h * 128 : (h + 1) * 128] = do_s[p] * keep[h]
        dqt[...] = jnp.zeros_like(dqt)

        @pl.loop(0, 4)
        def _(t):
            rows = rows_of(t * 256, 256)
            keys, values = k_s[p, rows], v_s[p, rows]
            dv, dk = None, None
            for h in range(2):
                qm, dom = a_s[:, h * 128 : (h + 1) * 128], gp_s[:, h * 128 : (h + 1) * 128]
                probs = jnp.exp(dot_t(keys, qm) - lse[p, pl.ds(h, 1), :])
                grads = dot_t(values, dom)
                ds = (probs * (grads - dlt[p, pl.ds(h, 1), :])).astype(BF)
                dv_h = dot(probs.astype(BF), dom)
                dk_h = dot(ds, qm)
                dv = dv_h if dv is None else dv + dv_h
                dk = dk_h if dk is None else dk + dk_h
                dqt[pl.ds(h * 64, 64)] += dot(kt_s[p, pl.ds(h * 64, 64), rows], ds)
            cos_t, sin_t = cos_v[rows], sin_v[rows]
            gq[rows, pl.ds(128, 128)] = (dk * cos_t - swap_halves(dk) * sin_t).astype(BF)
            gq[rows, pl.ds(256, 128)] = dv.astype(BF)

            for n in range(4):
                slot((AT_B, p, n), t == n)

        @pl.loop(0, 4)
        def _(t):
            rows = rows_of(t * 256, 256)
            block = dqt[:, rows] * 0.125
            cos_t, sin_t = cost[:, rows], sint[:, rows]
            parts = []
            for h in range(2):
                u, w = block[h * 64 : h * 64 + 32], block[h * 64 + 32 : h * 64 + 64]
                parts += [u * cos_t + w * sin_t, w * cos_t - u * sin_t]
            gq[rows, pl.ds(0, 128)] = jnp.concatenate(parts, axis=0).T.astype(BF)

        @pl.loop(0, 3)
        def _(r):
            rows = rows_of(r * 256, 256)
            b_s[1 + p, rows] = dot(ait[rows], gq[...]).astype(BF)

        slot((AT_B, p, 5))

        @pl.loop(0, 4)
        def _(t):
            rows = rows_of(t * 256, 256)
            part = dot_t(gq[rows], wq[p])
            if p == 0:
                gacc[rows] = part
            else:
                gacc[rows] += part

        slot((AT_B, p, 6))

    remote(gsend, grecv, 9, TO_CORE).wait_send()
    for p in range(3):
        attend_back(p)

    @pl.loop(0, 512 // TILE)
    def _(i):
        gsend[rows_of(i * TILE, TILE)] = gacc[rows_of(other + i * TILE, TILE)].astype(BF)

    remote(gsend, grecv, 11 + 26, TO_CORE).start()
    slot((AT_E, 0))
    remote(gsend, grecv, 11 + 26, TO_CORE).wait()

    @pl.loop(0, 512 // TILE)
    def _(i):
        tile = rows_of(i * TILE, TILE)
        near = rows_of(own + i * TILE, TILE)
        grad = gacc[near] + grecv[tile].astype(F32)
        normed = n1[tile]
        vec[0:1] += jnp.sum(grad, axis=0, keepdims=True)
        vec[1:2] += jnp.sum(grad * normed, axis=0, keepdims=True)
        rows_out(1, i, gm[tile] + norm_back(grad * mul_one, normed, i1[tile]))

    out_copy(gin_o, 1).start()
    slot((AT_E, 1))
    sums = vec[...]
    vec[6:7] = sums[1:2] * (1.0 + scale_one)
    vec[7:8] = sums[4:5] * (1.0 + scale_two)
    vec[1:2] = sums[1:2] * again
    vec[4:5] = sums[4:5] * fgain
    for core in range(2):
        @pl.when(c == core)
        def _():
            for j in range(4):
                vec[9 + 2 * core + j // 2, pl.ds((j % 2) * 384, 384)] = ubg[j, 0]

    both = cond[...].astype(F32)
    vec[13:14, :128] = 0.5 * jnp.where(x == 0, both[0:1], both[1:2])
    remote(vec, vecr, 30, TO_CORE).start()
    slot((AT_E, 2))
    remote(vec, vecr, 30, TO_CORE).wait_recv()
    chip = 2 * z + x
    vall[chip] = vec[...] + vecr[...]

    def vec_copy(n, slot):
        return pltpu.make_async_remote_copy(
            src_ref=vall.at[slot], dst_ref=vall.at[slot], send_sem=vss.at[n], recv_sem=vrs.at[n],
            device_id=peers[n], device_id_type=MESH,
        )

    for n in range(len(peers)):
        vec_copy(n, chip).start()
    slot((AT_D, 0))
    for n in range(len(peers)):
        vec_copy(n, 2 * peers[n]["mlp"] + peers[n]["seq"] // 2).wait_recv()

    vall_out = local(vall, vall_o, 57)
    vall_out.start()
    vall_out.wait()

    for number, ref in ((0, out_o), (1, gin_o)):
        out_copy(ref, number).wait()
        for part in range(2):
            cross_rows(ref, number, part).wait()
    for p in range(4):
        for item in piece_copies(p):
            item.wait()
    for h in range(CH):
        for item in final_copies(g_s.at[x, z, span(h)], x, h, 0) + final_copies(fxr.at[span(h)], 1 - x, h, 1):
            item.wait()
        own_copy(h).wait_send()
    for n in range(len(peers)):
        vec_copy(n, chip).wait_send()
    swap_x.wait_send()
    swap_c.wait_send()
    for p in range(3):
        att_copy(p, False).wait_send()
    core_rows(fi, own, 512, 8).wait_send()
    core_rows(gproj, own, 512, 11).wait_send()
    remote(vec, vecr, 30, TO_CORE).wait_send()
    for place in range(Z):
        @pl.when(z == place)
        def _(place=place):
            for make in pending[place]:
                make().wait_send()


def finish_kernel(
    out_h, gin_h, qkv_h, outw_h, ffn_h, vall_h, adaw_h,
    out_o, gin_o, cond_o, again_o, adaw_o, adab_o, qkv_o, outw_o, fgain_o, up_o, upb_o, down_o, downb_o,
    tok_b, qkv_b, outw_b, ffn_b, adaw, vall, tok_f, qkv_f, outw_f, ffn_f, adaw_f, cond_s, isem, osem,
):
    z = lax.axis_index("mlp")
    D = 768
    loads, steps = [], []

    def step(src, buffer, result, dst, turn=False):
        number = len(steps)
        loads.append(pltpu.make_async_copy(src, buffer, isem.at[number]))
        store = pltpu.make_async_copy(result, dst, osem.at[number])

        def body():
            loads[number].wait()
            values = buffer[...].astype(F32)
            result[...] = values.T if turn else values
            store.start()

        steps.append((body, store))

    vall_copy = pltpu.make_async_copy(vall_h, vall, isem.at[30])
    adaw_copy = pltpu.make_async_copy(adaw_h, adaw, isem.at[31])
    for n in range(6):
        rows = pl.ds(n * 128, 128)
        step(qkv_h.at[rows], qkv_b.at[rows], qkv_f.at[rows], qkv_o.at[rows])
    for n in range(2):
        rows = pl.ds(n * 384, 384)
        step(outw_h.at[rows], outw_b.at[rows], outw_f.at[rows], outw_o.at[rows])
        step(ffn_h.at[0, rows], ffn_b.at[0, rows], ffn_f.at[0, rows], up_o.at[rows])
    for n in range(3):
        rows = pl.ds(n * 256, 256)
        step(ffn_h.at[1, rows], ffn_b.at[1, rows], ffn_f.at[1, :, rows], down_o.at[:, rows], True)
    for n in range(2):
        step(out_h.at[n], tok_b.at[0, n], tok_f.at[0, n], out_o.at[n])
        step(gin_h.at[n], tok_b.at[1, n], tok_f.at[1, n], gin_o.at[n])
    for item in loads[:6] + [vall_copy, adaw_copy] + loads[6:]:
        item.start()
    for body, _ in steps[:6]:
        body()
    vall_copy.wait()
    adaw_copy.wait()
    high = lax.Precision.HIGHEST
    everyone = vall[:, 13, :128]
    total = vall[0]
    for n in range(1, 8):
        total = total + vall[n]
    acc, ada_out = None, []
    for part in range(6):
        lanes = pl.ds(part * D, D)
        grads = vall[:, part, :]
        adab_o[lanes] = total[part]
        adaw_f[part] = lax.dot_general(
            everyone, grads, (((0,), (0,)), ((), ())), precision=high, preferred_element_type=F32
        )
        ada_out.append(pltpu.make_async_copy(adaw_f.at[part], adaw_o.at[:, lanes], osem.at[26 + part]))
        ada_out[-1].start()
        piece = lax.dot_general(
            grads, adaw[:, lanes].astype(F32), (((1,), (1,)), ((), ())), precision=high,
            preferred_element_type=F32,
        )
        acc = piece if acc is None else acc + piece
    for body, _ in steps[6:]:
        body()
    cond_s[...] = acc
    cond_o[...] = cond_s[pl.ds(2 * z, 2), :]
    again_o[...] = total[6]
    fgain_o[...] = total[7]
    downb_o[...] = total[8]
    for core in range(2):
        halves = [total[9 + 2 * core + j // 2, (j % 2) * 384 : (j % 2 + 1) * 384] for j in range(4)]
        mine = halves[0]
        for j in range(1, 4):
            mine = jnp.where(z == j, halves[j], mine)
        upb_o[pl.ds(core * 384, 384)] = mine
    for item in ada_out:
        item.wait()
    for _, store in steps:
        store.wait()


def tables(seg_len, seq_size):
    half = np.arange(32)
    frequency = 10000.0 ** (-2.0 * half / 64)
    core, chip, token = np.meshgrid(
        np.arange(2), np.arange(seq_size // 2), np.arange(seg_len), indexing="ij"
    )
    place = ((chip * 2 + core) * seg_len + token).reshape(-1)
    angle = place[:, None] * frequency[None, :]
    cos, sin = np.cos(angle).astype(np.float32), np.sin(angle).astype(np.float32)
    return (
        np.tile(cos, (1, 4)),
        np.concatenate([-sin, sin, -sin, sin], axis=1),
        np.ascontiguousarray(cos.T),
        np.ascontiguousarray(sin.T),
    )


def fast_shards(
    inputs, condition, attn_gain, ada_weight, ada_bias, qkv_weight, out_weight, ffn_gain,
    up_weight, up_bias, down_weight, down_bias, cotangent,
):
    Z = lax.axis_size("mlp")
    tabs = [jnp.asarray(t) for t in tables(inputs.shape[1], lax.axis_size("seq"))]
    hbm, vm = pl.BlockSpec(memory_space=pl.ANY), pl.BlockSpec(memory_space=pltpu.VMEM)
    shape = jax.ShapeDtypeStruct
    V = pltpu.VMEM
    dma = pltpu.SemaphoreType.DMA
    scratch = [
        V((128, 4608), BF), V((3, 768, 384), BF), V((768, 768), BF), V((Z, 768, 384), BF),
        V((Z, 384, 768), BF), V((Z, 1, 768), F32), V((1024, 128), F32), V((1024, 128), F32),
        V((32, 1024), F32), V((32, 1024), F32),
        V((512, 768), BF), V((512, 768), BF), V((2, 4608), F32), V((512, 768), F32), V((512, 1), F32),
        V((1024, 768), BF), V((768, 1024), BF),
        V((3, 1024, 128), BF), V((3, 1024, 128), BF), V((3, 1024, 128), BF),
        V((3, 128, 1024), BF), V((3, 128, 1024), BF), V((3, 128, 1024), F32), V((3, 2, 1024), F32),
        V((512, 768), BF), V((512, 384), BF),
        V((512, 768), F32), V((512, 768), F32), V((512, 1), F32),
        V((768, 1024), BF), V((1024, 768), BF), V((768, 1024), BF),
        V((1024, 768), F32), V((1024, 768), F32), V((1024, 384), BF), V((1024, 384), BF),
        V((2, Z, 768, 384), BF), V((512, 768), BF),
        V((512, 768), F32), V((3, 1024, 128), BF), V((3, 2, 1024), F32), V((128, 1024), F32),
        V((1024, 384), BF), V((4, 768, 384), BF), V((2, 512, 768), BF),
        V((16, 768), F32), V((16, 768), F32), V((2 * Z, 16, 768), F32), V((Z, 1, 384), F32),
        V((Z, 768, 384), BF), V((Z, 768, 384), BF), V((768, 384), BF), V((4, 192, 384), BF),
        V((4, 768, 384), BF),
        dma((63,)), dma((38,)), dma((38,)), dma((2, Z, 3)), dma((2, Z, 3)), dma((Z, 2)), dma((Z, 2)),
        dma((Z, 3)), dma((Z, 3)), dma((4, 4, 4)), dma((4, 4, 4)), dma((6, 4)), dma((6, 4)), dma((7,)), dma((7,)),
        pltpu.SemaphoreType.REGULAR((2,)),
    ]
    token = shape(inputs.shape, BF)
    vall_shape = shape((2 * Z, 16, 768), F32)
    ffn_shape = shape((2, 768, 768), BF)
    out, gin, qkv, outw, ffn, vall = pl.pallas_call(
        fast_kernel,
        out_shape=[
            token, token, shape(qkv_weight.shape, BF), shape(out_weight.shape, BF), ffn_shape, vall_shape,
        ],
        in_specs=[hbm, vm, vm, hbm, vm, hbm, hbm, vm, hbm, vm, hbm, vm, hbm, hbm, hbm, hbm, hbm],
        out_specs=[hbm] * 6,
        scratch_shapes=scratch,
        compiler_params=pltpu.CompilerParams(
            collective_id=0, has_side_effects=True, vmem_limit_bytes=VMEM_LIMIT
        ),
        name="block",
    )(
        inputs, condition, attn_gain, ada_weight, ada_bias, qkv_weight, out_weight,
        ffn_gain, up_weight, up_bias, down_weight, down_bias, cotangent, *tabs,
    )
    same = lambda v: shape(v.shape, F32)
    tokens = shape(inputs.shape, F32)
    return pl.pallas_call(
        finish_kernel,
        out_shape=[
            tokens, tokens, same(condition), same(attn_gain), same(ada_weight), same(ada_bias),
            same(qkv_weight), same(out_weight), same(ffn_gain), same(up_weight), same(up_bias),
            same(down_weight), same(down_bias),
        ],
        in_specs=[hbm] * 7,
        out_specs=[hbm, hbm, vm, vm, hbm, vm, hbm, hbm, vm, hbm, vm, hbm, vm],
        scratch_shapes=[
            V((2, *inputs.shape), BF), V(qkv_weight.shape, BF), V(out_weight.shape, BF), V((2, 768, 768), BF),
            V(ada_weight.shape, BF), V((2 * Z, 16, 768), F32), V((2, *inputs.shape), F32),
            V(qkv_weight.shape, F32), V(out_weight.shape, F32), V((2, 768, 768), F32), V((6, 128, 768), F32),
            V((2 * Z, 128), F32), dma((32,)), dma((32,)),
        ],
        compiler_params=pltpu.CompilerParams(vmem_limit_bytes=VMEM_LIMIT),
        name="finish",
    )(out, gin, qkv, outw, ffn, vall, ada_weight)


def solution(mesh):
    placed = (
        P(("grp", "mlp"), "seq", None),
        P(("grp", "mlp"), None),
        P(),
        P(),
        P(),
        P(),
        P(),
        P(),
        P(None, "mlp"),
        P("mlp"),
        P("mlp", None),
        P(),
        P(("grp", "mlp"), "seq", None),
    )
    sizes = dict(mesh.shape)
    small = sizes["seq"] == 4 and sizes["grp"] == 2 and sizes["mlp"] == 4
    return jax.shard_map(
        fast_shards if small else shards,
        mesh=mesh,
        in_specs=placed,
        out_specs=(
            P(("grp", "mlp"), "seq", None),
            P(("grp", "mlp"), "seq", None),
            P(("grp", "mlp"), None),
            P("grp"),
            P("grp", None),
            P("grp"),
            P("grp", None),
            P("grp", None),
            P("grp"),
            P("grp", "mlp"),
            P(("grp", "mlp")),
            P(("grp", "mlp"), None),
            P("grp"),
        ),
        check_vma=False,
    )
```

```python
import math

import jax
import jax.numpy as jnp
import numpy as np
from jax import lax
from jax.experimental import pallas as pl
from jax.experimental.pallas import tpu as pltpu
from jax.sharding import PartitionSpec as P

HEADS = 12
VMEM_LIMIT = 63 * 2**20


gelu_coef = 0.7978845608028654


def layer_norm(values):
    center = values - jnp.mean(values, axis=-1, keepdims=True)
    inv_std = lax.rsqrt(jnp.mean(center * center, axis=-1, keepdims=True) + 1e-05)
    return (center * inv_std, inv_std)


def norm_back(grad_norm, normed, inv_std):
    return inv_std * (
        grad_norm
        - jnp.mean(grad_norm, axis=-1, keepdims=True)
        - normed * jnp.mean(grad_norm * normed, axis=-1, keepdims=True)
    )


def gelu_tanh(values):
    return (
        0.5 * values * (1.0 + jnp.tanh(gelu_coef * (values + 0.044715 * values * values * values)))
    )


def gelu_slope(values):
    tanh_val = jnp.tanh(gelu_coef * (values + 0.044715 * values * values * values))
    return 0.5 * (1.0 + tanh_val) + 0.5 * values * (1.0 - tanh_val * tanh_val) * gelu_coef * (
        1.0 + 3.0 * 0.044715 * values * values
    )


def rotary_tables(positions, head_size):
    half_dim = head_size // 2
    frequencies = jnp.power(10000.0, -2.0 * jnp.arange(half_dim, dtype=jnp.float32) / head_size)
    angles = positions[:, None] * frequencies[None, :]
    return (jnp.cos(angles), jnp.sin(angles))


def rotate(tensor, cos_tab, sine_tab):
    half_dim = tensor.shape[-1] // 2
    first_half = tensor[..., :half_dim]
    second_half = tensor[..., half_dim:]
    return jnp.concatenate(
        [
            first_half * cos_tab - second_half * sine_tab,
            second_half * cos_tab + first_half * sine_tab,
        ],
        axis=-1,
    )


def unrotate(tensor, cos_tab, sine_tab):
    half_dim = tensor.shape[-1] // 2
    first_half = tensor[..., :half_dim]
    second_half = tensor[..., half_dim:]
    return jnp.concatenate(
        [
            first_half * cos_tab + second_half * sine_tab,
            second_half * cos_tab - first_half * sine_tab,
        ],
        axis=-1,
    )


def score_of(query_rows, key_rows, scale_factor):
    return (
        jnp.einsum("sghd,skhd->shgk", query_rows, key_rows, preferred_element_type=jnp.float32)
        * scale_factor
    )


def score_grads(query_rows, dout_rows, lse_rows, delta_rows, key_rows, value_rows, scale_factor):
    prob_rows = jnp.exp(score_of(query_rows, key_rows, scale_factor) - lse_rows[..., None])
    grad_probs = jnp.einsum(
        "sghd,skhd->shgk", dout_rows, value_rows, preferred_element_type=jnp.float32
    )
    grad_scores = (prob_rows * (grad_probs - delta_rows[..., None])).astype(jnp.bfloat16)
    return (prob_rows.astype(jnp.bfloat16), grad_scores)


def shards(
    inputs,
    condition,
    attn_gain,
    ada_weight,
    ada_bias,
    qkv_weight,
    out_weight,
    ffn_gain,
    up_weight,
    up_bias,
    down_weight,
    down_bias,
    cotangent,
):
    seq_count, seg_len, model_width = inputs.shape
    head_count = HEADS
    head_size = model_width // head_count
    full_len = seg_len * lax.axis_size("seq")
    block_len = math.gcd(full_len, 512)
    block_count = full_len // block_len
    scale_factor = float(head_size) ** (-0.5)
    positions = (lax.axis_index("seq") * seg_len + jnp.arange(seg_len, dtype=jnp.int32)).astype(
        jnp.float32
    )
    cos_tab, sine_tab = rotary_tables(positions, head_size)
    cos_tab = cos_tab[None, :, None, :]
    sine_tab = sine_tab[None, :, None, :]

    def heads_view(matrix):
        return matrix.reshape(seq_count, seg_len, head_count, head_size)

    x_float = inputs.astype(jnp.float32)
    modulate = jnp.dot(condition, ada_weight, preferred_element_type=jnp.float32) + ada_bias
    shift_one, scale_one, gate_one, shift_two, scale_two, gate_two = [
        modulate[:, None, member * model_width : (member + 1) * model_width] for member in range(6)
    ]
    norm_one, inv_one = layer_norm(x_float)
    attn_in = (norm_one * attn_gain * (1.0 + scale_one) + shift_one).astype(jnp.bfloat16)
    projected = jnp.dot(attn_in, qkv_weight, preferred_element_type=jnp.float32)
    queries = rotate(heads_view(projected[..., :model_width]), cos_tab, sine_tab).astype(
        jnp.bfloat16
    )
    key_rot = rotate(
        heads_view(projected[..., model_width : 2 * model_width]), cos_tab, sine_tab
    ).astype(jnp.bfloat16)
    value_low = projected[..., 2 * model_width :].astype(jnp.bfloat16)
    kv_local = jnp.concatenate(
        [key_rot.reshape(seq_count, seg_len, model_width), value_low], axis=-1
    )
    kv_whole = lax.all_gather(kv_local, "seq", axis=1, tiled=True)
    kv_view = kv_whole.reshape(seq_count, full_len, 2, head_count, head_size)

    def key_block(block_num):
        sliced = lax.dynamic_slice_in_dim(kv_view, block_num * block_len, block_len, 1)
        return (sliced[:, :, 0], sliced[:, :, 1])

    def max_pass(block_num, running):
        run_max, run_sum = running
        key_rows, value_rows = key_block(block_num)
        scores = score_of(queries, key_rows, scale_factor)
        new_max = jnp.maximum(run_max, jnp.max(scores, axis=-1))
        run_sum = run_sum * jnp.exp(run_max - new_max) + jnp.sum(
            jnp.exp(scores - new_max[..., None]), axis=-1
        )
        return (new_max, run_sum)

    stat_shape = (seq_count, head_count, seg_len)
    run_max, run_sum = lax.fori_loop(
        0,
        block_count,
        max_pass,
        (jnp.full(stat_shape, -1e30, jnp.float32), jnp.zeros(stat_shape, jnp.float32)),
    )
    log_sum = run_max + jnp.log(run_sum)

    def out_pass(block_num, accums):
        accum_out, accum_exact = accums
        key_rows, value_rows = key_block(block_num)
        prob_rows = jnp.exp(score_of(queries, key_rows, scale_factor) - log_sum[..., None])
        accum_out = accum_out + jnp.einsum(
            "shgk,skhd->sghd",
            prob_rows.astype(jnp.bfloat16),
            value_rows,
            preferred_element_type=jnp.float32,
        )
        accum_exact = accum_exact + jnp.einsum(
            "shgk,skhd->sghd",
            prob_rows,
            value_rows.astype(jnp.float32),
            preferred_element_type=jnp.float32,
        )
        return (accum_out, accum_exact)

    head_shape = (seq_count, seg_len, head_count, head_size)
    attn_float, attn_exact = lax.fori_loop(
        0,
        block_count,
        out_pass,
        (jnp.zeros(head_shape, jnp.float32), jnp.zeros(head_shape, jnp.float32)),
    )
    attn_low = attn_float.reshape(seq_count, seg_len, model_width).astype(jnp.bfloat16)
    attn_proj = jnp.dot(attn_low, out_weight, preferred_element_type=jnp.float32)
    middle = x_float + gate_one * attn_proj
    norm_two, inv_two = layer_norm(middle)
    ffn_in = (norm_two * ffn_gain * (1.0 + scale_two) + shift_two).astype(jnp.bfloat16)
    ffn_rows = lax.all_gather(ffn_in, "mlp", axis=0, tiled=True)
    pre_act = jnp.dot(ffn_rows, up_weight, preferred_element_type=jnp.float32) + up_bias
    act_low = gelu_tanh(pre_act).astype(jnp.bfloat16)
    ffn_out = (
        lax.psum_scatter(
            jnp.dot(act_low, down_weight, preferred_element_type=jnp.float32).astype(jnp.bfloat16),
            "mlp",
            scatter_dimension=0,
            tiled=True,
        ).astype(jnp.float32)
        + down_bias
    )
    output = middle + gate_two * ffn_out
    cot_float = cotangent.astype(jnp.float32)
    grad_ffn = (gate_two * cot_float).astype(jnp.bfloat16)
    down_bias_part = jnp.sum(grad_ffn.astype(jnp.float32), axis=(0, 1))
    dgate_two = jnp.sum(cot_float * ffn_out, axis=1)
    grad_ffn_rows = lax.all_gather(grad_ffn, "mlp", axis=0, tiled=True)
    down_part = jnp.einsum(
        "sgf,sgd->fd", act_low, grad_ffn_rows, preferred_element_type=jnp.float32
    )
    grad_act = jnp.einsum(
        "sgd,fd->sgf", grad_ffn_rows, down_weight, preferred_element_type=jnp.float32
    )
    grad_pre = (grad_act * gelu_slope(pre_act)).astype(jnp.bfloat16)
    up_bias_part = jnp.sum(grad_pre.astype(jnp.float32), axis=(0, 1))
    up_part = jnp.einsum("sgd,sgf->df", ffn_rows, grad_pre, preferred_element_type=jnp.float32)
    grad_ffn_in = lax.psum_scatter(
        jnp.einsum("sgf,df->sgd", grad_pre, up_weight, preferred_element_type=jnp.float32).astype(
            jnp.bfloat16
        ),
        "mlp",
        scatter_dimension=0,
        tiled=True,
    ).astype(jnp.float32)
    dshift_two = jnp.sum(grad_ffn_in, axis=1)
    dscale_two = jnp.sum(grad_ffn_in * norm_two * ffn_gain, axis=1)
    gain_two_part = jnp.sum(grad_ffn_in * (1.0 + scale_two) * norm_two, axis=(0, 1))
    grad_middle = cot_float + norm_back(
        grad_ffn_in * (1.0 + scale_two) * ffn_gain, norm_two, inv_two
    )
    grad_proj = (gate_one * grad_middle).astype(jnp.bfloat16)
    dgate_one = jnp.sum(grad_middle * attn_proj, axis=1)
    out_part = jnp.einsum("sgd,sge->de", attn_low, grad_proj, preferred_element_type=jnp.float32)
    grad_attn = jnp.einsum(
        "sge,de->sgd", grad_proj, out_weight, preferred_element_type=jnp.float32
    ).astype(jnp.bfloat16)
    grad_attn_heads = heads_view(grad_attn)
    delta_rows = jnp.sum(grad_attn_heads.astype(jnp.float32) * attn_exact, axis=-1)
    delta_heads = jnp.transpose(delta_rows, (0, 2, 1))

    def back_pass(block_num, state_in):
        grad_query, key_grads = state_in
        key_rows, value_rows = key_block(block_num)
        prob_low, grad_scores = score_grads(
            queries, grad_attn_heads, log_sum, delta_heads, key_rows, value_rows, scale_factor
        )
        grad_query = (
            grad_query
            + jnp.einsum(
                "shgk,skhd->sghd", grad_scores, key_rows, preferred_element_type=jnp.float32
            )
            * scale_factor
        )
        grad_key = (
            jnp.einsum("shgk,sghd->skhd", grad_scores, queries, preferred_element_type=jnp.float32)
            * scale_factor
        )
        grad_value = jnp.einsum(
            "shgk,sghd->skhd", prob_low, grad_attn_heads, preferred_element_type=jnp.float32
        )
        stacked = jnp.concatenate(
            [
                grad_key.reshape(seq_count, block_len, model_width),
                grad_value.reshape(seq_count, block_len, model_width),
            ],
            axis=-1,
        )
        key_grads = lax.dynamic_update_slice_in_dim(key_grads, stacked, block_num * block_len, 1)
        return (grad_query, key_grads)

    grad_query, key_grads = lax.fori_loop(
        0,
        block_count,
        back_pass,
        (
            jnp.zeros(head_shape, jnp.float32),
            jnp.zeros((seq_count, full_len, 2 * model_width), jnp.float32),
        ),
    )
    kv_grads = lax.psum_scatter(
        key_grads.astype(jnp.bfloat16), "seq", scatter_dimension=1, tiled=True
    ).astype(jnp.float32)
    grad_key_rot = heads_view(kv_grads[..., :model_width])
    grad_values = kv_grads[..., model_width:]
    grad_qkv = jnp.concatenate(
        [
            unrotate(grad_query, cos_tab, sine_tab).reshape(seq_count, seg_len, model_width),
            unrotate(grad_key_rot, cos_tab, sine_tab).reshape(seq_count, seg_len, model_width),
            grad_values,
        ],
        axis=-1,
    ).astype(jnp.bfloat16)
    qkv_part = jnp.einsum("sgd,sge->de", attn_in, grad_qkv, preferred_element_type=jnp.float32)
    grad_attn_in = jnp.einsum(
        "sge,de->sgd", grad_qkv, qkv_weight, preferred_element_type=jnp.float32
    )
    dshift_one = jnp.sum(grad_attn_in, axis=1)
    dscale_one = jnp.sum(grad_attn_in * norm_one * attn_gain, axis=1)
    gain_one_part = jnp.sum(grad_attn_in * (1.0 + scale_one) * norm_one, axis=(0, 1))
    grad_inputs = grad_middle + norm_back(
        grad_attn_in * (1.0 + scale_one) * attn_gain, norm_one, inv_one
    )
    grad_modulate = jnp.concatenate(
        [dshift_one, dscale_one, dgate_one, dshift_two, dscale_two, dgate_two], axis=-1
    )
    ada_weight_part = jnp.dot(
        condition.astype(jnp.float32).T, grad_modulate, precision=lax.Precision.HIGHEST
    )
    ada_bias_part = jnp.sum(grad_modulate, axis=0)
    cond_part = jnp.dot(
        grad_modulate, ada_weight.astype(jnp.float32).T, precision=lax.Precision.HIGHEST
    )
    summed_all = lax.psum(
        (
            qkv_part,
            out_part,
            ada_weight_part,
            ada_bias_part,
            gain_one_part,
            gain_two_part,
            down_bias_part,
        ),
        ("seq", "mlp"),
    )
    summed_seq = (
        lax.psum(up_part.astype(jnp.bfloat16), "seq").astype(jnp.float32),
        lax.psum(up_bias_part.astype(jnp.bfloat16), "seq").astype(jnp.float32),
        lax.psum(down_part.astype(jnp.bfloat16), "seq").astype(jnp.float32),
        lax.psum(cond_part.astype(jnp.bfloat16), "seq").astype(jnp.float32),
    )
    return (
        output,
        grad_inputs,
        summed_seq[3],
        summed_all[4],
        summed_all[2],
        summed_all[3],
        summed_all[0],
        summed_all[1],
        summed_all[5],
        summed_seq[0],
        summed_seq[1],
        summed_seq[2],
        summed_all[6],
    )


FFN_X, FFN_Z, FFN_OWN, FFN_LAST, SUM_0, REL, SUM_3, SUM_4, FW, SUM_7, WL, WR, XS_, ZS, XO, OX, GX, WD_ = range(18)
AT_W, AT_F, AT_A, AT_T, AT_N, AT_B, AT_E, AT_D, AT_G = range(9)
ORDERS = ((1, 2, 3, 0), (0, 2, 3, 1), (3, 1, 0, 2), (2, 1, 0, 3))
OWN_STEP = 3
PLAN = {(AT_A, 1, 1): {0: [(WR, 2)], 1: [(WR, 2)], 2: [(WL, 2)], 3: [(WL, 2)]},
 (AT_A, 2, 0): {0: [(WD_, 1)], 1: [(WD_, 0)], 2: [(WD_, 1)], 3: [(WD_, 2)]},
 (AT_B, 0, 0): {0: [(FFN_X, 2, 2), (OX, 1)],
                1: [(FFN_Z, 3, 2), (ZS, 3, 2)],
                2: [(REL, 1, 0, 0)],
                3: [(FFN_X, 1, 2), (OX, 1)]},
 (AT_B, 0, 1): {0: [(XS_, 1, 1)],
                1: [(REL, 0, 3, 0), (XS_, 2, 1)],
                2: [(REL, 1, 1, 0), (XS_, 1, 1)],
                3: [(XS_, 2, 1)]},
 (AT_B, 0, 5): {0: [(SUM_0, 1)], 1: [(REL, 0, 2, 0)], 3: [(SUM_0, 1)]},
 (AT_B, 1, 0): {0: [(XS_, 1, 2)],
                1: [(XS_, 2, 2)],
                2: [(REL, 1, 0, 1), (REL, 0, 3, 0), (XS_, 1, 2)],
                3: [(XS_, 2, 2)]},
 (AT_B, 1, 1): {0: [(FFN_X, 1, 1), (XS_, 0, 0)],
                1: [(REL, 0, 3, 1), (REL, 1, 0, 0), (FFN_X, 2, 1), (XS_, 1, 0), (FFN_Z, 2, 1), (ZS, 2, 1)],
                2: [(REL, 1, 1, 1), (SUM_3, 0), (FFN_X, 1, 1), (FFN_Z, 1, 1), (ZS, 1, 1)],
                3: [(FFN_X, 2, 1), (XS_, 3, 0)]},
 (AT_B, 1, 5): {0: [(SUM_0, 2)], 2: [(REL, 0, 3, 1), (XS_, 2, 0)], 3: [(SUM_0, 2)]},
 (AT_B, 2, 0): {0: [(FFN_X, 1, 2), (XS_, 0, 1)],
                1: [(REL, 0, 2, 1), (SUM_3, 0), (FFN_X, 2, 2)],
                2: [(FFN_X, 1, 2)],
                3: [(FFN_X, 2, 2), (XS_, 3, 1)]},
 (AT_B, 2, 1): {0: [(FFN_X, 0, 0), (FFN_OWN, 0), (XO, 0), (SUM_3, 0)],
                1: [(REL, 1, 0, 1), (FFN_X, 1, 0), (FFN_OWN, 0), (SUM_3, 1), (REL, 0, 3, 2)],
                2: [(SUM_4, 0), (REL, 1, 0, 2), (XS_, 2, 1)],
                3: [(FFN_X, 3, 0), (FFN_OWN, 0), (XO, 0), (SUM_3, 0)]},
 (AT_B, 2, 5): {0: [(SUM_0, 3)],
                1: [(SUM_4, 0), (XO, 0)],
                2: [(SUM_3, 1), (REL, 1, 1, 2), (FFN_X, 2, 0), (FFN_OWN, 0)],
                3: [(SUM_0, 3)]},
 (AT_B, 3, 0): {1: [(REL, 0, 2, 2)]},
 (AT_B, 3, 1): {0: [(FFN_X, 0, 1), (FFN_OWN, 1)], 2: [(REL, 0, 3, 2)], 3: [(FFN_X, 3, 1), (FFN_OWN, 1)]},
 (AT_B, 3, 3): {1: [(SUM_4, 1), (XS_, 1, 1)], 2: [(XO, 0)], 3: [(SUM_3, 1)]},
 (AT_D, 0): {0: [(SUM_4, 1), (XO, 1), (XS_, 0, 2), (SUM_3, 2), (ZS, 2, 2), (FFN_LAST, 1), (SUM_3, 3), (ZS, 1, 1),
                 (FFN_X, 0, 2), (FFN_OWN, 2), (SUM_4, 2), (XO, 2), (SUM_4, 3), (GX, 0), (SUM_7, 0), (ZS, 1, 2),
                 (FFN_LAST, 2), (GX, 1), (SUM_7, 1), (SUM_7, 2), (SUM_7, 3)],
             1: [(REL, 0, 2, 3), (FFN_X, 1, 1), (SUM_3, 2), (REL, 1, 0, 3), (FFN_X, 1, 2), (FW, 2, 0, 0),
                 (FW, 3, 2, 1), (FW, 2, 0, 1), (GX, 0), (SUM_3, 3), (SUM_4, 2), (FFN_Z, 2, 2), (FW, 3, 3, 0),
                 (SUM_7, 0), (ZS, 2, 2), (FW, 3, 2, 2), (GX, 1), (FFN_OWN, 1), (SUM_4, 3), (FW, 3, 3, 1), (SUM_7, 1),
                 (FW, 2, 0, 2), (XO, 1), (FW, 3, 3, 2), (SUM_7, 2), (FW, 2, 0, 3), (FW, 3, 2, 3), (FFN_LAST, 1),
                 (FFN_OWN, 2), (XO, 2), (FW, 3, 3, 3), (SUM_7, 3), (FFN_LAST, 2)],
             2: [(FW, 2, 1, 1), (FFN_LAST, 0), (FW, 3, 3, 0), (REL, 0, 3, 3), (SUM_4, 2), (XS_, 2, 2), (FW, 3, 3, 1),
                 (SUM_3, 3), (FW, 2, 0, 0), (SUM_7, 0), (FFN_Z, 1, 2), (FFN_X, 2, 2), (FW, 2, 0, 1), (SUM_7, 1),
                 (GX, 0), (FW, 3, 3, 2), (SUM_4, 3), (FW, 2, 1, 2), (GX, 1), (FFN_OWN, 1), (ZS, 1, 2), (XO, 1),
                 (FFN_OWN, 2), (FW, 2, 1, 3), (FW, 3, 3, 3), (XO, 2), (FW, 2, 0, 2), (SUM_7, 2), (FFN_LAST, 1),
                 (FW, 2, 0, 3), (SUM_7, 3), (FFN_LAST, 2)],
             3: [(SUM_4, 1), (SUM_3, 2), (FFN_LAST, 1), (XS_, 3, 2), (ZS, 1, 2), (SUM_4, 2), (GX, 0), (SUM_3, 3),
                 (FFN_X, 3, 2), (FFN_OWN, 2), (ZS, 2, 1), (XO, 2), (ZS, 2, 2), (SUM_7, 0), (SUM_4, 3), (GX, 1),
                 (SUM_7, 1), (FFN_LAST, 2), (SUM_7, 2), (SUM_7, 3)]},
 (AT_E, 0): {2: [(REL, 1, 0, 3), (FW, 2, 1, 0), (FFN_X, 2, 1)]},
 (AT_E, 1): {0: [(SUM_3, 1), (FFN_LAST, 0), (SUM_4, 0)],
             1: [(FW, 3, 2, 0), (REL, 0, 3, 3), (XS_, 1, 2), (REL, 1, 0, 2), (FFN_LAST, 0)],
             2: [(SUM_4, 1), (REL, 1, 1, 3), (SUM_3, 2)],
             3: [(XO, 1), (SUM_4, 0), (FFN_LAST, 0)]},
 (AT_G, 0): {0: [(XS_, 1, 0)], 1: [(XS_, 0, 0)], 2: [(XS_, 3, 0)], 3: [(XS_, 2, 0)]},
 (AT_G, 1): {0: [(XS_, 2, 0)],
             1: [(FFN_X, 0, 0), (ZS, 0, 0), (XS_, 0, 2)],
             2: [(FFN_X, 3, 0), (ZS, 3, 0), (XS_, 3, 2)],
             3: [(XS_, 1, 0)]},
 (AT_G, 2): {0: [(FFN_X, 2, 0), (ZS, 2, 0), (XS_, 3, 0)], 3: [(FFN_X, 1, 0), (ZS, 1, 0), (XS_, 0, 0)]},
 (AT_G, 3): {0: [(FFN_X, 3, 0), (ZS, 3, 0), (XS_, 3, 2)],
             1: [(XS_, 3, 1), (FFN_X, 2, 0), (FFN_Z, 2, 0), (ZS, 2, 0)],
             2: [(XS_, 0, 1), (FFN_X, 1, 0), (FFN_Z, 1, 0), (ZS, 1, 0)],
             3: [(FFN_X, 0, 0), (ZS, 0, 0), (XS_, 0, 2)]},
 (AT_N, 1): {0: [(FFN_X, 3, 1), (ZS, 3, 1), (XS_, 2, 2)],
             1: [(FFN_X, 3, 0), (XS_, 3, 2)],
             2: [(FFN_X, 0, 0), (XS_, 0, 2), (FFN_Z, 0, 0), (ZS, 0, 0)],
             3: [(FFN_X, 0, 1), (ZS, 0, 1), (XS_, 1, 2)]},
 (AT_N, 2): {1: [(FFN_X, 3, 1), (OX, 0), (FFN_Z, 3, 0), (ZS, 3, 0)],
             2: [(FFN_X, 0, 1), (OX, 0), (FFN_Z, 0, 1), (ZS, 0, 1)]},
 (AT_N, 3): {0: [(FFN_X, 3, 2), (ZS, 3, 2), (OX, 0)],
             1: [(FFN_Z, 3, 1), (ZS, 3, 1)],
             3: [(FFN_X, 0, 2), (ZS, 0, 2), (OX, 0)]},
 (AT_N, 4): {0: [(SUM_0, 0)],
             1: [(FFN_X, 3, 2), (OX, 1)],
             2: [(FFN_X, 0, 2), (OX, 1), (FFN_Z, 0, 2), (ZS, 0, 2)],
             3: [(SUM_0, 0)]},
 (AT_T, 0, 0): {1: [(WD_, 3)], 2: [(WD_, 0)]},
 (AT_T, 1, 0): {1: [(XS_, 0, 1)], 2: [(XS_, 3, 1)]},
 (AT_T, 1, 1): {0: [(WD_, 3)], 3: [(WD_, 0)]},
 (AT_T, 2, 0): {0: [(XS_, 2, 1), (FFN_X, 1, 0), (ZS, 1, 0)], 3: [(XS_, 1, 1), (FFN_X, 2, 0), (ZS, 2, 0)]},
 (AT_T, 2, 1): {1: [(FFN_X, 0, 1), (ZS, 0, 1), (XS_, 2, 0)], 2: [(FFN_X, 3, 1), (ZS, 3, 1), (XS_, 1, 0)]},
 (AT_T, 3, 0): {0: [(FFN_X, 2, 1), (ZS, 2, 1), (XS_, 3, 1)],
                1: [(XS_, 3, 0), (FFN_X, 0, 2), (ZS, 0, 2)],
                2: [(XS_, 0, 0), (FFN_X, 3, 2), (ZS, 3, 2)],
                3: [(FFN_X, 1, 1), (ZS, 1, 1), (XS_, 0, 1)]},
 (AT_W, 0): {0: [(WR, 1)], 1: [(WL, 1), (WR, 1)], 2: [(WL, 1), (WR, 1)], 3: [(WL, 1)]},
 (AT_W, 4): {0: [(WD_, 2), (WR, 3)], 1: [(WD_, 2)], 2: [(WD_, 3)], 3: [(WD_, 1), (WL, 3)]}}
HALF = (0, 0, 0, 0)


BF = jnp.bfloat16
F32 = jnp.float32
MESH = pl.DeviceIdType.MESH


def dot(a, b):
    return jnp.dot(a, b, preferred_element_type=F32)


def dot_t(a, b):
    return lax.dot_general(a, b, (((1,), (1,)), ((), ())), preferred_element_type=F32)


def rows_of(start, size):
    return pl.ds(pl.multiple_of(start, size), size)


def pick(table, index):
    value = table[0]
    for place in range(1, len(table)):
        value = jnp.where(index == place, table[place], value)
    return value


def swap_halves(tile):
    lane = lax.broadcasted_iota(jnp.int32, tile.shape, 1)
    return jnp.where(
        lane % 64 < 32, pltpu.roll(tile, 96, 1), pltpu.roll(tile, 32, 1)
    )


def fast_kernel(
    inputs, cond, again, adaw_h, adab, qkv_h, outw_h, fgain, up_h, upb, down_h, downb, cot_h,
    cos_h, sin_h, cost_h, sint_h,
    out_o, gin_o, qkv_o, outw_o, ffn_o, vall_o,
    wq, wo, wu, wd, ub, cos_v, sin_v, cost, sint,
    xb, ctb, mod2, n1, i1, ai, ait, q_s, k_s, v_s, kt_s, vt_s, ot_s, lse, att,
    ap, n2, i2, fit, gf, gft, oacc, gacc, a_s, gp_s, g_s, grecv,
    do_s, dlt, dqt, gq, b_s, xs, vec, vecr, vall, ubg,
    rx, rz, fxr, rxb, fb,
    lsem, ssem, rsem, wss, wrs, yss, yrs, fss, frs, bss, brs, hss, hrs, vss, vrs, credit,
):
    Z = 4
    grp = lax.axis_index("grp")
    seq = lax.axis_index("seq")
    z = lax.axis_index("mlp")
    x, c = seq // 2, seq % 2
    D = 768
    flat = lambda ref: ref[...].reshape(1, -1)
    again, adab, fgain, downb = flat(again), flat(adab), flat(fgain), flat(downb)
    own = c * 512
    other = (1 - c) * 512
    TO_CORE = {"seq": x * 2 + (1 - c)}
    TO_X = {"seq": (1 - x) * 2 + c}
    TO_Y = {"grp": 1 - grp}
    RIGHT = {"mlp": jnp.minimum(z + 1, Z - 1)}
    LEFT = {"mlp": jnp.maximum(z - 1, 0)}

    def remote(src, dst, index, device):
        return pltpu.make_async_remote_copy(
            src_ref=src, dst_ref=dst, send_sem=ssem.at[index], recv_sem=rsem.at[index],
            device_id=device, device_id_type=MESH,
        )

    def local(src, dst, index):
        return pltpu.make_async_copy(src, dst, lsem.at[index])

    half = pl.ds(pl.multiple_of(c * 384, 128), 384)
    loads = [local(inputs.at[x], xb.at[rows_of(x * 256, 256)], 0), ]
    loads += [local(cos_h, cos_v, 2), local(sin_h, sin_v, 3), local(cost_h, cost, 4), local(sint_h, sint, 5)]
    for p in range(3):
        for part in range(3):
            loads.append(
                local(
                    qkv_h.at[:, pl.ds(pl.multiple_of(part * D + c * 384 + p * 128, 128), 128)],
                    wq.at[p, :, pl.ds(part * 128, 128)],
                    6 + p * 3 + part,
                )
            )
    loads.append(local(outw_h, wo, 15))
    loads.append(local(up_h.at[:, half], wu.at[z], 16))
    loads.append(local(down_h.at[rows_of(c * 384, 384)], wd.at[z], 17))
    loads.append(local(cot_h.at[x], ctb.at[rows_of(x * 256, 256)], 18))
    adaw = [
        local(adaw_h.at[:, pl.ds(part * D, D)], fit.at[pl.ds(part * 128, 128), pl.ds(0, D)], 15 + 43 + part)
        for part in range(6)
    ]
    for item in [loads[0]] + adaw + loads[1:]:
        item.start()

    ub[z] = flat(upb)

    barrier = pltpu.get_barrier_semaphore()
    peers = [{"seq": (x ^ dx) * 2 + c, "mlp": z ^ dz} for dx in range(2) for dz in range(Z) if dx or dz]
    for device in [TO_CORE, TO_Y] + peers:
        pl.semaphore_signal(barrier, 1, device_id=device, device_id_type=MESH)
    pl.semaphore_wait(barrier, 2 + len(peers))

    swap_x = remote(inputs.at[1 - x], xb.at[rows_of(x * 256, 256)], 0, TO_X)
    swap_x.start()
    swap_c = remote(cot_h.at[1 - x], ctb.at[rows_of(x * 256, 256)], 1, TO_X)
    swap_c.start()

    def rows_at(ref, rows, which, part=None):
        start = which * rows
        if part is None:
            return ref.at[rows_of(start, rows)]
        return ref.at[pl.ds(pl.multiple_of(start + part * (rows // 2), 16), rows // 2)]

    here = grp * 2 + x

    def z_copies(j, way, device, first):
        own_up, own_down = rows_at(wu.at[j], 192, here), rows_at(wd.at[j], 96, here)
        if first:
            src = (
                up_h.at[rows_of(here * 192, 192), half],
                down_h.at[rows_of(c * 384 + here * 96, 96)],
                ub.at[z],
            )
        else:
            src = (own_up, own_down, ub.at[j])
        dst = (own_up, own_down, ub.at[j])
        return [
            pltpu.make_async_remote_copy(
                src_ref=src[i], dst_ref=dst[i], send_sem=wss.at[way, j, i], recv_sem=wrs.at[way, j, i],
                device_id=device, device_id_type=MESH,
            )
            for i in range(3)
        ]

    def pair_copies(j, kind, which, part, device):
        return [
            pltpu.make_async_remote_copy(
                src_ref=ref, dst_ref=ref, send_sem=yss.at[j, kind, i], recv_sem=yrs.at[j, kind, i],
                device_id=device, device_id_type=MESH,
            )
            for i, ref in enumerate((rows_at(wu.at[j], 192, which, part), rows_at(wd.at[j], 96, which, part)))
        ]

    by_x, by_y, across = grp * 2 + 1 - x, (1 - grp) * 2 + x, (1 - grp) * 2 + 1 - x

    def quarter_sends(j):
        return pair_copies(j, 0, here, None, TO_X) + pair_copies(j, 1, here, None, TO_Y)

    def quarter_waits(j):
        return pair_copies(j, 0, by_x, None, TO_X) + pair_copies(j, 1, by_y, None, TO_Y)

    def across_sends(j):
        return pair_copies(j, 2, by_y, 0, TO_X) + pair_copies(j, 3, by_x, 1, TO_Y)

    def across_waits(j):
        return pair_copies(j, 2, across, 0, TO_X) + pair_copies(j, 3, across, 1, TO_Y)

    def start_all(items):
        for item in items:
            item.start()

    @pl.when(z < Z - 1)
    def _():
        start_all(z_copies(z, 0, RIGHT, True))

    @pl.when(z > 0)
    def _():
        start_all(z_copies(z, 1, LEFT, True))

    def order(n):
        return pick([ORDERS[a][n] for a in range(Z)], z)

    pending = {place: [] for place in range(Z)}
    CH = 3

    def send(place, *makes):
        for make in makes:
            make().start()
            pending[place].append(make)

    def span(h):
        return pl.ds(h * (768 // CH), 768 // CH)

    def ffn_copy(j, h):
        return pltpu.make_async_remote_copy(
            src_ref=g_s.at[1 - x, j, span(h)], dst_ref=rx.at[j, span(h)], send_sem=hss.at[j, h],
            recv_sem=hrs.at[j, h], device_id=TO_X, device_id_type=MESH,
        )

    def add_rows(ref, others):
        @pl.loop(0, 768 // CH // 64)
        def _(i):
            rows = rows_of(i * 64, 64)
            total = ref[rows].astype(F32)
            for other_ref in others:
                total = total + other_ref[rows].astype(F32)
            ref[rows] = total.astype(BF)

    def z_send(j, h, place):
        if place in (0, 3):
            target, slot = (1 if place == 0 else 2), j
        elif j in (0, 3):
            target, slot = j, place
        else:
            target, slot = j, (0 if j == 1 else 3)
        return lambda: pltpu.make_async_remote_copy(
            src_ref=g_s.at[x, j, span(h)], dst_ref=rz.at[slot, span(h)], send_sem=fss.at[j, h],
            recv_sem=frs.at[slot, h], device_id={"mlp": target}, device_id_type=MESH,
        )

    def z_wait(slot, h):
        ref = rz.at[slot, span(h)]
        pltpu.make_async_remote_copy(
            src_ref=ref, dst_ref=ref, send_sem=fss.at[0, h], recv_sem=frs.at[slot, h],
            device_id=LEFT, device_id_type=MESH,
        ).wait_recv()

    def ffn_x(place, j, h):
        ffn_copy(j, h).wait_recv()
        add_rows(g_s.at[x, j, span(h)], [rx.at[j, span(h)]])

    def ffn_z(place, j, h):
        z_wait(j, h)
        add_rows(g_s.at[x, j, span(h)], [rz.at[j, span(h)]])

    def zs(place, j, h):
        send(place, z_send(j, h, place))

    def xs_(place, j, h):
        send(place, lambda: ffn_copy(j, h))

    def final_copies(src, kind, h, first):
        dst = ffn_o.at[kind, span(h), half]
        return [local(src, dst, 21 + first * CH + h), remote(src, dst, 31 + first * CH + h, TO_CORE)]

    def own_copy(h):
        return pltpu.make_async_remote_copy(
            src_ref=g_s.at[x, z, span(h)], dst_ref=fxr.at[span(h)], send_sem=hss.at[5, h],
            recv_sem=hrs.at[5, h], device_id=TO_X, device_id_type=MESH,
        )

    def ffn_own(place, h):
        slots = {0: (1, 2), 3: (1, 2), 1: (1, 0), 2: (2, 3)}[place]
        for slot in slots:
            z_wait(slot, h)
        add_rows(g_s.at[x, place, span(h)], [rz.at[slot, span(h)] for slot in slots])
        for item in final_copies(g_s.at[x, z, span(h)], x, h, 0):
            item.start()

    def xo(place, h):
        own_copy(h).start()

    def ffn_last(place, h):
        own_copy(h).wait_recv()
        for item in final_copies(fxr.at[span(h)], 1 - x, h, 1):
            item.start()

    def quarter(ref, p, q):
        if ref is wd:
            return ref.at[p, pl.ds(q // 2 * 192, 192), pl.ds(q % 2 * 384, 384)]
        return ref.at[p, pl.ds(q * 192, 192)]

    def hop(kind, p, q, place):
        step = 1 if kind in (0, 2) else -1
        return lambda: pltpu.make_async_remote_copy(
            src_ref=quarter(b_s if kind < 2 else fb, p, q),
            dst_ref=quarter((wu, wd, fb, fb)[kind], p, q),
            send_sem=bss.at[kind, p, q],
            recv_sem=brs.at[kind, p, q],
            device_id={"mlp": place + step},
            device_id_type=MESH,
        )

    def hop_wait(kind, p, q):
        dst = quarter((wu, wd, fb, fb)[kind], p, q)
        pltpu.make_async_remote_copy(
            src_ref=dst, dst_ref=dst, send_sem=bss.at[kind, p, q], recv_sem=brs.at[kind, p, q],
            device_id=LEFT, device_id_type=MESH,
        ).wait_recv()

    def add_quarter(p, q, refs):
        total = quarter(b_s, p, q)[...].astype(F32)
        for ref in refs:
            total = total + quarter(ref, p, q)[...].astype(F32)
        quarter(b_s, p, q)[...] = total.astype(BF)

    def sum_0(place, p):
        kind, blocks = (0, (3, 2, 1)) if place == 0 else (1, (0, 1, 2))
        send(place, *[hop(kind, p, q, place) for q in blocks])

    def rel(place, kind, q, p):
        hop_wait(kind, p, q)
        add_quarter(p, q, [wd if kind else wu])
        send(place, hop(kind, p, q, place))

    def cross(p, place):
        return lambda: pltpu.make_async_remote_copy(
            src_ref=quarter(b_s, p, place), dst_ref=rxb.at[p], send_sem=hss.at[4, p],
            recv_sem=hrs.at[4, p], device_id=TO_X, device_id_type=MESH,
        )

    def sum_3(place, p):
        refs = []
        if place > 0:
            hop_wait(0, p, place)
            refs.append(wu)
        if place < 3:
            hop_wait(1, p, place)
            refs.append(wd)
        add_quarter(p, place, refs)
        send(place, cross(p, place))

    def sum_4(place, p):
        cross(p, place)().wait_recv()
        total = quarter(b_s, p, place)[...].astype(F32) + rxb[p].astype(F32)
        quarter(fb, p, place)[...] = total.astype(BF)
        if place < 3:
            send(place, hop(2, p, place, place))
        if place > 0:
            send(place, hop(3, p, place, place))

    def fw(place, kind, q, p):
        hop_wait(kind, p, q)
        send(place, hop(kind, p, q, place))

    def piece_copies(p):
        if p == 0:
            pairs = [
                (fb.at[0, pl.ds(n * 384, 384)], outw_o.at[rows_of(c * 384, 384), pl.ds(n * 384, 384)])
                for n in range(2)
            ]
        else:
            pairs = [
                (
                    fb.at[p, :, pl.ds(part * 128, 128)],
                    qkv_o.at[
                        :, pl.ds(pl.multiple_of(part * D + c * 384 + (p - 1) * 128, 128), 128)
                    ],
                )
                for part in range(3)
            ]
        copies = []
        for n, (src, dst) in enumerate(pairs):
            copies.append(local(src, dst, 43 + p * 3 + n))
            copies.append(remote(src, dst, 18 + p * 3 + n, TO_CORE))
        return copies

    def sum_7(place, p):
        for q in range(4):
            if place == 0 and q > 0:
                hop_wait(3, p, q)
            if place == 3 and q < 3:
                hop_wait(2, p, q)
        for item in piece_copies(p):
            item.start()

    def wl(place, k):
        for item in z_copies(place - k, 0, RIGHT, False):
            item.wait_recv()
        if place < 3:
            start_all(z_copies(place - k, 0, RIGHT, False))
        start_all(quarter_sends(place - k))

    def wr(place, k):
        for item in z_copies(place + k, 1, LEFT, False):
            item.wait_recv()
        if place > 0:
            start_all(z_copies(place + k, 1, LEFT, False))
        start_all(quarter_sends(place + k))

    def wd_(place, j):
        for item in quarter_waits(j):
            item.wait_recv()
        start_all(across_sends(j))

    def cross_rows(out_ref, number, part):
        rows = rows_of((1 - x) * 256 + part * 128, 128)
        return remote(
            xs.at[number, rows], out_ref.at[x, pl.ds(part * 128, 128)], 12 + number * 2 + part, TO_X
        )

    def ox(place, part):
        cross_rows(out_o, 0, part).start()

    def gx(place, part):
        cross_rows(gin_o, 1, part).start()

    jobs = (ffn_x, ffn_z, ffn_own, ffn_last, sum_0, rel, sum_3, sum_4, fw, sum_7, wl, wr, xs_, zs, xo, ox, gx, wd_)

    def slot(name, here=None):
        for place, names in PLAN.get(name, {}).items():
            @pl.when(z == place if here is None else (z == place) & here)
            def _(place=place, names=names):
                for job, *rest in names:
                    jobs[job](place, *rest)

    for part in range(6):
        lanes = pl.ds(part * D, D)
        adaw[part].wait()
        mod2[:, lanes] = dot(cond[...], fit[part * 128 : (part + 1) * 128, :D]) + adab[:, part * D : (part + 1) * D]
    modrow = mod2[pl.ds(x, 1), :]
    shift_one, scale_one, gate_one, shift_two, scale_two, gate_two = [
        modrow[:, part * D : (part + 1) * D] for part in range(6)
    ]

    def layer_norm(values):
        center = values - jnp.mean(values, axis=-1, keepdims=True)
        inv = lax.rsqrt(jnp.mean(center * center, axis=-1, keepdims=True) + 1e-05)
        return center * inv, inv

    TILE = 64
    mul_one = again * (1.0 + scale_one)
    mul_two = fgain * (1.0 + scale_two)

    def norm_one_block(block):
        @pl.loop(0, 256 // TILE)
        def _(i):
            at = block * 256 + i * TILE
            rows = rows_of(at, TILE)
            normed, inv = layer_norm(xb[rows].astype(F32))
            n1[rows] = normed
            i1[rows] = inv
            ai[rows_of(own + at, TILE)] = (normed * mul_one + shift_one).astype(BF)

    def core_rows(ref, start, size, index):
        part = ref.at[rows_of(start, size)]
        return remote(part, part, index, TO_CORE)

    for item in loads[1:14]:
        item.wait()

    def project_rows(start):
        rows = rows_of(start, 256)
        tile = ai[rows]
        cos_t, sin_t = cos_v[rows], sin_v[rows]

        @pl.loop(0, 3)
        def _(p):
            projected = dot(tile, wq[p])
            query = projected[:, :128]
            key = projected[:, 128:256]
            value = projected[:, 256:].astype(BF)
            query = (query * cos_t + swap_halves(query) * sin_t).astype(BF)
            key = (key * cos_t + swap_halves(key) * sin_t).astype(BF)
            q_s[p, rows] = query * jnp.asarray(0.125, BF)
            k_s[p, rows] = key
            v_s[p, rows] = value
            kt_s[p, :, rows] = key.T
            vt_s[p, :, rows] = value.T

        ait[:, rows] = tile.T

    loads[0].wait()
    norm_one_block(x)
    core_rows(ai, own + x * 256, 256, 2).start()
    project_rows(own + x * 256)
    core_rows(ai, other + x * 256, 256, 2).wait_recv()
    project_rows(other + x * 256)
    slot((AT_W, 5))
    swap_x.wait_recv()
    norm_one_block(1 - x)
    core_rows(ai, own + (1 - x) * 256, 256, 3).start()
    project_rows(own + (1 - x) * 256)
    core_rows(ai, other + (1 - x) * 256, 256, 3).wait_recv()
    project_rows(other + (1 - x) * 256)
    for item in loads[15:17]:
        item.wait()
    slot((AT_W, 0))

    att_s = a_s.at[pl.ds(0, 512)]
    low_lane = lax.broadcasted_iota(jnp.int32, (1, 128), 1) < 64
    keep = [low_lane.astype(F32).astype(BF), (~low_lane).astype(F32).astype(BF)]

    def att_copy(p, start):
        return remote(
            att_s.at[:, pl.ds(p * 128, 128)],
            att.at[:, pl.ds(pl.multiple_of(c * 384 + p * 128, 128), 128)],
            4 + p,
            TO_CORE,
        )

    def attend(p):
        @pl.loop(0, 2)
        def _(t):
            cols = rows_of(t * 512, 512)
            query = q_s[p, cols]
            outs = []
            for h in range(2):
                masked = query * keep[h]
                held = (oacc, gacc)[h]
                top = None
                for i in range(4):
                    keys = pl.ds(i * 256, 256)
                    scores = dot_t(k_s[p, keys], masked)
                    held[keys, :512] = scores
                    top = scores if top is None else jnp.maximum(top, scores)
                top = jnp.max(top, axis=0, keepdims=True)
                out, total = None, None
                for i in range(4):
                    keys = pl.ds(i * 256, 256)
                    expd = jnp.exp(held[keys, :512] - top)
                    part = dot(vt_s[p, pl.ds(h * 64, 64), keys], expd.astype(BF))
                    out = part if out is None else out + part
                    total = expd if total is None else total + expd
                total = jnp.sum(total, axis=0, keepdims=True)
                lse[p, pl.ds(h, 1), cols] = top + jnp.log(total)
                out = out / total
                ot_s[p, pl.ds(h * 64, 64), cols] = out
                outs.append(out)
            natural = jnp.concatenate(outs, axis=0).T.astype(BF)
            lanes = pl.ds(pl.multiple_of(c * 384 + p * 128, 128), 128)

            @pl.when(t == c)
            def _():
                att[:, lanes] = natural

            @pl.when(t != c)
            def _():
                att_s[:, pl.ds(p * 128, 128)] = natural

            for n in range(2):
                slot((AT_A, p, n), t == n)

        att_copy(p, True).start()

    attend(0)
    attend(1)

    loads[17].wait()
    swap_c.wait_recv()

    @pl.loop(0, 512 // TILE)
    def _(i):
        at = i * TILE
        gf[rows_of(own + at, TILE)] = (gate_two * ctb[rows_of(at, TILE)].astype(F32)).astype(BF)

    core_rows(gf, own, 512, 7).start()
    attend(2)
    vec[...] = jnp.zeros_like(vec)

    @pl.loop(0, 512 // TILE)
    def _(i):
        vec[8:9] += jnp.sum(gf[rows_of(own + i * TILE, TILE)].astype(F32), axis=0, keepdims=True)

    for p in range(3):
        remote(
            att_s.at[:, pl.ds(p * 128, 128)],
            att.at[:, pl.ds(pl.multiple_of((1 - c) * 384 + p * 128, 128), 128)],
            4 + p,
            TO_CORE,
        ).wait_recv()
    loads[14].wait()

    core_rows(ai, own + x * 256, 256, 2).wait_send()
    core_rows(ai, own + (1 - x) * 256, 256, 3).wait_send()
    fi = ai

    @pl.loop(0, 2)
    def _(b):
        rows = rows_of(b * 256, 256)
        ap[rows] = dot(att[rows], wo[...])
        slot((AT_W, 3), b == 0)
        slot((AT_W, 4), b == 1)

        @pl.loop(0, 256 // TILE)
        def _(i):
            at = b * 256 + i * TILE
            tile = rows_of(at, TILE)
            middle = xb[tile].astype(F32) + gate_one * ap[tile]
            normed, inv = layer_norm(middle)
            n2[tile] = normed
            i2[tile] = inv
            fi[rows_of(own + at, TILE)] = (normed * mul_two + shift_two).astype(BF)

    core_rows(fi, own, 512, 8).start()
    slot((AT_W, 1))

    def turn(src, dst, start):
        @pl.loop(0, 2)
        def _(t):
            rows = rows_of(start + t * 256, 256)
            dst[:, rows] = src[rows].T

    turn(gf, gft, own)
    core_rows(gf, other, 512, 7).wait_recv()
    turn(gf, gft, other)
    turn(fi, fit, own)
    core_rows(fi, other, 512, 8).wait_recv()
    turn(fi, fit, other)
    slot((AT_W, 2))

    for p in range(3):
        att_copy(p, False).wait_send()

    coef = 0.7978845608028654

    @pl.loop(0, Z)
    def _(k):
        j = pick([order(n) for n in range(Z)], k)

        for n in range(Z):
            slot((AT_F, n), k == n)

        @pl.when(k != OWN_STEP)
        def _():
            for item in across_waits(j):
                item.wait_recv()

        bias = ub[j][:, pl.ds(0, 384)]
        bias = jnp.where(c == 0, bias, ub[j][:, pl.ds(384, 384)])

        @pl.loop(0, 2)
        def _(t):
            rows = rows_of(t * 512, 512)
            pre = dot(fi[rows], wu[j]) + bias
            sq = pre * pre
            upper = 0.5 + 0.5 * jnp.tanh(pre * (coef + (coef * 0.044715) * sq))
            act = (pre * upper).astype(BF)
            slope = upper + pre * (2.0 * upper * (1.0 - upper)) * (coef + (3.0 * 0.044715 * coef) * sq)
            a_s[rows] = act
            grad_pre = (dot_t(gf[rows], wd[j]) * slope).astype(BF)
            gp_s[rows] = grad_pre
            bsum = jnp.sum(grad_pre.astype(F32), axis=0, keepdims=True)
            out = dot(act, wd[j])
            gin = dot_t(grad_pre, wu[j])

            @pl.when(k == 0)
            def _():
                oacc[rows] = out
                gacc[rows] = gin

            @pl.when(k > 0)
            def _():
                oacc[rows] += out
                gacc[rows] += gin

            for m in range(Z):
                for n in range(2):
                    slot((AT_T, m, n), (k == m) & (t == n))

            @pl.when(t == 0)
            def _():
                ubg[j] = bsum

            @pl.when(t > 0)
            def _():
                ubg[j] += bsum

        g_s[0, j] = dot(fit[...], gp_s[...]).astype(BF)
        g_s[1, j] = dot(gft[...], a_s[...]).astype(BF)

        for n in range(Z):
            slot((AT_G, n), k == n)

    def give_credit():
        @pl.when(z > 0)
        def _():
            pl.semaphore_signal(credit.at[0], 1, device_id=LEFT, device_id_type=MESH)

        @pl.when(z < Z - 1)
        def _():
            pl.semaphore_signal(credit.at[1], 1, device_id=RIGHT, device_id_type=MESH)

    def take_credit():
        @pl.when(z < Z - 1)
        def _():
            pl.semaphore_wait(credit.at[0], 1)

        @pl.when(z > 0)
        def _():
            pl.semaphore_wait(credit.at[1], 1)


    def weight_waits(k):
        @pl.when(z - k >= 0)
        def _():
            @pl.when(z < Z - 1)
            def _():
                for item in z_copies(z - k, 0, RIGHT, False):
                    item.wait_send()

            for item in quarter_sends(z - k) + across_sends(z - k):
                item.wait_send()

        @pl.when(z + k <= Z - 1)
        def _():
            @pl.when(z > 0)
            def _():
                for item in z_copies(z + k, 1, LEFT, False):
                    item.wait_send()

            for item in quarter_sends(z + k) + across_sends(z + k):
                item.wait_send()

    @pl.when(z < Z - 1)
    def _():
        for item in z_copies(z, 0, RIGHT, False):
            item.wait_send()

    @pl.when(z > 0)
    def _():
        for item in z_copies(z, 1, LEFT, False):
            item.wait_send()

    pl.loop(1, Z)(weight_waits)
    give_credit()

    osend, gsend = xs.at[0], xs.at[1]

    @pl.loop(0, 512 // TILE)
    def _(i):
        tile = rows_of(i * TILE, TILE)
        far = rows_of(other + i * TILE, TILE)
        gsend[tile] = gacc[far].astype(BF)

    remote(gsend, grecv, 9, TO_CORE).start()

    @pl.loop(0, 512 // TILE)
    def _(i):
        osend[rows_of(i * TILE, TILE)] = oacc[rows_of(other + i * TILE, TILE)].astype(BF)

    orecv = att
    remote(osend, orecv, 10, TO_CORE).start()
    remote(gsend, grecv, 9, TO_CORE).wait_recv()
    core_rows(gf, own, 512, 7).wait_send()

    def norm_back(grad, normed, inv):
        return inv * (
            grad
            - jnp.mean(grad, axis=-1, keepdims=True)
            - normed * jnp.mean(grad * normed, axis=-1, keepdims=True)
        )

    @pl.loop(0, 512 // TILE)
    def _(i):
        tile = rows_of(i * TILE, TILE)
        near = rows_of(own + i * TILE, TILE)
        grad = gacc[near] + grecv[tile].astype(F32)
        normed = n2[tile]
        vec[3:4] += jnp.sum(grad, axis=0, keepdims=True)
        vec[4:5] += jnp.sum(grad * normed, axis=0, keepdims=True)
        middle = ctb[tile].astype(F32) + norm_back(grad * mul_two, normed, i2[tile])
        n2[tile] = middle
        gf[near] = (gate_one * middle).astype(BF)
        vec[2:3] += jnp.sum(middle * ap[tile], axis=0, keepdims=True)

    gproj = gf
    core_rows(gproj, own, 512, 11).start()
    slot((AT_N, 1))

    remote(osend, orecv, 10, TO_CORE).wait()

    def rows_out(number, i, values):
        xs[number, rows_of(i * TILE, TILE)] = values.astype(BF)

    def out_copy(out_ref, number):
        return local(xs.at[number, rows_of(x * 256, 256)], out_ref.at[x], 55 + number)

    @pl.loop(0, 512 // TILE)
    def _(i):
        tile = rows_of(i * TILE, TILE)
        ffn = oacc[rows_of(own + i * TILE, TILE)] + orecv[tile].astype(F32) + downb
        vec[5:6] += jnp.sum(ctb[tile].astype(F32) * ffn, axis=0, keepdims=True)
        rows_out(0, i, xb[tile].astype(F32) + gate_one * ap[tile] + gate_two * ffn)

    out_copy(out_o, 0).start()

    core_rows(gproj, other, 512, 11).wait_recv()
    slot((AT_N, 2))

    @pl.loop(0, 4)
    def _(t):
        rows = rows_of(t * 256, 256)
        grad = dot_t(gproj[rows], wo[rows_of(c * 384, 384)])
        for p in range(3):
            part = grad[:, p * 128 : (p + 1) * 128].astype(BF)
            do_s[p, rows] = part
            product = part.astype(F32).T * ot_s[p, :, rows]
            for h in range(2):
                dlt[p, pl.ds(h, 1), rows] = jnp.sum(
                    product[h * 64 : (h + 1) * 64], axis=0, keepdims=True
                )

    slot((AT_N, 3))

    for p in range(3):
        @pl.loop(0, 2)
        def _(n):
            lanes = pl.ds(pl.multiple_of(n * 384, 128), 384)
            b_s[0, rows_of(n * 384 + p * 128, 128)] = dot(
                ot_s[p].astype(BF), gproj[:, lanes]
            ).astype(BF)

    take_credit()
    slot((AT_N, 4))

    def attend_back(p):
        for h in range(2):
            a_s[:, h * 128 : (h + 1) * 128] = q_s[p] * keep[h]
            gp_s[:, h * 128 : (h + 1) * 128] = do_s[p] * keep[h]
        dqt[...] = jnp.zeros_like(dqt)

        @pl.loop(0, 2)
        def _(t):
            rows = rows_of(t * 512, 512)
            keys, values = k_s[p, rows], v_s[p, rows]
            dv, dk = None, None
            for h in range(2):
                qm, dom = a_s[:, h * 128 : (h + 1) * 128], gp_s[:, h * 128 : (h + 1) * 128]
                probs = jnp.exp(dot_t(keys, qm) - lse[p, pl.ds(h, 1), :])
                grads = dot_t(values, dom)
                ds = (probs * (grads - dlt[p, pl.ds(h, 1), :])).astype(BF)
                dv_h = dot(probs.astype(BF), dom)
                dk_h = dot(ds, qm)
                dv = dv_h if dv is None else dv + dv_h
                dk = dk_h if dk is None else dk + dk_h
                dqt[pl.ds(h * 64, 64)] += dot(kt_s[p, pl.ds(h * 64, 64), rows], ds)
            cos_t, sin_t = cos_v[rows], sin_v[rows]
            gq[p, rows, pl.ds(128, 128)] = (dk * cos_t - swap_halves(dk) * sin_t).astype(BF)
            gq[p, rows, pl.ds(256, 128)] = dv.astype(BF)

            for n in range(2):
                slot((AT_B, p, n), t == n)

        @pl.loop(0, 4)
        def _(t):
            rows = rows_of(t * 256, 256)
            block = dqt[:, rows] * 0.125
            cos_t, sin_t = cost[:, rows], sint[:, rows]
            parts = []
            for h in range(2):
                u, w = block[h * 64 : h * 64 + 32], block[h * 64 + 32 : h * 64 + 64]
                parts += [u * cos_t + w * sin_t, w * cos_t - u * sin_t]
            gq[p, rows, pl.ds(0, 128)] = jnp.concatenate(parts, axis=0).T.astype(BF)

        b_s[1 + p] = dot(ait[...], gq[p]).astype(BF)
        slot((AT_B, p, 5))

    remote(gsend, grecv, 9, TO_CORE).wait_send()
    for p in range(3):
        attend_back(p)

    @pl.loop(0, 4)
    def _(t):
        rows = rows_of(t * 256, 256)
        part = dot_t(gq[0, rows], wq[0])
        for p in range(1, 3):
            part = part + dot_t(gq[p, rows], wq[p])
        gacc[rows] = part
        for n in range(4):
            slot((AT_B, 3, n), t == n)

    @pl.loop(0, 512 // TILE)
    def _(i):
        gsend[rows_of(i * TILE, TILE)] = gacc[rows_of(other + i * TILE, TILE)].astype(BF)

    remote(gsend, grecv, 11 + 26, TO_CORE).start()
    slot((AT_E, 0))
    remote(gsend, grecv, 11 + 26, TO_CORE).wait()

    @pl.loop(0, 512 // TILE)
    def _(i):
        tile = rows_of(i * TILE, TILE)
        near = rows_of(own + i * TILE, TILE)
        grad = gacc[near] + grecv[tile].astype(F32)
        normed = n1[tile]
        vec[0:1] += jnp.sum(grad, axis=0, keepdims=True)
        vec[1:2] += jnp.sum(grad * normed, axis=0, keepdims=True)
        rows_out(1, i, n2[tile] + norm_back(grad * mul_one, normed, i1[tile]))

    out_copy(gin_o, 1).start()
    slot((AT_E, 1))
    sums = vec[...]
    vec[6:7] = sums[1:2] * (1.0 + scale_one)
    vec[7:8] = sums[4:5] * (1.0 + scale_two)
    vec[1:2] = sums[1:2] * again
    vec[4:5] = sums[4:5] * fgain
    for core in range(2):
        @pl.when(c == core)
        def _():
            for j in range(4):
                vec[9 + 2 * core + j // 2, pl.ds((j % 2) * 384, 384)] = ubg[j, 0]

    both = cond[...].astype(F32)
    vec[13:14, :128] = 0.5 * jnp.where(x == 0, both[0:1], both[1:2])
    remote(vec, vecr, 30, TO_CORE).start()
    slot((AT_E, 2))
    remote(vec, vecr, 30, TO_CORE).wait_recv()
    chip = 2 * z + x
    vall[chip] = vec[...] + vecr[...]

    def vec_copy(n, slot):
        return pltpu.make_async_remote_copy(
            src_ref=vall.at[slot], dst_ref=vall.at[slot], send_sem=vss.at[n], recv_sem=vrs.at[n],
            device_id=peers[n], device_id_type=MESH,
        )

    for n in range(len(peers)):
        vec_copy(n, chip).start()
    slot((AT_D, 0))
    for n in range(len(peers)):
        vec_copy(n, 2 * peers[n]["mlp"] + peers[n]["seq"] // 2).wait_recv()

    vall_out = local(vall, vall_o, 57)
    vall_out.start()
    vall_out.wait()

    for number, ref in ((0, out_o), (1, gin_o)):
        out_copy(ref, number).wait()
        for part in range(2):
            cross_rows(ref, number, part).wait()
    for p in range(4):
        for item in piece_copies(p):
            item.wait()
    for h in range(CH):
        for item in final_copies(g_s.at[x, z, span(h)], x, h, 0) + final_copies(fxr.at[span(h)], 1 - x, h, 1):
            item.wait()
        own_copy(h).wait_send()
    for n in range(len(peers)):
        vec_copy(n, chip).wait_send()
    swap_x.wait_send()
    swap_c.wait_send()
    core_rows(fi, own, 512, 8).wait_send()
    core_rows(gproj, own, 512, 11).wait_send()
    remote(vec, vecr, 30, TO_CORE).wait_send()
    for place in range(Z):
        @pl.when(z == place)
        def _(place=place):
            for make in pending[place]:
                make().wait_send()


def finish_kernel(
    out_h, gin_h, qkv_h, outw_h, ffn_h, vall_h, adaw_h,
    out_o, gin_o, cond_o, again_o, adaw_o, adab_o, qkv_o, outw_o, fgain_o, up_o, upb_o, down_o, downb_o,
    tok_b, qkv_b, outw_b, ffn_b, adaw, vall, tok_f, qkv_f, outw_f, ffn_f, adaw_f, cond_s, isem, osem,
):
    z = lax.axis_index("mlp")
    D = 768
    loads, steps = [], []

    def step(src, buffer, result, dst, turn=False):
        number = len(steps)
        loads.append(pltpu.make_async_copy(src, buffer, isem.at[number]))
        store = pltpu.make_async_copy(result, dst, osem.at[number])

        def body():
            loads[number].wait()
            values = buffer[...].astype(F32)
            result[...] = values.T if turn else values
            store.start()

        steps.append((body, store))

    vall_copy = pltpu.make_async_copy(vall_h, vall, isem.at[30])
    adaw_copy = pltpu.make_async_copy(adaw_h, adaw, isem.at[31])
    for n in range(6):
        rows = pl.ds(n * 128, 128)
        step(qkv_h.at[rows], qkv_b.at[rows], qkv_f.at[rows], qkv_o.at[rows])
    for n in range(2):
        rows = pl.ds(n * 384, 384)
        step(outw_h.at[rows], outw_b.at[rows], outw_f.at[rows], outw_o.at[rows])
        step(ffn_h.at[0, rows], ffn_b.at[0, rows], ffn_f.at[0, rows], up_o.at[rows])
    for n in range(3):
        rows = pl.ds(n * 256, 256)
        step(ffn_h.at[1, rows], ffn_b.at[1, rows], ffn_f.at[1, :, rows], down_o.at[:, rows], True)
    for n in range(2):
        step(out_h.at[n], tok_b.at[0, n], tok_f.at[0, n], out_o.at[n])
        step(gin_h.at[n], tok_b.at[1, n], tok_f.at[1, n], gin_o.at[n])
    for item in loads[:6] + [vall_copy, adaw_copy] + loads[6:]:
        item.start()
    for body, _ in steps[:6]:
        body()
    vall_copy.wait()
    adaw_copy.wait()
    high = lax.Precision.HIGHEST
    everyone = vall[:, 13, :128]
    total = vall[0]
    for n in range(1, 8):
        total = total + vall[n]
    acc, ada_out = None, []
    for part in range(6):
        lanes = pl.ds(part * D, D)
        grads = vall[:, part, :]
        adab_o[lanes] = total[part]
        adaw_f[part] = lax.dot_general(
            everyone, grads, (((0,), (0,)), ((), ())), precision=high, preferred_element_type=F32
        )
        ada_out.append(pltpu.make_async_copy(adaw_f.at[part], adaw_o.at[:, lanes], osem.at[26 + part]))
        ada_out[-1].start()
        piece = lax.dot_general(
            grads, adaw[:, lanes].astype(F32), (((1,), (1,)), ((), ())), precision=high,
            preferred_element_type=F32,
        )
        acc = piece if acc is None else acc + piece
    for body, _ in steps[6:]:
        body()
    cond_s[...] = acc
    cond_o[...] = cond_s[pl.ds(2 * z, 2), :]
    again_o[...] = total[6]
    fgain_o[...] = total[7]
    downb_o[...] = total[8]
    for core in range(2):
        halves = [total[9 + 2 * core + j // 2, (j % 2) * 384 : (j % 2 + 1) * 384] for j in range(4)]
        mine = halves[0]
        for j in range(1, 4):
            mine = jnp.where(z == j, halves[j], mine)
        upb_o[pl.ds(core * 384, 384)] = mine
    for item in ada_out:
        item.wait()
    for _, store in steps:
        store.wait()


def tables(seg_len, seq_size):
    half = np.arange(32)
    frequency = 10000.0 ** (-2.0 * half / 64)
    core, chip, token = np.meshgrid(
        np.arange(2), np.arange(seq_size // 2), np.arange(seg_len), indexing="ij"
    )
    place = ((chip * 2 + core) * seg_len + token).reshape(-1)
    angle = place[:, None] * frequency[None, :]
    cos, sin = np.cos(angle).astype(np.float32), np.sin(angle).astype(np.float32)
    return (
        np.tile(cos, (1, 4)),
        np.concatenate([-sin, sin, -sin, sin], axis=1),
        np.ascontiguousarray(cos.T),
        np.ascontiguousarray(sin.T),
    )


def fast_shards(
    inputs, condition, attn_gain, ada_weight, ada_bias, qkv_weight, out_weight, ffn_gain,
    up_weight, up_bias, down_weight, down_bias, cotangent,
):
    Z = lax.axis_size("mlp")
    tabs = [jnp.asarray(t) for t in tables(inputs.shape[1], lax.axis_size("seq"))]
    hbm, vm = pl.BlockSpec(memory_space=pl.ANY), pl.BlockSpec(memory_space=pltpu.VMEM)
    shape = jax.ShapeDtypeStruct
    V = pltpu.VMEM
    dma = pltpu.SemaphoreType.DMA
    scratch = [
        V((3, 768, 384), BF), V((768, 768), BF), V((Z, 768, 384), BF),
        V((Z, 384, 768), BF), V((Z, 1, 768), F32), V((1024, 128), F32), V((1024, 128), F32),
        V((32, 1024), F32), V((32, 1024), F32),
        V((512, 768), BF), V((512, 768), BF), V((2, 4608), F32), V((512, 768), F32), V((512, 1), F32),
        V((1024, 768), BF), V((768, 1024), BF),
        V((3, 1024, 128), BF), V((3, 1024, 128), BF), V((3, 1024, 128), BF),
        V((3, 128, 1024), BF), V((3, 128, 1024), BF), V((3, 128, 1024), F32), V((3, 2, 1024), F32),
        V((512, 768), BF),
        V((512, 768), F32), V((512, 768), F32), V((512, 1), F32),
        V((768, 1024), BF), V((1024, 768), BF), V((768, 1024), BF),
        V((1024, 768), F32), V((1024, 768), F32), V((1024, 384), BF), V((1024, 384), BF),
        V((2, Z, 768, 384), BF), V((512, 768), BF),
        V((3, 1024, 128), BF), V((3, 2, 1024), F32), V((128, 1024), F32),
        V((3, 1024, 384), BF), V((4, 768, 384), BF), V((2, 512, 768), BF),
        V((16, 768), F32), V((16, 768), F32), V((2 * Z, 16, 768), F32), V((Z, 1, 384), F32),
        V((Z, 768, 384), BF), V((Z, 768, 384), BF), V((768, 384), BF), V((4, 192, 384), BF),
        V((4, 768, 384), BF),
        dma((64,)), dma((38,)), dma((38,)), dma((2, Z, 3)), dma((2, Z, 3)), dma((Z, 4, 2)), dma((Z, 4, 2)),
        dma((Z, 3)), dma((Z, 3)), dma((4, 4, 4)), dma((4, 4, 4)), dma((6, 4)), dma((6, 4)), dma((7,)), dma((7,)),
        pltpu.SemaphoreType.REGULAR((2,)),
    ]
    token = shape(inputs.shape, BF)
    vall_shape = shape((2 * Z, 16, 768), F32)
    ffn_shape = shape((2, 768, 768), BF)
    out, gin, qkv, outw, ffn, vall = pl.pallas_call(
        fast_kernel,
        out_shape=[
            token, token, shape(qkv_weight.shape, BF), shape(out_weight.shape, BF), ffn_shape, vall_shape,
        ],
        in_specs=[hbm, vm, vm, hbm, vm, hbm, hbm, vm, hbm, vm, hbm, vm, hbm, hbm, hbm, hbm, hbm],
        out_specs=[hbm] * 6,
        scratch_shapes=scratch,
        compiler_params=pltpu.CompilerParams(
            collective_id=0, has_side_effects=True, vmem_limit_bytes=VMEM_LIMIT
        ),
        name="block",
    )(
        inputs, condition, attn_gain, ada_weight, ada_bias, qkv_weight, out_weight,
        ffn_gain, up_weight, up_bias, down_weight, down_bias, cotangent, *tabs,
    )
    same = lambda v: shape(v.shape, F32)
    tokens = shape(inputs.shape, F32)
    return pl.pallas_call(
        finish_kernel,
        out_shape=[
            tokens, tokens, same(condition), same(attn_gain), same(ada_weight), same(ada_bias),
            same(qkv_weight), same(out_weight), same(ffn_gain), same(up_weight), same(up_bias),
            same(down_weight), same(down_bias),
        ],
        in_specs=[hbm] * 7,
        out_specs=[hbm, hbm, vm, vm, hbm, vm, hbm, hbm, vm, hbm, vm, hbm, vm],
        scratch_shapes=[
            V((2, *inputs.shape), BF), V(qkv_weight.shape, BF), V(out_weight.shape, BF), V((2, 768, 768), BF),
            V(ada_weight.shape, BF), V((2 * Z, 16, 768), F32), V((2, *inputs.shape), F32),
            V(qkv_weight.shape, F32), V(out_weight.shape, F32), V((2, 768, 768), F32), V((6, 128, 768), F32),
            V((2 * Z, 128), F32), dma((32,)), dma((32,)),
        ],
        compiler_params=pltpu.CompilerParams(vmem_limit_bytes=VMEM_LIMIT),
        name="finish",
    )(out, gin, qkv, outw, ffn, vall, ada_weight)


def solution(mesh):
    placed = (
        P(("grp", "mlp"), "seq", None),
        P(("grp", "mlp"), None),
        P(),
        P(),
        P(),
        P(),
        P(),
        P(),
        P(None, "mlp"),
        P("mlp"),
        P("mlp", None),
        P(),
        P(("grp", "mlp"), "seq", None),
    )
    sizes = dict(mesh.shape)
    small = sizes["seq"] == 4 and sizes["grp"] == 2 and sizes["mlp"] == 4
    return jax.shard_map(
        fast_shards if small else shards,
        mesh=mesh,
        in_specs=placed,
        out_specs=(
            P(("grp", "mlp"), "seq", None),
            P(("grp", "mlp"), "seq", None),
            P(("grp", "mlp"), None),
            P("grp"),
            P("grp", None),
            P("grp"),
            P("grp", None),
            P("grp", None),
            P("grp"),
            P("grp", "mlp"),
            P(("grp", "mlp")),
            P(("grp", "mlp"), None),
            P("grp"),
        ),
        check_vma=False,
    )
```

```python
import math

import jax
import jax.numpy as jnp
import numpy as np
from jax import lax
from jax.experimental import pallas as pl
from jax.experimental.pallas import tpu as pltpu
from jax.sharding import PartitionSpec as P

HEADS = 12
VMEM_LIMIT = 127 * 2**19


gelu_coef = 0.7978845608028654


def layer_norm(values):
    center = values - jnp.mean(values, axis=-1, keepdims=True)
    inv_std = lax.rsqrt(jnp.mean(center * center, axis=-1, keepdims=True) + 1e-05)
    return (center * inv_std, inv_std)


def norm_back(grad_norm, normed, inv_std):
    return inv_std * (
        grad_norm
        - jnp.mean(grad_norm, axis=-1, keepdims=True)
        - normed * jnp.mean(grad_norm * normed, axis=-1, keepdims=True)
    )


def gelu_tanh(values):
    return (
        0.5 * values * (1.0 + jnp.tanh(gelu_coef * (values + 0.044715 * values * values * values)))
    )


def gelu_slope(values):
    tanh_val = jnp.tanh(gelu_coef * (values + 0.044715 * values * values * values))
    return 0.5 * (1.0 + tanh_val) + 0.5 * values * (1.0 - tanh_val * tanh_val) * gelu_coef * (
        1.0 + 3.0 * 0.044715 * values * values
    )


def rotary_tables(positions, head_size):
    half_dim = head_size // 2
    frequencies = jnp.power(10000.0, -2.0 * jnp.arange(half_dim, dtype=jnp.float32) / head_size)
    angles = positions[:, None] * frequencies[None, :]
    return (jnp.cos(angles), jnp.sin(angles))


def rotate(tensor, cos_tab, sine_tab):
    half_dim = tensor.shape[-1] // 2
    first_half = tensor[..., :half_dim]
    second_half = tensor[..., half_dim:]
    return jnp.concatenate(
        [
            first_half * cos_tab - second_half * sine_tab,
            second_half * cos_tab + first_half * sine_tab,
        ],
        axis=-1,
    )


def unrotate(tensor, cos_tab, sine_tab):
    half_dim = tensor.shape[-1] // 2
    first_half = tensor[..., :half_dim]
    second_half = tensor[..., half_dim:]
    return jnp.concatenate(
        [
            first_half * cos_tab + second_half * sine_tab,
            second_half * cos_tab - first_half * sine_tab,
        ],
        axis=-1,
    )


def score_of(query_rows, key_rows, scale_factor):
    return (
        jnp.einsum("sghd,skhd->shgk", query_rows, key_rows, preferred_element_type=jnp.float32)
        * scale_factor
    )


def score_grads(query_rows, dout_rows, lse_rows, delta_rows, key_rows, value_rows, scale_factor):
    prob_rows = jnp.exp(score_of(query_rows, key_rows, scale_factor) - lse_rows[..., None])
    grad_probs = jnp.einsum(
        "sghd,skhd->shgk", dout_rows, value_rows, preferred_element_type=jnp.float32
    )
    grad_scores = (prob_rows * (grad_probs - delta_rows[..., None])).astype(jnp.bfloat16)
    return (prob_rows.astype(jnp.bfloat16), grad_scores)


def shards(
    inputs,
    condition,
    attn_gain,
    ada_weight,
    ada_bias,
    qkv_weight,
    out_weight,
    ffn_gain,
    up_weight,
    up_bias,
    down_weight,
    down_bias,
    cotangent,
):
    seq_count, seg_len, model_width = inputs.shape
    head_count = HEADS
    head_size = model_width // head_count
    full_len = seg_len * lax.axis_size("seq")
    block_len = math.gcd(full_len, 512)
    block_count = full_len // block_len
    scale_factor = float(head_size) ** (-0.5)
    positions = (lax.axis_index("seq") * seg_len + jnp.arange(seg_len, dtype=jnp.int32)).astype(
        jnp.float32
    )
    cos_tab, sine_tab = rotary_tables(positions, head_size)
    cos_tab = cos_tab[None, :, None, :]
    sine_tab = sine_tab[None, :, None, :]

    def heads_view(matrix):
        return matrix.reshape(seq_count, seg_len, head_count, head_size)

    x_float = inputs.astype(jnp.float32)
    modulate = jnp.dot(condition, ada_weight, preferred_element_type=jnp.float32) + ada_bias
    shift_one, scale_one, gate_one, shift_two, scale_two, gate_two = [
        modulate[:, None, member * model_width : (member + 1) * model_width] for member in range(6)
    ]
    norm_one, inv_one = layer_norm(x_float)
    attn_in = (norm_one * attn_gain * (1.0 + scale_one) + shift_one).astype(jnp.bfloat16)
    projected = jnp.dot(attn_in, qkv_weight, preferred_element_type=jnp.float32)
    queries = rotate(heads_view(projected[..., :model_width]), cos_tab, sine_tab).astype(
        jnp.bfloat16
    )
    key_rot = rotate(
        heads_view(projected[..., model_width : 2 * model_width]), cos_tab, sine_tab
    ).astype(jnp.bfloat16)
    value_low = projected[..., 2 * model_width :].astype(jnp.bfloat16)
    kv_local = jnp.concatenate(
        [key_rot.reshape(seq_count, seg_len, model_width), value_low], axis=-1
    )
    kv_whole = lax.all_gather(kv_local, "seq", axis=1, tiled=True)
    kv_view = kv_whole.reshape(seq_count, full_len, 2, head_count, head_size)

    def key_block(block_num):
        sliced = lax.dynamic_slice_in_dim(kv_view, block_num * block_len, block_len, 1)
        return (sliced[:, :, 0], sliced[:, :, 1])

    def max_pass(block_num, running):
        run_max, run_sum = running
        key_rows, value_rows = key_block(block_num)
        scores = score_of(queries, key_rows, scale_factor)
        new_max = jnp.maximum(run_max, jnp.max(scores, axis=-1))
        run_sum = run_sum * jnp.exp(run_max - new_max) + jnp.sum(
            jnp.exp(scores - new_max[..., None]), axis=-1
        )
        return (new_max, run_sum)

    stat_shape = (seq_count, head_count, seg_len)
    run_max, run_sum = lax.fori_loop(
        0,
        block_count,
        max_pass,
        (jnp.full(stat_shape, -1e30, jnp.float32), jnp.zeros(stat_shape, jnp.float32)),
    )
    log_sum = run_max + jnp.log(run_sum)

    def out_pass(block_num, accums):
        accum_out, accum_exact = accums
        key_rows, value_rows = key_block(block_num)
        prob_rows = jnp.exp(score_of(queries, key_rows, scale_factor) - log_sum[..., None])
        accum_out = accum_out + jnp.einsum(
            "shgk,skhd->sghd",
            prob_rows.astype(jnp.bfloat16),
            value_rows,
            preferred_element_type=jnp.float32,
        )
        accum_exact = accum_exact + jnp.einsum(
            "shgk,skhd->sghd",
            prob_rows,
            value_rows.astype(jnp.float32),
            preferred_element_type=jnp.float32,
        )
        return (accum_out, accum_exact)

    head_shape = (seq_count, seg_len, head_count, head_size)
    attn_float, attn_exact = lax.fori_loop(
        0,
        block_count,
        out_pass,
        (jnp.zeros(head_shape, jnp.float32), jnp.zeros(head_shape, jnp.float32)),
    )
    attn_low = attn_float.reshape(seq_count, seg_len, model_width).astype(jnp.bfloat16)
    attn_proj = jnp.dot(attn_low, out_weight, preferred_element_type=jnp.float32)
    middle = x_float + gate_one * attn_proj
    norm_two, inv_two = layer_norm(middle)
    ffn_in = (norm_two * ffn_gain * (1.0 + scale_two) + shift_two).astype(jnp.bfloat16)
    ffn_rows = lax.all_gather(ffn_in, "mlp", axis=0, tiled=True)
    pre_act = jnp.dot(ffn_rows, up_weight, preferred_element_type=jnp.float32) + up_bias
    act_low = gelu_tanh(pre_act).astype(jnp.bfloat16)
    ffn_out = (
        lax.psum_scatter(
            jnp.dot(act_low, down_weight, preferred_element_type=jnp.float32).astype(jnp.bfloat16),
            "mlp",
            scatter_dimension=0,
            tiled=True,
        ).astype(jnp.float32)
        + down_bias
    )
    output = middle + gate_two * ffn_out
    cot_float = cotangent.astype(jnp.float32)
    grad_ffn = (gate_two * cot_float).astype(jnp.bfloat16)
    down_bias_part = jnp.sum(grad_ffn.astype(jnp.float32), axis=(0, 1))
    dgate_two = jnp.sum(cot_float * ffn_out, axis=1)
    grad_ffn_rows = lax.all_gather(grad_ffn, "mlp", axis=0, tiled=True)
    down_part = jnp.einsum(
        "sgf,sgd->fd", act_low, grad_ffn_rows, preferred_element_type=jnp.float32
    )
    grad_act = jnp.einsum(
        "sgd,fd->sgf", grad_ffn_rows, down_weight, preferred_element_type=jnp.float32
    )
    grad_pre = (grad_act * gelu_slope(pre_act)).astype(jnp.bfloat16)
    up_bias_part = jnp.sum(grad_pre.astype(jnp.float32), axis=(0, 1))
    up_part = jnp.einsum("sgd,sgf->df", ffn_rows, grad_pre, preferred_element_type=jnp.float32)
    grad_ffn_in = lax.psum_scatter(
        jnp.einsum("sgf,df->sgd", grad_pre, up_weight, preferred_element_type=jnp.float32).astype(
            jnp.bfloat16
        ),
        "mlp",
        scatter_dimension=0,
        tiled=True,
    ).astype(jnp.float32)
    dshift_two = jnp.sum(grad_ffn_in, axis=1)
    dscale_two = jnp.sum(grad_ffn_in * norm_two * ffn_gain, axis=1)
    gain_two_part = jnp.sum(grad_ffn_in * (1.0 + scale_two) * norm_two, axis=(0, 1))
    grad_middle = cot_float + norm_back(
        grad_ffn_in * (1.0 + scale_two) * ffn_gain, norm_two, inv_two
    )
    grad_proj = (gate_one * grad_middle).astype(jnp.bfloat16)
    dgate_one = jnp.sum(grad_middle * attn_proj, axis=1)
    out_part = jnp.einsum("sgd,sge->de", attn_low, grad_proj, preferred_element_type=jnp.float32)
    grad_attn = jnp.einsum(
        "sge,de->sgd", grad_proj, out_weight, preferred_element_type=jnp.float32
    ).astype(jnp.bfloat16)
    grad_attn_heads = heads_view(grad_attn)
    delta_rows = jnp.sum(grad_attn_heads.astype(jnp.float32) * attn_exact, axis=-1)
    delta_heads = jnp.transpose(delta_rows, (0, 2, 1))

    def back_pass(block_num, state_in):
        grad_query, key_grads = state_in
        key_rows, value_rows = key_block(block_num)
        prob_low, grad_scores = score_grads(
            queries, grad_attn_heads, log_sum, delta_heads, key_rows, value_rows, scale_factor
        )
        grad_query = (
            grad_query
            + jnp.einsum(
                "shgk,skhd->sghd", grad_scores, key_rows, preferred_element_type=jnp.float32
            )
            * scale_factor
        )
        grad_key = (
            jnp.einsum("shgk,sghd->skhd", grad_scores, queries, preferred_element_type=jnp.float32)
            * scale_factor
        )
        grad_value = jnp.einsum(
            "shgk,sghd->skhd", prob_low, grad_attn_heads, preferred_element_type=jnp.float32
        )
        stacked = jnp.concatenate(
            [
                grad_key.reshape(seq_count, block_len, model_width),
                grad_value.reshape(seq_count, block_len, model_width),
            ],
            axis=-1,
        )
        key_grads = lax.dynamic_update_slice_in_dim(key_grads, stacked, block_num * block_len, 1)
        return (grad_query, key_grads)

    grad_query, key_grads = lax.fori_loop(
        0,
        block_count,
        back_pass,
        (
            jnp.zeros(head_shape, jnp.float32),
            jnp.zeros((seq_count, full_len, 2 * model_width), jnp.float32),
        ),
    )
    kv_grads = lax.psum_scatter(
        key_grads.astype(jnp.bfloat16), "seq", scatter_dimension=1, tiled=True
    ).astype(jnp.float32)
    grad_key_rot = heads_view(kv_grads[..., :model_width])
    grad_values = kv_grads[..., model_width:]
    grad_qkv = jnp.concatenate(
        [
            unrotate(grad_query, cos_tab, sine_tab).reshape(seq_count, seg_len, model_width),
            unrotate(grad_key_rot, cos_tab, sine_tab).reshape(seq_count, seg_len, model_width),
            grad_values,
        ],
        axis=-1,
    ).astype(jnp.bfloat16)
    qkv_part = jnp.einsum("sgd,sge->de", attn_in, grad_qkv, preferred_element_type=jnp.float32)
    grad_attn_in = jnp.einsum(
        "sge,de->sgd", grad_qkv, qkv_weight, preferred_element_type=jnp.float32
    )
    dshift_one = jnp.sum(grad_attn_in, axis=1)
    dscale_one = jnp.sum(grad_attn_in * norm_one * attn_gain, axis=1)
    gain_one_part = jnp.sum(grad_attn_in * (1.0 + scale_one) * norm_one, axis=(0, 1))
    grad_inputs = grad_middle + norm_back(
        grad_attn_in * (1.0 + scale_one) * attn_gain, norm_one, inv_one
    )
    grad_modulate = jnp.concatenate(
        [dshift_one, dscale_one, dgate_one, dshift_two, dscale_two, dgate_two], axis=-1
    )
    ada_weight_part = jnp.dot(
        condition.astype(jnp.float32).T, grad_modulate, precision=lax.Precision.HIGHEST
    )
    ada_bias_part = jnp.sum(grad_modulate, axis=0)
    cond_part = jnp.dot(
        grad_modulate, ada_weight.astype(jnp.float32).T, precision=lax.Precision.HIGHEST
    )
    summed_all = lax.psum(
        (
            qkv_part,
            out_part,
            ada_weight_part,
            ada_bias_part,
            gain_one_part,
            gain_two_part,
            down_bias_part,
        ),
        ("seq", "mlp"),
    )
    summed_seq = (
        lax.psum(up_part.astype(jnp.bfloat16), "seq").astype(jnp.float32),
        lax.psum(up_bias_part.astype(jnp.bfloat16), "seq").astype(jnp.float32),
        lax.psum(down_part.astype(jnp.bfloat16), "seq").astype(jnp.float32),
        lax.psum(cond_part.astype(jnp.bfloat16), "seq").astype(jnp.float32),
    )
    return (
        output,
        grad_inputs,
        summed_seq[3],
        summed_all[4],
        summed_all[2],
        summed_all[3],
        summed_all[0],
        summed_all[1],
        summed_all[5],
        summed_seq[0],
        summed_seq[1],
        summed_seq[2],
        summed_all[6],
    )


FFN_X, FFN_Z, FFN_OWN, FFN_LAST, SUM_0, REL, SUM_3, SUM_4, FW, SUM_7, WL, WR, XS_, ZS, XO, OX, GX, WD_, SUM_8, WX = range(20)
AT_W, AT_F, AT_A, AT_T, AT_N, AT_B, AT_E, AT_D, AT_G = range(9)
ORDERS = ((1, 2, 3, 0), (1, 0, 2, 3), (2, 3, 1, 0), (2, 1, 0, 3))
OWN_STEP = 3
PLAN = {(AT_A, 0, 0): {0: [(WR, 2), (WX, 1)], 1: [(WR, 2), (WX, 0)], 2: [(WL, 2), (WX, 1)], 3: [(WL, 2), (WX, 2)]},
 (AT_A, 1, 0): {0: [(WX, 2)], 1: [(WX, 2)], 2: [(WX, 3)], 3: [(WX, 1)]},
 (AT_A, 2, 0): {0: [(WR, 3)], 3: [(WL, 3)]},
 (AT_A, 2, 1): {0: [(WD_, 1)], 1: [(WD_, 0)], 2: [(WD_, 1)], 3: [(WD_, 2)]},
 (AT_B, 0, 0): {0: [(XS_, 1, 2), (FFN_X, 2, 1)],
                1: [(XS_, 3, 2), (FFN_Z, 3, 0), (ZS, 3, 0)],
                2: [(XS_, 1, 0), (FFN_X, 0, 1), (FFN_Z, 0, 1)],
                3: [(XS_, 2, 2), (FFN_X, 1, 1)]},
 (AT_B, 0, 1): {0: [(FFN_X, 2, 2)],
                1: [(XS_, 2, 0), (FFN_X, 3, 1), (FFN_Z, 3, 1)],
                2: [(ZS, 0, 1), (FFN_X, 0, 2), (FFN_Z, 0, 2)],
                3: [(FFN_X, 1, 2)]},
 (AT_B, 0, 5): {0: [(XS_, 0, 0), (SUM_0, 1)],
                1: [(ZS, 3, 1)],
                2: [(XS_, 1, 1), (ZS, 0, 2)],
                3: [(XS_, 3, 0), (SUM_0, 1)]},
 (AT_B, 1, 0): {0: [(XS_, 0, 1), (FFN_X, 1, 2)],
                1: [(XS_, 2, 1), (FFN_X, 3, 2), (FFN_Z, 3, 2), (ZS, 3, 2)],
                2: [(XS_, 1, 2), (FFN_X, 1, 0), (REL, 1, 0, 0), (FFN_Z, 1, 0)],
                3: [(XS_, 3, 1), (FFN_X, 2, 2)]},
 (AT_B, 1, 1): {1: [(XS_, 2, 2), (FFN_X, 2, 0), (FFN_Z, 2, 0)], 2: [(REL, 1, 1, 0)]},
 (AT_B, 1, 5): {0: [(SUM_0, 2), (XS_, 0, 2), (FFN_X, 0, 0), (FFN_OWN, 0)],
                1: [(REL, 0, 3, 0)],
                2: [(XS_, 2, 1), (FFN_X, 1, 1)],
                3: [(SUM_0, 2), (XS_, 3, 2), (FFN_X, 3, 0), (FFN_OWN, 0)]},
 (AT_B, 2, 0): {0: [(XO, 0), (FFN_X, 0, 1), (FFN_OWN, 1)],
                1: [(XS_, 1, 1), (REL, 0, 2, 0), (FFN_X, 2, 1)],
                2: [(XS_, 2, 2), (REL, 0, 3, 0), (ZS, 1, 0), (FFN_X, 1, 2)],
                3: [(XO, 0), (FFN_X, 3, 1), (FFN_OWN, 1)]},
 (AT_B, 2, 1): {1: [(XS_, 1, 2), (ZS, 2, 0), (FFN_X, 2, 2)], 2: [(REL, 1, 0, 1), (SUM_3, 0)]},
 (AT_B, 2, 5): {0: [(XO, 1), (SUM_0, 3), (FFN_X, 0, 2), (FFN_OWN, 2), (SUM_3, 0)],
                1: [(REL, 1, 0, 0)],
                2: [(FFN_OWN, 0), (XO, 0), (REL, 1, 1, 1), (FFN_X, 2, 1)],
                3: [(XO, 1), (SUM_0, 3), (FFN_X, 3, 2), (FFN_OWN, 2), (SUM_3, 0)]},
 (AT_B, 3, 0): {1: [(REL, 0, 3, 1)]},
 (AT_B, 3, 1): {1: [(OX, 0), (FFN_X, 1, 1), (SUM_3, 0)]},
 (AT_B, 3, 2): {0: [(FFN_LAST, 0)], 2: [(REL, 0, 3, 1), (FFN_X, 2, 2)], 3: [(FFN_LAST, 0)]},
 (AT_B, 3, 3): {1: [(REL, 0, 2, 1)], 2: [(SUM_4, 0), (OX, 0)]},
 (AT_D, 0): {0: [(SUM_3, 1), (FFN_LAST, 2), (GX, 0), (SUM_4, 1), (SUM_3, 2), (GX, 1), (ZS, 2, 1), (SUM_4, 2),
                 (SUM_3, 3), (OX, 0), (ZS, 2, 2), (SUM_4, 3), (OX, 1), (ZS, 1, 2), (SUM_7, 0), (SUM_7, 2), (SUM_7, 1),
                 (SUM_8, 0), (SUM_8, 1), (SUM_7, 3)],
             1: [(REL, 0, 3, 2), (REL, 1, 0, 1), (SUM_4, 0), (SUM_3, 1), (REL, 0, 2, 2), (FW, 3, 2, 0), (FFN_LAST, 0),
                 (GX, 0), (REL, 1, 0, 2), (SUM_4, 1), (REL, 0, 3, 3), (GX, 1), (SUM_3, 2), (REL, 0, 2, 3),
                 (REL, 1, 0, 3), (OX, 1), (FW, 2, 0, 0), (SUM_3, 3), (SUM_4, 2), (FW, 3, 2, 1), (FW, 2, 0, 1),
                 (FW, 3, 3, 0), (SUM_7, 0), (FFN_Z, 2, 1), (ZS, 2, 1), (FW, 3, 2, 2), (FW, 3, 3, 1), (SUM_4, 3),
                 (FW, 2, 0, 2), (SUM_7, 1), (FFN_OWN, 1), (FFN_Z, 2, 2), (SUM_8, 0), (FW, 3, 3, 2), (SUM_7, 2),
                 (ZS, 2, 2), (FW, 2, 0, 3), (XO, 1), (FW, 3, 2, 3), (SUM_8, 1), (FFN_OWN, 2), (XO, 2), (FFN_LAST, 1),
                 (FW, 3, 3, 3), (SUM_7, 3), (FFN_LAST, 2)],
             2: [(REL, 0, 3, 2), (FW, 2, 1, 0), (REL, 1, 0, 3), (SUM_3, 2), (REL, 1, 1, 3), (SUM_4, 1), (FW, 2, 1, 1),
                 (GX, 1), (REL, 0, 3, 3), (FW, 3, 3, 0), (SUM_4, 2), (OX, 1), (SUM_3, 3), (FW, 3, 3, 1),
                 (FW, 2, 0, 0), (FFN_Z, 1, 1), (ZS, 1, 1), (FW, 2, 1, 2), (FW, 2, 0, 1), (SUM_7, 0), (FW, 3, 3, 2),
                 (SUM_4, 3), (FFN_OWN, 1), (FFN_Z, 1, 2), (XO, 1), (FW, 2, 1, 3), (ZS, 1, 2), (SUM_8, 0),
                 (FW, 2, 0, 2), (SUM_7, 2), (SUM_7, 1), (FW, 3, 3, 3), (FFN_LAST, 1), (FFN_OWN, 2), (XO, 2),
                 (FW, 2, 0, 3), (SUM_7, 3), (SUM_8, 1), (FFN_LAST, 2)],
             3: [(FFN_LAST, 2), (GX, 0), (SUM_3, 2), (SUM_4, 1), (GX, 1), (ZS, 1, 1), (SUM_4, 2), (OX, 0), (SUM_3, 3),
                 (ZS, 1, 2), (OX, 1), (ZS, 2, 2), (SUM_4, 3), (SUM_7, 0), (SUM_7, 1), (SUM_7, 2), (SUM_8, 0),
                 (SUM_8, 1), (SUM_7, 3)]},
 (AT_E, 0): {2: [(REL, 1, 0, 2)]},
 (AT_E, 1): {0: [(XO, 2), (SUM_4, 0), (FFN_LAST, 1)],
             1: [(FFN_OWN, 0), (XO, 0), (FFN_X, 1, 2)],
             2: [(GX, 0), (REL, 1, 1, 2), (FFN_LAST, 0), (SUM_3, 1)],
             3: [(XO, 2), (SUM_4, 0), (FFN_LAST, 1), (SUM_3, 1)]},
 (AT_G, 0): {0: [(XS_, 1, 0)], 3: [(XS_, 2, 0)]},
 (AT_G, 2): {0: [(XS_, 3, 0), (FFN_X, 1, 1), (ZS, 1, 1)],
             1: [(XS_, 0, 1), (FFN_X, 1, 0)],
             2: [(XS_, 3, 1), (FFN_X, 2, 0)],
             3: [(XS_, 0, 0), (FFN_X, 2, 1), (ZS, 2, 1)]},
 (AT_G, 3): {0: [(XS_, 3, 2), (FFN_X, 3, 0), (ZS, 3, 0)],
             2: [(XS_, 0, 0), (FFN_X, 3, 1), (ZS, 3, 1)],
             3: [(XS_, 0, 2), (FFN_X, 0, 0), (ZS, 0, 0)]},
 (AT_N, 1): {0: [(XS_, 2, 1), (FFN_X, 3, 1), (ZS, 3, 1)],
             1: [(XS_, 3, 0), (FFN_X, 0, 1), (ZS, 0, 1), (FFN_X, 0, 2)],
             2: [(XS_, 0, 1), (FFN_X, 3, 2), (ZS, 3, 2)],
             3: [(XS_, 1, 1), (FFN_X, 0, 1), (ZS, 0, 1)]},
 (AT_N, 2): {1: [(XS_, 3, 1), (ZS, 0, 2)]},
 (AT_N, 3): {0: [(XS_, 2, 2), (FFN_X, 3, 2), (ZS, 3, 2)],
             2: [(XS_, 0, 2), (FFN_X, 0, 0), (FFN_Z, 0, 0), (ZS, 0, 0)],
             3: [(XS_, 1, 2), (FFN_X, 0, 2), (ZS, 0, 2)]},
 (AT_N, 4): {0: [(SUM_0, 0)], 1: [(FFN_X, 3, 0)], 3: [(SUM_0, 0)]},
 (AT_T, 0, 0): {0: [(WD_, 2)], 3: [(WD_, 1)]},
 (AT_T, 0, 1): {0: [(WD_, 3)], 1: [(WD_, 2)], 2: [(WD_, 3)], 3: [(WD_, 0)]},
 (AT_T, 1, 0): {1: [(WD_, 3)], 2: [(WD_, 0)]},
 (AT_T, 1, 1): {0: [(XS_, 1, 1)], 1: [(XS_, 1, 0)], 2: [(XS_, 2, 0)], 3: [(XS_, 2, 1)]},
 (AT_T, 2, 0): {0: [(XS_, 2, 0), (FFN_X, 1, 0), (ZS, 1, 0)],
                1: [(XS_, 0, 0)],
                2: [(XS_, 3, 0)],
                3: [(XS_, 1, 0), (FFN_X, 2, 0), (ZS, 2, 0)]},
 (AT_T, 3, 0): {0: [(XS_, 3, 1), (FFN_X, 2, 0), (ZS, 2, 0)], 3: [(XS_, 0, 1), (FFN_X, 1, 0), (ZS, 1, 0)]},
 (AT_T, 3, 1): {1: [(XS_, 0, 2), (FFN_X, 0, 0), (ZS, 0, 0)], 2: [(XS_, 3, 2), (FFN_X, 3, 0), (ZS, 3, 0)]},
 (AT_W, 4): {0: [(WX, 3)], 1: [(WX, 3)], 2: [(WX, 0)], 3: [(WX, 0)]},
 (AT_W, 5): {0: [(WR, 1)], 1: [(WL, 1), (WR, 1)], 2: [(WL, 1), (WR, 1)], 3: [(WL, 1)]}}
HALF = (1, 1, 0, 0)


BF = jnp.bfloat16
F32 = jnp.float32
MESH = pl.DeviceIdType.MESH


def dot(a, b):
    return jnp.dot(a, b, preferred_element_type=F32)


def dot_t(a, b):
    return lax.dot_general(a, b, (((1,), (1,)), ((), ())), preferred_element_type=F32)


def rows_of(start, size):
    return pl.ds(pl.multiple_of(start, size), size)


def pick(table, index):
    value = table[0]
    for place in range(1, len(table)):
        value = jnp.where(index == place, table[place], value)
    return value


def swap_halves(tile):
    lane = lax.broadcasted_iota(jnp.int32, tile.shape, 1)
    return jnp.where(
        lane % 64 < 32, pltpu.roll(tile, 96, 1), pltpu.roll(tile, 32, 1)
    )


def fast_kernel(
    inputs, cond, again, adaw_h, adab, qkv_h, outw_h, fgain, up_h, upb, down_h, downb, cot_h,
    cos_h, sin_h, cost_h, sint_h,
    out_o, gin_o, qkv_o, outw_o, ffn_o, vall_o,
    wq, wo, wu, wd, ub, cos_v, sin_v, cost, sint,
    xb, ctb, mod2, n1, i1, ai, ait, q_s, k_s, v_s, kt_s, vt_s, ot_s, lse, att,
    ap, n2, i2, fit, gf, gft, oacc, gacc, a_s, gp_s, g_s, grecv,
    do_s, dlt, dqt, gq, b_s, xs, vec, vecr, late, later, vall, ubg,
    rx, rz, fxr, rxb, fb,
    lsem, ssem, rsem, wss, wrs, yss, yrs, fss, frs, bss, brs, hss, hrs, vss, vrs, credit,
):
    Z = 4
    grp = lax.axis_index("grp")
    seq = lax.axis_index("seq")
    z = lax.axis_index("mlp")
    x, c = seq // 2, seq % 2
    D = 768
    flat = lambda ref: ref[...].reshape(1, -1)
    again, adab, fgain, downb = flat(again), flat(adab), flat(fgain), flat(downb)
    own = c * 512
    other = (1 - c) * 512
    TO_CORE = {"seq": x * 2 + (1 - c)}
    TO_X = {"seq": (1 - x) * 2 + c}
    TO_Y = {"grp": 1 - grp}
    RIGHT = {"mlp": jnp.minimum(z + 1, Z - 1)}
    LEFT = {"mlp": jnp.maximum(z - 1, 0)}

    def remote(src, dst, index, device):
        return pltpu.make_async_remote_copy(
            src_ref=src, dst_ref=dst, send_sem=ssem.at[index], recv_sem=rsem.at[index],
            device_id=device, device_id_type=MESH,
        )

    def local(src, dst, index):
        return pltpu.make_async_copy(src, dst, lsem.at[index])

    half = pl.ds(pl.multiple_of(c * 384, 128), 384)
    loads = [local(inputs.at[x], xb.at[rows_of(x * 256, 256)], 0), ]
    loads += [local(cos_h, cos_v, 2), local(sin_h, sin_v, 3), local(cost_h, cost, 4), local(sint_h, sint, 5)]
    for p in range(3):
        for part in range(3):
            loads.append(
                local(
                    qkv_h.at[:, pl.ds(pl.multiple_of(part * D + c * 384 + p * 128, 128), 128)],
                    wq.at[p, :, pl.ds(part * 128, 128)],
                    6 + p * 3 + part,
                )
            )
    loads.append(local(outw_h, wo, 15))
    loads.append(local(up_h.at[:, half], wu.at[z], 16))
    loads.append(local(down_h.at[rows_of(c * 384, 384)], wd.at[z], 17))
    loads.append(local(cot_h.at[x], ctb.at[rows_of(x * 256, 256)], 18))
    adaw = [
        local(adaw_h.at[:, pl.ds(part * D, D)], fit.at[pl.ds(part * 128, 128), pl.ds(0, D)], 15 + 43 + part)
        for part in range(6)
    ]
    for item in [loads[0]] + adaw + loads[1:]:
        item.start()

    ub[z] = flat(upb)

    barrier = pltpu.get_barrier_semaphore()
    peers = [{"seq": (x ^ dx) * 2 + c, "mlp": z ^ dz} for dx in range(2) for dz in range(Z) if dx or dz]
    for device in [TO_CORE, TO_Y] + peers:
        pl.semaphore_signal(barrier, 1, device_id=device, device_id_type=MESH)
    pl.semaphore_wait(barrier, 2 + len(peers))

    swap_x = remote(inputs.at[1 - x], xb.at[rows_of(x * 256, 256)], 0, TO_X)
    swap_x.start()
    swap_c = remote(cot_h.at[1 - x], ctb.at[rows_of(x * 256, 256)], 1, TO_X)
    swap_c.start()

    def rows_at(ref, rows, which, part=None):
        start = which * rows
        if part is None:
            return ref.at[rows_of(start, rows)]
        return ref.at[pl.ds(pl.multiple_of(start + part * (rows // 2), 16), rows // 2)]

    here = grp * 2 + x

    def z_copies(j, way, device, first):
        own_up, own_down = rows_at(wu.at[j], 192, here), rows_at(wd.at[j], 96, here)
        if first:
            src = (
                up_h.at[rows_of(here * 192, 192), half],
                down_h.at[rows_of(c * 384 + here * 96, 96)],
                ub.at[z],
            )
        else:
            src = (own_up, own_down, ub.at[j])
        dst = (own_up, own_down, ub.at[j])
        return [
            pltpu.make_async_remote_copy(
                src_ref=src[i], dst_ref=dst[i], send_sem=wss.at[way, j, i], recv_sem=wrs.at[way, j, i],
                device_id=device, device_id_type=MESH,
            )
            for i in range(3)
        ]

    def pair_copies(j, kind, which, part, device):
        return [
            pltpu.make_async_remote_copy(
                src_ref=ref, dst_ref=ref, send_sem=yss.at[j, kind, i], recv_sem=yrs.at[j, kind, i],
                device_id=device, device_id_type=MESH,
            )
            for i, ref in enumerate((rows_at(wu.at[j], 192, which, part), rows_at(wd.at[j], 96, which, part)))
        ]

    by_x, by_y, across = grp * 2 + 1 - x, (1 - grp) * 2 + x, (1 - grp) * 2 + 1 - x

    def quarter_sends(j):
        return pair_copies(j, 0, here, None, TO_X) + pair_copies(j, 1, here, None, TO_Y)

    def quarter_waits(j):
        return pair_copies(j, 0, by_x, None, TO_X) + pair_copies(j, 1, by_y, None, TO_Y)

    def across_sends(j):
        return pair_copies(j, 2, by_y, 0, TO_X) + pair_copies(j, 3, by_x, 1, TO_Y)

    def across_waits(j):
        return pair_copies(j, 2, across, 0, TO_X) + pair_copies(j, 3, across, 1, TO_Y)

    def start_all(items):
        for item in items:
            item.start()

    @pl.when(z < Z - 1)
    def _():
        start_all(z_copies(z, 0, RIGHT, True))

    @pl.when(z > 0)
    def _():
        start_all(z_copies(z, 1, LEFT, True))

    def order(n):
        return pick([ORDERS[a][n] for a in range(Z)], z)

    pending = {place: [] for place in range(Z)}
    CH = 3

    def send(place, *makes):
        for make in makes:
            make().start()
            pending[place].append(make)

    def span(h):
        return pl.ds(h * (768 // CH), 768 // CH)

    def ffn_copy(j, h):
        return pltpu.make_async_remote_copy(
            src_ref=g_s.at[1 - x, j, span(h)], dst_ref=rx.at[j, span(h)], send_sem=hss.at[j, h],
            recv_sem=hrs.at[j, h], device_id=TO_X, device_id_type=MESH,
        )

    def add_rows(ref, others):
        @pl.loop(0, 768 // CH // 64)
        def _(i):
            rows = rows_of(i * 64, 64)
            total = ref[rows].astype(F32)
            for other_ref in others:
                total = total + other_ref[rows].astype(F32)
            ref[rows] = total.astype(BF)

    def z_send(j, h, place):
        if place in (0, 3):
            target, slot = (1 if place == 0 else 2), j
        elif j in (0, 3):
            target, slot = j, place
        else:
            target, slot = j, (0 if j == 1 else 3)
        return lambda: pltpu.make_async_remote_copy(
            src_ref=g_s.at[x, j, span(h)], dst_ref=rz.at[slot, span(h)], send_sem=fss.at[j, h],
            recv_sem=frs.at[slot, h], device_id={"mlp": target}, device_id_type=MESH,
        )

    def z_wait(slot, h):
        ref = rz.at[slot, span(h)]
        pltpu.make_async_remote_copy(
            src_ref=ref, dst_ref=ref, send_sem=fss.at[0, h], recv_sem=frs.at[slot, h],
            device_id=LEFT, device_id_type=MESH,
        ).wait_recv()

    def ffn_x(place, j, h):
        ffn_copy(j, h).wait_recv()
        add_rows(g_s.at[x, j, span(h)], [rx.at[j, span(h)]])

    def ffn_z(place, j, h):
        z_wait(j, h)
        add_rows(g_s.at[x, j, span(h)], [rz.at[j, span(h)]])

    def zs(place, j, h):
        send(place, z_send(j, h, place))

    def xs_(place, j, h):
        send(place, lambda: ffn_copy(j, h))

    def final_copies(src, kind, h, first):
        dst = ffn_o.at[kind, span(h), half]
        return [local(src, dst, 21 + first * CH + h), remote(src, dst, 31 + first * CH + h, TO_CORE)]

    def own_copy(h):
        return pltpu.make_async_remote_copy(
            src_ref=g_s.at[x, z, span(h)], dst_ref=fxr.at[span(h)], send_sem=hss.at[5, h],
            recv_sem=hrs.at[5, h], device_id=TO_X, device_id_type=MESH,
        )

    def ffn_own(place, h):
        slots = {0: (1, 2), 3: (1, 2), 1: (1, 0), 2: (2, 3)}[place]
        for slot in slots:
            z_wait(slot, h)
        add_rows(g_s.at[x, place, span(h)], [rz.at[slot, span(h)] for slot in slots])
        for item in final_copies(g_s.at[x, z, span(h)], x, h, 0):
            item.start()

    def xo(place, h):
        own_copy(h).start()

    def ffn_last(place, h):
        own_copy(h).wait_recv()
        for item in final_copies(fxr.at[span(h)], 1 - x, h, 1):
            item.start()

    def quarter(ref, p, q):
        if ref is wd:
            return ref.at[p, pl.ds(q // 2 * 192, 192), pl.ds(q % 2 * 384, 384)]
        return ref.at[p, pl.ds(q * 192, 192)]

    def half_rows(ref, p, q, which):
        return ref.at[p, pl.ds(pl.multiple_of(q * 192 + which * 96, 32), 96)]

    def done_rows(p, q):
        return half_rows(fb, p, q, x) if HALF[p] else quarter(fb, p, q)

    def hop(kind, p, q, place):
        step = 1 if kind in (0, 2) else -1
        return lambda: pltpu.make_async_remote_copy(
            src_ref=quarter(b_s, p, q) if kind < 2 else done_rows(p, q),
            dst_ref=quarter((wu, wd)[kind], p, q) if kind < 2 else done_rows(p, q),
            send_sem=bss.at[kind, p, q],
            recv_sem=brs.at[kind, p, q],
            device_id={"mlp": place + step},
            device_id_type=MESH,
        )

    def hop_wait(kind, p, q):
        dst = quarter((wu, wd)[kind], p, q) if kind < 2 else done_rows(p, q)
        pltpu.make_async_remote_copy(
            src_ref=dst, dst_ref=dst, send_sem=bss.at[kind, p, q], recv_sem=brs.at[kind, p, q],
            device_id=LEFT, device_id_type=MESH,
        ).wait_recv()

    def add_quarter(p, q, refs):
        total = quarter(b_s, p, q)[...].astype(F32)
        for ref in refs:
            total = total + quarter(ref, p, q)[...].astype(F32)
        quarter(b_s, p, q)[...] = total.astype(BF)

    def sum_0(place, p):
        kind, blocks = (0, (3, 2, 1)) if place == 0 else (1, (0, 1, 2))
        send(place, *[hop(kind, p, q, place) for q in blocks])

    def rel(place, kind, q, p):
        hop_wait(kind, p, q)
        add_quarter(p, q, [wd if kind else wu])
        send(place, hop(kind, p, q, place))

    def cross(p, place):
        return lambda: pltpu.make_async_remote_copy(
            src_ref=half_rows(b_s, p, place, 1 - x) if HALF[p] else quarter(b_s, p, place),
            dst_ref=rxb.at[p, pl.ds(0, 96)] if HALF[p] else rxb.at[p],
            send_sem=hss.at[4, p],
            recv_sem=hrs.at[4, p], device_id=TO_X, device_id_type=MESH,
        )

    def sum_3(place, p):
        refs = []
        if place > 0:
            hop_wait(0, p, place)
            refs.append(wu)
        if place < 3:
            hop_wait(1, p, place)
            refs.append(wd)
        add_quarter(p, place, refs)
        send(place, cross(p, place))

    def sum_4(place, p):
        cross(p, place)().wait_recv()
        if HALF[p]:
            total = half_rows(b_s, p, place, x)[...].astype(F32) + rxb[p, :96].astype(F32)
        else:
            total = quarter(b_s, p, place)[...].astype(F32) + rxb[p].astype(F32)
        done_rows(p, place)[...] = total.astype(BF)
        if place < 3:
            send(place, hop(2, p, place, place))
        if place > 0:
            send(place, hop(3, p, place, place))

    def fw(place, kind, q, p):
        hop_wait(kind, p, q)
        send(place, hop(kind, p, q, place))

    def piece_copies(p):
        if p == 0:
            pairs = [
                (fb.at[0, pl.ds(n * 384, 384)], outw_o.at[rows_of(c * 384, 384), pl.ds(n * 384, 384)])
                for n in range(2)
            ]
        else:
            pairs = [
                (
                    fb.at[p, :, pl.ds(part * 128, 128)],
                    qkv_o.at[
                        :, pl.ds(pl.multiple_of(part * D + c * 384 + (p - 1) * 128, 128), 128)
                    ],
                )
                for part in range(3)
            ]
        copies = []
        for n, (src, dst) in enumerate(pairs):
            copies.append(local(src, dst, 43 + p * 3 + n))
            copies.append(remote(src, dst, 18 + p * 3 + n, TO_CORE))
        return copies

    def sum_7(place, p):
        for q in range(4):
            if place == 0 and q > 0:
                hop_wait(3, p, q)
            if place == 3 and q < 3:
                hop_wait(2, p, q)
        if HALF[p]:
            send(place, *[lambda q=q: half_copy(p, q) for q in range(4)])
        else:
            for item in piece_copies(p):
                item.start()

    def half_copy(p, q):
        rows = half_rows(fb, p, q, x)
        return pltpu.make_async_remote_copy(
            src_ref=rows, dst_ref=rows, send_sem=hss.at[6 + p, q], recv_sem=hrs.at[6 + p, q],
            device_id=TO_X, device_id_type=MESH,
        )

    def sum_8(place, p):
        for q in range(4):
            half_copy(p, q).wait_recv()
        for item in piece_copies(p):
            item.start()

    def wl(place, k):
        for item in z_copies(place - k, 0, RIGHT, False):
            item.wait_recv()
        if place < 3:
            start_all(z_copies(place - k, 0, RIGHT, False))
        start_all(pair_copies(place - k, 1, here, None, TO_Y))

    def wr(place, k):
        for item in z_copies(place + k, 1, LEFT, False):
            item.wait_recv()
        if place > 0:
            start_all(z_copies(place + k, 1, LEFT, False))
        start_all(pair_copies(place + k, 1, here, None, TO_Y))

    def wx(place, j):
        start_all(pair_copies(j, 0, here, None, TO_X))

    def wd_(place, j):
        for item in quarter_waits(j):
            item.wait_recv()
        start_all(across_sends(j))

    def cross_rows(out_ref, number, part):
        rows = rows_of((1 - x) * 256 + part * 128, 128)
        return remote(
            xs.at[number, rows], out_ref.at[x, pl.ds(part * 128, 128)], 12 + number * 2 + part, TO_X
        )

    def ox(place, part):
        cross_rows(out_o, 0, part).start()

    def gx(place, part):
        cross_rows(gin_o, 1, part).start()

    jobs = (ffn_x, ffn_z, ffn_own, ffn_last, sum_0, rel, sum_3, sum_4, fw, sum_7, wl, wr, xs_, zs, xo, ox, gx, wd_, sum_8, wx)

    def slot(name, here=None):
        for place, names in PLAN.get(name, {}).items():
            @pl.when(z == place if here is None else (z == place) & here)
            def _(place=place, names=names):
                for job, *rest in names:
                    jobs[job](place, *rest)

    for part in range(6):
        lanes = pl.ds(part * D, D)
        adaw[part].wait()
        mod2[:, lanes] = dot(cond[...], fit[part * 128 : (part + 1) * 128, :D]) + adab[:, part * D : (part + 1) * D]
    modrow = mod2[pl.ds(x, 1), :]
    shift_one, scale_one, gate_one, shift_two, scale_two, gate_two = [
        modrow[:, part * D : (part + 1) * D] for part in range(6)
    ]

    def layer_norm(values):
        center = values - jnp.mean(values, axis=-1, keepdims=True)
        inv = lax.rsqrt(jnp.mean(center * center, axis=-1, keepdims=True) + 1e-05)
        return center * inv, inv

    TILE = 64
    mul_one = again * (1.0 + scale_one)
    mul_two = fgain * (1.0 + scale_two)

    def norm_one_block(block):
        @pl.loop(0, 256 // TILE)
        def _(i):
            at = block * 256 + i * TILE
            rows = rows_of(at, TILE)
            normed, inv = layer_norm(xb[rows].astype(F32))
            n1[rows] = normed
            i1[rows] = inv
            ai[rows_of(own + at, TILE)] = (normed * mul_one + shift_one).astype(BF)

    def core_rows(ref, start, size, index):
        part = ref.at[rows_of(start, size)]
        return remote(part, part, index, TO_CORE)

    for item in loads[1:14]:
        item.wait()

    def project_rows(start):
        rows = rows_of(start, 256)
        tile = ai[rows]
        cos_t, sin_t = cos_v[rows], sin_v[rows]

        @pl.loop(0, 3)
        def _(p):
            projected = dot(tile, wq[p])
            query = projected[:, :128]
            key = projected[:, 128:256]
            value = projected[:, 256:].astype(BF)
            query = (query * cos_t + swap_halves(query) * sin_t).astype(BF)
            key = (key * cos_t + swap_halves(key) * sin_t).astype(BF)
            q_s[p, rows] = query * jnp.asarray(0.125, BF)
            k_s[p, rows] = key
            v_s[p, rows] = value
            kt_s[p, :, rows] = key.T
            vt_s[p, :, rows] = value.T

        ait[:, rows] = tile.T

    loads[0].wait()
    norm_one_block(x)
    core_rows(ai, own + x * 256, 256, 2).start()
    project_rows(own + x * 256)
    core_rows(ai, other + x * 256, 256, 2).wait_recv()
    project_rows(other + x * 256)
    slot((AT_W, 5))
    swap_x.wait_recv()
    norm_one_block(1 - x)
    core_rows(ai, own + (1 - x) * 256, 256, 3).start()
    project_rows(own + (1 - x) * 256)
    core_rows(ai, other + (1 - x) * 256, 256, 3).wait_recv()
    project_rows(other + (1 - x) * 256)
    for item in loads[15:17]:
        item.wait()
    slot((AT_W, 0))

    att_s = a_s.at[pl.ds(0, 512)]
    low_lane = lax.broadcasted_iota(jnp.int32, (1, 128), 1) < 64
    keep = [low_lane.astype(F32).astype(BF), (~low_lane).astype(F32).astype(BF)]

    def att_copy(p, start):
        return remote(
            att_s.at[:, pl.ds(p * 128, 128)],
            att.at[:, pl.ds(pl.multiple_of(c * 384 + p * 128, 128), 128)],
            4 + p,
            TO_CORE,
        )

    def attend(p):
        @pl.loop(0, 2)
        def _(t):
            cols = rows_of(t * 512, 512)
            query = q_s[p, cols]
            outs = []
            for h in range(2):
                masked = query * keep[h]
                held = (oacc, gacc)[h]
                top = None
                for i in range(4):
                    keys = pl.ds(i * 256, 256)
                    scores = dot_t(k_s[p, keys], masked)
                    held[keys, :512] = scores
                    top = scores if top is None else jnp.maximum(top, scores)
                top = jnp.max(top, axis=0, keepdims=True)
                out, total = None, None
                for i in range(4):
                    keys = pl.ds(i * 256, 256)
                    expd = jnp.exp(held[keys, :512] - top)
                    part = dot(vt_s[p, pl.ds(h * 64, 64), keys], expd.astype(BF))
                    out = part if out is None else out + part
                    total = expd if total is None else total + expd
                total = jnp.sum(total, axis=0, keepdims=True)
                lse[p, pl.ds(h, 1), cols] = top + jnp.log(total)
                out = out / total
                ot_s[p, pl.ds(h * 64, 64), cols] = out
                outs.append(out)
            natural = jnp.concatenate(outs, axis=0).T.astype(BF)
            lanes = pl.ds(pl.multiple_of(c * 384 + p * 128, 128), 128)

            @pl.when(t == c)
            def _():
                att[:, lanes] = natural

            @pl.when(t != c)
            def _():
                att_s[:, pl.ds(p * 128, 128)] = natural

            for n in range(2):
                slot((AT_A, p, n), t == n)

        att_copy(p, True).start()

    attend(0)
    attend(1)

    attend(2)

    loads[17].wait()
    swap_c.wait_recv()

    @pl.loop(0, 512 // TILE)
    def _(i):
        at = i * TILE
        gf[rows_of(own + at, TILE)] = (gate_two * ctb[rows_of(at, TILE)].astype(F32)).astype(BF)

    core_rows(gf, own, 512, 7).start()
    vec[...] = jnp.zeros_like(vec)
    late[...] = jnp.zeros_like(late)

    @pl.loop(0, 512 // TILE)
    def _(i):
        vec[8:9] += jnp.sum(gf[rows_of(own + i * TILE, TILE)].astype(F32), axis=0, keepdims=True)

    for p in range(3):
        remote(
            att_s.at[:, pl.ds(p * 128, 128)],
            att.at[:, pl.ds(pl.multiple_of((1 - c) * 384 + p * 128, 128), 128)],
            4 + p,
            TO_CORE,
        ).wait_recv()
    loads[14].wait()

    core_rows(ai, own + x * 256, 256, 2).wait_send()
    core_rows(ai, own + (1 - x) * 256, 256, 3).wait_send()
    fi = ai

    @pl.loop(0, 2)
    def _(b):
        rows = rows_of(b * 256, 256)
        ap[rows] = dot(att[rows], wo[...])
        slot((AT_W, 3), b == 0)
        slot((AT_W, 4), b == 1)

        @pl.loop(0, 256 // TILE)
        def _(i):
            at = b * 256 + i * TILE
            tile = rows_of(at, TILE)
            middle = xb[tile].astype(F32) + gate_one * ap[tile]
            normed, inv = layer_norm(middle)
            n2[tile] = normed
            i2[tile] = inv
            fi[rows_of(own + at, TILE)] = (normed * mul_two + shift_two).astype(BF)

    core_rows(fi, own, 512, 8).start()
    slot((AT_W, 1))

    def turn(src, dst, start):
        @pl.loop(0, 2)
        def _(t):
            rows = rows_of(start + t * 256, 256)
            dst[:, rows] = src[rows].T

    slot((AT_W, 2))

    for p in range(3):
        att_copy(p, False).wait_send()

    coef = 0.7978845608028654

    @pl.loop(0, Z)
    def _(k):
        j = pick([order(n) for n in range(Z)], k)

        for n in range(Z):
            slot((AT_F, n), k == n)

        @pl.when(j != z)
        def _():
            for item in across_waits(j):
                item.wait_recv()

        bias = ub[j][:, pl.ds(0, 384)]
        bias = jnp.where(c == 0, bias, ub[j][:, pl.ds(384, 384)])

        @pl.loop(0, 2)
        def _(t):
            @pl.when((k == 0) & (t == 1))
            def _():
                turn(gf, gft, own)
                turn(fi, fit, own)
                core_rows(gf, other, 512, 7).wait_recv()
                turn(gf, gft, other)
                core_rows(fi, other, 512, 8).wait_recv()
                turn(fi, fit, other)

            rows = rows_of(jnp.where(t == 0, own, other), 512)
            pre = dot(fi[rows], wu[j]) + bias
            sq = pre * pre
            upper = 0.5 + 0.5 * jnp.tanh(pre * (coef + (coef * 0.044715) * sq))
            act = (pre * upper).astype(BF)
            slope = upper + pre * (2.0 * upper * (1.0 - upper)) * (coef + (3.0 * 0.044715 * coef) * sq)
            a_s[rows] = act
            grad_pre = (dot_t(gf[rows], wd[j]) * slope).astype(BF)
            gp_s[rows] = grad_pre
            bsum = jnp.sum(grad_pre.astype(F32), axis=0, keepdims=True)
            out = dot(act, wd[j])
            gin = dot_t(grad_pre, wu[j])

            @pl.when(k == 0)
            def _():
                oacc[rows] = out
                gacc[rows] = gin

            @pl.when(k > 0)
            def _():
                oacc[rows] += out
                gacc[rows] += gin

            for m in range(Z):
                for n in range(2):
                    slot((AT_T, m, n), (k == m) & (t == n))

            @pl.when(t == 0)
            def _():
                ubg[j] = bsum

            @pl.when(t > 0)
            def _():
                ubg[j] += bsum

        g_s[0, j] = dot(fit[...], gp_s[...]).astype(BF)
        g_s[1, j] = dot(gft[...], a_s[...]).astype(BF)

        for n in range(Z):
            slot((AT_G, n), k == n)

    def give_credit():
        @pl.when(z > 0)
        def _():
            pl.semaphore_signal(credit.at[0], 1, device_id=LEFT, device_id_type=MESH)

        @pl.when(z < Z - 1)
        def _():
            pl.semaphore_signal(credit.at[1], 1, device_id=RIGHT, device_id_type=MESH)

    def take_credit():
        @pl.when(z < Z - 1)
        def _():
            pl.semaphore_wait(credit.at[0], 1)

        @pl.when(z > 0)
        def _():
            pl.semaphore_wait(credit.at[1], 1)


    def weight_waits(k):
        @pl.when(z - k >= 0)
        def _():
            @pl.when(z < Z - 1)
            def _():
                for item in z_copies(z - k, 0, RIGHT, False):
                    item.wait_send()

            for item in quarter_sends(z - k) + across_sends(z - k):
                item.wait_send()

        @pl.when(z + k <= Z - 1)
        def _():
            @pl.when(z > 0)
            def _():
                for item in z_copies(z + k, 1, LEFT, False):
                    item.wait_send()

            for item in quarter_sends(z + k) + across_sends(z + k):
                item.wait_send()

    @pl.when(z < Z - 1)
    def _():
        for item in z_copies(z, 0, RIGHT, False):
            item.wait_send()

    @pl.when(z > 0)
    def _():
        for item in z_copies(z, 1, LEFT, False):
            item.wait_send()

    pl.loop(1, Z)(weight_waits)
    give_credit()

    osend, gsend = xs.at[0], xs.at[1]

    @pl.loop(0, 512 // TILE)
    def _(i):
        tile = rows_of(i * TILE, TILE)
        far = rows_of(other + i * TILE, TILE)
        gsend[tile] = gacc[far].astype(BF)

    remote(gsend, grecv, 9, TO_CORE).start()

    @pl.loop(0, 512 // TILE)
    def _(i):
        osend[rows_of(i * TILE, TILE)] = oacc[rows_of(other + i * TILE, TILE)].astype(BF)

    orecv = att
    remote(osend, orecv, 10, TO_CORE).start()
    remote(gsend, grecv, 9, TO_CORE).wait_recv()
    core_rows(gf, own, 512, 7).wait_send()

    def norm_back(grad, normed, inv):
        return inv * (
            grad
            - jnp.mean(grad, axis=-1, keepdims=True)
            - normed * jnp.mean(grad * normed, axis=-1, keepdims=True)
        )

    @pl.loop(0, 512 // TILE)
    def _(i):
        tile = rows_of(i * TILE, TILE)
        near = rows_of(own + i * TILE, TILE)
        grad = gacc[near] + grecv[tile].astype(F32)
        normed = n2[tile]
        vec[3:4] += jnp.sum(grad, axis=0, keepdims=True)
        vec[4:5] += jnp.sum(grad * normed, axis=0, keepdims=True)
        middle = ctb[tile].astype(F32) + norm_back(grad * mul_two, normed, i2[tile])
        n2[tile] = middle
        gf[near] = (gate_one * middle).astype(BF)
        vec[2:3] += jnp.sum(middle * ap[tile], axis=0, keepdims=True)

    gproj = gf
    core_rows(gproj, own, 512, 11).start()
    slot((AT_N, 1))

    remote(osend, orecv, 10, TO_CORE).wait()

    def rows_out(number, i, values):
        xs[number, rows_of(i * TILE, TILE)] = values.astype(BF)

    def out_copy(out_ref, number):
        return local(xs.at[number, rows_of(x * 256, 256)], out_ref.at[x], 55 + number)

    @pl.loop(0, 512 // TILE)
    def _(i):
        tile = rows_of(i * TILE, TILE)
        ffn = oacc[rows_of(own + i * TILE, TILE)] + orecv[tile].astype(F32) + downb
        vec[5:6] += jnp.sum(ctb[tile].astype(F32) * ffn, axis=0, keepdims=True)
        rows_out(0, i, xb[tile].astype(F32) + gate_one * ap[tile] + gate_two * ffn)

    out_copy(out_o, 0).start()

    core_rows(gproj, other, 512, 11).wait_recv()
    slot((AT_N, 2))

    @pl.loop(0, 4)
    def _(t):
        rows = rows_of(t * 256, 256)
        grad = dot_t(gproj[rows], wo[rows_of(c * 384, 384)])
        for p in range(3):
            part = grad[:, p * 128 : (p + 1) * 128].astype(BF)
            do_s[p, rows] = part
            product = part.astype(F32).T * ot_s[p, :, rows]
            for h in range(2):
                dlt[p, pl.ds(h, 1), rows] = jnp.sum(
                    product[h * 64 : (h + 1) * 64], axis=0, keepdims=True
                )

    slot((AT_N, 3))

    slope_two = vec[4:5]
    vec[7:8] = slope_two * (1.0 + scale_two)
    vec[4:5] = slope_two * fgain
    for core in range(2):
        @pl.when(c == core)
        def _():
            for j in range(4):
                vec[9 + 2 * core + j // 2, pl.ds((j % 2) * 384, 384)] = ubg[j, 0]

    both = cond[...].astype(F32)
    vec[13:14, :128] = 0.5 * jnp.where(x == 0, both[0:1], both[1:2])
    remote(vec, vecr, 30, TO_CORE).start()
    chip = 2 * z + x

    def vec_part(ref, kind, slot_=None):
        ref = ref if slot_ is None else ref.at[pl.ds(slot_, 1)]
        if kind == 0:
            return ref.at[:, rows_of(c * 8, 8)]
        return ref.at[:, pl.ds(16, 8), half]

    def vec_copy(kind, n, slot_):
        part = vec_part(vall, kind, slot_)
        return pltpu.make_async_remote_copy(
            src_ref=part, dst_ref=part, send_sem=vss.at[kind, n], recv_sem=vrs.at[kind, n],
            device_id=peers[n], device_id_type=MESH,
        )

    for p in range(3):
        @pl.loop(0, 2)
        def _(n):
            lanes = pl.ds(pl.multiple_of(n * 384, 128), 384)
            b_s[0, rows_of(n * 384 + p * 128, 128)] = dot(
                ot_s[p].astype(BF), gproj[:, lanes]
            ).astype(BF)

    remote(vec, vecr, 30, TO_CORE).wait_recv()
    vall[chip, pl.ds(0, 16)] = vec[...] + vecr[...]
    for n in range(len(peers)):
        vec_copy(0, n, chip).start()

    take_credit()
    slot((AT_N, 4))

    def attend_back(p):
        for h in range(2):
            a_s[:, h * 128 : (h + 1) * 128] = q_s[p] * keep[h]
            gp_s[:, h * 128 : (h + 1) * 128] = do_s[p] * keep[h]
        dqt[...] = jnp.zeros_like(dqt)

        @pl.loop(0, 2)
        def _(t):
            rows = rows_of(t * 512, 512)
            keys, values = k_s[p, rows], v_s[p, rows]
            dv, dk = None, None
            for h in range(2):
                qm, dom = a_s[:, h * 128 : (h + 1) * 128], gp_s[:, h * 128 : (h + 1) * 128]
                probs = jnp.exp(dot_t(keys, qm) - lse[p, pl.ds(h, 1), :])
                grads = dot_t(values, dom)
                ds = (probs * (grads - dlt[p, pl.ds(h, 1), :])).astype(BF)
                dv_h = dot(probs.astype(BF), dom)
                dk_h = dot(ds, qm)
                dv = dv_h if dv is None else dv + dv_h
                dk = dk_h if dk is None else dk + dk_h
                dqt[pl.ds(h * 64, 64)] += dot(kt_s[p, pl.ds(h * 64, 64), rows], ds)
            cos_t, sin_t = cos_v[rows], sin_v[rows]
            gq[p, rows, pl.ds(128, 128)] = (dk * cos_t - swap_halves(dk) * sin_t).astype(BF)
            gq[p, rows, pl.ds(256, 128)] = dv.astype(BF)

            for n in range(2):
                slot((AT_B, p, n), t == n)

        @pl.loop(0, 4)
        def _(t):
            rows = rows_of(t * 256, 256)
            block = dqt[:, rows] * 0.125
            cos_t, sin_t = cost[:, rows], sint[:, rows]
            parts = []
            for h in range(2):
                u, w = block[h * 64 : h * 64 + 32], block[h * 64 + 32 : h * 64 + 64]
                parts += [u * cos_t + w * sin_t, w * cos_t - u * sin_t]
            gq[p, rows, pl.ds(0, 128)] = jnp.concatenate(parts, axis=0).T.astype(BF)

        b_s[1 + p] = dot(ait[...], gq[p]).astype(BF)
        slot((AT_B, p, 5))

    remote(gsend, grecv, 9, TO_CORE).wait_send()
    for p in range(3):
        attend_back(p)

    @pl.loop(0, 4)
    def _(t):
        rows = rows_of(t * 256, 256)
        part = dot_t(gq[0, rows], wq[0])
        for p in range(1, 3):
            part = part + dot_t(gq[p, rows], wq[p])
        gacc[rows] = part
        for n in range(4):
            slot((AT_B, 3, n), t == n)

    @pl.loop(0, 512 // TILE)
    def _(i):
        gsend[rows_of(i * TILE, TILE)] = gacc[rows_of(other + i * TILE, TILE)].astype(BF)

    remote(gsend, grecv, 11 + 26, TO_CORE).start()
    slot((AT_E, 0))
    remote(gsend, grecv, 11 + 26, TO_CORE).wait()

    @pl.loop(0, 512 // TILE)
    def _(i):
        tile = rows_of(i * TILE, TILE)
        near = rows_of(own + i * TILE, TILE)
        grad = gacc[near] + grecv[tile].astype(F32)
        normed = n1[tile]
        late[0:1] += jnp.sum(grad, axis=0, keepdims=True)
        late[1:2] += jnp.sum(grad * normed, axis=0, keepdims=True)
        rows_out(1, i, n2[tile] + norm_back(grad * mul_one, normed, i1[tile]))

    out_copy(gin_o, 1).start()
    slot((AT_E, 1))
    slope_one = late[1:2]
    late[2:3] = slope_one * (1.0 + scale_one)
    late[1:2] = slope_one * again
    remote(late, later, 38, TO_CORE).start()
    slot((AT_E, 2))
    remote(late, later, 38, TO_CORE).wait_recv()
    vall[chip, pl.ds(16, 8)] = late[...] + later[...]
    for n in range(len(peers)):
        vec_copy(1, n, chip).start()
    slot((AT_D, 0))
    for kind in range(2):
        for n in range(len(peers)):
            vec_copy(kind, n, 2 * peers[n]["mlp"] + peers[n]["seq"] // 2).wait_recv()

    def vec_out(kind):
        src, dst = vec_part(vall, kind), vec_part(vall_o, kind)
        return [local(src, dst, 57 - 56 * kind), remote(src, dst, 39 + kind, TO_CORE)]

    for item in vec_out(0) + vec_out(1):
        item.start()

    for number, ref in ((0, out_o), (1, gin_o)):
        out_copy(ref, number).wait()
        for part in range(2):
            cross_rows(ref, number, part).wait()
    for p in range(4):
        for item in piece_copies(p):
            item.wait()
    for h in range(CH):
        for item in final_copies(g_s.at[x, z, span(h)], x, h, 0) + final_copies(fxr.at[span(h)], 1 - x, h, 1):
            item.wait()
        own_copy(h).wait_send()
    for kind in range(2):
        for item in vec_out(kind):
            item.wait()
        for n in range(len(peers)):
            vec_copy(kind, n, chip).wait_send()
    swap_x.wait_send()
    swap_c.wait_send()
    core_rows(fi, own, 512, 8).wait_send()
    core_rows(gproj, own, 512, 11).wait_send()
    remote(vec, vecr, 30, TO_CORE).wait_send()
    remote(late, later, 38, TO_CORE).wait_send()
    for place in range(Z):
        @pl.when(z == place)
        def _(place=place):
            for make in pending[place]:
                make().wait_send()


def finish_kernel(
    out_h, gin_h, qkv_h, outw_h, ffn_h, vall_h, adaw_h,
    out_o, gin_o, cond_o, again_o, adaw_o, adab_o, qkv_o, outw_o, fgain_o, up_o, upb_o, down_o, downb_o,
    tok_b, qkv_b, outw_b, ffn_b, adaw, vall, tok_f, qkv_f, outw_f, ffn_f, adaw_f, cond_s, isem, osem,
):
    z = lax.axis_index("mlp")
    D = 768
    loads, steps = [], []

    def step(src, buffer, result, dst, turn=False):
        number = len(steps)
        loads.append(pltpu.make_async_copy(src, buffer, isem.at[number]))
        store = pltpu.make_async_copy(result, dst, osem.at[number])

        def body():
            loads[number].wait()
            values = buffer[...].astype(F32)
            result[...] = values.T if turn else values
            store.start()

        steps.append((body, store))

    vall_copy = pltpu.make_async_copy(vall_h, vall, isem.at[30])
    adaw_copy = pltpu.make_async_copy(adaw_h, adaw, isem.at[31])
    for n in range(6):
        rows = pl.ds(n * 128, 128)
        step(qkv_h.at[rows], qkv_b.at[rows], qkv_f.at[rows], qkv_o.at[rows])
    for n in range(2):
        rows = pl.ds(n * 384, 384)
        step(outw_h.at[rows], outw_b.at[rows], outw_f.at[rows], outw_o.at[rows])
        step(ffn_h.at[0, rows], ffn_b.at[0, rows], ffn_f.at[0, rows], up_o.at[rows])
    for n in range(3):
        rows = pl.ds(n * 256, 256)
        step(ffn_h.at[1, rows], ffn_b.at[1, rows], ffn_f.at[1, :, rows], down_o.at[:, rows], True)
    for n in range(2):
        step(out_h.at[n], tok_b.at[0, n], tok_f.at[0, n], out_o.at[n])
        step(gin_h.at[n], tok_b.at[1, n], tok_f.at[1, n], gin_o.at[n])
    for item in loads[:6] + [vall_copy, adaw_copy] + loads[6:]:
        item.start()
    for body, _ in steps[:6]:
        body()
    vall_copy.wait()
    adaw_copy.wait()
    high = lax.Precision.HIGHEST
    everyone = vall[:, 13, :128]
    total = vall[0]
    for n in range(1, 8):
        total = total + vall[n]
    acc, ada_out = None, []
    for part in range(6):
        lanes = pl.ds(part * D, D)
        row = part if part > 1 else 16 + part
        grads = vall[:, row, :]
        adab_o[lanes] = total[row]
        adaw_f[part] = lax.dot_general(
            everyone, grads, (((0,), (0,)), ((), ())), precision=high, preferred_element_type=F32
        )
        ada_out.append(pltpu.make_async_copy(adaw_f.at[part], adaw_o.at[:, lanes], osem.at[26 + part]))
        ada_out[-1].start()
        piece = lax.dot_general(
            grads, adaw[:, lanes].astype(F32), (((1,), (1,)), ((), ())), precision=high,
            preferred_element_type=F32,
        )
        acc = piece if acc is None else acc + piece
    for body, _ in steps[6:]:
        body()
    cond_s[...] = acc
    cond_o[...] = cond_s[pl.ds(2 * z, 2), :]
    again_o[...] = total[18]
    fgain_o[...] = total[7]
    downb_o[...] = total[8]
    for core in range(2):
        halves = [total[9 + 2 * core + j // 2, (j % 2) * 384 : (j % 2 + 1) * 384] for j in range(4)]
        mine = halves[0]
        for j in range(1, 4):
            mine = jnp.where(z == j, halves[j], mine)
        upb_o[pl.ds(core * 384, 384)] = mine
    for item in ada_out:
        item.wait()
    for _, store in steps:
        store.wait()


def tables(seg_len, seq_size):
    half = np.arange(32)
    frequency = 10000.0 ** (-2.0 * half / 64)
    core, chip, token = np.meshgrid(
        np.arange(2), np.arange(seq_size // 2), np.arange(seg_len), indexing="ij"
    )
    place = ((chip * 2 + core) * seg_len + token).reshape(-1)
    angle = place[:, None] * frequency[None, :]
    cos, sin = np.cos(angle).astype(np.float32), np.sin(angle).astype(np.float32)
    return (
        np.tile(cos, (1, 4)),
        np.concatenate([-sin, sin, -sin, sin], axis=1),
        np.ascontiguousarray(cos.T),
        np.ascontiguousarray(sin.T),
    )


def fast_shards(
    inputs, condition, attn_gain, ada_weight, ada_bias, qkv_weight, out_weight, ffn_gain,
    up_weight, up_bias, down_weight, down_bias, cotangent,
):
    Z = lax.axis_size("mlp")
    tabs = [jnp.asarray(t) for t in tables(inputs.shape[1], lax.axis_size("seq"))]
    hbm, vm = pl.BlockSpec(memory_space=pl.ANY), pl.BlockSpec(memory_space=pltpu.VMEM)
    shape = jax.ShapeDtypeStruct
    V = pltpu.VMEM
    dma = pltpu.SemaphoreType.DMA
    scratch = [
        V((3, 768, 384), BF), V((768, 768), BF), V((Z, 768, 384), BF),
        V((Z, 384, 768), BF), V((Z, 1, 768), F32), V((1024, 128), F32), V((1024, 128), F32),
        V((32, 1024), F32), V((32, 1024), F32),
        V((512, 768), BF), V((512, 768), BF), V((2, 4608), F32), V((512, 768), F32), V((512, 1), F32),
        V((1024, 768), BF), V((768, 1024), BF),
        V((3, 1024, 128), BF), V((3, 1024, 128), BF), V((3, 1024, 128), BF),
        V((3, 128, 1024), BF), V((3, 128, 1024), BF), V((3, 128, 1024), F32), V((3, 2, 1024), F32),
        V((512, 768), BF),
        V((512, 768), F32), V((512, 768), F32), V((512, 1), F32),
        V((768, 1024), BF), V((1024, 768), BF), V((768, 1024), BF),
        V((1024, 768), F32), V((1024, 768), F32), V((1024, 384), BF), V((1024, 384), BF),
        V((2, Z, 768, 384), BF), V((512, 768), BF),
        V((3, 1024, 128), BF), V((3, 2, 1024), F32), V((128, 1024), F32),
        V((3, 1024, 384), BF), V((4, 768, 384), BF), V((2, 512, 768), BF),
        V((16, 768), F32), V((16, 768), F32), V((8, 768), F32), V((8, 768), F32),
        V((2 * Z, 24, 768), F32), V((Z, 1, 384), F32),
        V((Z, 768, 384), BF), V((Z, 768, 384), BF), V((768, 384), BF), V((4, 192, 384), BF),
        V((4, 768, 384), BF),
        dma((64,)), dma((41,)), dma((41,)), dma((2, Z, 3)), dma((2, Z, 3)), dma((Z, 4, 2)), dma((Z, 4, 2)),
        dma((Z, 3)), dma((Z, 3)), dma((4, 4, 4)), dma((4, 4, 4)), dma((10, 4)), dma((10, 4)), dma((2, 7)), dma((2, 7)),
        pltpu.SemaphoreType.REGULAR((2,)),
    ]
    token = shape(inputs.shape, BF)
    vall_shape = shape((2 * Z, 24, 768), F32)
    ffn_shape = shape((2, 768, 768), BF)
    out, gin, qkv, outw, ffn, vall = pl.pallas_call(
        fast_kernel,
        out_shape=[
            token, token, shape(qkv_weight.shape, BF), shape(out_weight.shape, BF), ffn_shape, vall_shape,
        ],
        in_specs=[hbm, vm, vm, hbm, vm, hbm, hbm, vm, hbm, vm, hbm, vm, hbm, hbm, hbm, hbm, hbm],
        out_specs=[hbm] * 6,
        scratch_shapes=scratch,
        compiler_params=pltpu.CompilerParams(
            collective_id=0, has_side_effects=True, vmem_limit_bytes=VMEM_LIMIT
        ),
        name="block",
    )(
        inputs, condition, attn_gain, ada_weight, ada_bias, qkv_weight, out_weight,
        ffn_gain, up_weight, up_bias, down_weight, down_bias, cotangent, *tabs,
    )
    same = lambda v: shape(v.shape, F32)
    tokens = shape(inputs.shape, F32)
    return pl.pallas_call(
        finish_kernel,
        out_shape=[
            tokens, tokens, same(condition), same(attn_gain), same(ada_weight), same(ada_bias),
            same(qkv_weight), same(out_weight), same(ffn_gain), same(up_weight), same(up_bias),
            same(down_weight), same(down_bias),
        ],
        in_specs=[hbm] * 7,
        out_specs=[hbm, hbm, vm, vm, hbm, vm, hbm, hbm, vm, hbm, vm, hbm, vm],
        scratch_shapes=[
            V((2, *inputs.shape), BF), V(qkv_weight.shape, BF), V(out_weight.shape, BF), V((2, 768, 768), BF),
            V(ada_weight.shape, BF), V((2 * Z, 24, 768), F32), V((2, *inputs.shape), F32),
            V(qkv_weight.shape, F32), V(out_weight.shape, F32), V((2, 768, 768), F32), V((6, 128, 768), F32),
            V((2 * Z, 128), F32), dma((32,)), dma((32,)),
        ],
        compiler_params=pltpu.CompilerParams(vmem_limit_bytes=VMEM_LIMIT),
        name="finish",
    )(out, gin, qkv, outw, ffn, vall, ada_weight)


def solution(mesh):
    placed = (
        P(("grp", "mlp"), "seq", None),
        P(("grp", "mlp"), None),
        P(),
        P(),
        P(),
        P(),
        P(),
        P(),
        P(None, "mlp"),
        P("mlp"),
        P("mlp", None),
        P(),
        P(("grp", "mlp"), "seq", None),
    )
    sizes = dict(mesh.shape)
    small = sizes["seq"] == 4 and sizes["grp"] == 2 and sizes["mlp"] == 4
    return jax.shard_map(
        fast_shards if small else shards,
        mesh=mesh,
        in_specs=placed,
        out_specs=(
            P(("grp", "mlp"), "seq", None),
            P(("grp", "mlp"), "seq", None),
            P(("grp", "mlp"), None),
            P("grp"),
            P("grp", None),
            P("grp"),
            P("grp", None),
            P("grp", None),
            P("grp"),
            P("grp", "mlp"),
            P(("grp", "mlp")),
            P(("grp", "mlp"), None),
            P("grp"),
        ),
        check_vma=False,
    )
```

```python
import math

import jax
import jax.numpy as jnp
import numpy as np
from jax import lax
from jax.experimental import pallas as pl
from jax.experimental.pallas import tpu as pltpu
from jax.sharding import PartitionSpec as P

HEADS = 12
VMEM_LIMIT = 63 * 2**20


gelu_coef = 0.7978845608028654


def layer_norm(values):
    center = values - jnp.mean(values, axis=-1, keepdims=True)
    inv_std = lax.rsqrt(jnp.mean(center * center, axis=-1, keepdims=True) + 1e-05)
    return (center * inv_std, inv_std)


def norm_back(grad_norm, normed, inv_std):
    return inv_std * (
        grad_norm
        - jnp.mean(grad_norm, axis=-1, keepdims=True)
        - normed * jnp.mean(grad_norm * normed, axis=-1, keepdims=True)
    )


def gelu_tanh(values):
    return (
        0.5 * values * (1.0 + jnp.tanh(gelu_coef * (values + 0.044715 * values * values * values)))
    )


def gelu_slope(values):
    tanh_val = jnp.tanh(gelu_coef * (values + 0.044715 * values * values * values))
    return 0.5 * (1.0 + tanh_val) + 0.5 * values * (1.0 - tanh_val * tanh_val) * gelu_coef * (
        1.0 + 3.0 * 0.044715 * values * values
    )


def rotary_tables(positions, head_size):
    half_dim = head_size // 2
    frequencies = jnp.power(10000.0, -2.0 * jnp.arange(half_dim, dtype=jnp.float32) / head_size)
    angles = positions[:, None] * frequencies[None, :]
    return (jnp.cos(angles), jnp.sin(angles))


def rotate(tensor, cos_tab, sine_tab):
    half_dim = tensor.shape[-1] // 2
    first_half = tensor[..., :half_dim]
    second_half = tensor[..., half_dim:]
    return jnp.concatenate(
        [
            first_half * cos_tab - second_half * sine_tab,
            second_half * cos_tab + first_half * sine_tab,
        ],
        axis=-1,
    )


def unrotate(tensor, cos_tab, sine_tab):
    half_dim = tensor.shape[-1] // 2
    first_half = tensor[..., :half_dim]
    second_half = tensor[..., half_dim:]
    return jnp.concatenate(
        [
            first_half * cos_tab + second_half * sine_tab,
            second_half * cos_tab - first_half * sine_tab,
        ],
        axis=-1,
    )


def score_of(query_rows, key_rows, scale_factor):
    return (
        jnp.einsum("sghd,skhd->shgk", query_rows, key_rows, preferred_element_type=jnp.float32)
        * scale_factor
    )


def score_grads(query_rows, dout_rows, lse_rows, delta_rows, key_rows, value_rows, scale_factor):
    prob_rows = jnp.exp(score_of(query_rows, key_rows, scale_factor) - lse_rows[..., None])
    grad_probs = jnp.einsum(
        "sghd,skhd->shgk", dout_rows, value_rows, preferred_element_type=jnp.float32
    )
    grad_scores = (prob_rows * (grad_probs - delta_rows[..., None])).astype(jnp.bfloat16)
    return (prob_rows.astype(jnp.bfloat16), grad_scores)


def shards(
    inputs,
    condition,
    attn_gain,
    ada_weight,
    ada_bias,
    qkv_weight,
    out_weight,
    ffn_gain,
    up_weight,
    up_bias,
    down_weight,
    down_bias,
    cotangent,
):
    seq_count, seg_len, model_width = inputs.shape
    head_count = HEADS
    head_size = model_width // head_count
    full_len = seg_len * lax.axis_size("seq")
    block_len = math.gcd(full_len, 512)
    block_count = full_len // block_len
    scale_factor = float(head_size) ** (-0.5)
    positions = (lax.axis_index("seq") * seg_len + jnp.arange(seg_len, dtype=jnp.int32)).astype(
        jnp.float32
    )
    cos_tab, sine_tab = rotary_tables(positions, head_size)
    cos_tab = cos_tab[None, :, None, :]
    sine_tab = sine_tab[None, :, None, :]

    def heads_view(matrix):
        return matrix.reshape(seq_count, seg_len, head_count, head_size)

    x_float = inputs.astype(jnp.float32)
    modulate = jnp.dot(condition, ada_weight, preferred_element_type=jnp.float32) + ada_bias
    shift_one, scale_one, gate_one, shift_two, scale_two, gate_two = [
        modulate[:, None, member * model_width : (member + 1) * model_width] for member in range(6)
    ]
    norm_one, inv_one = layer_norm(x_float)
    attn_in = (norm_one * attn_gain * (1.0 + scale_one) + shift_one).astype(jnp.bfloat16)
    projected = jnp.dot(attn_in, qkv_weight, preferred_element_type=jnp.float32)
    queries = rotate(heads_view(projected[..., :model_width]), cos_tab, sine_tab).astype(
        jnp.bfloat16
    )
    key_rot = rotate(
        heads_view(projected[..., model_width : 2 * model_width]), cos_tab, sine_tab
    ).astype(jnp.bfloat16)
    value_low = projected[..., 2 * model_width :].astype(jnp.bfloat16)
    kv_local = jnp.concatenate(
        [key_rot.reshape(seq_count, seg_len, model_width), value_low], axis=-1
    )
    kv_whole = lax.all_gather(kv_local, "seq", axis=1, tiled=True)
    kv_view = kv_whole.reshape(seq_count, full_len, 2, head_count, head_size)

    def key_block(block_num):
        sliced = lax.dynamic_slice_in_dim(kv_view, block_num * block_len, block_len, 1)
        return (sliced[:, :, 0], sliced[:, :, 1])

    def max_pass(block_num, running):
        run_max, run_sum = running
        key_rows, value_rows = key_block(block_num)
        scores = score_of(queries, key_rows, scale_factor)
        new_max = jnp.maximum(run_max, jnp.max(scores, axis=-1))
        run_sum = run_sum * jnp.exp(run_max - new_max) + jnp.sum(
            jnp.exp(scores - new_max[..., None]), axis=-1
        )
        return (new_max, run_sum)

    stat_shape = (seq_count, head_count, seg_len)
    run_max, run_sum = lax.fori_loop(
        0,
        block_count,
        max_pass,
        (jnp.full(stat_shape, -1e30, jnp.float32), jnp.zeros(stat_shape, jnp.float32)),
    )
    log_sum = run_max + jnp.log(run_sum)

    def out_pass(block_num, accums):
        accum_out, accum_exact = accums
        key_rows, value_rows = key_block(block_num)
        prob_rows = jnp.exp(score_of(queries, key_rows, scale_factor) - log_sum[..., None])
        accum_out = accum_out + jnp.einsum(
            "shgk,skhd->sghd",
            prob_rows.astype(jnp.bfloat16),
            value_rows,
            preferred_element_type=jnp.float32,
        )
        accum_exact = accum_exact + jnp.einsum(
            "shgk,skhd->sghd",
            prob_rows,
            value_rows.astype(jnp.float32),
            preferred_element_type=jnp.float32,
        )
        return (accum_out, accum_exact)

    head_shape = (seq_count, seg_len, head_count, head_size)
    attn_float, attn_exact = lax.fori_loop(
        0,
        block_count,
        out_pass,
        (jnp.zeros(head_shape, jnp.float32), jnp.zeros(head_shape, jnp.float32)),
    )
    attn_low = attn_float.reshape(seq_count, seg_len, model_width).astype(jnp.bfloat16)
    attn_proj = jnp.dot(attn_low, out_weight, preferred_element_type=jnp.float32)
    middle = x_float + gate_one * attn_proj
    norm_two, inv_two = layer_norm(middle)
    ffn_in = (norm_two * ffn_gain * (1.0 + scale_two) + shift_two).astype(jnp.bfloat16)
    ffn_rows = lax.all_gather(ffn_in, "mlp", axis=0, tiled=True)
    pre_act = jnp.dot(ffn_rows, up_weight, preferred_element_type=jnp.float32) + up_bias
    act_low = gelu_tanh(pre_act).astype(jnp.bfloat16)
    ffn_out = (
        lax.psum_scatter(
            jnp.dot(act_low, down_weight, preferred_element_type=jnp.float32).astype(jnp.bfloat16),
            "mlp",
            scatter_dimension=0,
            tiled=True,
        ).astype(jnp.float32)
        + down_bias
    )
    output = middle + gate_two * ffn_out
    cot_float = cotangent.astype(jnp.float32)
    grad_ffn = (gate_two * cot_float).astype(jnp.bfloat16)
    down_bias_part = jnp.sum(grad_ffn.astype(jnp.float32), axis=(0, 1))
    dgate_two = jnp.sum(cot_float * ffn_out, axis=1)
    grad_ffn_rows = lax.all_gather(grad_ffn, "mlp", axis=0, tiled=True)
    down_part = jnp.einsum(
        "sgf,sgd->fd", act_low, grad_ffn_rows, preferred_element_type=jnp.float32
    )
    grad_act = jnp.einsum(
        "sgd,fd->sgf", grad_ffn_rows, down_weight, preferred_element_type=jnp.float32
    )
    grad_pre = (grad_act * gelu_slope(pre_act)).astype(jnp.bfloat16)
    up_bias_part = jnp.sum(grad_pre.astype(jnp.float32), axis=(0, 1))
    up_part = jnp.einsum("sgd,sgf->df", ffn_rows, grad_pre, preferred_element_type=jnp.float32)
    grad_ffn_in = lax.psum_scatter(
        jnp.einsum("sgf,df->sgd", grad_pre, up_weight, preferred_element_type=jnp.float32).astype(
            jnp.bfloat16
        ),
        "mlp",
        scatter_dimension=0,
        tiled=True,
    ).astype(jnp.float32)
    dshift_two = jnp.sum(grad_ffn_in, axis=1)
    dscale_two = jnp.sum(grad_ffn_in * norm_two * ffn_gain, axis=1)
    gain_two_part = jnp.sum(grad_ffn_in * (1.0 + scale_two) * norm_two, axis=(0, 1))
    grad_middle = cot_float + norm_back(
        grad_ffn_in * (1.0 + scale_two) * ffn_gain, norm_two, inv_two
    )
    grad_proj = (gate_one * grad_middle).astype(jnp.bfloat16)
    dgate_one = jnp.sum(grad_middle * attn_proj, axis=1)
    out_part = jnp.einsum("sgd,sge->de", attn_low, grad_proj, preferred_element_type=jnp.float32)
    grad_attn = jnp.einsum(
        "sge,de->sgd", grad_proj, out_weight, preferred_element_type=jnp.float32
    ).astype(jnp.bfloat16)
    grad_attn_heads = heads_view(grad_attn)
    delta_rows = jnp.sum(grad_attn_heads.astype(jnp.float32) * attn_exact, axis=-1)
    delta_heads = jnp.transpose(delta_rows, (0, 2, 1))

    def back_pass(block_num, state_in):
        grad_query, key_grads = state_in
        key_rows, value_rows = key_block(block_num)
        prob_low, grad_scores = score_grads(
            queries, grad_attn_heads, log_sum, delta_heads, key_rows, value_rows, scale_factor
        )
        grad_query = (
            grad_query
            + jnp.einsum(
                "shgk,skhd->sghd", grad_scores, key_rows, preferred_element_type=jnp.float32
            )
            * scale_factor
        )
        grad_key = (
            jnp.einsum("shgk,sghd->skhd", grad_scores, queries, preferred_element_type=jnp.float32)
            * scale_factor
        )
        grad_value = jnp.einsum(
            "shgk,sghd->skhd", prob_low, grad_attn_heads, preferred_element_type=jnp.float32
        )
        stacked = jnp.concatenate(
            [
                grad_key.reshape(seq_count, block_len, model_width),
                grad_value.reshape(seq_count, block_len, model_width),
            ],
            axis=-1,
        )
        key_grads = lax.dynamic_update_slice_in_dim(key_grads, stacked, block_num * block_len, 1)
        return (grad_query, key_grads)

    grad_query, key_grads = lax.fori_loop(
        0,
        block_count,
        back_pass,
        (
            jnp.zeros(head_shape, jnp.float32),
            jnp.zeros((seq_count, full_len, 2 * model_width), jnp.float32),
        ),
    )
    kv_grads = lax.psum_scatter(
        key_grads.astype(jnp.bfloat16), "seq", scatter_dimension=1, tiled=True
    ).astype(jnp.float32)
    grad_key_rot = heads_view(kv_grads[..., :model_width])
    grad_values = kv_grads[..., model_width:]
    grad_qkv = jnp.concatenate(
        [
            unrotate(grad_query, cos_tab, sine_tab).reshape(seq_count, seg_len, model_width),
            unrotate(grad_key_rot, cos_tab, sine_tab).reshape(seq_count, seg_len, model_width),
            grad_values,
        ],
        axis=-1,
    ).astype(jnp.bfloat16)
    qkv_part = jnp.einsum("sgd,sge->de", attn_in, grad_qkv, preferred_element_type=jnp.float32)
    grad_attn_in = jnp.einsum(
        "sge,de->sgd", grad_qkv, qkv_weight, preferred_element_type=jnp.float32
    )
    dshift_one = jnp.sum(grad_attn_in, axis=1)
    dscale_one = jnp.sum(grad_attn_in * norm_one * attn_gain, axis=1)
    gain_one_part = jnp.sum(grad_attn_in * (1.0 + scale_one) * norm_one, axis=(0, 1))
    grad_inputs = grad_middle + norm_back(
        grad_attn_in * (1.0 + scale_one) * attn_gain, norm_one, inv_one
    )
    grad_modulate = jnp.concatenate(
        [dshift_one, dscale_one, dgate_one, dshift_two, dscale_two, dgate_two], axis=-1
    )
    ada_weight_part = jnp.dot(
        condition.astype(jnp.float32).T, grad_modulate, precision=lax.Precision.HIGHEST
    )
    ada_bias_part = jnp.sum(grad_modulate, axis=0)
    cond_part = jnp.dot(
        grad_modulate, ada_weight.astype(jnp.float32).T, precision=lax.Precision.HIGHEST
    )
    summed_all = lax.psum(
        (
            qkv_part,
            out_part,
            ada_weight_part,
            ada_bias_part,
            gain_one_part,
            gain_two_part,
            down_bias_part,
        ),
        ("seq", "mlp"),
    )
    summed_seq = (
        lax.psum(up_part.astype(jnp.bfloat16), "seq").astype(jnp.float32),
        lax.psum(up_bias_part.astype(jnp.bfloat16), "seq").astype(jnp.float32),
        lax.psum(down_part.astype(jnp.bfloat16), "seq").astype(jnp.float32),
        lax.psum(cond_part.astype(jnp.bfloat16), "seq").astype(jnp.float32),
    )
    return (
        output,
        grad_inputs,
        summed_seq[3],
        summed_all[4],
        summed_all[2],
        summed_all[3],
        summed_all[0],
        summed_all[1],
        summed_all[5],
        summed_seq[0],
        summed_seq[1],
        summed_seq[2],
        summed_all[6],
    )


FFN_X, FFN_Z, FFN_OWN, FFN_LAST, SUM_0, REL, SUM_3, SUM_4, FW, SUM_7, WL, WR, XS_, ZS, XO, OX, GX, WD_, SUM_8, WX = range(20)
AT_W, AT_F, AT_A, AT_T, AT_N, AT_B, AT_E, AT_D, AT_G = range(9)
ORDERS = ((0, 1, 2, 3), (1, 0, 2, 3), (2, 3, 1, 0), (3, 2, 1, 0))
OWN_STEP = 0
PLAN = {(AT_A, 0, 0): {0: [(WX, 1)], 1: [(WX, 0)], 2: [(WX, 1)], 3: [(WX, 2)]},
 (AT_A, 1, 0): {1: [(WX, 2)], 2: [(WX, 3)]},
 (AT_A, 1, 1): {0: [(WR, 2), (WX, 2)], 1: [(WR, 2)], 2: [(WL, 2)], 3: [(WL, 2), (WX, 1)]},
 (AT_A, 2, 1): {0: [(WD_, 1)], 1: [(WD_, 0)], 2: [(WD_, 1)], 3: [(WD_, 2)]},
 (AT_B, 0, 0): {0: [(XS_, 2, 1)],
                1: [(XS_, 3, 2), (FFN_X, 3, 0)],
                2: [(XS_, 0, 2), (FFN_X, 0, 0), (FFN_Z, 0, 0), (ZS, 0, 0)],
                3: [(XS_, 1, 1)]},
 (AT_B, 0, 1): {0: [(FFN_X, 3, 2), (XS_, 2, 2)],
                1: [(FFN_Z, 3, 0), (ZS, 3, 0), (XS_, 2, 0), (FFN_X, 3, 1)],
                2: [(XS_, 1, 0), (FFN_X, 0, 1), (REL, 1, 0, 0)],
                3: [(FFN_X, 0, 2), (XS_, 1, 2)]},
 (AT_B, 0, 5): {0: [(ZS, 3, 1), (SUM_0, 1)], 3: [(ZS, 0, 1), (SUM_0, 1)]},
 (AT_B, 1, 0): {0: [(XS_, 1, 1), (FFN_X, 2, 1)],
                1: [(REL, 0, 3, 0), (XS_, 2, 1), (FFN_X, 3, 2)],
                2: [(REL, 1, 1, 0), (XS_, 1, 1), (FFN_X, 0, 2)],
                3: [(XS_, 2, 1), (FFN_X, 1, 1)]},
 (AT_B, 1, 1): {0: [(FFN_OWN, 0), (XO, 0), (FFN_X, 2, 2)],
                1: [(REL, 0, 2, 0), (XS_, 2, 2), (FFN_X, 2, 0), (FFN_Z, 2, 0), (ZS, 2, 0)],
                2: [(REL, 0, 3, 0), (XS_, 1, 2), (FFN_X, 1, 0), (FFN_Z, 1, 0), (ZS, 1, 0)],
                3: [(XS_, 2, 2), (FFN_X, 1, 2)]},
 (AT_B, 1, 5): {0: [(SUM_0, 2)],
                1: [(REL, 1, 0, 0)],
                2: [(FFN_Z, 0, 1), (SUM_3, 0), (ZS, 0, 1)],
                3: [(FFN_OWN, 0), (SUM_0, 2)]},
 (AT_B, 2, 0): {0: [(XS_, 1, 2), (FFN_X, 1, 1)],
                1: [(XS_, 1, 1), (FFN_X, 2, 1)],
                2: [(FFN_OWN, 0), (XO, 0), (REL, 1, 0, 1), (FFN_X, 1, 1)],
                3: [(XO, 0), (FFN_X, 2, 1)]},
 (AT_B, 2, 1): {0: [(FFN_LAST, 0), (SUM_3, 0)],
                1: [(FFN_Z, 3, 1), (SUM_3, 0), (ZS, 3, 1), (FFN_X, 2, 2)],
                2: [(REL, 1, 1, 1), (FFN_X, 1, 2)],
                3: [(XS_, 3, 1), (FFN_X, 2, 2)]},
 (AT_B, 2, 5): {0: [(SUM_0, 3), (XS_, 0, 1)],
                1: [(REL, 0, 3, 1), (FFN_OWN, 0), (XO, 0)],
                2: [(SUM_4, 0), (XS_, 2, 1)],
                3: [(SUM_3, 0), (SUM_0, 3)]},
 (AT_B, 3, 1): {1: [(REL, 0, 2, 1), (FFN_X, 1, 1)]},
 (AT_B, 3, 2): {0: [(FFN_X, 1, 2)],
                1: [(SUM_4, 0), (XS_, 1, 2)],
                2: [(FFN_LAST, 0), (XS_, 2, 2)],
                3: [(FFN_LAST, 0)]},
 (AT_B, 3, 3): {0: [(SUM_4, 0), (XS_, 0, 2)], 2: [(REL, 1, 0, 2), (REL, 0, 3, 1)], 3: [(XS_, 3, 2)]},
 (AT_D, 0): {0: [(FFN_X, 0, 2), (XO, 1), (SUM_3, 1), (GX, 1), (SUM_3, 2), (FFN_LAST, 1), (SUM_4, 1), (ZS, 3, 2),
                 (OX, 0), (SUM_3, 3), (SUM_4, 2), (ZS, 2, 1), (OX, 1), (SUM_4, 3), (SUM_7, 0), (FFN_OWN, 2),
                 (ZS, 2, 2), (ZS, 1, 1), (XO, 2), (SUM_8, 0), (ZS, 1, 2), (SUM_7, 1), (SUM_7, 2), (FFN_LAST, 2),
                 (SUM_7, 3), (SUM_8, 1)],
             1: [(REL, 0, 2, 2), (SUM_3, 1), (FFN_X, 1, 2), (FW, 3, 2, 0), (REL, 1, 0, 2), (GX, 1), (REL, 0, 3, 3),
                 (SUM_4, 1), (SUM_3, 2), (REL, 0, 2, 3), (OX, 0), (REL, 1, 0, 3), (FW, 2, 0, 0), (SUM_4, 2),
                 (SUM_3, 3), (FW, 2, 0, 1), (FW, 3, 2, 1), (FW, 3, 3, 0), (SUM_7, 0), (FW, 3, 3, 1), (FFN_Z, 3, 2),
                 (ZS, 3, 2), (SUM_4, 3), (FW, 3, 2, 2), (FW, 2, 0, 2), (SUM_7, 1), (SUM_8, 0), (FFN_Z, 2, 1),
                 (FW, 3, 3, 2), (SUM_7, 2), (ZS, 2, 1), (OX, 1), (FW, 2, 0, 3), (FW, 3, 2, 3), (SUM_8, 1),
                 (FFN_Z, 2, 2), (ZS, 2, 2), (FFN_OWN, 1), (XO, 1), (FW, 3, 3, 3), (SUM_7, 3), (FFN_OWN, 2), (XO, 2),
                 (FFN_LAST, 1), (FFN_LAST, 2)],
             2: [(REL, 0, 3, 2), (FFN_X, 2, 2), (REL, 1, 0, 3), (GX, 1), (REL, 1, 1, 3), (SUM_3, 2), (SUM_4, 1),
                 (REL, 0, 3, 3), (FW, 3, 3, 0), (FW, 2, 1, 1), (OX, 0), (FW, 3, 3, 1), (SUM_3, 3), (SUM_4, 2),
                 (FW, 2, 0, 0), (FFN_Z, 0, 2), (ZS, 0, 2), (FW, 2, 1, 2), (SUM_7, 0), (FW, 2, 0, 1), (FW, 3, 3, 2),
                 (SUM_4, 3), (FFN_Z, 1, 1), (SUM_7, 1), (FW, 2, 1, 3), (ZS, 1, 1), (FW, 3, 3, 3), (SUM_8, 0),
                 (FW, 2, 0, 2), (SUM_7, 2), (OX, 1), (FFN_Z, 1, 2), (SUM_8, 1), (ZS, 1, 2), (FFN_OWN, 1), (XO, 1),
                 (FW, 2, 0, 3), (SUM_7, 3), (FFN_OWN, 2), (XO, 2), (FFN_LAST, 1), (FFN_LAST, 2)],
             3: [(FFN_X, 3, 2), (SUM_3, 1), (XO, 1), (SUM_4, 1), (GX, 1), (SUM_3, 2), (FFN_LAST, 1), (ZS, 0, 2),
                 (OX, 0), (SUM_3, 3), (SUM_4, 2), (ZS, 1, 1), (OX, 1), (SUM_4, 3), (SUM_7, 0), (FFN_OWN, 2),
                 (ZS, 1, 2), (ZS, 2, 1), (XO, 2), (SUM_8, 0), (ZS, 2, 2), (SUM_7, 1), (FFN_LAST, 2), (SUM_7, 2),
                 (SUM_7, 3), (SUM_8, 1)]},
 (AT_E, 1): {0: [(GX, 0), (FFN_X, 0, 1), (FFN_OWN, 1)],
             1: [(REL, 0, 3, 2), (FFN_LAST, 0), (GX, 0), (REL, 1, 0, 1)],
             2: [(REL, 1, 1, 2), (GX, 0), (SUM_3, 1), (FFN_X, 2, 1), (FW, 2, 1, 0)],
             3: [(SUM_4, 0), (GX, 0), (FFN_X, 3, 1), (FFN_OWN, 1)]},
 (AT_G, 1): {0: [(WD_, 3)], 3: [(WD_, 0)]},
 (AT_G, 2): {1: [(XS_, 0, 1), (FFN_X, 1, 0)], 2: [(XS_, 3, 1), (FFN_X, 2, 0)]},
 (AT_G, 3): {0: [(XS_, 3, 0), (FFN_X, 1, 0), (ZS, 1, 0)], 3: [(XS_, 0, 0), (FFN_X, 2, 0), (ZS, 2, 0)]},
 (AT_N, 1): {0: [(XS_, 3, 1), (FFN_X, 2, 0), (ZS, 2, 0)],
             1: [(XS_, 3, 0), (FFN_X, 0, 1), (ZS, 0, 1)],
             2: [(XS_, 0, 0), (FFN_X, 3, 1), (ZS, 3, 1), (FFN_X, 3, 2), (ZS, 3, 2)],
             3: [(XS_, 0, 1), (FFN_X, 1, 0), (ZS, 1, 0)]},
 (AT_N, 2): {0: [(XS_, 3, 2), (FFN_X, 3, 0), (ZS, 3, 0)],
             1: [(XS_, 3, 1), (FFN_X, 0, 2), (ZS, 0, 2)],
             2: [(XS_, 0, 1)],
             3: [(XS_, 0, 2), (FFN_X, 0, 0), (ZS, 0, 0)]},
 (AT_N, 4): {0: [(SUM_0, 0), (FFN_X, 3, 1)], 3: [(SUM_0, 0), (FFN_X, 0, 1)]},
 (AT_T, 0, 0): {0: [(WR, 3), (WD_, 2)], 3: [(WL, 3), (WD_, 1)]},
 (AT_T, 0, 1): {0: [(WX, 3)], 1: [(WD_, 2)], 2: [(WD_, 3)], 3: [(WX, 0)]},
 (AT_T, 1, 0): {0: [(XS_, 0, 0)], 1: [(WD_, 3)], 2: [(WD_, 0)], 3: [(XS_, 3, 0)]},
 (AT_T, 1, 1): {1: [(XS_, 1, 0)], 2: [(XS_, 2, 0)]},
 (AT_T, 2, 0): {1: [(XS_, 0, 0)], 2: [(XS_, 3, 0)]},
 (AT_T, 2, 1): {0: [(XS_, 1, 0), (FFN_X, 0, 0)], 3: [(XS_, 2, 0), (FFN_X, 3, 0)]},
 (AT_T, 3, 0): {0: [(XS_, 2, 0)], 3: [(XS_, 1, 0)]},
 (AT_T, 3, 1): {1: [(XS_, 0, 2), (FFN_X, 0, 0), (ZS, 0, 0)], 2: [(XS_, 3, 2), (FFN_X, 3, 0), (ZS, 3, 0)]},
 (AT_W, 0): {0: [(WR, 1)], 1: [(WL, 1), (WR, 1)], 2: [(WL, 1), (WR, 1)], 3: [(WL, 1)]},
 (AT_W, 4): {1: [(WX, 3)], 2: [(WX, 0)]}}
HALF = (1, 1, 0, 0)


BF = jnp.bfloat16
F32 = jnp.float32
MESH = pl.DeviceIdType.MESH


def dot(a, b):
    return jnp.dot(a, b, preferred_element_type=F32)


def dot_t(a, b):
    return lax.dot_general(a, b, (((1,), (1,)), ((), ())), preferred_element_type=F32)


def rows_of(start, size):
    return pl.ds(pl.multiple_of(start, size), size)


def pick(table, index):
    value = table[0]
    for place in range(1, len(table)):
        value = jnp.where(index == place, table[place], value)
    return value


def swap_halves(tile):
    lane = lax.broadcasted_iota(jnp.int32, tile.shape, 1)
    return jnp.where(
        lane % 64 < 32, pltpu.roll(tile, 96, 1), pltpu.roll(tile, 32, 1)
    )


def fast_kernel(
    inputs, cond, again, adaw_h, adab, qkv_h, outw_h, fgain, up_h, upb, down_h, downb, cot_h,
    cos_h, sin_h, cost_h, sint_h,
    out_o, gin_o, qkv_o, outw_o, ffn_o, vall_o,
    wq, wo, wu, wd, ub, cos_v, sin_v, cost, sint,
    xb, ctb, mod2, n1, inv_s, ai, ait, q_s, k_s, v_s, kt_s, vt_s, ot_s, lse, att,
    ap, n2, fit, gf, gft, oacc, gacc, a_s, gp_s, g_s, grecv,
    do_s, dlt, dqt, gq, b_s, xs, vec, vecr, late, later, vall, ubg,
    rx, rz, fxr, rxb, fb,
    lsem, ssem, rsem, wss, wrs, yss, yrs, fss, frs, bss, brs, hss, hrs, vss, vrs, credit,
):
    Z = 4
    grp = lax.axis_index("grp")
    seq = lax.axis_index("seq")
    z = lax.axis_index("mlp")
    x, c = seq // 2, seq % 2
    D = 768
    flat = lambda ref: ref[...].reshape(1, -1)
    again, adab, fgain, downb = flat(again), flat(adab), flat(fgain), flat(downb)
    own = c * 512
    other = (1 - c) * 512
    TO_CORE = {"seq": x * 2 + (1 - c)}
    TO_X = {"seq": (1 - x) * 2 + c}
    TO_Y = {"grp": 1 - grp}
    RIGHT = {"mlp": jnp.minimum(z + 1, Z - 1)}
    LEFT = {"mlp": jnp.maximum(z - 1, 0)}

    def remote(src, dst, index, device):
        return pltpu.make_async_remote_copy(
            src_ref=src, dst_ref=dst, send_sem=ssem.at[index], recv_sem=rsem.at[index],
            device_id=device, device_id_type=MESH,
        )

    def local(src, dst, index):
        return pltpu.make_async_copy(src, dst, lsem.at[index])

    half = pl.ds(pl.multiple_of(c * 384, 128), 384)
    loads = [local(inputs.at[x], xb.at[rows_of(x * 256, 256)], 0), ]
    loads += [local(cos_h, cos_v, 2), local(sin_h, sin_v, 3), local(cost_h, cost, 4), local(sint_h, sint, 5)]
    for p in range(3):
        for part in range(3):
            loads.append(
                local(
                    qkv_h.at[:, pl.ds(pl.multiple_of(part * D + c * 384 + p * 128, 128), 128)],
                    wq.at[p, :, pl.ds(part * 128, 128)],
                    6 + p * 3 + part,
                )
            )
    loads.append(local(outw_h, wo, 15))
    loads.append(local(up_h.at[:, half], wu.at[z], 16))
    loads.append(local(down_h.at[rows_of(c * 384, 384)], wd.at[z], 17))
    loads.append(local(cot_h.at[x], ctb.at[rows_of(x * 256, 256)], 18))
    adaw = [
        local(adaw_h.at[:, pl.ds(part * D, D)], fit.at[pl.ds(part * 128, 128), pl.ds(0, D)], 15 + 43 + part)
        for part in range(6)
    ]
    for item in [loads[0]] + adaw + loads[1:]:
        item.start()

    ub[z] = flat(upb)

    barrier = pltpu.get_barrier_semaphore()
    peers = [{"seq": (x ^ dx) * 2 + c, "mlp": z ^ dz} for dx in range(2) for dz in range(Z) if dx or dz]
    for device in [TO_CORE, TO_Y] + peers:
        pl.semaphore_signal(barrier, 1, device_id=device, device_id_type=MESH)
    pl.semaphore_wait(barrier, 2 + len(peers))

    swap_x = remote(inputs.at[1 - x], xb.at[rows_of(x * 256, 256)], 0, TO_X)
    swap_x.start()
    swap_c = remote(cot_h.at[1 - x], ctb.at[rows_of(x * 256, 256)], 1, TO_X)
    swap_c.start()

    def rows_at(ref, rows, which, part=None):
        start = which * rows
        if part is None:
            return ref.at[rows_of(start, rows)]
        return ref.at[pl.ds(pl.multiple_of(start + part * (rows // 2), 16), rows // 2)]

    here = grp * 2 + x

    def z_copies(j, way, device, first):
        own_up, own_down = rows_at(wu.at[j], 192, here), rows_at(wd.at[j], 96, here)
        if first:
            src = (
                up_h.at[rows_of(here * 192, 192), half],
                down_h.at[rows_of(c * 384 + here * 96, 96)],
                ub.at[z],
            )
        else:
            src = (own_up, own_down, ub.at[j])
        dst = (own_up, own_down, ub.at[j])
        return [
            pltpu.make_async_remote_copy(
                src_ref=src[i], dst_ref=dst[i], send_sem=wss.at[way, j, i], recv_sem=wrs.at[way, j, i],
                device_id=device, device_id_type=MESH,
            )
            for i in range(3)
        ]

    def pair_copies(j, kind, which, part, device):
        return [
            pltpu.make_async_remote_copy(
                src_ref=ref, dst_ref=ref, send_sem=yss.at[j, kind, i], recv_sem=yrs.at[j, kind, i],
                device_id=device, device_id_type=MESH,
            )
            for i, ref in enumerate((rows_at(wu.at[j], 192, which, part), rows_at(wd.at[j], 96, which, part)))
        ]

    by_x, by_y, across = grp * 2 + 1 - x, (1 - grp) * 2 + x, (1 - grp) * 2 + 1 - x

    def quarter_sends(j):
        return pair_copies(j, 0, here, None, TO_X) + pair_copies(j, 1, here, None, TO_Y)

    def quarter_waits(j):
        return pair_copies(j, 0, by_x, None, TO_X) + pair_copies(j, 1, by_y, None, TO_Y)

    def across_sends(j):
        return pair_copies(j, 2, by_y, 0, TO_X) + pair_copies(j, 3, by_x, 1, TO_Y)

    def across_waits(j):
        return pair_copies(j, 2, across, 0, TO_X) + pair_copies(j, 3, across, 1, TO_Y)

    def start_all(items):
        for item in items:
            item.start()

    @pl.when(z < Z - 1)
    def _():
        start_all(z_copies(z, 0, RIGHT, True))

    @pl.when(z > 0)
    def _():
        start_all(z_copies(z, 1, LEFT, True))

    def order(n):
        return pick([ORDERS[a][n] for a in range(Z)], z)

    pending = {place: [] for place in range(Z)}
    CH = 3

    def send(place, *makes):
        for make in makes:
            make().start()
            pending[place].append(make)

    def span(h):
        return pl.ds(h * (768 // CH), 768 // CH)

    def ffn_copy(j, h):
        return pltpu.make_async_remote_copy(
            src_ref=g_s.at[1 - x, j, span(h)], dst_ref=rx.at[j, span(h)], send_sem=hss.at[j, h],
            recv_sem=hrs.at[j, h], device_id=TO_X, device_id_type=MESH,
        )

    def add_rows(ref, others):
        @pl.loop(0, 768 // CH // 64)
        def _(i):
            rows = rows_of(i * 64, 64)
            total = ref[rows].astype(F32)
            for other_ref in others:
                total = total + other_ref[rows].astype(F32)
            ref[rows] = total.astype(BF)

    def z_send(j, h, place):
        if place in (0, 3):
            target, slot = (1 if place == 0 else 2), j
        elif j in (0, 3):
            target, slot = j, place
        else:
            target, slot = j, (0 if j == 1 else 3)
        return lambda: pltpu.make_async_remote_copy(
            src_ref=g_s.at[x, j, span(h)], dst_ref=rz.at[slot, span(h)], send_sem=fss.at[j, h],
            recv_sem=frs.at[slot, h], device_id={"mlp": target}, device_id_type=MESH,
        )

    def z_wait(slot, h):
        ref = rz.at[slot, span(h)]
        pltpu.make_async_remote_copy(
            src_ref=ref, dst_ref=ref, send_sem=fss.at[0, h], recv_sem=frs.at[slot, h],
            device_id=LEFT, device_id_type=MESH,
        ).wait_recv()

    def ffn_x(place, j, h):
        ffn_copy(j, h).wait_recv()
        add_rows(g_s.at[x, j, span(h)], [rx.at[j, span(h)]])

    def ffn_z(place, j, h):
        z_wait(j, h)
        add_rows(g_s.at[x, j, span(h)], [rz.at[j, span(h)]])

    def zs(place, j, h):
        send(place, z_send(j, h, place))

    def xs_(place, j, h):
        send(place, lambda: ffn_copy(j, h))

    def final_copies(src, kind, h, first):
        dst = ffn_o.at[kind, span(h), half]
        return [local(src, dst, 21 + first * CH + h), remote(src, dst, 31 + first * CH + h, TO_CORE)]

    def own_copy(h):
        return pltpu.make_async_remote_copy(
            src_ref=g_s.at[x, z, span(h)], dst_ref=fxr.at[span(h)], send_sem=hss.at[5, h],
            recv_sem=hrs.at[5, h], device_id=TO_X, device_id_type=MESH,
        )

    def ffn_own(place, h):
        slots = {0: (1, 2), 3: (1, 2), 1: (1, 0), 2: (2, 3)}[place]
        for slot in slots:
            z_wait(slot, h)
        add_rows(g_s.at[x, place, span(h)], [rz.at[slot, span(h)] for slot in slots])
        for item in final_copies(g_s.at[x, z, span(h)], x, h, 0):
            item.start()

    def xo(place, h):
        own_copy(h).start()

    def ffn_last(place, h):
        own_copy(h).wait_recv()
        for item in final_copies(fxr.at[span(h)], 1 - x, h, 1):
            item.start()

    def quarter(ref, p, q):
        if ref is wd:
            return ref.at[p, pl.ds(q // 2 * 192, 192), pl.ds(q % 2 * 384, 384)]
        return ref.at[p, pl.ds(q * 192, 192)]

    def half_rows(ref, p, q, which):
        return ref.at[p, pl.ds(pl.multiple_of(q * 192 + which * 96, 32), 96)]

    def done_rows(p, q):
        return half_rows(fb, p, q, x) if HALF[p] else quarter(fb, p, q)

    def hop(kind, p, q, place):
        step = 1 if kind in (0, 2) else -1
        return lambda: pltpu.make_async_remote_copy(
            src_ref=quarter(b_s, p, q) if kind < 2 else done_rows(p, q),
            dst_ref=quarter((wu, wd)[kind], p, q) if kind < 2 else done_rows(p, q),
            send_sem=bss.at[kind, p, q],
            recv_sem=brs.at[kind, p, q],
            device_id={"mlp": place + step},
            device_id_type=MESH,
        )

    def hop_wait(kind, p, q):
        dst = quarter((wu, wd)[kind], p, q) if kind < 2 else done_rows(p, q)
        pltpu.make_async_remote_copy(
            src_ref=dst, dst_ref=dst, send_sem=bss.at[kind, p, q], recv_sem=brs.at[kind, p, q],
            device_id=LEFT, device_id_type=MESH,
        ).wait_recv()

    def add_quarter(p, q, refs):
        total = quarter(b_s, p, q)[...].astype(F32)
        for ref in refs:
            total = total + quarter(ref, p, q)[...].astype(F32)
        quarter(b_s, p, q)[...] = total.astype(BF)

    def sum_0(place, p):
        kind, blocks = (0, (3, 2, 1)) if place == 0 else (1, (0, 1, 2))
        send(place, *[hop(kind, p, q, place) for q in blocks])

    def rel(place, kind, q, p):
        hop_wait(kind, p, q)
        add_quarter(p, q, [wd if kind else wu])
        send(place, hop(kind, p, q, place))

    def cross(p, place):
        return lambda: pltpu.make_async_remote_copy(
            src_ref=half_rows(b_s, p, place, 1 - x) if HALF[p] else quarter(b_s, p, place),
            dst_ref=rxb.at[p, pl.ds(0, 96)] if HALF[p] else rxb.at[p],
            send_sem=hss.at[4, p],
            recv_sem=hrs.at[4, p], device_id=TO_X, device_id_type=MESH,
        )

    def sum_3(place, p):
        refs = []
        if place > 0:
            hop_wait(0, p, place)
            refs.append(wu)
        if place < 3:
            hop_wait(1, p, place)
            refs.append(wd)
        add_quarter(p, place, refs)
        send(place, cross(p, place))

    def sum_4(place, p):
        cross(p, place)().wait_recv()
        if HALF[p]:
            total = half_rows(b_s, p, place, x)[...].astype(F32) + rxb[p, :96].astype(F32)
        else:
            total = quarter(b_s, p, place)[...].astype(F32) + rxb[p].astype(F32)
        done_rows(p, place)[...] = total.astype(BF)
        if place < 3:
            send(place, hop(2, p, place, place))
        if place > 0:
            send(place, hop(3, p, place, place))

    def fw(place, kind, q, p):
        hop_wait(kind, p, q)
        send(place, hop(kind, p, q, place))

    def piece_copies(p):
        if p == 0:
            pairs = [
                (fb.at[0, pl.ds(n * 384, 384)], outw_o.at[rows_of(c * 384, 384), pl.ds(n * 384, 384)])
                for n in range(2)
            ]
        else:
            pairs = [
                (
                    fb.at[p, :, pl.ds(part * 128, 128)],
                    qkv_o.at[
                        :, pl.ds(pl.multiple_of(part * D + c * 384 + (p - 1) * 128, 128), 128)
                    ],
                )
                for part in range(3)
            ]
        copies = []
        for n, (src, dst) in enumerate(pairs):
            copies.append(local(src, dst, 43 + p * 3 + n))
            copies.append(remote(src, dst, 18 + p * 3 + n, TO_CORE))
        return copies

    def sum_7(place, p):
        for q in range(4):
            if place == 0 and q > 0:
                hop_wait(3, p, q)
            if place == 3 and q < 3:
                hop_wait(2, p, q)
        if HALF[p]:
            send(place, *[lambda q=q: half_copy(p, q) for q in range(4)])
        else:
            for item in piece_copies(p):
                item.start()

    def half_copy(p, q):
        rows = half_rows(fb, p, q, x)
        return pltpu.make_async_remote_copy(
            src_ref=rows, dst_ref=rows, send_sem=hss.at[6 + p, q], recv_sem=hrs.at[6 + p, q],
            device_id=TO_X, device_id_type=MESH,
        )

    def sum_8(place, p):
        for q in range(4):
            half_copy(p, q).wait_recv()
        for item in piece_copies(p):
            item.start()

    def wl(place, k):
        for item in z_copies(place - k, 0, RIGHT, False):
            item.wait_recv()
        if place < 3:
            start_all(z_copies(place - k, 0, RIGHT, False))
        start_all(pair_copies(place - k, 1, here, None, TO_Y))

    def wr(place, k):
        for item in z_copies(place + k, 1, LEFT, False):
            item.wait_recv()
        if place > 0:
            start_all(z_copies(place + k, 1, LEFT, False))
        start_all(pair_copies(place + k, 1, here, None, TO_Y))

    def wx(place, j):
        start_all(pair_copies(j, 0, here, None, TO_X))

    def wd_(place, j):
        for item in quarter_waits(j):
            item.wait_recv()
        start_all(across_sends(j))

    def cross_rows(out_ref, number, part):
        rows = rows_of((1 - x) * 256 + part * 128, 128)
        return remote(
            xs.at[number, rows], out_ref.at[x, pl.ds(part * 128, 128)], 12 + number * 2 + part, TO_X
        )

    def ox(place, part):
        cross_rows(out_o, 0, part).start()

    def gx(place, part):
        cross_rows(gin_o, 1, part).start()

    jobs = (ffn_x, ffn_z, ffn_own, ffn_last, sum_0, rel, sum_3, sum_4, fw, sum_7, wl, wr, xs_, zs, xo, ox, gx, wd_, sum_8, wx)

    def slot(name, here=None):
        for place, names in PLAN.get(name, {}).items():
            @pl.when(z == place if here is None else (z == place) & here)
            def _(place=place, names=names):
                for job, *rest in names:
                    jobs[job](place, *rest)

    for part in range(6):
        lanes = pl.ds(part * D, D)
        adaw[part].wait()
        mod2[:, lanes] = dot(cond[...], fit[part * 128 : (part + 1) * 128, :D]) + adab[:, part * D : (part + 1) * D]
    modrow = mod2[pl.ds(x, 1), :]
    shift_one, scale_one, gate_one, shift_two, scale_two, gate_two = [
        modrow[:, part * D : (part + 1) * D] for part in range(6)
    ]

    def layer_norm(values):
        center = values - jnp.mean(values, axis=-1, keepdims=True)
        inv = lax.rsqrt(jnp.mean(center * center, axis=-1, keepdims=True) + 1e-05)
        return center * inv, inv

    TILE = 64
    mul_one = again * (1.0 + scale_one)
    mul_two = fgain * (1.0 + scale_two)

    def norm_one_block(block):
        @pl.loop(0, 256 // TILE)
        def _(i):
            at = block * 256 + i * TILE
            rows = rows_of(at, TILE)
            normed, inv = layer_norm(xb[rows].astype(F32))
            n1[rows] = normed
            inv_s[rows, 0:1] = inv
            ai[rows_of(own + at, TILE)] = (normed * mul_one + shift_one).astype(BF)

    def core_rows(ref, start, size, index):
        part = ref.at[rows_of(start, size)]
        return remote(part, part, index, TO_CORE)

    for item in loads[1:14]:
        item.wait()

    def project_rows(start):
        rows = rows_of(start, 256)
        tile = ai[rows]
        cos_t, sin_t = cos_v[rows], sin_v[rows]

        @pl.loop(0, 3)
        def _(p):
            projected = dot(tile, wq[p])
            query = projected[:, :128]
            key = projected[:, 128:256]
            value = projected[:, 256:].astype(BF)
            query = (query * cos_t + swap_halves(query) * sin_t).astype(BF)
            key = (key * cos_t + swap_halves(key) * sin_t).astype(BF)
            q_s[p, rows] = query * jnp.asarray(0.125, BF)
            k_s[p, rows] = key
            v_s[p, rows] = value
            kt_s[p, :, rows] = key.T
            vt_s[p, :, rows] = value.T

        ait[:, rows] = tile.T

    loads[0].wait()
    norm_one_block(x)
    core_rows(ai, own + x * 256, 256, 2).start()
    project_rows(own + x * 256)
    core_rows(ai, other + x * 256, 256, 2).wait_recv()
    project_rows(other + x * 256)
    slot((AT_W, 5))
    swap_x.wait_recv()
    norm_one_block(1 - x)
    core_rows(ai, own + (1 - x) * 256, 256, 3).start()
    project_rows(own + (1 - x) * 256)
    core_rows(ai, other + (1 - x) * 256, 256, 3).wait_recv()
    project_rows(other + (1 - x) * 256)
    for item in loads[15:17]:
        item.wait()
    slot((AT_W, 0))

    att_s = a_s.at[pl.ds(0, 512)]
    low_lane = lax.broadcasted_iota(jnp.int32, (1, 128), 1) < 64
    keep = [low_lane.astype(F32).astype(BF), (~low_lane).astype(F32).astype(BF)]

    def att_copy(p, start):
        return remote(
            att_s.at[:, pl.ds(p * 128, 128)],
            att.at[:, pl.ds(pl.multiple_of(c * 384 + p * 128, 128), 128)],
            4 + p,
            TO_CORE,
        )

    def attend(p):
        @pl.loop(0, 2)
        def _(t):
            cols = rows_of(t * 512, 512)
            query = q_s[p, cols]
            outs = []
            for h in range(2):
                masked = query * keep[h]
                held = (oacc, gacc)[h]
                top = None
                for i in range(4):
                    keys = pl.ds(i * 256, 256)
                    scores = dot_t(k_s[p, keys], masked)
                    held[keys, :512] = scores
                    top = scores if top is None else jnp.maximum(top, scores)
                top = jnp.max(top, axis=0, keepdims=True)
                out, total = None, None
                for i in range(4):
                    keys = pl.ds(i * 256, 256)
                    expd = jnp.exp(held[keys, :512] - top)
                    part = dot(vt_s[p, pl.ds(h * 64, 64), keys], expd.astype(BF))
                    out = part if out is None else out + part
                    total = expd if total is None else total + expd
                total = jnp.sum(total, axis=0, keepdims=True)
                lse[p, pl.ds(h, 1), cols] = top + jnp.log(total)
                out = out / total
                ot_s[p, pl.ds(h * 64, 64), cols] = out
                outs.append(out)
            natural = jnp.concatenate(outs, axis=0).T.astype(BF)
            lanes = pl.ds(pl.multiple_of(c * 384 + p * 128, 128), 128)

            @pl.when(t == c)
            def _():
                att[:, lanes] = natural

            @pl.when(t != c)
            def _():
                att_s[:, pl.ds(p * 128, 128)] = natural

            for n in range(2):
                slot((AT_A, p, n), t == n)

        att_copy(p, True).start()

    attend(0)
    attend(1)

    attend(2)

    loads[17].wait()
    swap_c.wait_recv()

    @pl.loop(0, 512 // TILE)
    def _(i):
        at = i * TILE
        gf[rows_of(own + at, TILE)] = (gate_two * ctb[rows_of(at, TILE)].astype(F32)).astype(BF)

    core_rows(gf, own, 512, 7).start()
    vec[...] = jnp.zeros_like(vec)
    late[...] = jnp.zeros_like(late)

    @pl.loop(0, 512 // TILE)
    def _(i):
        vec[8:9] += jnp.sum(gf[rows_of(own + i * TILE, TILE)].astype(F32), axis=0, keepdims=True)

    for p in range(3):
        remote(
            att_s.at[:, pl.ds(p * 128, 128)],
            att.at[:, pl.ds(pl.multiple_of((1 - c) * 384 + p * 128, 128), 128)],
            4 + p,
            TO_CORE,
        ).wait_recv()
    loads[14].wait()

    core_rows(ai, own + x * 256, 256, 2).wait_send()
    core_rows(ai, own + (1 - x) * 256, 256, 3).wait_send()
    fi = ai

    @pl.loop(0, 2)
    def _(b):
        rows = rows_of(b * 256, 256)
        ap[rows] = dot(att[rows], wo[...])
        slot((AT_W, 3), b == 0)
        slot((AT_W, 4), b == 1)

        @pl.loop(0, 256 // TILE)
        def _(i):
            at = b * 256 + i * TILE
            tile = rows_of(at, TILE)
            middle = xb[tile].astype(F32) + gate_one * ap[tile]
            normed, inv = layer_norm(middle)
            n2[tile] = normed
            inv_s[tile, 1:2] = inv
            fi[rows_of(own + at, TILE)] = (normed * mul_two + shift_two).astype(BF)

    core_rows(fi, own, 512, 8).start()
    slot((AT_W, 1))

    def turn(src, dst, start):
        @pl.loop(0, 2)
        def _(t):
            rows = rows_of(start + t * 256, 256)
            dst[:, rows] = src[rows].T

    slot((AT_W, 2))

    for p in range(3):
        att_copy(p, False).wait_send()

    coef = 0.7978845608028654

    @pl.loop(0, Z)
    def _(k):
        j = pick([order(n) for n in range(Z)], k)

        for n in range(Z):
            slot((AT_F, n), k == n)

        @pl.when(j != z)
        def _():
            for item in across_waits(j):
                item.wait_recv()

        bias = ub[j][:, pl.ds(0, 384)]
        bias = jnp.where(c == 0, bias, ub[j][:, pl.ds(384, 384)])

        @pl.loop(0, 2)
        def _(t):
            @pl.when((k == 0) & (t == 1))
            def _():
                turn(gf, gft, own)
                turn(fi, fit, own)
                core_rows(gf, other, 512, 7).wait_recv()
                turn(gf, gft, other)
                core_rows(fi, other, 512, 8).wait_recv()
                turn(fi, fit, other)

            rows = rows_of(jnp.where(t == 0, own, other), 512)
            pre = dot(fi[rows], wu[j]) + bias
            sq = pre * pre
            upper = 0.5 + 0.5 * jnp.tanh(pre * (coef + (coef * 0.044715) * sq))
            act = (pre * upper).astype(BF)
            slope = upper + pre * (2.0 * upper * (1.0 - upper)) * (coef + (3.0 * 0.044715 * coef) * sq)
            a_s[rows] = act
            grad_pre = (dot_t(gf[rows], wd[j]) * slope).astype(BF)
            gp_s[rows] = grad_pre
            bsum = jnp.sum(grad_pre.astype(F32), axis=0, keepdims=True)
            out = dot(act, wd[j])
            gin = dot_t(grad_pre, wu[j])

            @pl.when(k == 0)
            def _():
                oacc[rows] = out
                gacc[rows] = gin

            @pl.when(k > 0)
            def _():
                oacc[rows] += out
                gacc[rows] += gin

            for m in range(Z):
                for n in range(2):
                    slot((AT_T, m, n), (k == m) & (t == n))

            @pl.when(t == 0)
            def _():
                ubg[j] = bsum

            @pl.when(t > 0)
            def _():
                ubg[j] += bsum

        g_s[0, j] = dot(fit[...], gp_s[...]).astype(BF)
        g_s[1, j] = dot(gft[...], a_s[...]).astype(BF)

        for n in range(Z):
            slot((AT_G, n), k == n)

    def give_credit():
        @pl.when(z > 0)
        def _():
            pl.semaphore_signal(credit.at[0], 1, device_id=LEFT, device_id_type=MESH)

        @pl.when(z < Z - 1)
        def _():
            pl.semaphore_signal(credit.at[1], 1, device_id=RIGHT, device_id_type=MESH)

    def take_credit():
        @pl.when(z < Z - 1)
        def _():
            pl.semaphore_wait(credit.at[0], 1)

        @pl.when(z > 0)
        def _():
            pl.semaphore_wait(credit.at[1], 1)


    def weight_waits(k):
        @pl.when(z - k >= 0)
        def _():
            @pl.when(z < Z - 1)
            def _():
                for item in z_copies(z - k, 0, RIGHT, False):
                    item.wait_send()

            for item in quarter_sends(z - k) + across_sends(z - k):
                item.wait_send()

        @pl.when(z + k <= Z - 1)
        def _():
            @pl.when(z > 0)
            def _():
                for item in z_copies(z + k, 1, LEFT, False):
                    item.wait_send()

            for item in quarter_sends(z + k) + across_sends(z + k):
                item.wait_send()

    @pl.when(z < Z - 1)
    def _():
        for item in z_copies(z, 0, RIGHT, False):
            item.wait_send()

    @pl.when(z > 0)
    def _():
        for item in z_copies(z, 1, LEFT, False):
            item.wait_send()

    pl.loop(1, Z)(weight_waits)
    give_credit()

    osend, gsend = xs.at[0], xs.at[1]

    @pl.loop(0, 512 // TILE)
    def _(i):
        tile = rows_of(i * TILE, TILE)
        far = rows_of(other + i * TILE, TILE)
        gsend[tile] = gacc[far].astype(BF)

    remote(gsend, grecv, 9, TO_CORE).start()

    @pl.loop(0, 512 // TILE)
    def _(i):
        osend[rows_of(i * TILE, TILE)] = oacc[rows_of(other + i * TILE, TILE)].astype(BF)

    orecv = att
    remote(osend, orecv, 10, TO_CORE).start()
    remote(gsend, grecv, 9, TO_CORE).wait_recv()
    core_rows(gf, own, 512, 7).wait_send()

    def norm_back(grad, normed, inv):
        return inv * (
            grad
            - jnp.mean(grad, axis=-1, keepdims=True)
            - normed * jnp.mean(grad * normed, axis=-1, keepdims=True)
        )

    @pl.loop(0, 512 // TILE)
    def _(i):
        tile = rows_of(i * TILE, TILE)
        near = rows_of(own + i * TILE, TILE)
        grad = gacc[near] + grecv[tile].astype(F32)
        normed = n2[tile]
        vec[3:4] += jnp.sum(grad, axis=0, keepdims=True)
        vec[4:5] += jnp.sum(grad * normed, axis=0, keepdims=True)
        middle = ctb[tile].astype(F32) + norm_back(grad * mul_two, normed, inv_s[tile, 1:2])
        n2[tile] = middle
        gf[near] = (gate_one * middle).astype(BF)
        vec[2:3] += jnp.sum(middle * ap[tile], axis=0, keepdims=True)

    gproj = gf
    core_rows(gproj, own, 512, 11).start()
    slot((AT_N, 1))

    remote(osend, orecv, 10, TO_CORE).wait()

    def rows_out(number, i, values):
        xs[number, rows_of(i * TILE, TILE)] = values.astype(BF)

    def out_copy(out_ref, number):
        return local(xs.at[number, rows_of(x * 256, 256)], out_ref.at[x], 55 + number)

    @pl.loop(0, 512 // TILE)
    def _(i):
        tile = rows_of(i * TILE, TILE)
        ffn = oacc[rows_of(own + i * TILE, TILE)] + orecv[tile].astype(F32) + downb
        vec[5:6] += jnp.sum(ctb[tile].astype(F32) * ffn, axis=0, keepdims=True)
        rows_out(0, i, xb[tile].astype(F32) + gate_one * ap[tile] + gate_two * ffn)

    out_copy(out_o, 0).start()

    core_rows(gproj, other, 512, 11).wait_recv()
    slot((AT_N, 2))

    @pl.loop(0, 4)
    def _(t):
        rows = rows_of(t * 256, 256)
        grad = dot_t(gproj[rows], wo[rows_of(c * 384, 384)])
        for p in range(3):
            part = grad[:, p * 128 : (p + 1) * 128].astype(BF)
            do_s[p, rows] = part
            product = part.astype(F32).T * ot_s[p, :, rows]
            for h in range(2):
                dlt[p, pl.ds(h, 1), rows] = jnp.sum(
                    product[h * 64 : (h + 1) * 64], axis=0, keepdims=True
                )

    slot((AT_N, 3))

    slope_two = vec[4:5]
    vec[7:8] = slope_two * (1.0 + scale_two)
    vec[4:5] = slope_two * fgain
    for core in range(2):
        @pl.when(c == core)
        def _():
            for j in range(4):
                vec[9 + 2 * core + j // 2, pl.ds((j % 2) * 384, 384)] = ubg[j, 0]

    both = cond[...].astype(F32)
    vec[13:14, :128] = 0.5 * jnp.where(x == 0, both[0:1], both[1:2])
    remote(vec, vecr, 30, TO_CORE).start()
    chip = 2 * z + x

    def vec_part(ref, kind, slot_=None):
        ref = ref if slot_ is None else ref.at[pl.ds(slot_, 1)]
        if kind == 0:
            return ref.at[:, rows_of(c * 8, 8)]
        return ref.at[:, pl.ds(16, 8), half]

    def vec_copy(kind, n, slot_):
        part = vec_part(vall, kind, slot_)
        return pltpu.make_async_remote_copy(
            src_ref=part, dst_ref=part, send_sem=vss.at[kind, n], recv_sem=vrs.at[kind, n],
            device_id=peers[n], device_id_type=MESH,
        )

    for p in range(3):
        @pl.loop(0, 2)
        def _(n):
            lanes = pl.ds(pl.multiple_of(n * 384, 128), 384)
            b_s[0, rows_of(n * 384 + p * 128, 128)] = dot(
                ot_s[p].astype(BF), gproj[:, lanes]
            ).astype(BF)

    remote(vec, vecr, 30, TO_CORE).wait_recv()
    vall[chip, pl.ds(0, 16)] = vec[...] + vecr[...]
    for n in range(len(peers)):
        vec_copy(0, n, chip).start()

    take_credit()
    slot((AT_N, 4))

    def attend_back(p):
        for h in range(2):
            a_s[:, h * 128 : (h + 1) * 128] = q_s[p] * keep[h]
            gp_s[:, h * 128 : (h + 1) * 128] = do_s[p] * keep[h]
        dqt[...] = jnp.zeros_like(dqt)

        @pl.loop(0, 2)
        def _(t):
            rows = rows_of(t * 512, 512)
            keys, values = k_s[p, rows], v_s[p, rows]
            dv, dk = None, None
            for h in range(2):
                qm, dom = a_s[:, h * 128 : (h + 1) * 128], gp_s[:, h * 128 : (h + 1) * 128]
                probs = jnp.exp(dot_t(keys, qm) - lse[p, pl.ds(h, 1), :])
                grads = dot_t(values, dom)
                ds = (probs * (grads - dlt[p, pl.ds(h, 1), :])).astype(BF)
                dv_h = dot(probs.astype(BF), dom)
                dk_h = dot(ds, qm)
                dv = dv_h if dv is None else dv + dv_h
                dk = dk_h if dk is None else dk + dk_h
                dqt[pl.ds(h * 64, 64)] += dot(kt_s[p, pl.ds(h * 64, 64), rows], ds)
            cos_t, sin_t = cos_v[rows], sin_v[rows]
            gq[p, rows, pl.ds(128, 128)] = (dk * cos_t - swap_halves(dk) * sin_t).astype(BF)
            gq[p, rows, pl.ds(256, 128)] = dv.astype(BF)

            for n in range(2):
                slot((AT_B, p, n), t == n)

        @pl.loop(0, 4)
        def _(t):
            rows = rows_of(t * 256, 256)
            block = dqt[:, rows] * 0.125
            cos_t, sin_t = cost[:, rows], sint[:, rows]
            parts = []
            for h in range(2):
                u, w = block[h * 64 : h * 64 + 32], block[h * 64 + 32 : h * 64 + 64]
                parts += [u * cos_t + w * sin_t, w * cos_t - u * sin_t]
            gq[p, rows, pl.ds(0, 128)] = jnp.concatenate(parts, axis=0).T.astype(BF)

        b_s[1 + p] = dot(ait[...], gq[p]).astype(BF)
        slot((AT_B, p, 5))

    remote(gsend, grecv, 9, TO_CORE).wait_send()
    for p in range(3):
        attend_back(p)

    @pl.loop(0, 4)
    def _(t):
        rows = rows_of(t * 256, 256)
        part = dot_t(gq[0, rows], wq[0])
        for p in range(1, 3):
            part = part + dot_t(gq[p, rows], wq[p])
        gacc[rows] = part
        for n in range(4):
            slot((AT_B, 3, n), t == n)

    @pl.loop(0, 512 // TILE)
    def _(i):
        gsend[rows_of(i * TILE, TILE)] = gacc[rows_of(other + i * TILE, TILE)].astype(BF)

    remote(gsend, grecv, 11 + 26, TO_CORE).start()
    slot((AT_E, 0))
    remote(gsend, grecv, 11 + 26, TO_CORE).wait()

    @pl.loop(0, 512 // TILE)
    def _(i):
        tile = rows_of(i * TILE, TILE)
        near = rows_of(own + i * TILE, TILE)
        grad = gacc[near] + grecv[tile].astype(F32)
        normed = n1[tile]
        late[0:1] += jnp.sum(grad, axis=0, keepdims=True)
        late[1:2] += jnp.sum(grad * normed, axis=0, keepdims=True)
        rows_out(1, i, n2[tile] + norm_back(grad * mul_one, normed, inv_s[tile, 0:1]))

    out_copy(gin_o, 1).start()
    slot((AT_E, 1))
    slope_one = late[1:2]
    late[2:3] = slope_one * (1.0 + scale_one)
    late[1:2] = slope_one * again
    remote(late, later, 38, TO_CORE).start()
    slot((AT_E, 2))
    remote(late, later, 38, TO_CORE).wait_recv()
    vall[chip, pl.ds(16, 8)] = late[...] + later[...]
    for n in range(len(peers)):
        vec_copy(1, n, chip).start()
    slot((AT_D, 0))
    for kind in range(2):
        for n in range(len(peers)):
            vec_copy(kind, n, 2 * peers[n]["mlp"] + peers[n]["seq"] // 2).wait_recv()

    def vec_out(kind):
        src, dst = vec_part(vall, kind), vec_part(vall_o, kind)
        return [local(src, dst, 57 - 56 * kind), remote(src, dst, 39 + kind, TO_CORE)]

    for item in vec_out(0) + vec_out(1):
        item.start()

    for number, ref in ((0, out_o), (1, gin_o)):
        out_copy(ref, number).wait()
        for part in range(2):
            cross_rows(ref, number, part).wait()
    for p in range(4):
        for item in piece_copies(p):
            item.wait()
    for h in range(CH):
        for item in final_copies(g_s.at[x, z, span(h)], x, h, 0) + final_copies(fxr.at[span(h)], 1 - x, h, 1):
            item.wait()
        own_copy(h).wait_send()
    for kind in range(2):
        for item in vec_out(kind):
            item.wait()
        for n in range(len(peers)):
            vec_copy(kind, n, chip).wait_send()
    swap_x.wait_send()
    swap_c.wait_send()
    core_rows(fi, own, 512, 8).wait_send()
    core_rows(gproj, own, 512, 11).wait_send()
    remote(vec, vecr, 30, TO_CORE).wait_send()
    remote(late, later, 38, TO_CORE).wait_send()
    for place in range(Z):
        @pl.when(z == place)
        def _(place=place):
            for make in pending[place]:
                make().wait_send()


def finish_kernel(
    out_h, gin_h, qkv_h, outw_h, ffn_h, vall_h, adaw_h,
    out_o, gin_o, cond_o, again_o, adaw_o, adab_o, qkv_o, outw_o, fgain_o, up_o, upb_o, down_o, downb_o,
    tok_b, qkv_b, outw_b, ffn_b, adaw, vall, tok_f, qkv_f, outw_f, ffn_f, adaw_f, cond_s, isem, osem,
):
    z = lax.axis_index("mlp")
    D = 768
    loads, steps = [], []

    def step(src, buffer, result, dst, turn=False):
        number = len(steps)
        loads.append(pltpu.make_async_copy(src, buffer, isem.at[number]))
        store = pltpu.make_async_copy(result, dst, osem.at[number])

        def body():
            loads[number].wait()
            values = buffer[...].astype(F32)
            result[...] = values.T if turn else values
            store.start()

        steps.append((body, store))

    vall_copy = pltpu.make_async_copy(vall_h, vall, isem.at[30])
    adaw_copy = pltpu.make_async_copy(adaw_h, adaw, isem.at[31])
    for n in range(6):
        rows = pl.ds(n * 128, 128)
        step(qkv_h.at[rows], qkv_b.at[rows], qkv_f.at[rows], qkv_o.at[rows])
    for n in range(2):
        rows = pl.ds(n * 384, 384)
        step(outw_h.at[rows], outw_b.at[rows], outw_f.at[rows], outw_o.at[rows])
        step(ffn_h.at[0, rows], ffn_b.at[0, rows], ffn_f.at[0, rows], up_o.at[rows])
    for n in range(3):
        rows = pl.ds(n * 256, 256)
        step(ffn_h.at[1, rows], ffn_b.at[1, rows], ffn_f.at[1, :, rows], down_o.at[:, rows], True)
    for n in range(2):
        step(out_h.at[n], tok_b.at[0, n], tok_f.at[0, n], out_o.at[n])
        step(gin_h.at[n], tok_b.at[1, n], tok_f.at[1, n], gin_o.at[n])
    for item in loads[:6] + [vall_copy, adaw_copy] + loads[6:]:
        item.start()
    for body, _ in steps[:6]:
        body()
    vall_copy.wait()
    adaw_copy.wait()
    high = lax.Precision.HIGHEST
    everyone = vall[:, 13, :128]
    total = vall[0]
    for n in range(1, 8):
        total = total + vall[n]
    acc, ada_out = None, []
    for part in range(6):
        lanes = pl.ds(part * D, D)
        row = part if part > 1 else 16 + part
        grads = vall[:, row, :]
        adab_o[lanes] = total[row]
        adaw_f[part] = lax.dot_general(
            everyone, grads, (((0,), (0,)), ((), ())), precision=high, preferred_element_type=F32
        )
        ada_out.append(pltpu.make_async_copy(adaw_f.at[part], adaw_o.at[:, lanes], osem.at[26 + part]))
        ada_out[-1].start()
        piece = lax.dot_general(
            grads, adaw[:, lanes].astype(F32), (((1,), (1,)), ((), ())), precision=high,
            preferred_element_type=F32,
        )
        acc = piece if acc is None else acc + piece
    for body, _ in steps[6:]:
        body()
    cond_s[...] = acc
    cond_o[...] = cond_s[pl.ds(2 * z, 2), :]
    again_o[...] = total[18]
    fgain_o[...] = total[7]
    downb_o[...] = total[8]
    for core in range(2):
        halves = [total[9 + 2 * core + j // 2, (j % 2) * 384 : (j % 2 + 1) * 384] for j in range(4)]
        mine = halves[0]
        for j in range(1, 4):
            mine = jnp.where(z == j, halves[j], mine)
        upb_o[pl.ds(core * 384, 384)] = mine
    for item in ada_out:
        item.wait()
    for _, store in steps:
        store.wait()


def tables(seg_len, seq_size):
    half = np.arange(32)
    frequency = 10000.0 ** (-2.0 * half / 64)
    core, chip, token = np.meshgrid(
        np.arange(2), np.arange(seq_size // 2), np.arange(seg_len), indexing="ij"
    )
    place = ((chip * 2 + core) * seg_len + token).reshape(-1)
    angle = place[:, None] * frequency[None, :]
    cos, sin = np.cos(angle).astype(np.float32), np.sin(angle).astype(np.float32)
    return (
        np.tile(cos, (1, 4)),
        np.concatenate([-sin, sin, -sin, sin], axis=1),
        np.ascontiguousarray(cos.T),
        np.ascontiguousarray(sin.T),
    )


def fast_shards(
    inputs, condition, attn_gain, ada_weight, ada_bias, qkv_weight, out_weight, ffn_gain,
    up_weight, up_bias, down_weight, down_bias, cotangent,
):
    Z = lax.axis_size("mlp")
    tabs = [jnp.asarray(t) for t in tables(inputs.shape[1], lax.axis_size("seq"))]
    hbm, vm = pl.BlockSpec(memory_space=pl.ANY), pl.BlockSpec(memory_space=pltpu.VMEM)
    shape = jax.ShapeDtypeStruct
    V = pltpu.VMEM
    dma = pltpu.SemaphoreType.DMA
    scratch = [
        V((3, 768, 384), BF), V((768, 768), BF), V((Z, 768, 384), BF),
        V((Z, 384, 768), BF), V((Z, 1, 768), F32), V((1024, 128), F32), V((1024, 128), F32),
        V((32, 1024), F32), V((32, 1024), F32),
        V((512, 768), BF), V((512, 768), BF), V((2, 4608), F32), V((512, 768), F32), V((512, 2), F32),
        V((1024, 768), BF), V((768, 1024), BF),
        V((3, 1024, 128), BF), V((3, 1024, 128), BF), V((3, 1024, 128), BF),
        V((3, 128, 1024), BF), V((3, 128, 1024), BF), V((3, 128, 1024), F32), V((3, 2, 1024), F32),
        V((512, 768), BF),
        V((512, 768), F32), V((512, 768), F32),
        V((768, 1024), BF), V((1024, 768), BF), V((768, 1024), BF),
        V((1024, 768), F32), V((1024, 768), F32), V((1024, 384), BF), V((1024, 384), BF),
        V((2, Z, 768, 384), BF), V((512, 768), BF),
        V((3, 1024, 128), BF), V((3, 2, 1024), F32), V((128, 1024), F32),
        V((3, 1024, 384), BF), V((4, 768, 384), BF), V((2, 512, 768), BF),
        V((16, 768), F32), V((16, 768), F32), V((8, 768), F32), V((8, 768), F32),
        V((2 * Z, 24, 768), F32), V((Z, 1, 384), F32),
        V((Z, 768, 384), BF), V((Z, 768, 384), BF), V((768, 384), BF), V((4, 192, 384), BF),
        V((4, 768, 384), BF),
        dma((64,)), dma((41,)), dma((41,)), dma((2, Z, 3)), dma((2, Z, 3)), dma((Z, 4, 2)), dma((Z, 4, 2)),
        dma((Z, 3)), dma((Z, 3)), dma((4, 4, 4)), dma((4, 4, 4)), dma((10, 4)), dma((10, 4)), dma((2, 7)), dma((2, 7)),
        pltpu.SemaphoreType.REGULAR((2,)),
    ]
    token = shape(inputs.shape, BF)
    vall_shape = shape((2 * Z, 24, 768), F32)
    ffn_shape = shape((2, 768, 768), BF)
    out, gin, qkv, outw, ffn, vall = pl.pallas_call(
        fast_kernel,
        out_shape=[
            token, token, shape(qkv_weight.shape, BF), shape(out_weight.shape, BF), ffn_shape, vall_shape,
        ],
        in_specs=[hbm, vm, vm, hbm, vm, hbm, hbm, vm, hbm, vm, hbm, vm, hbm, hbm, hbm, hbm, hbm],
        out_specs=[hbm] * 6,
        scratch_shapes=scratch,
        compiler_params=pltpu.CompilerParams(
            collective_id=0, has_side_effects=True, vmem_limit_bytes=VMEM_LIMIT
        ),
        name="block",
    )(
        inputs, condition, attn_gain, ada_weight, ada_bias, qkv_weight, out_weight,
        ffn_gain, up_weight, up_bias, down_weight, down_bias, cotangent, *tabs,
    )
    same = lambda v: shape(v.shape, F32)
    tokens = shape(inputs.shape, F32)
    return pl.pallas_call(
        finish_kernel,
        out_shape=[
            tokens, tokens, same(condition), same(attn_gain), same(ada_weight), same(ada_bias),
            same(qkv_weight), same(out_weight), same(ffn_gain), same(up_weight), same(up_bias),
            same(down_weight), same(down_bias),
        ],
        in_specs=[hbm] * 7,
        out_specs=[hbm, hbm, vm, vm, hbm, vm, hbm, hbm, vm, hbm, vm, hbm, vm],
        scratch_shapes=[
            V((2, *inputs.shape), BF), V(qkv_weight.shape, BF), V(out_weight.shape, BF), V((2, 768, 768), BF),
            V(ada_weight.shape, BF), V((2 * Z, 24, 768), F32), V((2, *inputs.shape), F32),
            V(qkv_weight.shape, F32), V(out_weight.shape, F32), V((2, 768, 768), F32), V((6, 128, 768), F32),
            V((2 * Z, 128), F32), dma((32,)), dma((32,)),
        ],
        compiler_params=pltpu.CompilerParams(vmem_limit_bytes=VMEM_LIMIT),
        name="finish",
    )(out, gin, qkv, outw, ffn, vall, ada_weight)


def solution(mesh):
    placed = (
        P(("grp", "mlp"), "seq", None),
        P(("grp", "mlp"), None),
        P(),
        P(),
        P(),
        P(),
        P(),
        P(),
        P(None, "mlp"),
        P("mlp"),
        P("mlp", None),
        P(),
        P(("grp", "mlp"), "seq", None),
    )
    sizes = dict(mesh.shape)
    small = sizes["seq"] == 4 and sizes["grp"] == 2 and sizes["mlp"] == 4
    return jax.shard_map(
        fast_shards if small else shards,
        mesh=mesh,
        in_specs=placed,
        out_specs=(
            P(("grp", "mlp"), "seq", None),
            P(("grp", "mlp"), "seq", None),
            P(("grp", "mlp"), None),
            P("grp"),
            P("grp", None),
            P("grp"),
            P("grp", None),
            P("grp", None),
            P("grp"),
            P("grp", "mlp"),
            P(("grp", "mlp")),
            P(("grp", "mlp"), None),
            P("grp"),
        ),
        check_vma=False,
    )
```
